32 devices in a mesh: ctx: 4 (over x, core), fsdp: 8 (over z, y).
Axes of the slice: x: 2, y: 2, z: 4, core: 2. Of those that a mesh axis runs over, the one named last changes fastest.
Arguments:
- tokens: bfloat16 [8, 2048, 768], P('fsdp', 'ctx'), may hold values from -6 to 6
- dealt: int32 [8, 2048], P('fsdp'), may hold values from 0 to 2047, as said below
- segments: int32 [8, 2048], P('fsdp'), may hold values from 0 to 2, never falling along the last dimension, each value on 1 to 1024 neighbouring positions
- query_weight: bfloat16 [768, 768], P('fsdp'), may hold values from -0.14433757 to 0.14433757
- key_weight: bfloat16 [768, 768], P('fsdp'), may hold values from -0.14433757 to 0.14433757
- value_weight: bfloat16 [768, 768], P('fsdp'), may hold values from -0.14433757 to 0.14433757
- query_bias: bfloat16 [768], P('fsdp'), may hold values from -3 to 3
- value_bias: bfloat16 [768], P('fsdp'), may hold values from -3 to 3
- output_weight: bfloat16 [768, 768], P('fsdp'), may hold values from -0.875 to 0.875
- output_bias: bfloat16 [768], P('fsdp'), may hold values from -3 to 3
- first_gain: bfloat16 [768], P('fsdp'), may hold values from 0.099609375 to 1.8984375
- first_shift: bfloat16 [768], P('fsdp'), may hold values from -2 to 2
- inner_weight: bfloat16 [768, 3072], P('fsdp'), may hold values from -0.21875 to 0.21875
- inner_bias: bfloat16 [3072], P('fsdp'), may hold values from -3 to 3
- outer_weight: bfloat16 [3072, 768], P('fsdp'), may hold values from -0.15625 to 0.15625
- outer_bias: bfloat16 [768], P('fsdp'), may hold values from -2 to 2
- second_gain: bfloat16 [768], P('fsdp'), may hold values from 0.099609375 to 1.8984375
- second_shift: bfloat16 [768], P('fsdp'), may hold values from -2 to 2
- project_weight: bfloat16 [768, 128], P('fsdp'), may hold values from -0.21875 to 0.21875
- cotangent: bfloat16 [8, 2048, 128], P('fsdp', 'ctx'), may hold values from -6 to 6
Outputs:
- embeddings: bfloat16 [8, 2048, 128], P('fsdp', 'ctx')
- tokens_delta: bfloat16 [8, 2048, 768], P('fsdp', 'ctx')
- query_weight_delta: float32 [768, 768], P('fsdp')
- key_weight_delta: float32 [768, 768], P('fsdp')
- value_weight_delta: float32 [768, 768], P('fsdp')
- query_bias_delta: float32 [768], P('fsdp')
- value_bias_delta: float32 [768], P('fsdp')
- output_weight_delta: float32 [768, 768], P('fsdp')
- output_bias_delta: float32 [768], P('fsdp')
- first_gain_delta: float32 [768], P('fsdp')
- first_shift_delta: float32 [768], P('fsdp')
- inner_weight_delta: float32 [768, 3072], P('fsdp')
- inner_bias_delta: float32 [3072], P('fsdp')
- outer_weight_delta: float32 [3072, 768], P('fsdp')
- outer_bias_delta: float32 [768], P('fsdp')
- second_gain_delta: float32 [768], P('fsdp')
- second_shift_delta: float32 [768], P('fsdp')
- project_weight_delta: float32 [768, 128], P('fsdp')
The draws below stay inside these ranges and needn't reach their ends.
Inputs may be any that keep to these rules, and one draw needn't show every extreme that they name: Each group's row is a permutation of the group's positions; dealt position d * 512 + s * 128 + i, 0 <= i < 128, holds a token of given positions s * 512 to (s + 1) * 512 - 1. `segments`: sequence numbers never fall along a group.
All inputs are finite; a program needn't handle non-finite values.
Results may differ from the reference program's by a relative error of at most 0.025.
Values may be sent and summed in bfloat16 or wider, within the bound.
No kernel may reach another device: no remote copies, remote signals or barrier semaphores. Data moves between devices by JAX's collectives and lax.ppermute only.
A program may use at most 256 MiB of HBM per device.

```python
import math
import jax
import jax.numpy as jnp
import numpy as np
from jax import lax

HEADS = 12
HEAD_DIM = 64
FF = 3072
P_SIZE = 128
TOK_DEV = 512
SEQS = 3
D = 768
PEERS = 4
GROUPS = 8
GROUP_TOK = 2048
SHARE = 128


def shuffle_one(single):
    return jax.random.permutation(single, TOK_DEV)


def clipped_normal(key, shape, spread, limit):
    values = jax.random.normal(key, shape, jnp.float32)
    return jnp.clip(values, -limit, limit) * spread


def draw_dealt(key, part):
    key = jax.random.fold_in(key, 11)
    many = jax.random.split(key, GROUPS * PEERS)
    shuffled = jax.vmap(shuffle_one)(many).astype(jnp.int32)
    shuffled = shuffled.reshape(GROUPS, PEERS, PEERS, SHARE)
    offsets = (jnp.arange(PEERS, dtype=jnp.int32) * TOK_DEV).reshape(1, PEERS, 1, 1)
    placed = jnp.transpose(shuffled + offsets, (0, 2, 1, 3))
    return placed.reshape(GROUPS, GROUP_TOK).astype(jnp.int32)


def draw_tokens(key, part):
    key = jax.random.fold_in(key, 21)
    return clipped_normal(key, (GROUPS, GROUP_TOK, D), 1.0, 6.0).astype(jnp.bfloat16)


def draw_query_weight(key, part):
    key = jax.random.fold_in(key, 31)
    return clipped_normal(key, (D, D), D ** (-0.5), 3.9).astype(jnp.bfloat16)


def draw_key_weight(key, part):
    key = jax.random.fold_in(key, 41)
    return clipped_normal(key, (D, D), D ** (-0.5), 3.9).astype(jnp.bfloat16)


def draw_value_weight(key, part):
    key = jax.random.fold_in(key, 51)
    return clipped_normal(key, (D, D), D ** (-0.5), 3.9).astype(jnp.bfloat16)


def block_scale(own_key, extent, cuts, low, high):
    loudness = 1.0
    for dim, parts in cuts:
        heights = jax.random.uniform(jax.random.fold_in(jax.random.fold_in(own_key, 6), dim), (parts,), jnp.float32, low / len(cuts), high / len(cuts))
        loudness = loudness * jnp.repeat(jnp.exp(heights), extent[dim] // parts).reshape((-1,) + (1,) * (len(extent) - 1 - dim))
    return loudness


def split_up(count, total, most, lean):
    loads = [(1 << 20) // math.isqrt(grade ** lean) + 1 for grade in range(2, count + 1)]
    rest, given = total - most - (count - 1), [1] * (count - 1)
    while rest > 0:
        free = [i for i in range(count - 1) if given[i] < most]
        mass, left = sum([loads[i] for i in free]), rest
        for i in free:
            more = min(most - given[i], max(1, left * loads[i] // mass), rest)
            given[i] = given[i] + more
            rest = rest - more
    return np.array([most] + given)


def ragged_sizes(own_key, number_of, total, most, lean):
    if number_of == 2:
        one = jax.random.randint(own_key, (), max(1, total - most), min(most, total - 1) + 1)
        return jnp.stack([one, total - one])
    lengths = jnp.asarray(split_up(number_of, total, most, lean), jnp.int32)
    twos = (number_of - 1) // 2
    donor, taker = lengths[1:1 + 2 * twos:2], lengths[2:2 + 2 * twos:2]
    margin = jnp.minimum(donor - 1, most - taker)
    shifted = jax.random.randint(jax.random.fold_in(own_key, 1), (twos,), 0, 1 << 20) % (margin + 1)
    lengths = lengths.at[1:1 + 2 * twos:2].set(donor - shifted).at[2:2 + 2 * twos:2].set(taker + shifted)
    return lengths[jax.random.permutation(jax.random.fold_in(own_key, 2), number_of)]


def normal_values(stream_key, shape, width, bound, cuts=(), kind=jnp.bfloat16):
    level = block_scale(stream_key, shape, cuts, -0.22, 0.18) if cuts else 1.0
    drawn = jax.random.normal(stream_key, shape, jnp.float32) * width * level
    return jnp.minimum(jnp.maximum(drawn, -bound), bound).astype(kind)


def setup_inputs(seed: int = 0) -> dict:
    seeds = jax.random.split(jax.random.key(seed), 21)
    return {
        "tokens": draw_tokens(jax.random.fold_in(seeds[20], 71), 0),
        "dealt": draw_dealt(jax.random.fold_in(seeds[20], 71), 0),
        "segments": jax.vmap(lambda own: jnp.searchsorted(jnp.cumsum(ragged_sizes(own, SEQS, GROUP_TOK, GROUP_TOK // 2, 2)), jnp.arange(GROUP_TOK), side="right"))(jax.random.split(seeds[2], GROUPS)).reshape((GROUPS, GROUP_TOK)).astype(jnp.int32),
        "query_weight": draw_query_weight(jax.random.fold_in(seeds[20], 71), 0),
        "key_weight": draw_key_weight(jax.random.fold_in(seeds[20], 71), 0),
        "value_weight": draw_value_weight(jax.random.fold_in(seeds[20], 71), 0),
        "query_bias": normal_values(seeds[6], (D,), 0.5, 3.0, ((0, 8),)),
        "value_bias": normal_values(seeds[7], (D,), 0.5, 3.0, ((0, 8),)),
        "output_weight": normal_values(seeds[8], (D, D), (D // 16) ** -0.5, 0.875, ((0, 8),)),
        "output_bias": normal_values(seeds[9], (D,), 0.5, 3.0, ((0, 8),)),
        "first_gain": jnp.clip(1.0 + 0.18 * jax.random.normal(seeds[10], (D,), jnp.float32), 0.099609375, 1.8984375).astype(jnp.bfloat16),
        "first_shift": normal_values(seeds[11], (D,), 0.3, 2.0, ((0, 8),)),
        "inner_weight": normal_values(seeds[12], (D, FF), D ** -0.5, 0.21875, ((0, 8),)),
        "inner_bias": normal_values(seeds[13], (FF,), 0.5, 3.0, ((0, 8),)),
        "outer_weight": normal_values(seeds[14], (FF, D), (FF // 2) ** -0.5, 0.15625, ((0, 8),)),
        "outer_bias": normal_values(seeds[15], (D,), 0.3, 2.0, ((0, 8),)),
        "second_gain": jnp.clip(1.0 + 0.18 * jax.random.normal(seeds[16], (D,), jnp.float32), 0.099609375, 1.8984375).astype(jnp.bfloat16),
        "second_shift": normal_values(seeds[17], (D,), 0.3, 2.0, ((0, 8),)),
        "project_weight": normal_values(seeds[18], (D, P_SIZE), D ** -0.5, 0.21875, ((0, 8),)),
        "cotangent": normal_values(seeds[19], (GROUPS, GROUP_TOK, P_SIZE), 1.0, 6.0, ((0, 8), (1, 4))),
    }


@jax.custom_vjp
def low(v):
    return lax.optimization_barrier(v.astype(jnp.bfloat16)).astype(jnp.float32)

@jax.custom_vjp
def low_back(v):
    return v

def low_keep(v):
    return (low(v), None)

def low_pass(kept, grad):
    return (grad,)

def back_keep(v):
    return (v, None)

def back_low(kept, grad):
    return (low(grad),)
low.defvjp(low_keep, low_pass)
low_back.defvjp(back_keep, back_low)

def rounded(value):
    return low(low_back(value))

def product(left, right):
    return jnp.dot(left, right, precision=lax.Precision.HIGHEST, preferred_element_type=jnp.float32)

def layer_norm(value, gain, shift):
    centred = value - lax.optimization_barrier(jnp.mean(value, axis=-1, keepdims=True))
    inverse = lax.rsqrt(lax.optimization_barrier(jnp.mean(centred * centred, axis=-1, keepdims=True)) + 1e-12)
    return centred * inverse * gain + shift

def forward(params, group_tokens, group_segments, group_dealt):
    query_weight, key_weight, value_weight, query_bias, value_bias, output_weight, output_bias, first_gain, first_shift, inner_weight, inner_bias, outer_weight, outer_bias, second_gain, second_shift, project_weight = params
    length = group_tokens.shape[0]
    block = min(512, length)
    scale = HEAD_DIM ** (-0.5)
    queries = rounded(product(group_tokens, query_weight) + query_bias)
    keys_all = rounded(product(group_tokens, key_weight))
    values_all = rounded(product(group_tokens, value_weight) + value_bias)
    key_heads = keys_all.reshape(length, HEADS, HEAD_DIM)
    value_heads = values_all.reshape(length, HEADS, HEAD_DIM)

    def attend(pieces):
        query_block, segment_block = pieces
        raw = jnp.einsum('qhd,khd->hqk', query_block, key_heads, precision=lax.Precision.HIGHEST)
        scores = low_back(raw * scale)
        allowed = (segment_block[:, None] == group_segments[None, :])[None]
        masked = jnp.where(allowed, scores, -1e+30)
        summit = lax.optimization_barrier(jnp.max(masked, axis=-1, keepdims=True))
        weights = jnp.where(allowed, jnp.exp(masked - summit), 0.0)
        probs = low(weights / lax.optimization_barrier(jnp.sum(weights, axis=-1, keepdims=True)))
        return jnp.einsum('hqk,khd->qhd', probs, value_heads, precision=lax.Precision.HIGHEST)
    mixed = lax.map(jax.checkpoint(attend), (queries.reshape(length // block, block, HEADS, HEAD_DIM), group_segments.reshape(length // block, block)))
    context = rounded(mixed.reshape(length, HEADS * HEAD_DIM))
    attended = low_back(product(context, output_weight) + output_bias)
    first = layer_norm(group_tokens + attended, first_gain, first_shift)
    inner = low_back(product(low(first), inner_weight) + inner_bias)
    active = low(jax.nn.gelu(inner, approximate=False))
    outer = low_back(product(active, outer_weight) + outer_bias)
    second = layer_norm(first + outer, second_gain, second_shift)
    projected = low_back(product(low(second), project_weight))
    normed = projected * lax.rsqrt(lax.optimization_barrier(jnp.sum(projected * projected, axis=-1, keepdims=True)) + 1e-06)
    return normed[group_dealt]

def reference(tokens, dealt, segments, query_weight, key_weight, value_weight, query_bias, value_bias, output_weight, output_bias, first_gain, first_shift, inner_weight, inner_bias, outer_weight, outer_bias, second_gain, second_shift, project_weight, cotangent):
    params = (query_weight.astype(jnp.float32), key_weight.astype(jnp.float32), value_weight.astype(jnp.float32), query_bias.astype(jnp.float32), value_bias.astype(jnp.float32), output_weight.astype(jnp.float32), output_bias.astype(jnp.float32), first_gain.astype(jnp.float32), first_shift.astype(jnp.float32), inner_weight.astype(jnp.float32), inner_bias.astype(jnp.float32), outer_weight.astype(jnp.float32), outer_bias.astype(jnp.float32), second_gain.astype(jnp.float32), second_shift.astype(jnp.float32), project_weight.astype(jnp.float32))

    def one_group(totals, pieces):
        group_tokens, group_dealt, group_segments, group_cotangent = pieces

        def run(params_in, tokens_in):
            return forward(params_in, tokens_in, group_segments, group_dealt)
        result, pullback = jax.vjp(run, params, group_tokens.astype(jnp.float32))
        param_deltas, token_delta = pullback(group_cotangent.astype(jnp.float32))
        totals = tuple((total + change for total, change in zip(totals, param_deltas)))
        return (totals, (result.astype(jnp.bfloat16), token_delta.astype(jnp.bfloat16)))
    zeros = tuple((jnp.zeros_like(param) for param in params))
    totals, outputs = lax.scan(one_group, zeros, (tokens, dealt, segments, cotangent))
    return (outputs[0], outputs[1], totals[0], totals[1], totals[2], totals[3], totals[4], totals[5], totals[6], totals[7], totals[8], totals[9], totals[10], totals[11], totals[12], totals[13], totals[14], totals[15])
```

```python
import functools

import jax
import jax.numpy as jnp
from jax import lax
from jax.experimental import pallas as pl
from jax.experimental.pallas import tpu as pltpu
from jax.sharding import PartitionSpec as P

HEADS = 12
HEAD_DIM = 64


def matmul(left, right):
    return jnp.dot(left, right, preferred_element_type=jnp.float32)


def norm_forward(value, gain, shift):
    centred = value - jnp.mean(value, axis=-1, keepdims=True)
    inverse = lax.rsqrt(jnp.mean(centred * centred, axis=-1, keepdims=True) + 1e-12)
    normal = centred * inverse
    return (normal * gain + shift, normal, inverse)


def norm_backward(upstream, normal, inverse, gain):
    scaled = upstream * gain
    first_mean = jnp.mean(scaled, axis=-1, keepdims=True)
    second_mean = jnp.mean(scaled * normal, axis=-1, keepdims=True)
    inward = inverse * (scaled - first_mean - normal * second_mean)
    return (inward, jnp.sum(upstream * normal, axis=0), jnp.sum(upstream, axis=0))


def gelu_slope(value):
    cumulative = 0.5 * (1.0 + jax.scipy.special.erf(value * 0.7071067811865476))
    return cumulative + value * jnp.exp(-0.5 * value * value) * 0.3989422804014327


def scored(query_heads, key_block, query_segments, segment_block, scale):
    scores = (
        jnp.einsum("qhd,khd->hqk", query_heads, key_block, preferred_element_type=jnp.float32)
        * scale
    )
    allowed = (query_segments[:, None] == segment_block[None, :])[None]
    return (scores, allowed)


def probabilities(scores, allowed, log_total):
    return jnp.where(allowed, jnp.exp(scores - log_total[..., None]), 0.0)


def log_totals(query_heads, key_blocks, query_segments, segment_blocks, scale):

    def log_advance(carry, pieces):
        running_max, running_sum = carry
        scores, allowed = scored(query_heads, pieces[0], query_segments, pieces[1], scale)
        masked = jnp.where(allowed, scores, -1e30)
        new_max = jnp.maximum(running_max, jnp.max(masked, axis=-1))
        fresh = jnp.sum(jnp.where(allowed, jnp.exp(masked - new_max[..., None]), 0.0), axis=-1)
        return ((new_max, running_sum * jnp.exp(running_max - new_max) + fresh), None)

    shape = (query_heads.shape[1], query_heads.shape[0])
    start = (jnp.full(shape, -1e30, jnp.float32), jnp.zeros(shape, jnp.float32))
    final = lax.scan(log_advance, start, (key_blocks, segment_blocks))[0]
    return final[0] + jnp.log(final[1])


def attend(query_heads, key_blocks, value_blocks, query_segments, segment_blocks, scale):
    log_total = log_totals(query_heads, key_blocks, query_segments, segment_blocks, scale)

    def attend_advance(carry, pieces):
        scores, allowed = scored(query_heads, pieces[0], query_segments, pieces[2], scale)
        probs = probabilities(scores, allowed, log_total).astype(jnp.bfloat16)
        return (
            carry
            + jnp.einsum("hqk,khd->qhd", probs, pieces[1], preferred_element_type=jnp.float32),
            None,
        )

    start = jnp.zeros(query_heads.shape, jnp.float32)
    mixed = lax.scan(attend_advance, start, (key_blocks, value_blocks, segment_blocks))[0]
    return (mixed, log_total)


def attend_backward(
    query_heads,
    key_blocks,
    value_blocks,
    query_segments,
    segment_blocks,
    scale,
    log_total,
    upstream,
):

    def first_pass(carry, pieces):
        scores, allowed = scored(query_heads, pieces[0], query_segments, pieces[2], scale)
        probs = probabilities(scores, allowed, log_total)
        delta_probs = jnp.einsum(
            "qhd,khd->hqk", upstream, pieces[1], preferred_element_type=jnp.float32
        )
        value_terms = jnp.einsum(
            "hqk,qhd->khd", probs.astype(jnp.bfloat16), upstream, preferred_element_type=jnp.float32
        )
        return (carry + jnp.sum(probs * delta_probs, axis=-1), value_terms)

    shape = (query_heads.shape[1], query_heads.shape[0])
    weighted, value_terms = lax.scan(
        first_pass, jnp.zeros(shape, jnp.float32), (key_blocks, value_blocks, segment_blocks)
    )

    def second_pass(carry, pieces):
        scores, allowed = scored(query_heads, pieces[0], query_segments, pieces[2], scale)
        probs = probabilities(scores, allowed, log_total)
        delta_probs = jnp.einsum(
            "qhd,khd->hqk", upstream, pieces[1], preferred_element_type=jnp.float32
        )
        delta_scores = (probs * (delta_probs - weighted[..., None])).astype(jnp.bfloat16)
        key_terms = jnp.einsum(
            "hqk,qhd->khd", delta_scores, query_heads, preferred_element_type=jnp.float32
        )
        return (
            carry
            + jnp.einsum(
                "hqk,khd->qhd", delta_scores, pieces[0], preferred_element_type=jnp.float32
            ),
            key_terms,
        )

    query_terms, key_terms = lax.scan(
        second_pass,
        jnp.zeros(query_heads.shape, jnp.float32),
        (key_blocks, value_blocks, segment_blocks),
    )
    return (query_terms * scale, key_terms * scale, value_terms)


def generic_device(
    tokens,
    dealt,
    segments,
    query_weight,
    key_weight,
    value_weight,
    query_bias,
    value_bias,
    output_weight,
    output_bias,
    first_gain,
    first_shift,
    inner_weight,
    inner_bias,
    outer_weight,
    outer_bias,
    second_gain,
    second_shift,
    project_weight,
    cotangent,
):
    peers = lax.axis_size("ctx")
    place = lax.axis_index("ctx")
    local_rows = tokens.shape[1]
    share = local_rows // peers
    order = dealt[0]
    table = (
        lax.dynamic_index_in_dim(order.reshape(peers, peers, share), place, 1, keepdims=False)
        - place * local_rows
    )
    flat_table = table.reshape(-1)
    home_tokens = tokens[0]
    width = home_tokens.shape[1]
    (
        query_full,
        key_full,
        value_full,
        output_full,
        query_shift,
        value_shift,
        output_shift,
        gain_one,
        shift_one,
    ) = (
        lax.all_gather(query_weight, "fsdp", axis=0, tiled=True),
        lax.all_gather(key_weight, "fsdp", axis=0, tiled=True),
        lax.all_gather(value_weight, "fsdp", axis=0, tiled=True),
        lax.all_gather(output_weight, "fsdp", axis=0, tiled=True),
        lax.all_gather(query_bias, "fsdp", axis=0, tiled=True),
        lax.all_gather(value_bias, "fsdp", axis=0, tiled=True),
        lax.all_gather(output_bias, "fsdp", axis=0, tiled=True),
        lax.all_gather(first_gain, "fsdp", axis=0, tiled=True),
        lax.all_gather(first_shift, "fsdp", axis=0, tiled=True),
    )
    outgoing = jnp.take(home_tokens, table, axis=0)
    here_tokens = lax.all_to_all(outgoing, "ctx", split_axis=0, concat_axis=0, tiled=True).reshape(
        local_rows, width
    )
    key_segments = jnp.take(segments[0], order, axis=0)
    query_segments = lax.dynamic_slice_in_dim(key_segments, place * local_rows, local_rows)
    queries = (matmul(here_tokens, query_full) + query_shift.astype(jnp.float32)).astype(
        jnp.bfloat16
    )
    own_keys = matmul(here_tokens, key_full).astype(jnp.bfloat16)
    own_values = (matmul(here_tokens, value_full) + value_shift.astype(jnp.float32)).astype(
        jnp.bfloat16
    )
    all_keys, all_values = (
        lax.all_gather(own_keys, "ctx", axis=0, tiled=True),
        lax.all_gather(own_values, "ctx", axis=0, tiled=True),
    )
    total = all_keys.shape[0]
    block = min(1024, total)
    count = total // block
    scale = HEAD_DIM ** (-0.5)
    query_heads = queries.reshape(local_rows, HEADS, HEAD_DIM)
    key_blocks = all_keys.reshape(count, block, HEADS, HEAD_DIM)
    value_blocks = all_values.reshape(count, block, HEADS, HEAD_DIM)
    segment_blocks = key_segments.reshape(count, block)
    mixed, log_total = attend(
        query_heads, key_blocks, value_blocks, query_segments, segment_blocks, scale
    )
    context = mixed.reshape(local_rows, width).astype(jnp.bfloat16)
    inner_full, inner_shift, outer_full, outer_shift, gain_two, shift_two, project_full = (
        lax.all_gather(inner_weight, "fsdp", axis=0, tiled=True),
        lax.all_gather(inner_bias, "fsdp", axis=0, tiled=True),
        lax.all_gather(outer_weight, "fsdp", axis=0, tiled=True),
        lax.all_gather(outer_bias, "fsdp", axis=0, tiled=True),
        lax.all_gather(second_gain, "fsdp", axis=0, tiled=True),
        lax.all_gather(second_shift, "fsdp", axis=0, tiled=True),
        lax.all_gather(project_weight, "fsdp", axis=0, tiled=True),
    )
    attended = matmul(context, output_full) + output_shift.astype(jnp.float32)
    first, first_normal, first_inverse = norm_forward(
        here_tokens.astype(jnp.float32) + attended,
        gain_one.astype(jnp.float32),
        shift_one.astype(jnp.float32),
    )
    first_low = first.astype(jnp.bfloat16)
    inner = matmul(first_low, inner_full) + inner_shift.astype(jnp.float32)
    active = jax.nn.gelu(inner, approximate=False).astype(jnp.bfloat16)
    outer = matmul(active, outer_full) + outer_shift.astype(jnp.float32)
    second, second_normal, second_inverse = norm_forward(
        first + outer, gain_two.astype(jnp.float32), shift_two.astype(jnp.float32)
    )
    second_low = second.astype(jnp.bfloat16)
    projected = matmul(second_low, project_full)
    inverse_length = lax.rsqrt(jnp.sum(projected * projected, axis=-1, keepdims=True) + 1e-06)
    normed = projected * inverse_length
    embedded = normed.astype(jnp.bfloat16)
    incoming = cotangent[0].astype(jnp.float32)
    along = jnp.sum(normed * incoming, axis=-1, keepdims=True)
    delta_projected = (inverse_length * (incoming - normed * along)).astype(jnp.bfloat16)
    project_delta = matmul(second_low.T, delta_projected)
    delta_second = matmul(delta_projected, project_full.T)
    residual_two, second_gain_delta, second_shift_delta = norm_backward(
        delta_second, second_normal, second_inverse, gain_two.astype(jnp.float32)
    )
    delta_outer = residual_two.astype(jnp.bfloat16)
    outer_bias_delta = jnp.sum(delta_outer, axis=0, dtype=jnp.float32)
    outer_delta = matmul(active.T, delta_outer)
    delta_active = matmul(delta_outer, outer_full.T)
    delta_inner = (delta_active * gelu_slope(inner)).astype(jnp.bfloat16)
    inner_bias_delta = jnp.sum(delta_inner, axis=0, dtype=jnp.float32)
    inner_delta = matmul(first_low.T, delta_inner)
    delta_first = residual_two + matmul(delta_inner, inner_full.T)
    residual_one, first_gain_delta, first_shift_delta = norm_backward(
        delta_first, first_normal, first_inverse, gain_one.astype(jnp.float32)
    )
    delta_attended = residual_one.astype(jnp.bfloat16)
    output_bias_delta = jnp.sum(delta_attended, axis=0, dtype=jnp.float32)
    output_delta = matmul(context.T, delta_attended)
    delta_context = matmul(delta_attended, output_full.T).astype(jnp.bfloat16)
    upstream = delta_context.reshape(local_rows, HEADS, HEAD_DIM)
    query_terms, key_terms, value_terms = attend_backward(
        query_heads,
        key_blocks,
        value_blocks,
        query_segments,
        segment_blocks,
        scale,
        log_total,
        upstream,
    )
    key_sums, value_sums = (
        lax.psum_scatter(
            key_terms.reshape(total, width).astype(jnp.bfloat16),
            "ctx",
            scatter_dimension=0,
            tiled=True,
        ).astype(jnp.float32),
        lax.psum_scatter(
            value_terms.reshape(total, width).astype(jnp.bfloat16),
            "ctx",
            scatter_dimension=0,
            tiled=True,
        ).astype(jnp.float32),
    )
    delta_keys = key_sums.astype(jnp.bfloat16)
    delta_values = value_sums.astype(jnp.bfloat16)
    delta_queries = query_terms.reshape(local_rows, width).astype(jnp.bfloat16)
    query_bias_delta = jnp.sum(delta_queries, axis=0, dtype=jnp.float32)
    value_bias_delta = jnp.sum(delta_values, axis=0, dtype=jnp.float32)
    query_delta = matmul(here_tokens.T, delta_queries)
    key_delta = matmul(here_tokens.T, delta_keys)
    value_delta = matmul(here_tokens.T, delta_values)
    delta_here = (
        residual_one
        + matmul(delta_queries, query_full.T)
        + matmul(delta_keys, key_full.T)
        + matmul(delta_values, value_full.T)
    ).astype(jnp.bfloat16)
    coming_home = lax.all_to_all(
        delta_here.reshape(peers, share, width), "ctx", split_axis=0, concat_axis=0, tiled=True
    )
    delta_home = (
        jnp.zeros((local_rows, width), jnp.bfloat16)
        .at[flat_table]
        .set(coming_home.reshape(local_rows, width))
    )
    (
        inner_part,
        inner_bias_part,
        outer_part,
        outer_bias_part,
        second_gain_part,
        second_shift_part,
        project_part,
    ) = (
        lax.psum_scatter(
            inner_delta.astype(jnp.bfloat16), "fsdp", scatter_dimension=0, tiled=True
        ).astype(jnp.float32),
        lax.psum_scatter(
            inner_bias_delta.astype(jnp.bfloat16), "fsdp", scatter_dimension=0, tiled=True
        ).astype(jnp.float32),
        lax.psum_scatter(
            outer_delta.astype(jnp.bfloat16), "fsdp", scatter_dimension=0, tiled=True
        ).astype(jnp.float32),
        lax.psum_scatter(
            outer_bias_delta.astype(jnp.bfloat16), "fsdp", scatter_dimension=0, tiled=True
        ).astype(jnp.float32),
        lax.psum_scatter(
            second_gain_delta.astype(jnp.bfloat16), "fsdp", scatter_dimension=0, tiled=True
        ).astype(jnp.float32),
        lax.psum_scatter(
            second_shift_delta.astype(jnp.bfloat16), "fsdp", scatter_dimension=0, tiled=True
        ).astype(jnp.float32),
        lax.psum_scatter(
            project_delta.astype(jnp.bfloat16), "fsdp", scatter_dimension=0, tiled=True
        ).astype(jnp.float32),
    )
    (
        query_part,
        key_part,
        value_part,
        query_bias_part,
        value_bias_part,
        output_part,
        output_bias_part,
        first_gain_part,
        first_shift_part,
    ) = (
        lax.psum_scatter(
            query_delta.astype(jnp.bfloat16), "fsdp", scatter_dimension=0, tiled=True
        ).astype(jnp.float32),
        lax.psum_scatter(
            key_delta.astype(jnp.bfloat16), "fsdp", scatter_dimension=0, tiled=True
        ).astype(jnp.float32),
        lax.psum_scatter(
            value_delta.astype(jnp.bfloat16), "fsdp", scatter_dimension=0, tiled=True
        ).astype(jnp.float32),
        lax.psum_scatter(
            query_bias_delta.astype(jnp.bfloat16), "fsdp", scatter_dimension=0, tiled=True
        ).astype(jnp.float32),
        lax.psum_scatter(
            value_bias_delta.astype(jnp.bfloat16), "fsdp", scatter_dimension=0, tiled=True
        ).astype(jnp.float32),
        lax.psum_scatter(
            output_delta.astype(jnp.bfloat16), "fsdp", scatter_dimension=0, tiled=True
        ).astype(jnp.float32),
        lax.psum_scatter(
            output_bias_delta.astype(jnp.bfloat16), "fsdp", scatter_dimension=0, tiled=True
        ).astype(jnp.float32),
        lax.psum_scatter(
            first_gain_delta.astype(jnp.bfloat16), "fsdp", scatter_dimension=0, tiled=True
        ).astype(jnp.float32),
        lax.psum_scatter(
            first_shift_delta.astype(jnp.bfloat16), "fsdp", scatter_dimension=0, tiled=True
        ).astype(jnp.float32),
    )
    results = (
        lax.psum(query_part.astype(jnp.bfloat16), "ctx").astype(jnp.float32),
        lax.psum(key_part.astype(jnp.bfloat16), "ctx").astype(jnp.float32),
        lax.psum(value_part.astype(jnp.bfloat16), "ctx").astype(jnp.float32),
        lax.psum(query_bias_part.astype(jnp.bfloat16), "ctx").astype(jnp.float32),
        lax.psum(value_bias_part.astype(jnp.bfloat16), "ctx").astype(jnp.float32),
        lax.psum(output_part.astype(jnp.bfloat16), "ctx").astype(jnp.float32),
        lax.psum(output_bias_part.astype(jnp.bfloat16), "ctx").astype(jnp.float32),
        lax.psum(first_gain_part.astype(jnp.bfloat16), "ctx").astype(jnp.float32),
        lax.psum(first_shift_part.astype(jnp.bfloat16), "ctx").astype(jnp.float32),
        lax.psum(inner_part.astype(jnp.bfloat16), "ctx").astype(jnp.float32),
        lax.psum(inner_bias_part.astype(jnp.bfloat16), "ctx").astype(jnp.float32),
        lax.psum(outer_part.astype(jnp.bfloat16), "ctx").astype(jnp.float32),
        lax.psum(outer_bias_part.astype(jnp.bfloat16), "ctx").astype(jnp.float32),
        lax.psum(second_gain_part.astype(jnp.bfloat16), "ctx").astype(jnp.float32),
        lax.psum(second_shift_part.astype(jnp.bfloat16), "ctx").astype(jnp.float32),
        lax.psum(project_part.astype(jnp.bfloat16), "ctx").astype(jnp.float32),
    )
    return (
        embedded[None],
        delta_home[None],
        results[0],
        results[1],
        results[2],
        results[3],
        results[4],
        results[5],
        results[6],
        results[7],
        results[8],
        results[9],
        results[10],
        results[11],
        results[12],
        results[13],
        results[14],
        results[15],
    )


BF = jnp.bfloat16
F32 = jnp.float32
ROWS = 512
WIDTH = 768
FAR = 2.0**100
QROWS = 512
KROWS = 256


def nt(left, right):
    return lax.dot_general(left, right, (((1,), (1,)), ((), ())), preferred_element_type=F32)


def nn(left, right):
    return lax.dot_general(left, right, (((1,), (0,)), ((), ())), preferred_element_type=F32)


def tn(left, right):
    return lax.dot_general(left, right, (((0,), (0,)), ((), ())), preferred_element_type=F32)


def to_core(value):
    return lax.ppermute(value, "ctx", [(i, i ^ 1) for i in range(4)])


def to_x(value):
    return lax.ppermute(value, "ctx", [(i, i ^ 2) for i in range(4)])


def to_cross(value):
    return lax.ppermute(value, "ctx", [(i, i ^ 3) for i in range(4)])


def to_fsdp(value, bit):
    return lax.ppermute(value, "fsdp", [(i, i ^ bit) for i in range(8)])


def along_z(value, step):
    return lax.ppermute(value, "fsdp", [(i, (i + 2 * step) % 8) for i in range(8)])


def to_mixed(value, first):
    pairs = []
    for c in range(4):
        for f in range(8):
            target = (c ^ 2) * 8 + f if (c % 2 == 0) == first else c * 8 + (f ^ 1)
            pairs.append((c * 8 + f, target))
    return lax.ppermute(value, ("ctx", "fsdp"), pairs)


def three_parts(value):
    high = value.astype(BF).astype(F32)
    rest = value - high
    middle = rest.astype(BF).astype(F32)
    return high, middle, rest - middle


def whole(shape):
    return pl.BlockSpec(shape, lambda *_: (0,) * len(shape))


def project_kernel(info, *refs):
    x_refs, w_refs = refs[0:4], refs[4:12]
    qa_ref, ka_ref = refs[12:14]
    q_out, k_out, v_out, kt_out, vt_out, w_out, vec_out, x_out = refs[14:]
    c, f = info[0], info[1]
    z, y = f // 2, lax.rem(f, 2)
    for k in range(4):
        source = lax.rem(z + 4 - k, 4)
        for j in range(2):
            row = pl.multiple_of((source * 2 + (y if j == 0 else 1 - y)) * 96, 32)
            w_out[pl.ds(row, 96), :] = w_refs[2 * k + j][...]
    weights = w_out[...]
    turned = weights[:, 512:640].astype(F32).T
    vec_out[...] = turned[64:80]
    lane = lax.broadcasted_iota(jnp.int32, (WIDTH, 640), 1)
    row = lax.broadcasted_iota(jnp.int32, (WIDTH, 640), 0)
    wanted = jnp.where(lane < 384, lane, lane - 384) + 192 * c
    chosen = nn(turned[64:80].astype(BF), (row == wanted).astype(F32).astype(BF))
    lane1 = lax.broadcasted_iota(jnp.int32, (1, 640), 1)
    bias = jnp.where(
        lane1 < 192,
        chosen[0:1],
        jnp.where((lane1 >= 384) & (lane1 < 576), chosen[1:2], 0.0),
    )
    lanes = lax.broadcasted_iota(jnp.int32, (ROWS, 128), 1)
    for r in range(4):
        at = pl.multiple_of(jnp.bitwise_xor(c, r) * ROWS, ROWS)
        rows = pl.ds(at, ROWS)
        x = x_refs[r][...]
        x_out[rows, :] = x
        result = nn(x, weights) + bias
        qa = qa_ref[rows, :].astype(F32)
        ka = ka_ref[rows, :].astype(F32)
        for slot in range(9):
            pair = result[:, 128 * (slot // 2) : 128 * (slot // 2) + 128]
            if slot % 2:
                pair = pltpu.roll(pair, 64, 1)
            kind, h = slot // 3, slot % 3
            if kind == 0:
                low = pair.astype(BF).astype(F32) * (HEAD_DIM ** (-0.5))
                q_out[h, rows, :] = jnp.where(lanes < 64, low, qa).astype(BF)
            elif kind == 1:
                value = jnp.where(lanes < 64, pair, ka)
                k_out[h, rows, :] = value.astype(BF)
                kt_out[h, :, rows] = value.T[:64].astype(BF)
            else:
                value = jnp.where(lanes < 64, pair, jnp.where(lanes < 67, 1.0, 0.0))
                v_out[h, rows, :] = value.astype(BF)
                vt_out[h, :, rows] = value.T[:80].astype(BF)


def project(info, xs, ws, query_marks, key_marks, total):
    heads = 3
    shapes = [
        ((heads, total, 128), BF),
        ((heads, total, 128), BF),
        ((heads, total, 128), BF),
        ((heads, 64, total), BF),
        ((heads, 80, total), BF),
        ((WIDTH, 640), BF),
        ((16, WIDTH), F32),
        ((total, WIDTH), BF),
    ]
    inputs = [*xs, *ws, query_marks, key_marks]
    return pl.pallas_call(
        project_kernel,
        grid_spec=pltpu.PrefetchScalarGridSpec(
            num_scalar_prefetch=1,
            grid=(1,),
            in_specs=[whole(a.shape) for a in inputs],
            out_specs=[whole(s) for s, _ in shapes],
        ),
        out_shape=[jax.ShapeDtypeStruct(s, t) for s, t in shapes],
        compiler_params=pltpu.CompilerParams(vmem_limit_bytes=56 << 20),
        cost_estimate=pl.CostEstimate(
            flops=2 * total * WIDTH * 640, bytes_accessed=16 << 20, transcendentals=0
        ),
        name="project",
    )(info, *inputs)


def attend_kernel(info, q_ref, k_ref, vt_ref, o_ref, ql_ref, pack_ref, top_s, sum_s, *, chip):
    heads = 3
    c = info[0]
    place = jnp.bitwise_xor(c, pl.program_id(0) + 2 * chip)
    top_s[...] = jnp.full_like(top_s, -3e38)
    sum_s[...] = jnp.zeros_like(sum_s)

    def advance(block, carry):
        rows = pl.ds(pl.multiple_of(block * KROWS, KROWS), KROWS)
        each = range(heads)
        scores = [nt(k_ref[h, rows], q_ref[h]) for h in each]
        before = [top_s[h, :1] for h in each]
        after = [jnp.maximum(before[h], jnp.max(scores[h], axis=0, keepdims=True)) for h in each]
        probs = [jnp.exp(scores[h] - after[h]).astype(BF) for h in each]
        shrink = [jnp.exp(before[h] - after[h]) for h in each]
        fresh = [nn(vt_ref[h, :, rows], probs[h]) for h in each]
        for h in each:
            sum_s[h] = sum_s[h] * shrink[h] + fresh[h]
            top_s[h] = jnp.broadcast_to(after[h], top_s.shape[1:])
        return carry

    lax.fori_loop(info[4 + place], info[8 + place], advance, 0)
    lanes = lax.broadcasted_iota(jnp.int32, (QROWS, 128), 1)
    subs = lax.broadcasted_iota(jnp.int32, (128, QROWS), 0)
    outs = []
    for h in range(heads):
        sums = sum_s[h]
        total = sums[64:65]
        parts = three_parts(top_s[h, :1] + jnp.log(total))
        tall = jnp.concatenate([sums[:64] / total, jnp.zeros((64, QROWS), F32)], axis=0)
        for i in range(3):
            tall = jnp.where(subs == 67 + i, -parts[i], tall)
        turned = tall.T
        out = jnp.where(lanes < 64, turned, 0.0)
        outs.append(out)
        o_ref[h] = out.astype(BF)
        ql_ref[h] = jnp.where(lanes < 67, q_ref[h].astype(F32), turned).astype(BF)
    pack_ref[0, 0:512] = (outs[0] + pltpu.roll(outs[1], 64, 1)).astype(BF)
    pack_ref[0, 512:768] = (outs[2][:256] + pltpu.roll(outs[2][256:], 64, 1)).astype(BF)


def attend_rows(info, q, k, vt, chip):
    heads, total, _ = k.shape
    block = pl.BlockSpec(
        (heads, QROWS, 128), lambda i, n: (0, jnp.bitwise_xor(n[0], i + 2 * chip), 0)
    )
    local = pl.BlockSpec((heads, QROWS, 128), lambda i, n: (0, i, 0))
    return pl.pallas_call(
        functools.partial(attend_kernel, chip=chip),
        grid_spec=pltpu.PrefetchScalarGridSpec(
            num_scalar_prefetch=1,
            grid=(2,),
            in_specs=[block, whole(k.shape), whole(vt.shape)],
            out_specs=[local, local, pl.BlockSpec((1, 768, 128), lambda i, n: (i, 0, 0))],
            scratch_shapes=[pltpu.VMEM((heads, 8, QROWS), F32), pltpu.VMEM((heads, 80, QROWS), F32)],
        ),
        out_shape=[
            jax.ShapeDtypeStruct((heads, 2 * QROWS, 128), BF),
            jax.ShapeDtypeStruct((heads, 2 * QROWS, 128), BF),
            jax.ShapeDtypeStruct((2, 768, 128), BF),
        ],
        compiler_params=pltpu.CompilerParams(vmem_limit_bytes=40 << 20),
        cost_estimate=pl.CostEstimate(
            flops=8_000_000_000, bytes_accessed=8 << 20, transcendentals=0
        ),
        name="attend_rows",
    )(info, q, k, vt)


def attend_back_kernel(
    info, ql_ref, do_ref, o_ref, k_ref, kt_ref, v_ref, dq_ref, dk_ref, dv_ref, dk_s, dv_s, dq_s, do_s
):
    heads = 3
    step = pl.program_id(0)

    @pl.when(step == 0)
    def _():
        dk_s[...] = jnp.zeros_like(dk_s)
        dv_s[...] = jnp.zeros_like(dv_s)

    place = jnp.bitwise_xor(info[0], step)
    dq_s[...] = jnp.zeros_like(dq_s)
    lanes = lax.broadcasted_iota(jnp.int32, (QROWS, 128), 1)
    pair = do_ref[0, 0:512].astype(F32)
    last = do_ref[0, 512:768].astype(F32)
    ups = [pair, pltpu.roll(pair, 64, 1), jnp.concatenate([last, pltpu.roll(last, 64, 1)], axis=0)]
    for h in range(heads):
        up = jnp.where(lanes < 64, ups[h], 0.0)
        parts = three_parts(jnp.sum(up * o_ref[h].astype(F32), axis=1, keepdims=True))
        for i in range(3):
            up = jnp.where(lanes == 64 + i, -parts[i], up)
        do_s[h] = up.astype(BF)

    def advance(block, carry):
        rows = pl.ds(pl.multiple_of(block * KROWS, KROWS), KROWS)
        each = range(heads)
        scores = [nt(k_ref[h, rows], ql_ref[h]) for h in each]
        rises = [nt(v_ref[h, rows], do_s[h]) for h in each]
        probs = [jnp.exp(scores[h]) for h in each]
        deltas = [(probs[h] * rises[h]).astype(BF) for h in each]
        lows = [probs[h].astype(BF) for h in each]
        for_values = [nn(lows[h], do_s[h]) for h in each]
        for_keys = [nn(deltas[h], ql_ref[h]) for h in each]
        for_queries = [nn(kt_ref[h, :, rows], deltas[h]) for h in each]
        for h in each:
            dv_s[h, rows] += for_values[h]
            dk_s[h, rows] += for_keys[h]
            dq_s[h] += for_queries[h]
        return carry

    lax.fori_loop(info[4 + place], info[8 + place], advance, 0)
    for h in range(heads):
        tall = jnp.concatenate([dq_s[h], jnp.zeros((64, QROWS), F32)], axis=0)
        dq_ref[h] = (tall.T * (HEAD_DIM ** (-0.5))).astype(BF)

    @pl.when(step == pl.num_programs(0) - 1)
    def _():
        dk_ref[...] = dk_s[...].astype(BF)
        dv_ref[...] = dv_s[...].astype(BF)


def attend_back(info, ql, ups, o, k, kt, v):
    heads, total, _ = k.shape
    local = pl.BlockSpec((heads, QROWS, 128), lambda i, n: (0, i, 0))
    placed = pl.BlockSpec((heads, QROWS, 128), lambda i, n: (0, jnp.bitwise_xor(n[0], i), 0))
    return pl.pallas_call(
        attend_back_kernel,
        grid_spec=pltpu.PrefetchScalarGridSpec(
            num_scalar_prefetch=1,
            grid=(4,),
            in_specs=[
                local,
                pl.BlockSpec((1, 768, 128), lambda i, n: (i, 0, 0)),
                local,
                whole(k.shape),
                whole(kt.shape),
                whole(v.shape),
            ],
            out_specs=[placed, whole(k.shape), whole(k.shape)],
            scratch_shapes=[
                pltpu.VMEM(k.shape, F32),
                pltpu.VMEM(k.shape, F32),
                pltpu.VMEM((heads, 64, QROWS), F32),
                pltpu.VMEM((heads, QROWS, 128), BF),
            ],
        ),
        out_shape=[jax.ShapeDtypeStruct(k.shape, BF)] * 3,
        compiler_params=pltpu.CompilerParams(vmem_limit_bytes=50 << 20),
        cost_estimate=pl.CostEstimate(
            flops=36_000_000_000, bytes_accessed=16 << 20, transcendentals=0
        ),
        name="attend_back",
    )(info, ql, ups, o, k, kt, v)


def spots(info, f):
    z, y = f // 2, f % 2
    mine = info[1]
    my_z, my_y = mine // 2, lax.rem(mine, 2)
    apart = jnp.bitwise_xor(my_z, z)
    return jnp.bitwise_xor(my_y, y), lax.rem(apart, 2), apart // 2


def input_back_kernel(
    info, dq_ref, dk_ref, dv_ref, w_ref, x_ref, vec_ref, own_ref, rest_ref, pack_ref, all_s
):
    total = x_ref.shape[0]
    c = info[0]
    lanes = lax.broadcasted_iota(jnp.int32, (ROWS, 128), 1)
    for b in range(total // ROWS):
        rows = pl.ds(b * ROWS, ROWS)
        heads = [ref[h, rows, :].astype(F32) for ref in (dq_ref, dk_ref, dv_ref) for h in range(3)]
        heads = [jnp.where(lanes < 64, value, 0.0) for value in heads]
        for p in range(5):
            value = heads[2 * p]
            if 2 * p + 1 < 9:
                value = value + pltpu.roll(heads[2 * p + 1], 64, 1)
            all_s[rows, 128 * p : 128 * p + 128] = value.astype(BF)
    delta = tn(x_ref[...], all_s[...])
    sums = jnp.sum(all_s[...].astype(F32), axis=0, keepdims=True)
    row = lax.broadcasted_iota(jnp.int32, (640, WIDTH), 0)
    lane = lax.broadcasted_iota(jnp.int32, (640, WIDTH), 1)
    spread = jnp.zeros((16, WIDTH), F32)
    at = lax.broadcasted_iota(jnp.int32, (16, WIDTH), 0)
    parts = three_parts(sums)
    for kind, first in ((0, 0), (1, 384)):
        sel = ((row - first + 192 * c == lane) & (row >= first) & (row < first + 192))
        sel = sel.astype(F32).astype(BF)
        value = sum(nn(jnp.broadcast_to(part, (16, 640)).astype(BF), sel) for part in parts)
        spread = jnp.where(at == kind, value, spread)
    vectors = jnp.where(at < 2, spread, vec_ref[...])
    tall = jnp.concatenate(
        [jnp.zeros((64, WIDTH), F32), vectors, jnp.zeros((48, WIDTH), F32)], axis=0
    )
    side = tall.T
    for f in range(8):
        i, j, k = spots(info, f)
        piece = delta[96 * f : 96 * f + 96]
        pack_ref[i, j, k, :, 0:512] = piece[:, :512].astype(BF)
        pack_ref[i, j, k, :, 512:640] = (piece[:, 512:] + side[96 * f : 96 * f + 96]).astype(BF)
    for r in range(4):
        rows = pl.ds(pl.multiple_of(jnp.bitwise_xor(c, r) * ROWS, ROWS), ROWS)
        value = nt(all_s[rows, :], w_ref[...])
        if r == 0:
            own_ref[...] = value
        else:
            rest_ref[(0, 2, 1)[r - 1]] = value.astype(BF)


def input_back(info, dq, dk, dv, w, x_all, vectors):
    shapes = [((ROWS, WIDTH), F32), ((3, ROWS, WIDTH), BF), ((2, 2, 2, 96, 640), BF)]
    inputs = [dq, dk, dv, w, x_all, vectors]
    return pl.pallas_call(
        input_back_kernel,
        grid_spec=pltpu.PrefetchScalarGridSpec(
            num_scalar_prefetch=1,
            grid=(1,),
            in_specs=[whole(a.shape) for a in inputs],
            out_specs=[whole(s) for s, _ in shapes],
            scratch_shapes=[pltpu.VMEM((x_all.shape[0], 640), BF)],
        ),
        out_shape=[jax.ShapeDtypeStruct(s, t) for s, t in shapes],
        compiler_params=pltpu.CompilerParams(vmem_limit_bytes=56 << 20),
        cost_estimate=pl.CostEstimate(
            flops=4 * x_all.shape[0] * WIDTH * 640, bytes_accessed=12 << 20, transcendentals=0
        ),
        name="input_back",
    )(info, *inputs)


def pair_index(info, keep, x, yr):
    xr = jnp.bitwise_xor(info[0] // 2, x)
    order = jnp.bitwise_xor(lax.rem(info[0], 2), keep)
    first = jnp.where(order == 0, xr, yr)
    second = jnp.where(order == 0, yr, xr)
    return first, second


def outer_pack_kernel(info, active_ref, do_ref, second_ref, dp_ref, keep_ref, send_ref, proj_s):
    core = lax.rem(info[0], 2)
    proj_s[...] = tn(second_ref[...], dp_ref[...])
    for f in range(8):
        yr, z0, z1 = spots(info, f)
        left = active_ref[:, 384 * f : 384 * f + 384]
        for k, ref in ((0, keep_ref), (1, send_ref)):
            half = jnp.bitwise_xor(core, k)
            right = do_ref[:, pl.ds(pl.multiple_of(half * 384, 128), 384)]
            value = tn(left, right).astype(BF)
            for x in range(2):
                a, b = pair_index(info, k, x, yr)
                ref[a, b, z0, z1, 0:192, :] = value[192 * x : 192 * x + 192]
                start = 96 * f + 24 * (2 * x + half)
                wide = jnp.concatenate(
                    [proj_s[pl.ds(pl.multiple_of(start + 8 * g, 8), 8), :] for g in range(3)],
                    axis=1,
                )
                ref[a, b, z0, z1, 192:208, :] = jnp.concatenate(
                    [wide, jnp.zeros((8, 384), F32)], axis=0
                ).astype(BF)


def outer_pack(info, active, delta_outer, second_low, delta_projected):
    shape = (2, 2, 2, 2, 208, 384)
    inputs = [active, delta_outer, second_low, delta_projected]
    return pl.pallas_call(
        outer_pack_kernel,
        grid_spec=pltpu.PrefetchScalarGridSpec(
            num_scalar_prefetch=1,
            grid=(1,),
            in_specs=[whole(a.shape) for a in inputs],
            out_specs=[whole(shape)] * 2,
            scratch_shapes=[pltpu.VMEM((WIDTH, 128), F32)],
        ),
        out_shape=[jax.ShapeDtypeStruct(shape, BF)] * 2,
        compiler_params=pltpu.CompilerParams(vmem_limit_bytes=56 << 20),
        cost_estimate=pl.CostEstimate(
            flops=2 * ROWS * 3072 * WIDTH, bytes_accessed=10 << 20, transcendentals=0
        ),
        name="outer_pack",
    )(info, *inputs)


def inner_pack_kernel(info, first_ref, di_ref, context_ref, da_ref, keep_ref, send_ref):
    core = lax.rem(info[0], 2)
    for k, ref in ((0, keep_ref), (1, send_ref)):
        half = jnp.bitwise_xor(core, k)
        for x in range(2):
            for part in range(2):
                start = (2 * x + half) * 768 + 384 * part
                right = di_ref[:, pl.ds(pl.multiple_of(start, 128), 384)]
                value = tn(first_ref[...], right).astype(BF)
                for f in range(8):
                    yr, z0, z1 = spots(info, f)
                    a, b = pair_index(info, k, x, yr)
                    ref[a, b, z0, z1, 96 * part : 96 * part + 96, :] = value[96 * f : 96 * f + 96]
        value = tn(
            context_ref[...], da_ref[:, pl.ds(pl.multiple_of(half * 384, 128), 384)]
        ).astype(BF)
        for f in range(8):
            yr, z0, z1 = spots(info, f)
            for x in range(2):
                a, b = pair_index(info, k, x, yr)
                ref[a, b, z0, z1, 192:240, :] = value[96 * f + 48 * x : 96 * f + 48 * x + 48]


def inner_pack(info, first_low, delta_inner, context, delta_attended):
    shape = (2, 2, 2, 2, 240, 384)
    inputs = [first_low, delta_inner, context, delta_attended]
    return pl.pallas_call(
        inner_pack_kernel,
        grid_spec=pltpu.PrefetchScalarGridSpec(
            num_scalar_prefetch=1,
            grid=(1,),
            in_specs=[whole(a.shape) for a in inputs],
            out_specs=[whole(shape)] * 2,
        ),
        out_shape=[jax.ShapeDtypeStruct(shape, BF)] * 2,
        compiler_params=pltpu.CompilerParams(vmem_limit_bytes=56 << 20),
        cost_estimate=pl.CostEstimate(
            flops=2 * ROWS * 3840 * WIDTH, bytes_accessed=10 << 20, transcendentals=0
        ),
        name="inner_pack",
    )(info, *inputs)


def wide(value):
    return value.astype(F32)


def sum_pack(keep, send):
    came = to_core(send)
    one = to_mixed((wide(keep[1]) + wide(came[1])).astype(BF), True)
    two = to_mixed((wide(keep[0, 1]) + wide(came[0, 1]) + wide(one[1])).astype(BF), False)
    half = wide(keep[0, 0]) + wide(came[0, 0]) + wide(one[0]) + wide(two)
    three = to_fsdp(half[1].astype(BF), 2)
    quarter = half[0] + wide(three)
    four = to_fsdp(quarter[1].astype(BF), 4)
    return (quarter[0] + wide(four)).astype(BF)


def head_pack(value):
    a, b = value[:, :128], value[:, 128:]
    return jnp.concatenate([a, jnp.concatenate([b[:256], b[256:]], axis=1)], axis=0)


def head_unpack(pack):
    last = pack[512:]
    return jnp.concatenate(
        [pack[:512], jnp.concatenate([last[:, :64], last[:, 64:]], axis=0)], axis=1
    )


def fast_device(
    tokens,
    dealt,
    segments,
    query_weight,
    key_weight,
    value_weight,
    query_bias,
    value_bias,
    output_weight,
    output_bias,
    first_gain,
    first_shift,
    inner_weight,
    inner_bias,
    outer_weight,
    outer_bias,
    second_gain,
    second_shift,
    project_weight,
    cotangent,
):
    c = lax.axis_index("ctx")
    f = lax.axis_index("fsdp")
    core = lax.rem(c, 2)
    total = segments.shape[1]
    x = tokens[0]

    def columns(weight):
        return lax.dynamic_slice_in_dim(weight, 192 * c, 192, 1)

    vectors = jnp.stack(
        [
            query_bias,
            value_bias,
            output_bias,
            first_gain,
            first_shift,
            outer_bias,
            second_gain,
            second_shift,
        ],
        axis=1,
    )
    heads_pack = jnp.concatenate(
        [
            columns(query_weight),
            columns(key_weight),
            columns(value_weight),
            vectors,
            inner_bias.reshape(4, 96).T,
            jnp.zeros((96, 52), BF),
        ],
        axis=1,
    )
    pieces = [heads_pack, to_fsdp(heads_pack, 1)]
    for k in range(1, 4):
        moved = along_z(heads_pack, k)
        pieces += [moved, to_fsdp(moved, 1)]
    x_core = to_core(x)
    x_next = to_x(x)
    x_cross = to_core(x_next)

    def half_columns(weight, n):
        return lax.dynamic_slice_in_dim(weight, core * n, n, 1)

    inner_own = lax.all_gather(
        jnp.concatenate(
            [half_columns(inner_weight, 1536), half_columns(output_weight, 384), project_weight],
            axis=1,
        ),
        "fsdp",
        axis=0,
        tiled=True,
    )
    outer_own = lax.all_gather(half_columns(outer_weight, 384), "fsdp", axis=0, tiled=True)
    inner_other = to_core(inner_own)
    outer_other = to_core(outer_own)

    def both(own, other):
        return jnp.concatenate(
            [jnp.where(core == 0, own, other), jnp.where(core == 0, other, own)], axis=1
        )

    local = dealt[0].reshape(4, 4, 128)
    table = lax.dynamic_index_in_dim(local, c, 1, keepdims=False) - c * ROWS
    onehot = (
        table.reshape(1, ROWS) == lax.broadcasted_iota(jnp.int32, (ROWS, ROWS), 0)
    ).astype(BF)
    sent = cotangent[0].reshape(4, 128, 128)

    def other_block(blocks, r):
        return lax.dynamic_index_in_dim(blocks, jnp.bitwise_xor(c, r), 0, keepdims=False)

    def canonical(parts):
        stacked = jnp.stack(parts)
        return [other_block(stacked, r) for r in range(4)]

    def exchange(blocks):
        moves = (lambda v: v, to_core, to_x, to_cross)
        return canonical([moves[r](other_block(blocks, r)) for r in range(4)])

    arrived = jnp.concatenate(exchange(sent), axis=0)
    incoming = matmul(onehot, arrived)

    seg = segments[0]
    starts, ends = seg[::QROWS], seg[QROWS - 1 :: QROWS]
    lows = jnp.sum(seg[None, :] < starts[:, None], axis=1) // KROWS
    highs = (jnp.sum(seg[None, :] <= ends[:, None], axis=1) + KROWS - 1) // KROWS
    info = jnp.concatenate(
        [jnp.stack([c, f, c * 0, c * 0]), lows, highs, jnp.zeros((4,), jnp.int32)]
    ).astype(jnp.int32)
    lane = lax.broadcasted_iota(jnp.int32, (total, 128), 1)
    same = (lane - 64) == seg[:, None]
    query_marks = same.astype(BF)
    key_marks = jnp.where(
        (lane >= 64) & (lane < 67),
        jnp.where(same, 0.0, -FAR),
        jnp.where((lane >= 67) & (lane < 70), 1.0, 0.0),
    ).astype(BF)

    q, k, v, kt, vt, heads_weight, vec, x_all = project(
        info, [x, x_core, x_next, x_cross], pieces, query_marks, key_marks, total
    )
    o_far, ql_far, pack_far = attend_rows(info, q, k, vt, 1)
    from_x, from_cross = to_x(pack_far[0]), to_cross(pack_far[1])
    o_near, ql_near, pack_near = attend_rows(info, q, k, vt, 0)
    from_core = to_core(pack_near[1])
    context = jnp.concatenate(
        [head_unpack(p) for p in canonical([pack_near[0], from_core, from_x, from_cross])], axis=1
    )

    inner_full = both(inner_own[:, :1536], inner_other[:, :1536])
    output_full = both(inner_own[:, 1536:1920], inner_other[:, 1536:1920])
    project_full = inner_own[:, 1920:]
    outer_full = both(outer_own, outer_other)
    inner_shift = vec[8:12].reshape(4, 8, 96).transpose(1, 0, 2).reshape(3072)

    attended = matmul(context, output_full) + vec[2]
    first, first_normal, first_inverse = norm_forward(wide(x) + attended, vec[3], vec[4])
    first_low = first.astype(BF)
    inner = matmul(first_low, inner_full) + inner_shift
    active = jax.nn.gelu(inner, approximate=False).astype(BF)
    slope = gelu_slope(inner)
    outer = matmul(active, outer_full) + vec[5]
    second, second_normal, second_inverse = norm_forward(first + outer, vec[6], vec[7])
    second_low = second.astype(BF)
    projected = matmul(second_low, project_full)
    inverse_length = lax.rsqrt(jnp.sum(projected * projected, axis=-1, keepdims=True) + 1e-06)
    normed = projected * inverse_length
    given = tn(onehot, normed.astype(BF)).astype(BF).reshape(4, 128, 128)
    embedded = jnp.concatenate(exchange(given), axis=0)
    along = jnp.sum(normed * incoming, axis=-1, keepdims=True)
    delta_projected = (inverse_length * (incoming - normed * along)).astype(BF)
    delta_second = matmul(delta_projected, project_full.T)
    residual_two, second_gain_delta, second_shift_delta = norm_backward(
        delta_second, second_normal, second_inverse, vec[6]
    )
    delta_outer = residual_two.astype(BF)
    outer_bias_delta = jnp.sum(delta_outer, axis=0, dtype=F32)
    outer_sum = sum_pack(*outer_pack(info, active, delta_outer, second_low, delta_projected))
    delta_active = matmul(delta_outer, outer_full.T)
    delta_inner = (delta_active * slope).astype(BF)
    inner_bias_delta = jnp.sum(delta_inner, axis=0, dtype=F32)
    delta_first = residual_two + matmul(delta_inner, inner_full.T)
    residual_one, first_gain_delta, first_shift_delta = norm_backward(
        delta_first, first_normal, first_inverse, vec[3]
    )
    delta_attended = residual_one.astype(BF)
    output_bias_delta = jnp.sum(delta_attended, axis=0, dtype=F32)
    delta_context = matmul(delta_attended, output_full.T).astype(BF)
    by_group = jnp.stack([delta_context[:, 192 * g : 192 * g + 192] for g in range(4)])
    ups = [head_pack(other_block(by_group, r)) for r in range(4)]
    ups = jnp.stack([ups[0], to_core(ups[1]), to_x(ups[2]), to_cross(ups[3])])
    inner_sum = sum_pack(*inner_pack(info, first_low, delta_inner, context, delta_attended))
    dq, dk, dv = attend_back(
        info,
        jnp.concatenate([ql_near, ql_far], axis=1),
        ups,
        jnp.concatenate([o_near, o_far], axis=1),
        k,
        kt,
        v,
    )
    sums = jnp.concatenate(
        [
            jnp.zeros((2, WIDTH), F32),
            jnp.stack(
                [
                    output_bias_delta,
                    first_gain_delta,
                    first_shift_delta,
                    outer_bias_delta,
                    second_gain_delta,
                    second_shift_delta,
                ]
            ),
            inner_bias_delta.reshape(8, 4, 96).transpose(1, 0, 2).reshape(4, WIDTH),
            jnp.zeros((4, WIDTH), F32),
        ],
        axis=0,
    )
    own, rest, pack = input_back(info, dq, dk, dv, heads_weight, x_all, sums)
    came = to_core(rest[0:2])
    passed = to_x((wide(rest[2]) + wide(came[1])).astype(BF))
    delta_home = (residual_one + own + wide(came[0]) + wide(passed)).astype(BF)

    half = wide(pack[0]) + wide(to_fsdp(pack[1], 1))
    quarter = half[0] + wide(to_fsdp(half[1].astype(BF), 2))
    mine = (quarter[0] + wide(to_fsdp(quarter[1].astype(BF), 4))).astype(BF)
    heads_all = wide(lax.all_gather(mine, "ctx"))
    outer_all = wide(lax.all_gather(outer_sum, "ctx"))
    inner_all = wide(lax.all_gather(inner_sum, "ctx"))

    def heads_columns(start):
        return jnp.concatenate([heads_all[g, :, start : start + 192] for g in range(4)], axis=1)

    vec_all = jnp.sum(heads_all[:, :, 576:588], axis=0)
    inner_grad = jnp.concatenate(
        [inner_all[g, 96 * h : 96 * h + 96] for g in range(4) for h in range(2)], axis=1
    )
    outer_grad = jnp.concatenate(
        [
            jnp.concatenate([outer_all[2 * a + b, :192] for b in range(2)], axis=1)
            for a in range(2)
        ],
        axis=0,
    )
    output_grad = jnp.concatenate(
        [
            jnp.concatenate([inner_all[2 * a + b, 192:240] for b in range(2)], axis=1)
            for a in range(2)
        ],
        axis=0,
    )
    project_grad = outer_all[:, 192:200].reshape(4, 8, 3, 128).transpose(0, 2, 1, 3).reshape(96, 128)
    return (
        embedded[None],
        delta_home[None],
        heads_columns(0),
        heads_columns(192),
        heads_columns(384),
        vec_all[:, 0],
        vec_all[:, 1],
        output_grad,
        vec_all[:, 2],
        vec_all[:, 3],
        vec_all[:, 4],
        inner_grad,
        vec_all[:, 8:12].T.reshape(384),
        outer_grad,
        vec_all[:, 5],
        vec_all[:, 6],
        vec_all[:, 7],
        project_grad,
    )


def suits(mesh):
    return mesh.shape["ctx"] == 4 and mesh.shape["fsdp"] == 8


def solution(mesh):
    on_device = fast_device if suits(mesh) else generic_device

    return jax.shard_map(
        on_device,
        mesh=mesh,
        in_specs=(
            P("fsdp", "ctx", None),
            P("fsdp", None),
            P("fsdp", None),
            P("fsdp", None),
            P("fsdp", None),
            P("fsdp", None),
            P("fsdp"),
            P("fsdp"),
            P("fsdp", None),
            P("fsdp"),
            P("fsdp"),
            P("fsdp"),
            P("fsdp", None),
            P("fsdp"),
            P("fsdp", None),
            P("fsdp"),
            P("fsdp"),
            P("fsdp"),
            P("fsdp", None),
            P("fsdp", "ctx", None),
        ),
        out_specs=(
            P("fsdp", "ctx", None),
            P("fsdp", "ctx", None),
            P("fsdp", None),
            P("fsdp", None),
            P("fsdp", None),
            P("fsdp"),
            P("fsdp"),
            P("fsdp", None),
            P("fsdp"),
            P("fsdp"),
            P("fsdp"),
            P("fsdp", None),
            P("fsdp"),
            P("fsdp", None),
            P("fsdp"),
            P("fsdp"),
            P("fsdp"),
            P("fsdp", None),
        ),
        check_vma=False,
    )
```

```python
import functools

import jax
import jax.numpy as jnp
from jax import lax
from jax.experimental import pallas as pl
from jax.experimental.pallas import tpu as pltpu
from jax.sharding import PartitionSpec as P

HEADS = 12
HEAD_DIM = 64


def matmul(left, right):
    return jnp.dot(left, right, preferred_element_type=jnp.float32)


def norm_forward(value, gain, shift):
    centred = value - jnp.mean(value, axis=-1, keepdims=True)
    inverse = lax.rsqrt(jnp.mean(centred * centred, axis=-1, keepdims=True) + 1e-12)
    normal = centred * inverse
    return (normal * gain + shift, normal, inverse)


def norm_backward(upstream, normal, inverse, gain):
    scaled = upstream * gain
    first_mean = jnp.mean(scaled, axis=-1, keepdims=True)
    second_mean = jnp.mean(scaled * normal, axis=-1, keepdims=True)
    inward = inverse * (scaled - first_mean - normal * second_mean)
    return (inward, jnp.sum(upstream * normal, axis=0), jnp.sum(upstream, axis=0))


def gelu_slope(value):
    cumulative = 0.5 * (1.0 + jax.scipy.special.erf(value * 0.7071067811865476))
    return cumulative + value * jnp.exp(-0.5 * value * value) * 0.3989422804014327


def scored(query_heads, key_block, query_segments, segment_block, scale):
    scores = (
        jnp.einsum("qhd,khd->hqk", query_heads, key_block, preferred_element_type=jnp.float32)
        * scale
    )
    allowed = (query_segments[:, None] == segment_block[None, :])[None]
    return (scores, allowed)


def probabilities(scores, allowed, log_total):
    return jnp.where(allowed, jnp.exp(scores - log_total[..., None]), 0.0)


def log_totals(query_heads, key_blocks, query_segments, segment_blocks, scale):

    def log_advance(carry, pieces):
        running_max, running_sum = carry
        scores, allowed = scored(query_heads, pieces[0], query_segments, pieces[1], scale)
        masked = jnp.where(allowed, scores, -1e30)
        new_max = jnp.maximum(running_max, jnp.max(masked, axis=-1))
        fresh = jnp.sum(jnp.where(allowed, jnp.exp(masked - new_max[..., None]), 0.0), axis=-1)
        return ((new_max, running_sum * jnp.exp(running_max - new_max) + fresh), None)

    shape = (query_heads.shape[1], query_heads.shape[0])
    start = (jnp.full(shape, -1e30, jnp.float32), jnp.zeros(shape, jnp.float32))
    final = lax.scan(log_advance, start, (key_blocks, segment_blocks))[0]
    return final[0] + jnp.log(final[1])


def attend(query_heads, key_blocks, value_blocks, query_segments, segment_blocks, scale):
    log_total = log_totals(query_heads, key_blocks, query_segments, segment_blocks, scale)

    def attend_advance(carry, pieces):
        scores, allowed = scored(query_heads, pieces[0], query_segments, pieces[2], scale)
        probs = probabilities(scores, allowed, log_total).astype(jnp.bfloat16)
        return (
            carry
            + jnp.einsum("hqk,khd->qhd", probs, pieces[1], preferred_element_type=jnp.float32),
            None,
        )

    start = jnp.zeros(query_heads.shape, jnp.float32)
    mixed = lax.scan(attend_advance, start, (key_blocks, value_blocks, segment_blocks))[0]
    return (mixed, log_total)


def attend_backward(
    query_heads,
    key_blocks,
    value_blocks,
    query_segments,
    segment_blocks,
    scale,
    log_total,
    upstream,
):

    def first_pass(carry, pieces):
        scores, allowed = scored(query_heads, pieces[0], query_segments, pieces[2], scale)
        probs = probabilities(scores, allowed, log_total)
        delta_probs = jnp.einsum(
            "qhd,khd->hqk", upstream, pieces[1], preferred_element_type=jnp.float32
        )
        value_terms = jnp.einsum(
            "hqk,qhd->khd", probs.astype(jnp.bfloat16), upstream, preferred_element_type=jnp.float32
        )
        return (carry + jnp.sum(probs * delta_probs, axis=-1), value_terms)

    shape = (query_heads.shape[1], query_heads.shape[0])
    weighted, value_terms = lax.scan(
        first_pass, jnp.zeros(shape, jnp.float32), (key_blocks, value_blocks, segment_blocks)
    )

    def second_pass(carry, pieces):
        scores, allowed = scored(query_heads, pieces[0], query_segments, pieces[2], scale)
        probs = probabilities(scores, allowed, log_total)
        delta_probs = jnp.einsum(
            "qhd,khd->hqk", upstream, pieces[1], preferred_element_type=jnp.float32
        )
        delta_scores = (probs * (delta_probs - weighted[..., None])).astype(jnp.bfloat16)
        key_terms = jnp.einsum(
            "hqk,qhd->khd", delta_scores, query_heads, preferred_element_type=jnp.float32
        )
        return (
            carry
            + jnp.einsum(
                "hqk,khd->qhd", delta_scores, pieces[0], preferred_element_type=jnp.float32
            ),
            key_terms,
        )

    query_terms, key_terms = lax.scan(
        second_pass,
        jnp.zeros(query_heads.shape, jnp.float32),
        (key_blocks, value_blocks, segment_blocks),
    )
    return (query_terms * scale, key_terms * scale, value_terms)


def generic_device(
    tokens,
    dealt,
    segments,
    query_weight,
    key_weight,
    value_weight,
    query_bias,
    value_bias,
    output_weight,
    output_bias,
    first_gain,
    first_shift,
    inner_weight,
    inner_bias,
    outer_weight,
    outer_bias,
    second_gain,
    second_shift,
    project_weight,
    cotangent,
):
    peers = lax.axis_size("ctx")
    place = lax.axis_index("ctx")
    local_rows = tokens.shape[1]
    share = local_rows // peers
    order = dealt[0]
    table = (
        lax.dynamic_index_in_dim(order.reshape(peers, peers, share), place, 1, keepdims=False)
        - place * local_rows
    )
    flat_table = table.reshape(-1)
    home_tokens = tokens[0]
    width = home_tokens.shape[1]
    (
        query_full,
        key_full,
        value_full,
        output_full,
        query_shift,
        value_shift,
        output_shift,
        gain_one,
        shift_one,
    ) = (
        lax.all_gather(query_weight, "fsdp", axis=0, tiled=True),
        lax.all_gather(key_weight, "fsdp", axis=0, tiled=True),
        lax.all_gather(value_weight, "fsdp", axis=0, tiled=True),
        lax.all_gather(output_weight, "fsdp", axis=0, tiled=True),
        lax.all_gather(query_bias, "fsdp", axis=0, tiled=True),
        lax.all_gather(value_bias, "fsdp", axis=0, tiled=True),
        lax.all_gather(output_bias, "fsdp", axis=0, tiled=True),
        lax.all_gather(first_gain, "fsdp", axis=0, tiled=True),
        lax.all_gather(first_shift, "fsdp", axis=0, tiled=True),
    )
    outgoing = jnp.take(home_tokens, table, axis=0)
    here_tokens = lax.all_to_all(outgoing, "ctx", split_axis=0, concat_axis=0, tiled=True).reshape(
        local_rows, width
    )
    key_segments = jnp.take(segments[0], order, axis=0)
    query_segments = lax.dynamic_slice_in_dim(key_segments, place * local_rows, local_rows)
    queries = (matmul(here_tokens, query_full) + query_shift.astype(jnp.float32)).astype(
        jnp.bfloat16
    )
    own_keys = matmul(here_tokens, key_full).astype(jnp.bfloat16)
    own_values = (matmul(here_tokens, value_full) + value_shift.astype(jnp.float32)).astype(
        jnp.bfloat16
    )
    all_keys, all_values = (
        lax.all_gather(own_keys, "ctx", axis=0, tiled=True),
        lax.all_gather(own_values, "ctx", axis=0, tiled=True),
    )
    total = all_keys.shape[0]
    block = min(1024, total)
    count = total // block
    scale = HEAD_DIM ** (-0.5)
    query_heads = queries.reshape(local_rows, HEADS, HEAD_DIM)
    key_blocks = all_keys.reshape(count, block, HEADS, HEAD_DIM)
    value_blocks = all_values.reshape(count, block, HEADS, HEAD_DIM)
    segment_blocks = key_segments.reshape(count, block)
    mixed, log_total = attend(
        query_heads, key_blocks, value_blocks, query_segments, segment_blocks, scale
    )
    context = mixed.reshape(local_rows, width).astype(jnp.bfloat16)
    inner_full, inner_shift, outer_full, outer_shift, gain_two, shift_two, project_full = (
        lax.all_gather(inner_weight, "fsdp", axis=0, tiled=True),
        lax.all_gather(inner_bias, "fsdp", axis=0, tiled=True),
        lax.all_gather(outer_weight, "fsdp", axis=0, tiled=True),
        lax.all_gather(outer_bias, "fsdp", axis=0, tiled=True),
        lax.all_gather(second_gain, "fsdp", axis=0, tiled=True),
        lax.all_gather(second_shift, "fsdp", axis=0, tiled=True),
        lax.all_gather(project_weight, "fsdp", axis=0, tiled=True),
    )
    attended = matmul(context, output_full) + output_shift.astype(jnp.float32)
    first, first_normal, first_inverse = norm_forward(
        here_tokens.astype(jnp.float32) + attended,
        gain_one.astype(jnp.float32),
        shift_one.astype(jnp.float32),
    )
    first_low = first.astype(jnp.bfloat16)
    inner = matmul(first_low, inner_full) + inner_shift.astype(jnp.float32)
    active = jax.nn.gelu(inner, approximate=False).astype(jnp.bfloat16)
    outer = matmul(active, outer_full) + outer_shift.astype(jnp.float32)
    second, second_normal, second_inverse = norm_forward(
        first + outer, gain_two.astype(jnp.float32), shift_two.astype(jnp.float32)
    )
    second_low = second.astype(jnp.bfloat16)
    projected = matmul(second_low, project_full)
    inverse_length = lax.rsqrt(jnp.sum(projected * projected, axis=-1, keepdims=True) + 1e-06)
    normed = projected * inverse_length
    embedded = normed.astype(jnp.bfloat16)
    incoming = cotangent[0].astype(jnp.float32)
    along = jnp.sum(normed * incoming, axis=-1, keepdims=True)
    delta_projected = (inverse_length * (incoming - normed * along)).astype(jnp.bfloat16)
    project_delta = matmul(second_low.T, delta_projected)
    delta_second = matmul(delta_projected, project_full.T)
    residual_two, second_gain_delta, second_shift_delta = norm_backward(
        delta_second, second_normal, second_inverse, gain_two.astype(jnp.float32)
    )
    delta_outer = residual_two.astype(jnp.bfloat16)
    outer_bias_delta = jnp.sum(delta_outer, axis=0, dtype=jnp.float32)
    outer_delta = matmul(active.T, delta_outer)
    delta_active = matmul(delta_outer, outer_full.T)
    delta_inner = (delta_active * gelu_slope(inner)).astype(jnp.bfloat16)
    inner_bias_delta = jnp.sum(delta_inner, axis=0, dtype=jnp.float32)
    inner_delta = matmul(first_low.T, delta_inner)
    delta_first = residual_two + matmul(delta_inner, inner_full.T)
    residual_one, first_gain_delta, first_shift_delta = norm_backward(
        delta_first, first_normal, first_inverse, gain_one.astype(jnp.float32)
    )
    delta_attended = residual_one.astype(jnp.bfloat16)
    output_bias_delta = jnp.sum(delta_attended, axis=0, dtype=jnp.float32)
    output_delta = matmul(context.T, delta_attended)
    delta_context = matmul(delta_attended, output_full.T).astype(jnp.bfloat16)
    upstream = delta_context.reshape(local_rows, HEADS, HEAD_DIM)
    query_terms, key_terms, value_terms = attend_backward(
        query_heads,
        key_blocks,
        value_blocks,
        query_segments,
        segment_blocks,
        scale,
        log_total,
        upstream,
    )
    key_sums, value_sums = (
        lax.psum_scatter(
            key_terms.reshape(total, width).astype(jnp.bfloat16),
            "ctx",
            scatter_dimension=0,
            tiled=True,
        ).astype(jnp.float32),
        lax.psum_scatter(
            value_terms.reshape(total, width).astype(jnp.bfloat16),
            "ctx",
            scatter_dimension=0,
            tiled=True,
        ).astype(jnp.float32),
    )
    delta_keys = key_sums.astype(jnp.bfloat16)
    delta_values = value_sums.astype(jnp.bfloat16)
    delta_queries = query_terms.reshape(local_rows, width).astype(jnp.bfloat16)
    query_bias_delta = jnp.sum(delta_queries, axis=0, dtype=jnp.float32)
    value_bias_delta = jnp.sum(delta_values, axis=0, dtype=jnp.float32)
    query_delta = matmul(here_tokens.T, delta_queries)
    key_delta = matmul(here_tokens.T, delta_keys)
    value_delta = matmul(here_tokens.T, delta_values)
    delta_here = (
        residual_one
        + matmul(delta_queries, query_full.T)
        + matmul(delta_keys, key_full.T)
        + matmul(delta_values, value_full.T)
    ).astype(jnp.bfloat16)
    coming_home = lax.all_to_all(
        delta_here.reshape(peers, share, width), "ctx", split_axis=0, concat_axis=0, tiled=True
    )
    delta_home = (
        jnp.zeros((local_rows, width), jnp.bfloat16)
        .at[flat_table]
        .set(coming_home.reshape(local_rows, width))
    )
    (
        inner_part,
        inner_bias_part,
        outer_part,
        outer_bias_part,
        second_gain_part,
        second_shift_part,
        project_part,
    ) = (
        lax.psum_scatter(
            inner_delta.astype(jnp.bfloat16), "fsdp", scatter_dimension=0, tiled=True
        ).astype(jnp.float32),
        lax.psum_scatter(
            inner_bias_delta.astype(jnp.bfloat16), "fsdp", scatter_dimension=0, tiled=True
        ).astype(jnp.float32),
        lax.psum_scatter(
            outer_delta.astype(jnp.bfloat16), "fsdp", scatter_dimension=0, tiled=True
        ).astype(jnp.float32),
        lax.psum_scatter(
            outer_bias_delta.astype(jnp.bfloat16), "fsdp", scatter_dimension=0, tiled=True
        ).astype(jnp.float32),
        lax.psum_scatter(
            second_gain_delta.astype(jnp.bfloat16), "fsdp", scatter_dimension=0, tiled=True
        ).astype(jnp.float32),
        lax.psum_scatter(
            second_shift_delta.astype(jnp.bfloat16), "fsdp", scatter_dimension=0, tiled=True
        ).astype(jnp.float32),
        lax.psum_scatter(
            project_delta.astype(jnp.bfloat16), "fsdp", scatter_dimension=0, tiled=True
        ).astype(jnp.float32),
    )
    (
        query_part,
        key_part,
        value_part,
        query_bias_part,
        value_bias_part,
        output_part,
        output_bias_part,
        first_gain_part,
        first_shift_part,
    ) = (
        lax.psum_scatter(
            query_delta.astype(jnp.bfloat16), "fsdp", scatter_dimension=0, tiled=True
        ).astype(jnp.float32),
        lax.psum_scatter(
            key_delta.astype(jnp.bfloat16), "fsdp", scatter_dimension=0, tiled=True
        ).astype(jnp.float32),
        lax.psum_scatter(
            value_delta.astype(jnp.bfloat16), "fsdp", scatter_dimension=0, tiled=True
        ).astype(jnp.float32),
        lax.psum_scatter(
            query_bias_delta.astype(jnp.bfloat16), "fsdp", scatter_dimension=0, tiled=True
        ).astype(jnp.float32),
        lax.psum_scatter(
            value_bias_delta.astype(jnp.bfloat16), "fsdp", scatter_dimension=0, tiled=True
        ).astype(jnp.float32),
        lax.psum_scatter(
            output_delta.astype(jnp.bfloat16), "fsdp", scatter_dimension=0, tiled=True
        ).astype(jnp.float32),
        lax.psum_scatter(
            output_bias_delta.astype(jnp.bfloat16), "fsdp", scatter_dimension=0, tiled=True
        ).astype(jnp.float32),
        lax.psum_scatter(
            first_gain_delta.astype(jnp.bfloat16), "fsdp", scatter_dimension=0, tiled=True
        ).astype(jnp.float32),
        lax.psum_scatter(
            first_shift_delta.astype(jnp.bfloat16), "fsdp", scatter_dimension=0, tiled=True
        ).astype(jnp.float32),
    )
    results = (
        lax.psum(query_part.astype(jnp.bfloat16), "ctx").astype(jnp.float32),
        lax.psum(key_part.astype(jnp.bfloat16), "ctx").astype(jnp.float32),
        lax.psum(value_part.astype(jnp.bfloat16), "ctx").astype(jnp.float32),
        lax.psum(query_bias_part.astype(jnp.bfloat16), "ctx").astype(jnp.float32),
        lax.psum(value_bias_part.astype(jnp.bfloat16), "ctx").astype(jnp.float32),
        lax.psum(output_part.astype(jnp.bfloat16), "ctx").astype(jnp.float32),
        lax.psum(output_bias_part.astype(jnp.bfloat16), "ctx").astype(jnp.float32),
        lax.psum(first_gain_part.astype(jnp.bfloat16), "ctx").astype(jnp.float32),
        lax.psum(first_shift_part.astype(jnp.bfloat16), "ctx").astype(jnp.float32),
        lax.psum(inner_part.astype(jnp.bfloat16), "ctx").astype(jnp.float32),
        lax.psum(inner_bias_part.astype(jnp.bfloat16), "ctx").astype(jnp.float32),
        lax.psum(outer_part.astype(jnp.bfloat16), "ctx").astype(jnp.float32),
        lax.psum(outer_bias_part.astype(jnp.bfloat16), "ctx").astype(jnp.float32),
        lax.psum(second_gain_part.astype(jnp.bfloat16), "ctx").astype(jnp.float32),
        lax.psum(second_shift_part.astype(jnp.bfloat16), "ctx").astype(jnp.float32),
        lax.psum(project_part.astype(jnp.bfloat16), "ctx").astype(jnp.float32),
    )
    return (
        embedded[None],
        delta_home[None],
        results[0],
        results[1],
        results[2],
        results[3],
        results[4],
        results[5],
        results[6],
        results[7],
        results[8],
        results[9],
        results[10],
        results[11],
        results[12],
        results[13],
        results[14],
        results[15],
    )


BF = jnp.bfloat16
F32 = jnp.float32
ROWS = 512
WIDTH = 768
HIDDEN = 3072
LOCAL = 3
FAR = 2.0**100
KROWS = 256
SCALE = HEAD_DIM ** (-0.5)


def nt(left, right):
    return lax.dot_general(left, right, (((1,), (1,)), ((), ())), preferred_element_type=F32)


def nn(left, right):
    return lax.dot_general(left, right, (((1,), (0,)), ((), ())), preferred_element_type=F32)


def tn(left, right):
    return lax.dot_general(left, right, (((0,), (0,)), ((), ())), preferred_element_type=F32)


def wide(value):
    return value.astype(F32)


def to_core(value):
    return lax.ppermute(value, "ctx", [(i, i ^ 1) for i in range(4)])


def to_x(value):
    return lax.ppermute(value, "ctx", [(i, i ^ 2) for i in range(4)])


def to_cross(value):
    return lax.ppermute(value, "ctx", [(i, i ^ 3) for i in range(4)])


def to_fsdp(value, bit):
    return lax.ppermute(value, "fsdp", [(i, i ^ bit) for i in range(8)])


def along_z(value, step):
    return lax.ppermute(value, "fsdp", [(i, (i + 2 * step) % 8) for i in range(8)])


def to_mixed(value, first):
    pairs = []
    for c in range(4):
        for f in range(8):
            target = (c ^ 2) * 8 + f if (c % 2 == 0) == first else c * 8 + (f ^ 1)
            pairs.append((c * 8 + f, target))
    return lax.ppermute(value, ("ctx", "fsdp"), pairs)


def after(value, *others):
    return lax.optimization_barrier((value, *others))[0]


def together(*values):
    return lax.optimization_barrier(values)


def three_parts(value):
    high = wide(value.astype(BF))
    rest = value - high
    middle = wide(rest.astype(BF))
    return high, middle, rest - middle


def lanes_of(rows, n=128):
    return lax.broadcasted_iota(jnp.int32, (rows, n), 1)


def run(
    kernel, name, info, inputs, outs, scratch=(), limit=10, loose=(), loose_outs=(), alias=(), small=False
):
    memory = pl.BlockSpec(memory_space=pltpu.VMEM)
    outside = pl.BlockSpec(memory_space=pltpu.HBM)
    return pl.pallas_call(
        kernel,
        in_specs=[pl.BlockSpec(memory_space=pltpu.SMEM)]
        + [outside if i in loose else memory for i in range(len(inputs))],
        out_specs=[pl.BlockSpec(memory_space=pltpu.SMEM)]
        if small
        else [outside if i in loose_outs else memory for i in range(len(outs))],
        out_shape=[jax.ShapeDtypeStruct(s, t) for s, t in outs],
        scratch_shapes=list(scratch),
        input_output_aliases={i + 1: o for i, o in alias},
        compiler_params=pltpu.CompilerParams(vmem_limit_bytes=limit << 20),
        cost_estimate=pl.CostEstimate(flops=1000, bytes_accessed=1000, transcendentals=0),
        name=name,
    )(info, *inputs)


def start_copies(pairs, sems):
    copies = [pltpu.make_async_copy(a, b, sems.at[i]) for i, (a, b) in enumerate(pairs)]
    for copy in copies:
        copy.start()
    return copies


def aligned(value, n):
    return pl.multiple_of(value, n)


def piece_rows(info, n):
    z, y = info[1] // 2, lax.rem(info[1], 2)
    rows = []
    for k in range(4):
        source = lax.rem(z + 4 - k, 4)
        rows += [aligned((source * 2 + t) * n, 32) for t in (y, 1 - y)]
    return rows


def prepare_forward_kernel(info, wi_in, wo_in, w2_in, p_in, outer_out, inner_out, sems):
    core = lax.rem(info[0], 2)
    copies = start_copies(
        [
            (w2_in.at[pl.ds(aligned(core * 192, 64), 96)], outer_out.at[:, 0:768]),
            (w2_in.at[pl.ds(aligned(core * 192 + 96, 32), 96)], outer_out.at[:, 768:1536]),
            (p_in, outer_out.at[:, 1536:1664]),
            (wi_in.at[:, pl.ds(aligned(core * 1536, 512), 1536)], inner_out.at[:, 0:1536]),
            (wo_in.at[:, pl.ds(aligned(core * 384, 128), 384)], inner_out.at[:, 1536:1920]),
        ],
        sems,
    )
    for copy in copies:
        copy.wait()


def prepare_heads_kernel(info, *refs):
    ins, heads_out, held, sems = refs[:4], refs[4], refs[5:9], refs[9]
    c = info[0]
    copies = start_copies(zip(ins, held), sems)
    q_ref, k_ref, v_ref, vec_ref = held
    for copy in copies:
        copy.wait()
    side = vec_ref[...].T[:96, :64]
    for value in range(4):

        @pl.when(c == value)
        def _():
            at = slice(192 * value, 192 * value + 192)
            parts = [wide(ref[:, at]) for ref in (q_ref, k_ref, v_ref)]
            heads_out[...] = jnp.concatenate([*parts, side], axis=1).astype(BF)


def lay_kernel(info, *refs):
    pieces, outs, sems = refs[:8], refs[8:-1], refs[-1]
    pairs, start = [], 0
    for out in outs:
        stop = start + out.shape[1]
        for ref, row in zip(pieces, piece_rows(info, 96)):
            pairs.append((ref.at[:, start:stop], out.at[pl.ds(row, 96)]))
        start = stop
    copies = start_copies(pairs, sems)
    for copy in copies:
        copy.wait()


def lay(info, pieces, widths):
    return run(
        lay_kernel,
        "lay",
        info,
        pieces,
        [((WIDTH, n), BF) for n in widths],
        [pltpu.SemaphoreType.DMA((8 * len(widths),))],
        loose=range(8),
    )


def places_kernel(place, seg_ref, info_out):
    seg = wide(seg_ref[...])
    at = lanes_of(1, seg.shape[1])
    for i in range(4):
        info_out[i] = place[i]
        info_out[12 + i] = 0
        start = jnp.sum(jnp.where(at == ROWS * i, seg, 0.0))
        end = jnp.sum(jnp.where(at == ROWS * i + ROWS - 1, seg, 0.0))
        low = jnp.sum(jnp.where(seg < start, 1.0, 0.0)).astype(jnp.int32)
        high = jnp.sum(jnp.where(seg <= end, 1.0, 0.0)).astype(jnp.int32)
        info_out[4 + i] = low // KROWS
        info_out[8 + i] = (high + KROWS - 1) // KROWS


def project_kernel(info, *refs):
    x_refs, w_refs = refs[0:4], refs[4:12]
    seg_ref = refs[12]
    q_out, k_out, v_out, kt_out, vt_out, w_out, vec_out, x_s, sems = refs[13:]
    c = info[0]
    copies = start_copies(
        [(ref, w_out.at[pl.ds(row, 96)]) for ref, row in zip(w_refs, piece_rows(info, 96))]
        + [(ref, x_s.at[r]) for r, ref in enumerate(x_refs)],
        sems,
    )
    for copy in copies[:8]:
        copy.wait()
    weights = w_out[...]
    turned = wide(weights[:, 512:640]).T
    vec_out[...] = turned[64:80]
    lane = lanes_of(WIDTH, 640)
    row = lax.broadcasted_iota(jnp.int32, (WIDTH, 640), 0)
    wanted = jnp.where(lane < 384, lane, lane - 384) + 192 * c
    chosen = nn(turned[64:80].astype(BF), wide(row == wanted).astype(BF))
    lane1 = lanes_of(1, 640)
    bias = jnp.where(
        lane1 < 192,
        chosen[0:1],
        jnp.where((lane1 >= 384) & (lane1 < 576), chosen[1:2], 0.0),
    )
    lanes = lanes_of(ROWS)
    for r in range(4):
        rows = pl.ds(aligned(jnp.bitwise_xor(c, r) * ROWS, ROWS), ROWS)
        copies[8 + r].wait()
        result = nn(x_s[r], weights) + bias
        seg = seg_ref[:, pl.ds(aligned(jnp.bitwise_xor(c, r) * ROWS, ROWS), ROWS)]
        same = jnp.broadcast_to(wide(seg), (128, ROWS)).T == wide(lanes - 64)
        qa = jnp.where(same & (lanes < 67), 1.0, 0.0)
        ka = jnp.where(lanes < 67, jnp.where(same, 0.0, -FAR), jnp.where(lanes < 70, 1.0, 0.0))
        for slot in range(9):
            pair = result[:, 128 * (slot // 2) : 128 * (slot // 2) + 128]
            if slot % 2:
                pair = pltpu.roll(pair, 64, 1)
            kind, h = slot // 3, slot % 3
            if kind == 0:
                low = wide(pair.astype(BF)) * SCALE
                q_out[h, rows, :] = jnp.where(lanes < 64, low, qa).astype(BF)
            elif kind == 1:
                value = jnp.where(lanes < 64, pair, ka)
                k_out[h, rows, :] = value.astype(BF)
                kt_out[h, :, rows] = value.T[:64].astype(BF)
            else:
                value = jnp.where(lanes < 64, pair, jnp.where(lanes < 67, 1.0, 0.0))
                v_out[h, rows, :] = value.astype(BF)
                vt_out[h, :, rows] = value.T[:80].astype(BF)


def attend_kernel(info, q_ref, k_ref, vt_ref, cot_ref, *refs, chip):
    each = range(LOCAL)
    top_s, sum_s = refs[6:]
    for step in range(2):
        o_ref, ql_ref, pack_ref = refs[3 * step : 3 * step + 3]
        place = jnp.bitwise_xor(info[0], step + 2 * chip)
        mine = pl.ds(aligned(place * ROWS, ROWS), ROWS)
        top_s[...] = jnp.full_like(top_s, -3e38)
        sum_s[...] = jnp.zeros_like(sum_s)

        def advance(block, carry):
            rows = pl.ds(aligned(block * KROWS, KROWS), KROWS)
            scores = [nt(k_ref[h, rows], q_ref[h, mine]) for h in each]
            before = [top_s[h, :1] for h in each]
            peaks = [
                jnp.maximum(before[h], jnp.max(scores[h], axis=0, keepdims=True)) for h in each
            ]
            probs = [jnp.exp(scores[h] - peaks[h]).astype(BF) for h in each]
            shrink = [jnp.exp(before[h] - peaks[h]) for h in each]
            fresh = [nn(vt_ref[h, :, rows], probs[h]) for h in each]
            for h in each:
                sum_s[h] = sum_s[h] * shrink[h] + fresh[h]
                top_s[h] = jnp.broadcast_to(peaks[h], top_s.shape[1:])
            return carry

        lax.fori_loop(info[4 + place], info[8 + place], advance, 0)
        lanes = lanes_of(ROWS)
        subs = lax.broadcasted_iota(jnp.int32, (128, ROWS), 0)
        outs = []
        for h in each:
            sums = sum_s[h]
            total = sums[64:65]
            parts = three_parts(top_s[h, :1] + jnp.log(total))
            tall = jnp.concatenate([sums[:64] / total, jnp.zeros((64, ROWS), F32)], axis=0)
            for i in range(3):
                tall = jnp.where(subs == 67 + i, -parts[i], tall)
            turned = tall.T
            out = jnp.where(lanes < 64, turned, 0.0)
            outs.append(out)
            o_ref[h] = out.astype(BF)
            ql_ref[h] = jnp.where(lanes < 67, wide(q_ref[h, mine]), turned).astype(BF)
        pack_ref[0:512] = (outs[0] + pltpu.roll(outs[1], 64, 1)).astype(BF)
        pack_ref[512:768] = (outs[2][:256] + pltpu.roll(outs[2][256:], 64, 1)).astype(BF)
        pack_ref[768:896] = cot_ref[pl.ds(aligned(place * 128, 128), 128), :]


def attend_rows(info, q, k, vt, cotangent, chip):
    return run(
        functools.partial(attend_kernel, chip=chip),
        "attend_rows",
        info,
        [q, k, vt, cotangent],
        ([((LOCAL, ROWS, 128), BF)] * 2 + [((896, 128), BF)]) * 2,
        [pltpu.VMEM((LOCAL, 8, ROWS), F32), pltpu.VMEM((LOCAL, 80, ROWS), F32)],
    )


def attend_back_kernel(info, *refs, r):
    each = range(LOCAL)
    ql_ref, up_ref, o_ref, k_ref, kt_ref, v_ref = refs[:6]
    *outs, dk_s, dv_s, dq_s, do_s = refs[6:]
    lanes = lanes_of(ROWS)
    if r == 0:
        (dq_ref,) = outs
        dk_s[...] = jnp.zeros_like(dk_s)
        dv_s[...] = jnp.zeros_like(dv_s)
    elif r < 3:
        _, _, dq_ref = outs
    else:
        all_ref, emb_ref = outs[8:]
        for i, ref in enumerate((*outs[5:8], up_ref)):
            at = pl.ds(aligned(jnp.bitwise_xor(info[0], i) * 128, 128), 128)
            emb_ref[at, :] = ref[768:896]
    place = jnp.bitwise_xor(info[0], r)
    dq_s[...] = jnp.zeros_like(dq_s)
    pair = wide(up_ref[0:512])
    last = wide(up_ref[512:768])
    ups = [
        pair,
        pltpu.roll(pair, 64, 1),
        jnp.concatenate([last, pltpu.roll(last, 64, 1)], axis=0),
    ]
    for h in each:
        up = jnp.where(lanes < 64, ups[h], 0.0)
        parts = three_parts(jnp.sum(up * wide(o_ref[h]), axis=1, keepdims=True))
        for i in range(3):
            up = jnp.where(lanes == 64 + i, -parts[i], up)
        do_s[h] = up.astype(BF)

    def advance(block, carry):
        rows = pl.ds(aligned(block * KROWS, KROWS), KROWS)
        scores = [nt(k_ref[h, rows], ql_ref[h]) for h in each]
        rises = [nt(v_ref[h, rows], do_s[h]) for h in each]
        probs = [jnp.exp(scores[h]) for h in each]
        deltas = [(probs[h] * rises[h]).astype(BF) for h in each]
        lows = [probs[h].astype(BF) for h in each]
        for_values = [nn(lows[h], do_s[h]) for h in each]
        for_keys = [nn(deltas[h], ql_ref[h]) for h in each]
        for_queries = [nn(kt_ref[h, :, rows], deltas[h]) for h in each]
        for h in each:
            dv_s[h, rows] += for_values[h]
            dk_s[h, rows] += for_keys[h]
            dq_s[h] += for_queries[h]
        return carry

    lax.fori_loop(info[4 + place], info[8 + place], advance, 0)
    turned = []
    for h in each:
        tall = jnp.concatenate([dq_s[h], jnp.zeros((64, ROWS), F32)], axis=0)
        turned.append(tall.T * SCALE)
    both = (turned[0] + pltpu.roll(turned[1], 64, 1)).astype(BF)
    if r < 3:
        dq_ref[:, 0:128] = both
        dq_ref[:, 128:256] = turned[2].astype(BF)
        return
    mine = pl.ds(aligned(place * ROWS, ROWS), ROWS)
    all_ref[mine, 0:128] = both
    all_ref[mine, 128:256] = turned[2].astype(BF)
    for i, ref in enumerate(outs[2:5]):
        at = pl.ds(aligned(jnp.bitwise_xor(info[0], i) * ROWS, ROWS), ROWS)
        all_ref[at, 0:256] = ref[...]
    for b in range(4):
        rows = pl.ds(b * ROWS, ROWS)
        low = [jnp.where(lanes < 64, ref[h, rows], 0.0) for ref in (dk_s, dv_s) for h in each]
        high = [pltpu.roll(value, 64, 1) for value in low]
        all_ref[rows, 128:256] = (wide(all_ref[rows, 128:256]) + high[0]).astype(BF)
        all_ref[rows, 256:384] = (low[1] + high[2]).astype(BF)
        all_ref[rows, 384:512] = (low[3] + high[4]).astype(BF)
        all_ref[rows, 512:640] = low[5].astype(BF)


def attend_back(info, r, ql, up, o, k, kt, v, carried=(), earlier=()):
    sums = [(k.shape, F32)] * 2
    part = [((ROWS, 256), BF)]
    whole = [((k.shape[1], 640), BF), ((ROWS, 128), BF)]
    first = len(part if r < 3 else whole)
    return run(
        functools.partial(attend_back_kernel, r=r),
        "attend_back",
        info,
        [ql, up, o, k, kt, v, *carried, *earlier],
        (part if r < 3 else whole) + sums,
        [pltpu.VMEM((LOCAL, 64, ROWS), F32), pltpu.VMEM((LOCAL, ROWS, 128), BF)],
        alias=((6, first), (7, first + 1)) if r else (),
    )


def gaussian(value):
    below = 0.5 * (1.0 + lax.erf(value * 0.7071067811865476))
    return below, jnp.exp(-0.5 * value * value) * 0.3989422804014327


def norm_rows(value):
    centred = value - jnp.mean(value, axis=-1, keepdims=True)
    inverse = lax.rsqrt(jnp.mean(centred * centred, axis=-1, keepdims=True) + 1e-12)
    return centred * inverse, inverse


def norm_rows_back(upstream, normal, inverse, gain):
    scaled = upstream * gain
    first_mean = jnp.mean(scaled, axis=-1, keepdims=True)
    second_mean = jnp.mean(scaled * normal, axis=-1, keepdims=True)
    return inverse * (scaled - first_mean - normal * second_mean)


def column_sums(value):
    return jnp.sum(value, axis=0, keepdims=True)


def hidden_half(half, first, wi_ref, vec_ref, active_out, slope_out):
    shift = jnp.concatenate(
        [vec_ref[8 + k : 9 + k, 96 * f : 96 * f + 96] for f in range(8) for k in range(4)], axis=1
    )
    shift = jnp.where(half == 0, shift[:, :1536], shift[:, 1536:])
    for block in range(3):
        at = pl.ds(aligned(half * 1536 + block * 512, 512), 512)
        value = nn(first, wi_ref[:, at]) + shift[:, block * 512 : block * 512 + 512]
        below, bell = gaussian(value)
        active_out[:, at] = (value * below).astype(BF)
        slope_out[:, at] = (below + value * bell).astype(BF)


def inner_own_kernel(info, *refs):
    x_ref, *packs = refs[:5]
    vec_ref, wo_own, wo_other, g_ref = refs[5:9]
    (
        normal_out,
        inverse_out,
        first_out,
        active_out,
        slope_out,
        context_out,
        wo_out,
        wi_out,
        arrived_out,
        sems,
    ) = refs[9:]
    c = info[0]
    core = lax.rem(c, 2)
    own = pl.ds(aligned(core * 1536, 512), 1536)
    (copy,) = start_copies([(g_ref, wi_out.at[:, own])], sems)
    for r in range(4):
        group = jnp.bitwise_xor(c, r)
        arrived_out[pl.ds(aligned(group * 128, 128), 128), :] = packs[r][768:896]
        rows = pl.ds(aligned(group * 192, 64), 192)
        for half, ref in ((core, wo_own), (1 - core, wo_other)):
            at = pl.ds(aligned(half * 384, 128), 384)
            wo_out[256 * r : 256 * r + 192, at] = ref[rows, :]
        wo_out[256 * r + 192 : 256 * r + 256, :] = jnp.zeros((64, WIDTH), BF)
        context_out[:, 256 * r : 256 * r + 128] = packs[r][0:512]
        last = wide(packs[r][512:768])
        last = jnp.concatenate([last, pltpu.roll(last, 64, 1)], axis=0)
        context_out[:, 256 * r + 128 : 256 * r + 256] = jnp.where(
            lanes_of(ROWS) < 64, last, 0.0
        ).astype(BF)
    attended = nn(context_out[...], wo_out[...]) + vec_ref[2:3]
    normal, inverse = norm_rows(wide(x_ref[...]) + attended)
    normal_out[...] = normal
    inverse_out[...] = inverse
    first = (normal * vec_ref[3:4] + vec_ref[4:5]).astype(BF)
    first_out[...] = first
    copy.wait()
    hidden_half(core, first, wi_out, vec_ref, active_out, slope_out)


def inner_other_kernel(info, first_ref, vec_ref, g_ref, a_ref, s_ref, w_ref, *refs):
    active_out, slope_out, wi_out, sems = refs
    core = 1 - lax.rem(info[0], 2)
    other = pl.ds(aligned(core * 1536, 512), 1536)
    (copy,) = start_copies([(g_ref, wi_out.at[:, other])], sems)
    copy.wait()
    hidden_half(core, first_ref[...], wi_out, vec_ref, active_out, slope_out)


def outer_kernel(
    info,
    active_ref,
    own_ref,
    other_ref,
    normal_ref,
    vec_ref,
    table_ref,
    arrived_ref,
    residual_out,
    do_out,
    second_out,
    dp_out,
    given_out,
    sums_out,
    w2_out,
    wp_ref,
    sems,
):
    core = lax.rem(info[0], 2)
    copies = start_copies(
        [
            (
                ref.at[pl.ds(96 * f, 96), 768 * t : 768 * t + 768],
                w2_out.at[pl.ds(aligned(384 * f + 192 * half + 96 * t, 32), 96)],
            )
            for f in range(8)
            for half, ref in ((core, own_ref), (1 - core, other_ref))
            for t in range(2)
        ]
        + [(own_ref.at[:, 1536:1664], wp_ref)],
        sems,
    )
    outer = vec_ref[5:6]
    for part in range(2):
        for copy in copies[16 * part : 16 * part + 16]:
            copy.wait()
        at = slice(1536 * part, 1536 * part + 1536)
        outer = outer + nn(active_ref[:, at], w2_out[at, :])
    copies[32].wait()
    first = normal_ref[...] * vec_ref[3:4] + vec_ref[4:5]
    normal, inverse = norm_rows(first + outer)
    second = (normal * vec_ref[6:7] + vec_ref[7:8]).astype(BF)
    second_out[...] = second
    projected = nn(second, wp_ref[...])
    scale = lax.rsqrt(jnp.sum(projected * projected, axis=-1, keepdims=True) + 1e-06)
    normed = projected * scale
    where = lax.broadcasted_iota(jnp.int32, (ROWS, ROWS), 0) + info[0] * ROWS
    table = jnp.concatenate(
        [table_ref[:, pl.ds(aligned(ROWS * d + info[0] * 128, 128), 128)] for d in range(4)],
        axis=1,
    )
    onehot = wide(table == where).astype(BF)
    given_out[...] = tn(onehot, normed.astype(BF)).astype(BF)
    incoming = nn(onehot, arrived_ref[...])
    along = jnp.sum(normed * incoming, axis=-1, keepdims=True)
    delta = (scale * (incoming - normed * along)).astype(BF)
    dp_out[...] = delta
    upstream = nt(delta, wp_ref[...])
    residual = norm_rows_back(upstream, normal, inverse, vec_ref[6:7])
    residual_out[...] = residual
    low = residual.astype(BF)
    do_out[...] = low
    sums_out[...] = jnp.concatenate(
        [
            column_sums(wide(low)),
            column_sums(upstream * normal),
            column_sums(upstream),
            jnp.zeros((5, WIDTH), F32),
        ],
        axis=0,
    )


def hidden_back_kernel(info, do_ref, w2_ref, slope_ref, di_out, side_out):
    for block in range(HIDDEN // 512):
        at = slice(block * 512, block * 512 + 512)
        value = nt(do_ref[...], w2_ref[at, :]) * wide(slope_ref[:, at])
        low = value.astype(BF)
        di_out[:, at] = low
        side_out[:, at] = column_sums(wide(low))


def first_kernel(
    info,
    di_ref,
    wi_ref,
    residual_ref,
    normal_ref,
    inverse_ref,
    vec_ref,
    wo_ref,
    given_ref,
    residual_out,
    da_out,
    sums_out,
    *up_outs,
):
    upstream = residual_ref[...] + nt(di_ref[...], wi_ref[...])
    normal = normal_ref[...]
    residual = norm_rows_back(upstream, normal, inverse_ref[...], vec_ref[3:4])
    residual_out[...] = residual
    low = residual.astype(BF)
    da_out[...] = low
    sums_out[...] = jnp.concatenate(
        [
            column_sums(wide(low)),
            column_sums(upstream * normal),
            column_sums(upstream),
            jnp.zeros((5, WIDTH), F32),
        ],
        axis=0,
    )
    for r in (2, 3, 1, 0):
        out = up_outs[r]
        up = nt(low, wo_ref[256 * r : 256 * r + 256, :])
        out[0:512] = up[:, 0:128].astype(BF)
        last = up[:, 128:256]
        out[512:768] = (last[:256] + pltpu.roll(last[256:], 64, 1)).astype(BF)
        place = jnp.bitwise_xor(info[0], r)
        out[768:896] = given_ref[pl.ds(aligned(place * 128, 128), 128), :]


def spots(info, f):
    mine = info[1]
    my_z, my_y = mine // 2, lax.rem(mine, 2)
    z, y = (f // 2, f % 2) if isinstance(f, int) else (f // 2, lax.rem(f, 2))
    apart = jnp.bitwise_xor(my_z, z)
    return jnp.bitwise_xor(my_y, y), lax.rem(apart, 2), apart // 2


def heads_grad_kernel(info, *refs):
    x_refs, (all_ref, first_ref, outer_ref, side_ref, pack_ref, x_s, sems) = refs[:4], refs[4:]
    c = info[0]
    copies = start_copies(
        [
            (ref, x_s.at[pl.ds(aligned(jnp.bitwise_xor(c, r) * ROWS, ROWS), ROWS)])
            for r, ref in enumerate(x_refs)
        ],
        sems,
    )
    sums = column_sums(wide(all_ref[...]))
    row = lax.broadcasted_iota(jnp.int32, (640, WIDTH), 0)
    lane = lanes_of(640, WIDTH)
    at = lax.broadcasted_iota(jnp.int32, (16, WIDTH), 0)
    rows = [jnp.zeros((2, WIDTH), F32), first_ref[0:3], outer_ref[0:3]]
    for k in range(4):
        starts = [384 * f + 96 * k for f in range(8)]
        rows.append(jnp.concatenate([side_ref[:, i : i + 96] for i in starts], axis=1))
    vectors = jnp.concatenate([*rows, jnp.zeros((4, WIDTH), F32)], axis=0)
    parts = three_parts(sums)
    for kind, first in ((0, 0), (1, 384)):
        chosen = (row - first + 192 * c == lane) & (row >= first) & (row < first + 192)
        chosen = wide(chosen).astype(BF)
        value = sum(nn(jnp.broadcast_to(part, (16, 640)).astype(BF), chosen) for part in parts)
        vectors = jnp.where(at == kind, value, vectors)
    tall = jnp.concatenate(
        [jnp.zeros((64, WIDTH), F32), vectors, jnp.zeros((48, WIDTH), F32)], axis=0
    )
    side = tall.T
    for copy in copies:
        copy.wait()
    delta = tn(x_s[...], all_ref[...])
    for f in range(8):
        i, j, k = spots(info, f)
        piece = delta[96 * f : 96 * f + 96]
        pack_ref[i, j, k, :, 0:512] = piece[:, :512].astype(BF)
        pack_ref[i, j, k, :, 512:640] = (piece[:, 512:] + side[96 * f : 96 * f + 96]).astype(BF)


def input_grad_kernel(info, all_ref, w_ref, residual_ref, own_ref, core_ref, next_ref):
    for r in (1, 3, 2, 0):
        rows = pl.ds(aligned(jnp.bitwise_xor(info[0], r) * ROWS, ROWS), ROWS)
        value = nt(all_ref[rows, :], w_ref[...])
        if r == 0:
            own_ref[...] = residual_ref[...] + value
        elif r == 2:
            next_ref[...] = value
        else:
            core_ref[r // 2] = value.astype(BF)


def finish_heads_kernel(info, heads_ref, q_out, k_out, v_out, *refs):
    vec_outs, held, sems = refs[:9], refs[9:12], refs[12]
    copies = []
    for kind, (out, ref) in enumerate(zip((q_out, k_out, v_out), held)):
        parts = [wide(heads_ref[g, :, 192 * kind : 192 * kind + 192]) for g in range(4)]
        ref[...] = jnp.concatenate(parts, axis=1)
        copy = pltpu.make_async_copy(ref, out, sems.at[kind])
        copy.start()
        copies.append(copy)
    side = sum(wide(heads_ref[g, :, 512:640]) for g in range(4))
    tall = jnp.concatenate([side, jnp.zeros((32, 128), F32)], axis=0).T
    for i in range(8):
        vec_outs[i][...] = tall[64 + i : 65 + i, :96]
    vec_outs[8][...] = jnp.concatenate([tall[72 + i : 73 + i, :96] for i in range(4)], axis=1)
    for copy in copies:
        copy.wait()


def finish_forward_kernel(info, near_ref, far_ref, wi_out, w2_out, wo_out, wp_out, *scratch):
    wi_s, w2_s, wo_s, wp_s, sems = scratch
    for r in range(4):
        ref = far_ref if r % 2 else near_ref
        g = jnp.bitwise_xor(info[0], r)
        a, b = g // 2, lax.rem(g, 2)
        block = wide(ref[r // 2])
        across = pl.ds(aligned(b * 384, 128), 384)
        w2_s[pl.ds(aligned(a * 192, 64), 192), across] = block[0:192]
        for h in range(2):
            at = pl.ds(aligned(g * 768 + 384 * h, 128), 384)
            wi_s[:, at] = block[208 + 96 * h : 304 + 96 * h]
        wo_s[pl.ds(aligned(a * 48, 16), 48), across] = block[400:448]
        for t in range(3):
            at = pl.ds(aligned(24 * g + 8 * t, 8), 8)
            wp_s[at, :] = block[192:200, 128 * t : 128 * t + 128]
    copies = start_copies(
        [(wi_s, wi_out), (w2_s, w2_out), (wo_s, wo_out), (wp_s, wp_out)], sems
    )
    for copy in copies:
        copy.wait()


def pair_index(info, keep, x, yr):
    xr = jnp.bitwise_xor(info[0] // 2, x)
    order = jnp.bitwise_xor(lax.rem(info[0], 2), keep)
    first = jnp.where(order == 0, xr, yr)
    second = jnp.where(order == 0, yr, xr)
    return first, second


def outer_pack_kernel(info, active_ref, do_ref, second_ref, dp_ref, keep_ref, send_ref, proj_s):
    core = lax.rem(info[0], 2)
    proj_s[...] = tn(second_ref[...], dp_ref[...])
    for f in range(8):
        yr, z0, z1 = spots(info, f)
        left = active_ref[:, 384 * f : 384 * f + 384]
        for k, ref in ((0, keep_ref), (1, send_ref)):
            half = jnp.bitwise_xor(core, k)
            right = do_ref[:, pl.ds(aligned(half * 384, 128), 384)]
            value = tn(left, right).astype(BF)
            for x in range(2):
                a, b = pair_index(info, k, x, yr)
                ref[a, b, z0, z1, 0:192, :] = value[192 * x : 192 * x + 192]
                start = 96 * f + 24 * (2 * x + half)
                across = jnp.concatenate(
                    [proj_s[pl.ds(aligned(start + 8 * g, 8), 8), :] for g in range(3)], axis=1
                )
                ref[a, b, z0, z1, 192:208, :] = jnp.concatenate(
                    [across, jnp.zeros((8, 384), F32)], axis=0
                ).astype(BF)


def inner_pack_kernel(info, first_ref, di_ref, context_ref, da_ref, keep_ref, send_ref):
    c = info[0]
    core = lax.rem(c, 2)
    for k, ref in ((0, keep_ref), (1, send_ref)):
        half = jnp.bitwise_xor(core, k)
        for x in range(2):
            for part in range(2):
                start = (2 * x + half) * 768 + 384 * part
                right = di_ref[:, pl.ds(aligned(start, 128), 384)]
                value = tn(first_ref[...], right).astype(BF)
                for f in range(8):
                    yr, z0, z1 = spots(info, f)
                    a, b = pair_index(info, k, x, yr)
                    ref[a, b, z0, z1, 96 * part : 96 * part + 96, :] = value[96 * f : 96 * f + 96]
        right = da_ref[:, pl.ds(aligned(half * 384, 128), 384)]
        for r in range(4):
            value = tn(context_ref[:, 256 * r : 256 * r + 256], right).astype(BF)
            for t in range(2):
                yr, z0, z1 = spots(info, 2 * jnp.bitwise_xor(c, r) + t)
                for x in range(2):
                    a, b = pair_index(info, k, x, yr)
                    start = 96 * t + 48 * x
                    ref[a, b, z0, z1, 192:240, :] = value[start : start + 48]


def fast_device(
    tokens,
    dealt,
    segments,
    query_weight,
    key_weight,
    value_weight,
    query_bias,
    value_bias,
    output_weight,
    output_bias,
    first_gain,
    first_shift,
    inner_weight,
    inner_bias,
    outer_weight,
    outer_bias,
    second_gain,
    second_shift,
    project_weight,
    cotangent,
):
    c = lax.axis_index("ctx")
    f = lax.axis_index("fsdp")
    core = lax.rem(c, 2)
    total = segments.shape[1]
    x = tokens[0]

    place = jnp.stack([c, f, c * 0, c * 0]).astype(jnp.int32)
    (info,) = run(
        places_kernel, "places", place, [segments], [((16,), jnp.int32)], small=True
    )

    vectors = jnp.concatenate(
        [
            jnp.stack(
                [
                    query_bias,
                    value_bias,
                    output_bias,
                    first_gain,
                    first_shift,
                    outer_bias,
                    second_gain,
                    second_shift,
                ]
            ),
            inner_bias.reshape(4, 96),
        ]
    ).astype(F32)
    vectors = jnp.pad(vectors, ((0, 116), (0, 32)))
    outer_pack, inner_pack = run(
        prepare_forward_kernel,
        "prepare_forward",
        place,
        [inner_weight, output_weight, outer_weight, project_weight],
        [((96, 1664), BF), ((96, 1920), BF)],
        [pltpu.SemaphoreType.DMA((5,))],
        limit=60,
        loose=range(4),
    )
    (heads_pack,) = run(
        prepare_heads_kernel,
        "prepare_heads",
        place,
        [query_weight, key_weight, value_weight, vectors],
        [((96, 640), BF)],
        [pltpu.VMEM(query_weight.shape, BF)] * 3
        + [pltpu.VMEM((128, 128), F32), pltpu.SemaphoreType.DMA((4,))],
        limit=60,
        loose=range(4),
    )
    x_core = to_core(x)
    x_next = to_x(x)
    moved = [along_z(heads_pack, k) for k in range(1, 4)]
    inner_0y = to_fsdp(inner_pack, 1)
    x_core, x_next, heads_pack, inner_pack, outer_pack, inner_0y, *moved = together(
        x_core, x_next, heads_pack, inner_pack, outer_pack, inner_0y, *moved
    )
    x_cross = to_core(x_next)
    moved_y = [to_fsdp(piece, 1) for piece in (heads_pack, *moved)]
    inner_1 = along_z(inner_pack, 1)
    inner_pack = after(inner_pack, x_cross)
    inner_3 = along_z(inner_pack, 3)
    x_cross, inner_pack, outer_pack, *moved_y = together(
        x_cross, inner_pack, outer_pack, *moved_y
    )
    pieces = []
    for one, two in zip((heads_pack, *moved), moved_y):
        pieces += [one, two]
    inner_2 = along_z(inner_pack, 2)
    outer_0y = to_fsdp(outer_pack, 1)

    heads = (LOCAL, total, 128)
    q, k, v, kt, vt, heads_weight, vec = run(
        project_kernel,
        "project",
        info,
        [x, x_core, x_next, after(x_cross, inner_pack), *pieces, segments],
        [
            (heads, BF),
            (heads, BF),
            (heads, BF),
            ((LOCAL, 64, total), BF),
            ((LOCAL, 80, total), BF),
            ((WIDTH, 640), BF),
            ((16, WIDTH), F32),
        ],
        [
            pltpu.VMEM((4, ROWS, WIDTH), BF),
            pltpu.SemaphoreType.DMA((12,)),
        ],
        loose=range(12),
    )
    q, inner_1, inner_3 = together(q, inner_1, inner_3)
    inner_1y = to_fsdp(inner_1, 1)
    o_2, ql_2, pack_2, o_3, ql_3, pack_3 = attend_rows(
        info, after(q, inner_1), k, vt, cotangent[0], 1
    )
    pack_2, pack_3, inner_2, inner_1y, outer_0y, outer_pack, q = together(
        pack_2, pack_3, inner_2, inner_1y, outer_0y, outer_pack, q
    )
    inner_2y, inner_3y = to_fsdp(inner_2, 1), to_fsdp(after(inner_3, inner_2), 1)
    outer_1, outer_3 = along_z(outer_pack, 1), along_z(outer_pack, 3)
    o_0, ql_0, pack_0, o_1, ql_1, pack_1 = attend_rows(info, q, k, vt, cotangent[0], 0)
    pack_0, pack_1, pack_2, pack_3, inner_2y, inner_3y, outer_1, outer_3, outer_pack = together(
        pack_0, pack_1, pack_2, pack_3, inner_2y, inner_3y, outer_1, outer_3, outer_pack
    )
    from_x, from_cross = to_x(pack_2), to_cross(pack_3)
    outer_2 = along_z(outer_pack, 2)
    outer_1y, outer_3y = to_fsdp(outer_1, 1), to_fsdp(outer_3, 1)
    inner_half, output_own = lay(
        info,
        [inner_pack, inner_0y, inner_1, inner_1y, inner_2, inner_2y, inner_3, inner_3y],
        (1536, 384),
    )
    from_x, from_cross, inner_half, output_own, pack_1 = together(
        from_x, from_cross, inner_half, output_own, pack_1
    )
    from_core = to_core(pack_1)
    output_other = to_core(output_own)
    inner_other = to_core(inner_half)
    from_core, output_other, outer_2, outer_1y, outer_3y = together(
        from_core, output_other, outer_2, outer_1y, outer_3y
    )
    outer_2y = to_fsdp(outer_2, 1)
    (
        normal,
        inverse,
        first_low,
        active,
        slope,
        context,
        output_full,
        inner_full,
        arrived,
    ) = run(
        inner_own_kernel,
        "inner_own",
        info,
        [
            after(x, outer_2),
            pack_0,
            from_core,
            from_x,
            from_cross,
            vec,
            output_own,
            output_other,
            inner_half,
        ],
        [
            ((ROWS, WIDTH), F32),
            ((ROWS, 1), F32),
            ((ROWS, WIDTH), BF),
            ((ROWS, HIDDEN), BF),
            ((ROWS, HIDDEN), BF),
            ((ROWS, 1024), BF),
            ((1024, WIDTH), BF),
            ((WIDTH, HIDDEN), BF),
            ((ROWS, 128), BF),
        ],
        [pltpu.SemaphoreType.DMA((1,))],
        loose=(8,),
    )
    first_low, inner_other, outer_2y = together(first_low, inner_other, outer_2y)
    (outer_own,) = lay(
        info,
        [outer_pack, outer_0y, outer_1, outer_1y, outer_2, outer_2y, outer_3, outer_3y],
        (1664,),
    )
    outer_other = to_core(outer_own)
    active, slope, inner_full = run(
        inner_other_kernel,
        "inner_other",
        info,
        [after(first_low, outer_own), vec, inner_other, active, slope, inner_full],
        [((ROWS, HIDDEN), BF), ((ROWS, HIDDEN), BF), ((WIDTH, HIDDEN), BF)],
        [pltpu.SemaphoreType.DMA((1,))],
        loose=(2,),
        alias=((3, 0), (4, 1), (5, 2)),
    )
    residual_two, delta_outer, second_low, delta_projected, given, outer_sums, outer_full = run(
        outer_kernel,
        "outer",
        info,
        [active, outer_own, outer_other, normal, vec, dealt, arrived],
        [
            ((ROWS, WIDTH), F32),
            ((ROWS, WIDTH), BF),
            ((ROWS, WIDTH), BF),
            ((ROWS, 128), BF),
            ((ROWS, 128), BF),
            ((8, WIDTH), F32),
            ((HIDDEN, WIDTH), BF),
        ],
        [pltpu.VMEM((WIDTH, 128), BF), pltpu.SemaphoreType.DMA((33,))],
        loose=(1, 2),
    )
    keep_o, send_o = run(
        outer_pack_kernel,
        "outer_pack",
        info,
        [active, delta_outer, second_low, delta_projected],
        [((2, 2, 2, 2, 208, 384), BF)] * 2,
        [pltpu.VMEM((WIDTH, 128), F32)],
    )
    core_o = to_core(send_o)
    delta_inner, inner_side = run(
        hidden_back_kernel,
        "hidden_back",
        info,
        [after(delta_outer, send_o), outer_full, slope],
        [((ROWS, HIDDEN), BF), ((1, HIDDEN), F32)],
    )
    core_o, delta_inner, inner_side = together(core_o, delta_inner, inner_side)

    give_o = (wide(keep_o[1]) + wide(core_o[1])).astype(BF)
    one_o = to_mixed(give_o, True)
    residual_one, delta_attended, first_sums, *ups = run(
        first_kernel,
        "first",
        info,
        [
            after(delta_inner, give_o),
            inner_full,
            residual_two,
            normal,
            inverse,
            vec,
            output_full,
            given,
        ],
        [((ROWS, WIDTH), F32), ((ROWS, WIDTH), BF), ((8, WIDTH), F32)] + [((896, 128), BF)] * 4,
    )
    up_0 = ups[0]
    ups = [to_core(ups[1]), to_x(ups[2]), to_cross(ups[3])]
    keep_i, send_i = run(
        inner_pack_kernel,
        "inner_pack",
        info,
        [first_low, delta_inner, context, delta_attended],
        [((2, 2, 2, 2, 240, 384), BF)] * 2,
    )
    keys = (k, kt, v)
    dq_0, dk, dv = attend_back(info, 0, after(ql_0, send_i), up_0, o_0, *keys)
    one_o, dq_0, dk, dv, keep_i, send_i, *ups = together(
        one_o, dq_0, dk, dv, keep_i, send_i, *ups
    )

    core_i = to_core(send_i)
    half_o = wide(keep_o[0]) + wide(core_o[0]) + wide(one_o)
    give_o = half_o[1].astype(BF)
    two_o = to_mixed(give_o, False)
    dq_1, dk, dv = attend_back(info, 1, after(ql_1, give_o), ups[0], o_1, *keys, (dk, dv))
    core_i, two_o, dq_1, dk, dv = together(core_i, two_o, dq_1, dk, dv)

    give_i = (wide(keep_i[1]) + wide(core_i[1])).astype(BF)
    one_i = to_mixed(give_i, True)
    half_o = half_o[0] + wide(two_o)
    give_o = half_o[1].astype(BF)
    three_o = to_fsdp(give_o, 2)
    dq_2, dk, dv = attend_back(info, 2, after(ql_2, give_i, give_o), ups[1], o_2, *keys, (dk, dv))
    delta_heads, embedded, _, _ = attend_back(
        info, 3, ql_3, ups[2], o_3, *keys, (dk, dv), (dq_0, dq_1, dq_2, up_0, *ups[:2])
    )
    one_i, three_o, delta_heads, embedded = together(one_i, three_o, delta_heads, embedded)

    half_i = wide(keep_i[0]) + wide(core_i[0]) + wide(one_i)
    give_i = half_i[1].astype(BF)
    two_i = to_mixed(give_i, False)
    half_o = half_o[0] + wide(three_o)
    give_o = half_o[1].astype(BF)
    four_o = to_fsdp(give_o, 4)
    (pack,) = run(
        heads_grad_kernel,
        "heads_grad",
        info,
        [
            x,
            x_core,
            x_next,
            x_cross,
            after(delta_heads, give_i, give_o),
            first_sums,
            outer_sums,
            inner_side,
        ],
        [((2, 2, 2, 96, 640), BF)],
        [pltpu.VMEM((total, WIDTH), BF), pltpu.SemaphoreType.DMA((4,))],
        loose=range(4),
    )
    one_h = to_fsdp(pack[1], 1)
    own, for_core, for_next = run(
        input_grad_kernel,
        "input_grad",
        info,
        [after(delta_heads, pack), heads_weight, residual_one],
        [((ROWS, WIDTH), F32), ((2, ROWS, WIDTH), BF), ((ROWS, WIDTH), F32)],
    )
    two_i, own, for_core, for_next = together(two_i, own, for_core, for_next)

    came = to_core(for_core)
    half_i = half_i[0] + wide(two_i)
    give_i = half_i[1].astype(BF)
    three_i = to_fsdp(give_i, 2)
    give_x = (for_next + wide(came[1])).astype(BF)
    passed = to_x(give_x)
    one_h, three_i, four_o = together(one_h, three_i, four_o)

    half_i = half_i[0] + wide(three_i)
    give_i = half_i[1].astype(BF)
    four_i = to_fsdp(give_i, 4)
    half_h = wide(pack[0]) + wide(one_h)
    give_h = half_h.astype(BF)
    last_h = [to_fsdp(give_h[1, 0], 2), to_fsdp(give_h[0, 1], 4), to_fsdp(give_h[1, 1], 6)]
    four_i, passed, *last_h = together(four_i, passed, *last_h)

    forward_sum = jnp.concatenate(
        [
            (half_o[0] + wide(four_o)).astype(BF),
            (half_i[0] + wide(four_i)).astype(BF),
        ],
        axis=0,
    )
    forward_next = to_x(forward_sum)
    mine = (half_h[0, 0] + wide(last_h[0]) + wide(last_h[1]) + wide(last_h[2])).astype(BF)
    heads_all = lax.all_gather(mine, "ctx")
    near = jnp.stack([forward_sum, after(forward_next, heads_all)])
    far = to_core(near)
    delta_home = (own + wide(came[0]) + wide(passed)).astype(BF)
    inner_grad, outer_grad, output_grad, project_grad = run(
        finish_forward_kernel,
        "finish_forward",
        info,
        [near, far],
        [((96, HIDDEN), F32), ((384, WIDTH), F32), ((96, WIDTH), F32), ((96, 128), F32)],
        [
            pltpu.VMEM((96, HIDDEN), F32),
            pltpu.VMEM((384, WIDTH), F32),
            pltpu.VMEM((96, WIDTH), F32),
            pltpu.VMEM((96, 128), F32),
            pltpu.SemaphoreType.DMA((4,)),
        ],
        loose_outs=range(4),
    )
    query_grad, key_grad, value_grad, *vec_all = run(
        finish_heads_kernel,
        "finish_heads",
        info,
        [heads_all],
        [((96, WIDTH), F32)] * 3 + [((1, 96), F32)] * 8 + [((1, 384), F32)],
        [pltpu.VMEM((96, WIDTH), F32)] * 3 + [pltpu.SemaphoreType.DMA((3,))],
        loose_outs=range(3),
    )
    return (
        embedded[None],
        delta_home[None],
        query_grad,
        key_grad,
        value_grad,
        vec_all[0].reshape(96),
        vec_all[1].reshape(96),
        output_grad,
        vec_all[2].reshape(96),
        vec_all[3].reshape(96),
        vec_all[4].reshape(96),
        inner_grad,
        vec_all[8].reshape(384),
        outer_grad,
        vec_all[5].reshape(96),
        vec_all[6].reshape(96),
        vec_all[7].reshape(96),
        project_grad,
    )


def suits(mesh):
    return mesh.shape["ctx"] == 4 and mesh.shape["fsdp"] == 8


def solution(mesh):
    on_device = fast_device if suits(mesh) else generic_device

    return jax.shard_map(
        on_device,
        mesh=mesh,
        in_specs=(
            P("fsdp", "ctx", None),
            P("fsdp", None),
            P("fsdp", None),
            P("fsdp", None),
            P("fsdp", None),
            P("fsdp", None),
            P("fsdp"),
            P("fsdp"),
            P("fsdp", None),
            P("fsdp"),
            P("fsdp"),
            P("fsdp"),
            P("fsdp", None),
            P("fsdp"),
            P("fsdp", None),
            P("fsdp"),
            P("fsdp"),
            P("fsdp"),
            P("fsdp", None),
            P("fsdp", "ctx", None),
        ),
        out_specs=(
            P("fsdp", "ctx", None),
            P("fsdp", "ctx", None),
            P("fsdp", None),
            P("fsdp", None),
            P("fsdp", None),
            P("fsdp"),
            P("fsdp"),
            P("fsdp", None),
            P("fsdp"),
            P("fsdp"),
            P("fsdp"),
            P("fsdp", None),
            P("fsdp"),
            P("fsdp", None),
            P("fsdp"),
            P("fsdp"),
            P("fsdp"),
            P("fsdp", None),
        ),
        check_vma=False,
    )
```

```python
import functools

import jax
import jax.numpy as jnp
from jax import lax
from jax.experimental import pallas as pl
from jax.experimental.pallas import tpu as pltpu
from jax.sharding import PartitionSpec as P

HEADS = 12
HEAD_DIM = 64


def matmul(left, right):
    return jnp.dot(left, right, preferred_element_type=jnp.float32)


def norm_forward(value, gain, shift):
    centred = value - jnp.mean(value, axis=-1, keepdims=True)
    inverse = lax.rsqrt(jnp.mean(centred * centred, axis=-1, keepdims=True) + 1e-12)
    normal = centred * inverse
    return (normal * gain + shift, normal, inverse)


def norm_backward(upstream, normal, inverse, gain):
    scaled = upstream * gain
    first_mean = jnp.mean(scaled, axis=-1, keepdims=True)
    second_mean = jnp.mean(scaled * normal, axis=-1, keepdims=True)
    inward = inverse * (scaled - first_mean - normal * second_mean)
    return (inward, jnp.sum(upstream * normal, axis=0), jnp.sum(upstream, axis=0))


def gelu_slope(value):
    cumulative = 0.5 * (1.0 + jax.scipy.special.erf(value * 0.7071067811865476))
    return cumulative + value * jnp.exp(-0.5 * value * value) * 0.3989422804014327


def scored(query_heads, key_block, query_segments, segment_block, scale):
    scores = (
        jnp.einsum("qhd,khd->hqk", query_heads, key_block, preferred_element_type=jnp.float32)
        * scale
    )
    allowed = (query_segments[:, None] == segment_block[None, :])[None]
    return (scores, allowed)


def probabilities(scores, allowed, log_total):
    return jnp.where(allowed, jnp.exp(scores - log_total[..., None]), 0.0)


def log_totals(query_heads, key_blocks, query_segments, segment_blocks, scale):

    def log_advance(carry, pieces):
        running_max, running_sum = carry
        scores, allowed = scored(query_heads, pieces[0], query_segments, pieces[1], scale)
        masked = jnp.where(allowed, scores, -1e30)
        new_max = jnp.maximum(running_max, jnp.max(masked, axis=-1))
        fresh = jnp.sum(jnp.where(allowed, jnp.exp(masked - new_max[..., None]), 0.0), axis=-1)
        return ((new_max, running_sum * jnp.exp(running_max - new_max) + fresh), None)

    shape = (query_heads.shape[1], query_heads.shape[0])
    start = (jnp.full(shape, -1e30, jnp.float32), jnp.zeros(shape, jnp.float32))
    final = lax.scan(log_advance, start, (key_blocks, segment_blocks))[0]
    return final[0] + jnp.log(final[1])


def attend(query_heads, key_blocks, value_blocks, query_segments, segment_blocks, scale):
    log_total = log_totals(query_heads, key_blocks, query_segments, segment_blocks, scale)

    def attend_advance(carry, pieces):
        scores, allowed = scored(query_heads, pieces[0], query_segments, pieces[2], scale)
        probs = probabilities(scores, allowed, log_total).astype(jnp.bfloat16)
        return (
            carry
            + jnp.einsum("hqk,khd->qhd", probs, pieces[1], preferred_element_type=jnp.float32),
            None,
        )

    start = jnp.zeros(query_heads.shape, jnp.float32)
    mixed = lax.scan(attend_advance, start, (key_blocks, value_blocks, segment_blocks))[0]
    return (mixed, log_total)


def attend_backward(
    query_heads,
    key_blocks,
    value_blocks,
    query_segments,
    segment_blocks,
    scale,
    log_total,
    upstream,
):

    def first_pass(carry, pieces):
        scores, allowed = scored(query_heads, pieces[0], query_segments, pieces[2], scale)
        probs = probabilities(scores, allowed, log_total)
        delta_probs = jnp.einsum(
            "qhd,khd->hqk", upstream, pieces[1], preferred_element_type=jnp.float32
        )
        value_terms = jnp.einsum(
            "hqk,qhd->khd", probs.astype(jnp.bfloat16), upstream, preferred_element_type=jnp.float32
        )
        return (carry + jnp.sum(probs * delta_probs, axis=-1), value_terms)

    shape = (query_heads.shape[1], query_heads.shape[0])
    weighted, value_terms = lax.scan(
        first_pass, jnp.zeros(shape, jnp.float32), (key_blocks, value_blocks, segment_blocks)
    )

    def second_pass(carry, pieces):
        scores, allowed = scored(query_heads, pieces[0], query_segments, pieces[2], scale)
        probs = probabilities(scores, allowed, log_total)
        delta_probs = jnp.einsum(
            "qhd,khd->hqk", upstream, pieces[1], preferred_element_type=jnp.float32
        )
        delta_scores = (probs * (delta_probs - weighted[..., None])).astype(jnp.bfloat16)
        key_terms = jnp.einsum(
            "hqk,qhd->khd", delta_scores, query_heads, preferred_element_type=jnp.float32
        )
        return (
            carry
            + jnp.einsum(
                "hqk,khd->qhd", delta_scores, pieces[0], preferred_element_type=jnp.float32
            ),
            key_terms,
        )

    query_terms, key_terms = lax.scan(
        second_pass,
        jnp.zeros(query_heads.shape, jnp.float32),
        (key_blocks, value_blocks, segment_blocks),
    )
    return (query_terms * scale, key_terms * scale, value_terms)


def generic_device(
    tokens,
    dealt,
    segments,
    query_weight,
    key_weight,
    value_weight,
    query_bias,
    value_bias,
    output_weight,
    output_bias,
    first_gain,
    first_shift,
    inner_weight,
    inner_bias,
    outer_weight,
    outer_bias,
    second_gain,
    second_shift,
    project_weight,
    cotangent,
):
    peers = lax.axis_size("ctx")
    place = lax.axis_index("ctx")
    local_rows = tokens.shape[1]
    share = local_rows // peers
    order = dealt[0]
    table = (
        lax.dynamic_index_in_dim(order.reshape(peers, peers, share), place, 1, keepdims=False)
        - place * local_rows
    )
    flat_table = table.reshape(-1)
    home_tokens = tokens[0]
    width = home_tokens.shape[1]
    (
        query_full,
        key_full,
        value_full,
        output_full,
        query_shift,
        value_shift,
        output_shift,
        gain_one,
        shift_one,
    ) = (
        lax.all_gather(query_weight, "fsdp", axis=0, tiled=True),
        lax.all_gather(key_weight, "fsdp", axis=0, tiled=True),
        lax.all_gather(value_weight, "fsdp", axis=0, tiled=True),
        lax.all_gather(output_weight, "fsdp", axis=0, tiled=True),
        lax.all_gather(query_bias, "fsdp", axis=0, tiled=True),
        lax.all_gather(value_bias, "fsdp", axis=0, tiled=True),
        lax.all_gather(output_bias, "fsdp", axis=0, tiled=True),
        lax.all_gather(first_gain, "fsdp", axis=0, tiled=True),
        lax.all_gather(first_shift, "fsdp", axis=0, tiled=True),
    )
    outgoing = jnp.take(home_tokens, table, axis=0)
    here_tokens = lax.all_to_all(outgoing, "ctx", split_axis=0, concat_axis=0, tiled=True).reshape(
        local_rows, width
    )
    key_segments = jnp.take(segments[0], order, axis=0)
    query_segments = lax.dynamic_slice_in_dim(key_segments, place * local_rows, local_rows)
    queries = (matmul(here_tokens, query_full) + query_shift.astype(jnp.float32)).astype(
        jnp.bfloat16
    )
    own_keys = matmul(here_tokens, key_full).astype(jnp.bfloat16)
    own_values = (matmul(here_tokens, value_full) + value_shift.astype(jnp.float32)).astype(
        jnp.bfloat16
    )
    all_keys, all_values = (
        lax.all_gather(own_keys, "ctx", axis=0, tiled=True),
        lax.all_gather(own_values, "ctx", axis=0, tiled=True),
    )
    total = all_keys.shape[0]
    block = min(1024, total)
    count = total // block
    scale = HEAD_DIM ** (-0.5)
    query_heads = queries.reshape(local_rows, HEADS, HEAD_DIM)
    key_blocks = all_keys.reshape(count, block, HEADS, HEAD_DIM)
    value_blocks = all_values.reshape(count, block, HEADS, HEAD_DIM)
    segment_blocks = key_segments.reshape(count, block)
    mixed, log_total = attend(
        query_heads, key_blocks, value_blocks, query_segments, segment_blocks, scale
    )
    context = mixed.reshape(local_rows, width).astype(jnp.bfloat16)
    inner_full, inner_shift, outer_full, outer_shift, gain_two, shift_two, project_full = (
        lax.all_gather(inner_weight, "fsdp", axis=0, tiled=True),
        lax.all_gather(inner_bias, "fsdp", axis=0, tiled=True),
        lax.all_gather(outer_weight, "fsdp", axis=0, tiled=True),
        lax.all_gather(outer_bias, "fsdp", axis=0, tiled=True),
        lax.all_gather(second_gain, "fsdp", axis=0, tiled=True),
        lax.all_gather(second_shift, "fsdp", axis=0, tiled=True),
        lax.all_gather(project_weight, "fsdp", axis=0, tiled=True),
    )
    attended = matmul(context, output_full) + output_shift.astype(jnp.float32)
    first, first_normal, first_inverse = norm_forward(
        here_tokens.astype(jnp.float32) + attended,
        gain_one.astype(jnp.float32),
        shift_one.astype(jnp.float32),
    )
    first_low = first.astype(jnp.bfloat16)
    inner = matmul(first_low, inner_full) + inner_shift.astype(jnp.float32)
    active = jax.nn.gelu(inner, approximate=False).astype(jnp.bfloat16)
    outer = matmul(active, outer_full) + outer_shift.astype(jnp.float32)
    second, second_normal, second_inverse = norm_forward(
        first + outer, gain_two.astype(jnp.float32), shift_two.astype(jnp.float32)
    )
    second_low = second.astype(jnp.bfloat16)
    projected = matmul(second_low, project_full)
    inverse_length = lax.rsqrt(jnp.sum(projected * projected, axis=-1, keepdims=True) + 1e-06)
    normed = projected * inverse_length
    embedded = normed.astype(jnp.bfloat16)
    incoming = cotangent[0].astype(jnp.float32)
    along = jnp.sum(normed * incoming, axis=-1, keepdims=True)
    delta_projected = (inverse_length * (incoming - normed * along)).astype(jnp.bfloat16)
    project_delta = matmul(second_low.T, delta_projected)
    delta_second = matmul(delta_projected, project_full.T)
    residual_two, second_gain_delta, second_shift_delta = norm_backward(
        delta_second, second_normal, second_inverse, gain_two.astype(jnp.float32)
    )
    delta_outer = residual_two.astype(jnp.bfloat16)
    outer_bias_delta = jnp.sum(delta_outer, axis=0, dtype=jnp.float32)
    outer_delta = matmul(active.T, delta_outer)
    delta_active = matmul(delta_outer, outer_full.T)
    delta_inner = (delta_active * gelu_slope(inner)).astype(jnp.bfloat16)
    inner_bias_delta = jnp.sum(delta_inner, axis=0, dtype=jnp.float32)
    inner_delta = matmul(first_low.T, delta_inner)
    delta_first = residual_two + matmul(delta_inner, inner_full.T)
    residual_one, first_gain_delta, first_shift_delta = norm_backward(
        delta_first, first_normal, first_inverse, gain_one.astype(jnp.float32)
    )
    delta_attended = residual_one.astype(jnp.bfloat16)
    output_bias_delta = jnp.sum(delta_attended, axis=0, dtype=jnp.float32)
    output_delta = matmul(context.T, delta_attended)
    delta_context = matmul(delta_attended, output_full.T).astype(jnp.bfloat16)
    upstream = delta_context.reshape(local_rows, HEADS, HEAD_DIM)
    query_terms, key_terms, value_terms = attend_backward(
        query_heads,
        key_blocks,
        value_blocks,
        query_segments,
        segment_blocks,
        scale,
        log_total,
        upstream,
    )
    key_sums, value_sums = (
        lax.psum_scatter(
            key_terms.reshape(total, width).astype(jnp.bfloat16),
            "ctx",
            scatter_dimension=0,
            tiled=True,
        ).astype(jnp.float32),
        lax.psum_scatter(
            value_terms.reshape(total, width).astype(jnp.bfloat16),
            "ctx",
            scatter_dimension=0,
            tiled=True,
        ).astype(jnp.float32),
    )
    delta_keys = key_sums.astype(jnp.bfloat16)
    delta_values = value_sums.astype(jnp.bfloat16)
    delta_queries = query_terms.reshape(local_rows, width).astype(jnp.bfloat16)
    query_bias_delta = jnp.sum(delta_queries, axis=0, dtype=jnp.float32)
    value_bias_delta = jnp.sum(delta_values, axis=0, dtype=jnp.float32)
    query_delta = matmul(here_tokens.T, delta_queries)
    key_delta = matmul(here_tokens.T, delta_keys)
    value_delta = matmul(here_tokens.T, delta_values)
    delta_here = (
        residual_one
        + matmul(delta_queries, query_full.T)
        + matmul(delta_keys, key_full.T)
        + matmul(delta_values, value_full.T)
    ).astype(jnp.bfloat16)
    coming_home = lax.all_to_all(
        delta_here.reshape(peers, share, width), "ctx", split_axis=0, concat_axis=0, tiled=True
    )
    delta_home = (
        jnp.zeros((local_rows, width), jnp.bfloat16)
        .at[flat_table]
        .set(coming_home.reshape(local_rows, width))
    )
    (
        inner_part,
        inner_bias_part,
        outer_part,
        outer_bias_part,
        second_gain_part,
        second_shift_part,
        project_part,
    ) = (
        lax.psum_scatter(
            inner_delta.astype(jnp.bfloat16), "fsdp", scatter_dimension=0, tiled=True
        ).astype(jnp.float32),
        lax.psum_scatter(
            inner_bias_delta.astype(jnp.bfloat16), "fsdp", scatter_dimension=0, tiled=True
        ).astype(jnp.float32),
        lax.psum_scatter(
            outer_delta.astype(jnp.bfloat16), "fsdp", scatter_dimension=0, tiled=True
        ).astype(jnp.float32),
        lax.psum_scatter(
            outer_bias_delta.astype(jnp.bfloat16), "fsdp", scatter_dimension=0, tiled=True
        ).astype(jnp.float32),
        lax.psum_scatter(
            second_gain_delta.astype(jnp.bfloat16), "fsdp", scatter_dimension=0, tiled=True
        ).astype(jnp.float32),
        lax.psum_scatter(
            second_shift_delta.astype(jnp.bfloat16), "fsdp", scatter_dimension=0, tiled=True
        ).astype(jnp.float32),
        lax.psum_scatter(
            project_delta.astype(jnp.bfloat16), "fsdp", scatter_dimension=0, tiled=True
        ).astype(jnp.float32),
    )
    (
        query_part,
        key_part,
        value_part,
        query_bias_part,
        value_bias_part,
        output_part,
        output_bias_part,
        first_gain_part,
        first_shift_part,
    ) = (
        lax.psum_scatter(
            query_delta.astype(jnp.bfloat16), "fsdp", scatter_dimension=0, tiled=True
        ).astype(jnp.float32),
        lax.psum_scatter(
            key_delta.astype(jnp.bfloat16), "fsdp", scatter_dimension=0, tiled=True
        ).astype(jnp.float32),
        lax.psum_scatter(
            value_delta.astype(jnp.bfloat16), "fsdp", scatter_dimension=0, tiled=True
        ).astype(jnp.float32),
        lax.psum_scatter(
            query_bias_delta.astype(jnp.bfloat16), "fsdp", scatter_dimension=0, tiled=True
        ).astype(jnp.float32),
        lax.psum_scatter(
            value_bias_delta.astype(jnp.bfloat16), "fsdp", scatter_dimension=0, tiled=True
        ).astype(jnp.float32),
        lax.psum_scatter(
            output_delta.astype(jnp.bfloat16), "fsdp", scatter_dimension=0, tiled=True
        ).astype(jnp.float32),
        lax.psum_scatter(
            output_bias_delta.astype(jnp.bfloat16), "fsdp", scatter_dimension=0, tiled=True
        ).astype(jnp.float32),
        lax.psum_scatter(
            first_gain_delta.astype(jnp.bfloat16), "fsdp", scatter_dimension=0, tiled=True
        ).astype(jnp.float32),
        lax.psum_scatter(
            first_shift_delta.astype(jnp.bfloat16), "fsdp", scatter_dimension=0, tiled=True
        ).astype(jnp.float32),
    )
    results = (
        lax.psum(query_part.astype(jnp.bfloat16), "ctx").astype(jnp.float32),
        lax.psum(key_part.astype(jnp.bfloat16), "ctx").astype(jnp.float32),
        lax.psum(value_part.astype(jnp.bfloat16), "ctx").astype(jnp.float32),
        lax.psum(query_bias_part.astype(jnp.bfloat16), "ctx").astype(jnp.float32),
        lax.psum(value_bias_part.astype(jnp.bfloat16), "ctx").astype(jnp.float32),
        lax.psum(output_part.astype(jnp.bfloat16), "ctx").astype(jnp.float32),
        lax.psum(output_bias_part.astype(jnp.bfloat16), "ctx").astype(jnp.float32),
        lax.psum(first_gain_part.astype(jnp.bfloat16), "ctx").astype(jnp.float32),
        lax.psum(first_shift_part.astype(jnp.bfloat16), "ctx").astype(jnp.float32),
        lax.psum(inner_part.astype(jnp.bfloat16), "ctx").astype(jnp.float32),
        lax.psum(inner_bias_part.astype(jnp.bfloat16), "ctx").astype(jnp.float32),
        lax.psum(outer_part.astype(jnp.bfloat16), "ctx").astype(jnp.float32),
        lax.psum(outer_bias_part.astype(jnp.bfloat16), "ctx").astype(jnp.float32),
        lax.psum(second_gain_part.astype(jnp.bfloat16), "ctx").astype(jnp.float32),
        lax.psum(second_shift_part.astype(jnp.bfloat16), "ctx").astype(jnp.float32),
        lax.psum(project_part.astype(jnp.bfloat16), "ctx").astype(jnp.float32),
    )
    return (
        embedded[None],
        delta_home[None],
        results[0],
        results[1],
        results[2],
        results[3],
        results[4],
        results[5],
        results[6],
        results[7],
        results[8],
        results[9],
        results[10],
        results[11],
        results[12],
        results[13],
        results[14],
        results[15],
    )


BF = jnp.bfloat16
F32 = jnp.float32
ROWS = 512
WIDTH = 768
HIDDEN = 3072
LOCAL = 3
FAR = 2.0**100
KROWS = 256
SCALE = HEAD_DIM ** (-0.5)


def nt(left, right):
    return lax.dot_general(left, right, (((1,), (1,)), ((), ())), preferred_element_type=F32)


def nn(left, right):
    return lax.dot_general(left, right, (((1,), (0,)), ((), ())), preferred_element_type=F32)


def tn(left, right):
    return lax.dot_general(left, right, (((0,), (0,)), ((), ())), preferred_element_type=F32)


def wide(value):
    return value.astype(F32)


def to_core(value):
    return lax.ppermute(value, "ctx", [(i, i ^ 1) for i in range(4)])


def to_x(value):
    return lax.ppermute(value, "ctx", [(i, i ^ 2) for i in range(4)])


def to_cross(value):
    return lax.ppermute(value, "ctx", [(i, i ^ 3) for i in range(4)])


def to_fsdp(value, bit):
    return lax.ppermute(value, "fsdp", [(i, i ^ bit) for i in range(8)])


def along_z(value, step):
    return lax.ppermute(value, "fsdp", [(i, (i + 2 * step) % 8) for i in range(8)])


def to_mixed(value, first):
    pairs = []
    for c in range(4):
        for f in range(8):
            target = (c ^ 2) * 8 + f if (c % 2 == 0) == first else c * 8 + (f ^ 1)
            pairs.append((c * 8 + f, target))
    return lax.ppermute(value, ("ctx", "fsdp"), pairs)


def after(value, *others):
    return lax.optimization_barrier((value, *others))[0]


def added(parts):
    total = wide(parts[0])
    for part in parts[1:]:
        total = total + wide(part)
    return total.astype(BF)


def together(*values):
    return lax.optimization_barrier(values)


def three_parts(value):
    high = wide(value.astype(BF))
    rest = value - high
    middle = wide(rest.astype(BF))
    return high, middle, rest - middle


def lanes_of(rows, n=128):
    return lax.broadcasted_iota(jnp.int32, (rows, n), 1)


def run(
    kernel, name, info, inputs, outs, scratch=(), limit=9, loose=(), loose_outs=(), alias=(), small=False
):
    memory = pl.BlockSpec(memory_space=pltpu.VMEM)
    outside = pl.BlockSpec(memory_space=pltpu.HBM)
    return pl.pallas_call(
        kernel,
        in_specs=[pl.BlockSpec(memory_space=pltpu.SMEM)]
        + [outside if i in loose else memory for i in range(len(inputs))],
        out_specs=[pl.BlockSpec(memory_space=pltpu.SMEM)]
        if small
        else [outside if i in loose_outs else memory for i in range(len(outs))],
        out_shape=[jax.ShapeDtypeStruct(s, t) for s, t in outs],
        scratch_shapes=list(scratch),
        input_output_aliases={i + 1: o for i, o in alias},
        compiler_params=pltpu.CompilerParams(vmem_limit_bytes=limit << 20),
        cost_estimate=pl.CostEstimate(flops=1000, bytes_accessed=1000, transcendentals=0),
        name=name,
    )(info, *inputs)


def start_copies(pairs, sems):
    copies = [pltpu.make_async_copy(a, b, sems.at[i]) for i, (a, b) in enumerate(pairs)]
    for copy in copies:
        copy.start()
    return copies


def aligned(value, n):
    return pl.multiple_of(value, n)


def piece_rows(info, n):
    z, y = info[1] // 2, lax.rem(info[1], 2)
    rows = []
    for k in range(4):
        source = lax.rem(z + 4 - k, 4)
        rows += [aligned((source * 2 + t) * n, 32) for t in (y, 1 - y)]
    return rows


def prepare_forward_kernel(info, wi_in, wo_in, w2_in, p_in, outer_out, inner_out, sems):
    core = lax.rem(info[0], 2)
    copies = start_copies(
        [
            (w2_in.at[pl.ds(aligned(core * 192, 64), 96)], outer_out.at[:, 0:768]),
            (w2_in.at[pl.ds(aligned(core * 192 + 96, 32), 96)], outer_out.at[:, 768:1536]),
            (p_in, outer_out.at[:, 1536:1664]),
            (wi_in.at[:, pl.ds(aligned(core * 1536, 512), 1536)], inner_out.at[:, 0:1536]),
            (wo_in.at[:, pl.ds(aligned(core * 384, 128), 384)], inner_out.at[:, 1536:1920]),
        ],
        sems,
    )
    for copy in copies:
        copy.wait()


def prepare_heads_kernel(info, *refs):
    ins, last_ref, heads_out, held, sems = refs[:11], refs[11], refs[12], refs[13:24], refs[24]
    c = info[0]
    copies = start_copies(zip(ins, held), sems)
    q_ref, k_ref, v_ref, *rows = held
    for copy in copies:
        copy.wait()
    rows = [wide(ref[...]) for ref in (*rows, last_ref)]
    rows = jnp.concatenate([*rows, jnp.zeros((116, 96), F32)], axis=0)
    rows = jnp.concatenate([rows, jnp.zeros((128, 32), F32)], axis=1)
    side = rows.T[:96, :64]
    for value in range(4):

        @pl.when(c == value)
        def _():
            at = slice(192 * value, 192 * value + 192)
            parts = [wide(ref[:, at]) for ref in (q_ref, k_ref, v_ref)]
            heads_out[...] = jnp.concatenate([*parts, side], axis=1).astype(BF)


def lay_kernel(info, *refs):
    pieces, outs, sems = refs[:8], refs[8:-1], refs[-1]
    pairs, start = [], 0
    for out in outs:
        stop = start + out.shape[1]
        for ref, row in zip(pieces, piece_rows(info, 96)):
            pairs.append((ref.at[:, start:stop], out.at[pl.ds(row, 96)]))
        start = stop
    copies = start_copies(pairs, sems)
    for copy in copies:
        copy.wait()


def lay(info, pieces, widths):
    return run(
        lay_kernel,
        "lay",
        info,
        pieces,
        [((WIDTH, n), BF) for n in widths],
        [pltpu.SemaphoreType.DMA((8 * len(widths),))],
        loose=range(8),
    )


def places_kernel(place, seg_ref, info_out):
    seg = wide(seg_ref[...])
    at = lanes_of(1, seg.shape[1])
    for i in range(4):
        info_out[i] = place[i]
        info_out[12 + i] = 0
        start = jnp.sum(jnp.where(at == ROWS * i, seg, 0.0))
        end = jnp.sum(jnp.where(at == ROWS * i + ROWS - 1, seg, 0.0))
        low = jnp.sum(jnp.where(seg < start, 1.0, 0.0)).astype(jnp.int32)
        high = jnp.sum(jnp.where(seg <= end, 1.0, 0.0)).astype(jnp.int32)
        info_out[4 + i] = low // KROWS
        info_out[8 + i] = (high + KROWS - 1) // KROWS


def project_kernel(info, *refs):
    x_refs, w_refs = refs[0:4], refs[4:12]
    seg_ref = refs[12]
    q_out, k_out, v_out, kt_out, vt_out, w_out, vec_out, sems = refs[13:]
    c = info[0]
    copies = start_copies(
        [(ref, w_out.at[pl.ds(row, 96)]) for ref, row in zip(w_refs, piece_rows(info, 96))], sems
    )
    for copy in copies:
        copy.wait()
    weights = w_out[...]
    turned = wide(weights[:, 512:640]).T
    vec_out[...] = turned[64:80]
    lane = lanes_of(WIDTH, 640)
    row = lax.broadcasted_iota(jnp.int32, (WIDTH, 640), 0)
    wanted = jnp.where(lane < 384, lane, lane - 384) + 192 * c
    chosen = nn(turned[64:80].astype(BF), wide(row == wanted).astype(BF))
    lane1 = lanes_of(1, 640)
    bias = jnp.where(
        lane1 < 192,
        chosen[0:1],
        jnp.where((lane1 >= 384) & (lane1 < 576), chosen[1:2], 0.0),
    )
    lanes = lanes_of(ROWS)
    for r in range(4):
        rows = pl.ds(aligned(jnp.bitwise_xor(c, r) * ROWS, ROWS), ROWS)
        result = nn(x_refs[r][...], weights) + bias
        seg = seg_ref[:, pl.ds(aligned(jnp.bitwise_xor(c, r) * ROWS, ROWS), ROWS)]
        same = jnp.broadcast_to(wide(seg), (128, ROWS)).T == wide(lanes - 64)
        qa = jnp.where(same & (lanes < 67), 1.0, 0.0)
        ka = jnp.where(lanes < 67, jnp.where(same, 0.0, -FAR), jnp.where(lanes < 70, 1.0, 0.0))
        for slot in range(9):
            pair = result[:, 128 * (slot // 2) : 128 * (slot // 2) + 128]
            if slot % 2:
                pair = pltpu.roll(pair, 64, 1)
            kind, h = slot // 3, slot % 3
            if kind == 0:
                low = wide(pair.astype(BF)) * SCALE
                q_out[h, rows, :] = jnp.where(lanes < 64, low, qa).astype(BF)
            elif kind == 1:
                value = jnp.where(lanes < 64, pair, ka)
                k_out[h, rows, :] = value.astype(BF)
                kt_out[h, :, rows] = value.T[:64].astype(BF)
            else:
                value = jnp.where(lanes < 64, pair, jnp.where(lanes < 67, 1.0, 0.0))
                v_out[h, rows, :] = value.astype(BF)
                vt_out[h, :, rows] = value.T[:80].astype(BF)


def over_keys(low, high, step):
    pairs = (high - low) // 2

    def two(i, carry):
        step(pl.ds(aligned((low + 2 * i) * KROWS, KROWS), 2 * KROWS))
        return carry

    def one(i, carry):
        step(pl.ds(aligned((low + 2 * pairs + i) * KROWS, KROWS), KROWS))
        return carry

    lax.fori_loop(0, pairs, two, 0)
    lax.fori_loop(0, high - low - 2 * pairs, one, 0)


def attend_kernel(info, q_ref, k_ref, vt_ref, cot_ref, *refs, chip):
    each = range(LOCAL)
    top_s, sum_s = refs[6:]
    for step in range(2):
        o_ref, ql_ref, pack_ref = refs[3 * step : 3 * step + 3]
        place = jnp.bitwise_xor(info[0], step + 2 * chip)
        mine = pl.ds(aligned(place * ROWS, ROWS), ROWS)
        top_s[...] = jnp.full_like(top_s, -3e38)
        sum_s[...] = jnp.zeros_like(sum_s)

        def advance(rows):
            scores = [nt(k_ref[h, rows], q_ref[h, mine]) for h in each]
            before = [top_s[h, :1] for h in each]
            peaks = [
                jnp.maximum(before[h], jnp.max(scores[h], axis=0, keepdims=True)) for h in each
            ]
            probs = [jnp.exp(scores[h] - peaks[h]).astype(BF) for h in each]
            shrink = [jnp.exp(before[h] - peaks[h]) for h in each]
            fresh = [nn(vt_ref[h, :, rows], probs[h]) for h in each]
            for h in each:
                sum_s[h] = sum_s[h] * shrink[h] + fresh[h]
                top_s[h] = jnp.broadcast_to(peaks[h], top_s.shape[1:])

        over_keys(info[4 + place], info[8 + place], advance)
        lanes = lanes_of(ROWS)
        subs = lax.broadcasted_iota(jnp.int32, (128, ROWS), 0)
        outs = []
        for h in each:
            sums = sum_s[h]
            total = sums[64:65]
            parts = three_parts(top_s[h, :1] + jnp.log(total))
            tall = jnp.concatenate([sums[:64] / total, jnp.zeros((64, ROWS), F32)], axis=0)
            for i in range(3):
                tall = jnp.where(subs == 67 + i, -parts[i], tall)
            turned = tall.T
            out = jnp.where(lanes < 64, turned, 0.0)
            outs.append(out)
            o_ref[h] = out.astype(BF)
            ql_ref[h] = jnp.where(lanes < 67, wide(q_ref[h, mine]), turned).astype(BF)
        pack_ref[0:512] = (outs[0] + pltpu.roll(outs[1], 64, 1)).astype(BF)
        pack_ref[512:768] = (outs[2][:256] + pltpu.roll(outs[2][256:], 64, 1)).astype(BF)
        pack_ref[768:896] = cot_ref[pl.ds(aligned(place * 128, 128), 128), :]


def attend_rows(info, q, k, vt, cotangent, chip):
    return run(
        functools.partial(attend_kernel, chip=chip),
        "attend_rows",
        info,
        [q, k, vt, cotangent],
        ([((LOCAL, ROWS, 128), BF)] * 2 + [((896, 128), BF)]) * 2,
        [pltpu.VMEM((LOCAL, 8, ROWS), F32), pltpu.VMEM((LOCAL, 80, ROWS), F32)],
    )


def attend_back_kernel(info, *refs, r):
    each = range(LOCAL)
    ql_ref, up_ref, o_ref, k_ref, kt_ref, v_ref = refs[:6]
    *outs, dk_s, dv_s, dq_s, do_s = refs[6:]
    lanes = lanes_of(ROWS)
    if r == 0:
        (dq_ref,) = outs
        dk_s[...] = jnp.zeros_like(dk_s)
        dv_s[...] = jnp.zeros_like(dv_s)
    elif r < 3:
        _, _, dq_ref = outs
    else:
        w_ref, residual_ref, all_ref, emb_ref, *grads = outs[8:]
        for i, ref in enumerate((*outs[5:8], up_ref)):
            at = pl.ds(aligned(jnp.bitwise_xor(info[0], i) * 128, 128), 128)
            emb_ref[at, :] = ref[768:896]
    place = jnp.bitwise_xor(info[0], r)
    dq_s[...] = jnp.zeros_like(dq_s)
    pair = wide(up_ref[0:512])
    last = wide(up_ref[512:768])
    ups = [
        pair,
        pltpu.roll(pair, 64, 1),
        jnp.concatenate([last, pltpu.roll(last, 64, 1)], axis=0),
    ]
    for h in each:
        up = jnp.where(lanes < 64, ups[h], 0.0)
        parts = three_parts(jnp.sum(up * wide(o_ref[h]), axis=1, keepdims=True))
        for i in range(3):
            up = jnp.where(lanes == 64 + i, -parts[i], up)
        do_s[h] = up.astype(BF)

    def advance(rows):
        scores = [nt(k_ref[h, rows], ql_ref[h]) for h in each]
        rises = [nt(v_ref[h, rows], do_s[h]) for h in each]
        probs = [jnp.exp(scores[h]) for h in each]
        deltas = [(probs[h] * rises[h]).astype(BF) for h in each]
        lows = [probs[h].astype(BF) for h in each]
        for_values = [nn(lows[h], do_s[h]) for h in each]
        for_keys = [nn(deltas[h], ql_ref[h]) for h in each]
        for_queries = [nn(kt_ref[h, :, rows], deltas[h]) for h in each]
        for h in each:
            dv_s[h, rows] += for_values[h]
            dk_s[h, rows] += for_keys[h]
            dq_s[h] += for_queries[h]

    over_keys(info[4 + place], info[8 + place], advance)
    turned = []
    for h in each:
        tall = jnp.concatenate([dq_s[h], jnp.zeros((64, ROWS), F32)], axis=0)
        turned.append(tall.T * SCALE)
    both = (turned[0] + pltpu.roll(turned[1], 64, 1)).astype(BF)
    if r < 3:
        dq_ref[:, 0:128] = both
        dq_ref[:, 128:256] = turned[2].astype(BF)
        return
    mine = pl.ds(aligned(place * ROWS, ROWS), ROWS)
    all_ref[mine, 0:128] = both
    all_ref[mine, 128:256] = turned[2].astype(BF)
    for i, ref in enumerate(outs[2:5]):
        at = pl.ds(aligned(jnp.bitwise_xor(info[0], i) * ROWS, ROWS), ROWS)
        all_ref[at, 0:256] = ref[...]
    for b in range(4):
        rows = pl.ds(b * ROWS, ROWS)
        low = [jnp.where(lanes < 64, ref[h, rows], 0.0) for ref in (dk_s, dv_s) for h in each]
        high = [pltpu.roll(value, 64, 1) for value in low]
        all_ref[rows, 128:256] = (wide(all_ref[rows, 128:256]) + high[0]).astype(BF)
        all_ref[rows, 256:384] = (low[1] + high[2]).astype(BF)
        all_ref[rows, 384:512] = (low[3] + high[4]).astype(BF)
        all_ref[rows, 512:640] = low[5].astype(BF)
    input_grad(info, all_ref, w_ref, residual_ref, *grads)


def attend_back(info, r, ql, up, o, k, kt, v, carried=(), earlier=()):
    sums = [(k.shape, F32)] * 2
    part = [((ROWS, 256), BF)]
    whole = [
        ((k.shape[1], 640), BF),
        ((ROWS, 128), BF),
        ((ROWS, WIDTH), F32),
        ((2, ROWS, WIDTH), BF),
        ((ROWS, WIDTH), F32),
    ]
    first = len(part if r < 3 else whole)
    return run(
        functools.partial(attend_back_kernel, r=r),
        "attend_back",
        info,
        [ql, up, o, k, kt, v, *carried, *earlier],
        (part if r < 3 else whole) + sums,
        [pltpu.VMEM((LOCAL, 64, ROWS), F32), pltpu.VMEM((LOCAL, ROWS, 128), BF)],
        alias=((6, first), (7, first + 1)) if r else (),
    )


def gaussian(value):
    below = 0.5 * (1.0 + lax.erf(value * 0.7071067811865476))
    return below, jnp.exp(-0.5 * value * value) * 0.3989422804014327


def norm_rows(value):
    centred = value - jnp.mean(value, axis=-1, keepdims=True)
    inverse = lax.rsqrt(jnp.mean(centred * centred, axis=-1, keepdims=True) + 1e-12)
    return centred * inverse, inverse


def norm_rows_back(upstream, normal, inverse, gain):
    scaled = upstream * gain
    first_mean = jnp.mean(scaled, axis=-1, keepdims=True)
    second_mean = jnp.mean(scaled * normal, axis=-1, keepdims=True)
    return inverse * (scaled - first_mean - normal * second_mean)


def column_sums(value):
    return jnp.sum(value, axis=0, keepdims=True)


def hidden_half(half, first, wi_ref, vec_ref, active_out, slope_out):
    shift = jnp.concatenate(
        [vec_ref[8 + k : 9 + k, 96 * f : 96 * f + 96] for f in range(8) for k in range(4)], axis=1
    )
    shift = jnp.where(half == 0, shift[:, :1536], shift[:, 1536:])
    for block in range(3):
        at = pl.ds(aligned(half * 1536 + block * 512, 512), 512)
        value = nn(first, wi_ref[:, at]) + shift[:, block * 512 : block * 512 + 512]
        below, bell = gaussian(value)
        active_out[:, at] = (value * below).astype(BF)
        slope_out[:, at] = (below + value * bell).astype(BF)


def inner_own_kernel(info, *refs):
    x_ref, *packs = refs[:5]
    vec_ref, wo_own, wo_other, g_ref = refs[5:9]
    (
        normal_out,
        inverse_out,
        first_out,
        active_out,
        slope_out,
        context_out,
        wo_out,
        wi_out,
        arrived_out,
        sems,
    ) = refs[9:]
    c = info[0]
    core = lax.rem(c, 2)
    own = pl.ds(aligned(core * 1536, 512), 1536)
    (copy,) = start_copies([(g_ref, wi_out.at[:, own])], sems)
    for r in range(4):
        group = jnp.bitwise_xor(c, r)
        arrived_out[pl.ds(aligned(group * 128, 128), 128), :] = packs[r][768:896]
        rows = pl.ds(aligned(group * 192, 64), 192)
        for half, ref in ((core, wo_own), (1 - core, wo_other)):
            at = pl.ds(aligned(half * 384, 128), 384)
            wo_out[256 * r : 256 * r + 192, at] = ref[rows, :]
        wo_out[256 * r + 192 : 256 * r + 256, :] = jnp.zeros((64, WIDTH), BF)
        context_out[:, 256 * r : 256 * r + 128] = packs[r][0:512]
        last = wide(packs[r][512:768])
        last = jnp.concatenate([last, pltpu.roll(last, 64, 1)], axis=0)
        context_out[:, 256 * r + 128 : 256 * r + 256] = jnp.where(
            lanes_of(ROWS) < 64, last, 0.0
        ).astype(BF)
    attended = nn(context_out[...], wo_out[...]) + vec_ref[2:3]
    normal, inverse = norm_rows(wide(x_ref[...]) + attended)
    normal_out[...] = normal
    inverse_out[...] = inverse
    first = (normal * vec_ref[3:4] + vec_ref[4:5]).astype(BF)
    first_out[...] = first
    copy.wait()
    hidden_half(core, first, wi_out, vec_ref, active_out, slope_out)


def inner_other_kernel(info, first_ref, vec_ref, g_ref, a_ref, s_ref, w_ref, *refs):
    active_out, slope_out, wi_out, sems = refs
    core = 1 - lax.rem(info[0], 2)
    other = pl.ds(aligned(core * 1536, 512), 1536)
    (copy,) = start_copies([(g_ref, wi_out.at[:, other])], sems)
    copy.wait()
    hidden_half(core, first_ref[...], wi_out, vec_ref, active_out, slope_out)


def outer_kernel(
    info,
    active_ref,
    own_ref,
    other_ref,
    normal_ref,
    vec_ref,
    table_ref,
    arrived_ref,
    residual_out,
    do_out,
    second_out,
    dp_out,
    given_out,
    sums_out,
    w2_out,
    wp_ref,
    sems,
):
    core = lax.rem(info[0], 2)
    copies = start_copies(
        [
            (
                ref.at[pl.ds(96 * f, 96), 768 * t : 768 * t + 768],
                w2_out.at[pl.ds(aligned(384 * f + 192 * half + 96 * t, 32), 96)],
            )
            for f in range(8)
            for half, ref in ((core, own_ref), (1 - core, other_ref))
            for t in range(2)
        ]
        + [(own_ref.at[:, 1536:1664], wp_ref)],
        sems,
    )
    outer = vec_ref[5:6]
    for part in range(2):
        for copy in copies[16 * part : 16 * part + 16]:
            copy.wait()
        at = slice(1536 * part, 1536 * part + 1536)
        outer = outer + nn(active_ref[:, at], w2_out[at, :])
    copies[32].wait()
    first = normal_ref[...] * vec_ref[3:4] + vec_ref[4:5]
    normal, inverse = norm_rows(first + outer)
    second = (normal * vec_ref[6:7] + vec_ref[7:8]).astype(BF)
    second_out[...] = second
    projected = nn(second, wp_ref[...])
    scale = lax.rsqrt(jnp.sum(projected * projected, axis=-1, keepdims=True) + 1e-06)
    normed = projected * scale
    where = lax.broadcasted_iota(jnp.int32, (ROWS, ROWS), 0) + info[0] * ROWS
    table = jnp.concatenate(
        [table_ref[:, pl.ds(aligned(ROWS * d + info[0] * 128, 128), 128)] for d in range(4)],
        axis=1,
    )
    onehot = wide(table == where).astype(BF)
    given_out[...] = tn(onehot, normed.astype(BF)).astype(BF)
    incoming = nn(onehot, arrived_ref[...])
    along = jnp.sum(normed * incoming, axis=-1, keepdims=True)
    delta = (scale * (incoming - normed * along)).astype(BF)
    dp_out[...] = delta
    upstream = nt(delta, wp_ref[...])
    residual = norm_rows_back(upstream, normal, inverse, vec_ref[6:7])
    residual_out[...] = residual
    low = residual.astype(BF)
    do_out[...] = low
    sums_out[...] = jnp.concatenate(
        [
            column_sums(wide(low)),
            column_sums(upstream * normal),
            column_sums(upstream),
            jnp.zeros((5, WIDTH), F32),
        ],
        axis=0,
    )


def hidden_back_kernel(info, do_ref, w2_ref, slope_ref, di_out, side_out):
    for block in range(HIDDEN // 512):
        at = slice(block * 512, block * 512 + 512)
        value = nt(do_ref[...], w2_ref[at, :]) * wide(slope_ref[:, at])
        low = value.astype(BF)
        di_out[:, at] = low
        side_out[:, at] = column_sums(wide(low))


def first_kernel(
    info,
    di_ref,
    wi_ref,
    residual_ref,
    normal_ref,
    inverse_ref,
    vec_ref,
    wo_ref,
    given_ref,
    residual_out,
    da_out,
    sums_out,
    *up_outs,
):
    upstream = residual_ref[...] + nt(di_ref[...], wi_ref[...])
    normal = normal_ref[...]
    residual = norm_rows_back(upstream, normal, inverse_ref[...], vec_ref[3:4])
    residual_out[...] = residual
    low = residual.astype(BF)
    da_out[...] = low
    sums_out[...] = jnp.concatenate(
        [
            column_sums(wide(low)),
            column_sums(upstream * normal),
            column_sums(upstream),
            jnp.zeros((5, WIDTH), F32),
        ],
        axis=0,
    )
    for r in (2, 3, 1, 0):
        out = up_outs[r]
        up = nt(low, wo_ref[256 * r : 256 * r + 256, :])
        out[0:512] = up[:, 0:128].astype(BF)
        last = up[:, 128:256]
        out[512:768] = (last[:256] + pltpu.roll(last[256:], 64, 1)).astype(BF)
        place = jnp.bitwise_xor(info[0], r)
        out[768:896] = given_ref[pl.ds(aligned(place * 128, 128), 128), :]


def spots(info, f):
    mine = info[1]
    my_z, my_y = mine // 2, lax.rem(mine, 2)
    z, y = (f // 2, f % 2) if isinstance(f, int) else (f // 2, lax.rem(f, 2))
    apart = jnp.bitwise_xor(my_z, z)
    return jnp.bitwise_xor(my_y, y), lax.rem(apart, 2), apart // 2


def heads_grad_kernel(info, *refs):
    x_refs, (all_ref, first_ref, outer_ref, side_ref, pack_ref) = refs[:4], refs[4:]
    c = info[0]
    sums = column_sums(wide(all_ref[...]))
    row = lax.broadcasted_iota(jnp.int32, (640, WIDTH), 0)
    lane = lanes_of(640, WIDTH)
    at = lax.broadcasted_iota(jnp.int32, (16, WIDTH), 0)
    rows = [jnp.zeros((2, WIDTH), F32), first_ref[0:3], outer_ref[0:3]]
    for k in range(4):
        starts = [384 * f + 96 * k for f in range(8)]
        rows.append(jnp.concatenate([side_ref[:, i : i + 96] for i in starts], axis=1))
    vectors = jnp.concatenate([*rows, jnp.zeros((4, WIDTH), F32)], axis=0)
    parts = three_parts(sums)
    for kind, first in ((0, 0), (1, 384)):
        chosen = (row - first + 192 * c == lane) & (row >= first) & (row < first + 192)
        chosen = wide(chosen).astype(BF)
        value = sum(nn(jnp.broadcast_to(part, (16, 640)).astype(BF), chosen) for part in parts)
        vectors = jnp.where(at == kind, value, vectors)
    tall = jnp.concatenate(
        [jnp.zeros((64, WIDTH), F32), vectors, jnp.zeros((48, WIDTH), F32)], axis=0
    )
    side = tall.T
    delta = jnp.zeros((WIDTH, 640), F32)
    for r, ref in enumerate(x_refs):
        at = pl.ds(aligned(jnp.bitwise_xor(c, r) * ROWS, ROWS), ROWS)
        delta = delta + tn(ref[...], all_ref[at, :])
    for f in range(8):
        i, j, k = spots(info, f)
        piece = delta[96 * f : 96 * f + 96]
        pack_ref[i, j, k, :, 0:512] = piece[:, :512].astype(BF)
        pack_ref[i, j, k, :, 512:640] = (piece[:, 512:] + side[96 * f : 96 * f + 96]).astype(BF)


def input_grad(info, all_ref, w_ref, residual_ref, own_ref, core_ref, next_ref):
    for r in (1, 3, 2, 0):
        rows = pl.ds(aligned(jnp.bitwise_xor(info[0], r) * ROWS, ROWS), ROWS)
        value = nt(all_ref[rows, :], w_ref[...])
        if r == 0:
            own_ref[...] = residual_ref[...] + value
        elif r == 2:
            next_ref[...] = value
        else:
            core_ref[r // 2] = value.astype(BF)


def finish_kernel(info, near_ref, far_ref, heads_ref, own_ref, came_ref, passed_ref, *refs):
    wi_out, w2_out, wo_out, wp_out, q_out, k_out, v_out, home_out = refs[:8]
    vec_outs = refs[8:17]
    wi_s, w2_s, wo_s, wp_s, q_s, k_s, v_s, home_s, sems = refs[17:]
    for r in range(4):
        ref = far_ref if r % 2 else near_ref
        g = jnp.bitwise_xor(info[0], r)
        a, b = g // 2, lax.rem(g, 2)
        block = wide(ref[r // 2])
        across = pl.ds(aligned(b * 384, 128), 384)
        w2_s[pl.ds(aligned(a * 192, 64), 192), across] = block[0:192]
        for h in range(2):
            at = pl.ds(aligned(g * 768 + 384 * h, 128), 384)
            wi_s[:, at] = block[208 + 96 * h : 304 + 96 * h]
        wo_s[pl.ds(aligned(a * 48, 16), 48), across] = block[400:448]
        for t in range(3):
            at = pl.ds(aligned(24 * g + 8 * t, 8), 8)
            wp_s[at, :] = block[192:200, 128 * t : 128 * t + 128]
    copies = start_copies(
        [(wi_s, wi_out), (w2_s, w2_out), (wo_s, wo_out), (wp_s, wp_out)], sems
    )
    home_s[...] = (own_ref[...] + wide(came_ref[0]) + wide(passed_ref[...])).astype(BF)
    for kind, ref in enumerate((q_s, k_s, v_s)):
        parts = [wide(heads_ref[g, :, 192 * kind : 192 * kind + 192]) for g in range(4)]
        ref[...] = jnp.concatenate(parts, axis=1)
    for i, pair in enumerate(((q_s, q_out), (k_s, k_out), (v_s, v_out), (home_s, home_out))):
        copy = pltpu.make_async_copy(*pair, sems.at[4 + i])
        copy.start()
        copies.append(copy)
    side = sum(wide(heads_ref[g, :, 512:640]) for g in range(4))
    tall = jnp.concatenate([side, jnp.zeros((32, 128), F32)], axis=0).T
    for i in range(8):
        vec_outs[i][...] = tall[64 + i : 65 + i, :96]
    last = jnp.concatenate([tall[72 + i : 73 + i, :96] for i in range(4)], axis=1)
    vec_outs[8][...] = last.reshape(384)
    for copy in copies:
        copy.wait()


def pair_index(info, keep, x, yr):
    xr = jnp.bitwise_xor(info[0] // 2, x)
    order = jnp.bitwise_xor(lax.rem(info[0], 2), keep)
    first = jnp.where(order == 0, xr, yr)
    second = jnp.where(order == 0, yr, xr)
    return first, second


def outer_pack_kernel(info, active_ref, do_ref, second_ref, dp_ref, keep_ref, send_ref, proj_s):
    core = lax.rem(info[0], 2)
    proj_s[...] = tn(second_ref[...], dp_ref[...])
    for f in range(8):
        yr, z0, z1 = spots(info, f)
        left = active_ref[:, 384 * f : 384 * f + 384]
        for k, ref in ((0, keep_ref), (1, send_ref)):
            half = jnp.bitwise_xor(core, k)
            right = do_ref[:, pl.ds(aligned(half * 384, 128), 384)]
            value = tn(left, right).astype(BF)
            for x in range(2):
                a, b = pair_index(info, k, x, yr)
                ref[a, b, z0, z1, 0:192, :] = value[192 * x : 192 * x + 192]
                start = 96 * f + 24 * (2 * x + half)
                across = jnp.concatenate(
                    [proj_s[pl.ds(aligned(start + 8 * g, 8), 8), :] for g in range(3)], axis=1
                )
                ref[a, b, z0, z1, 192:208, :] = jnp.concatenate(
                    [across, jnp.zeros((8, 384), F32)], axis=0
                ).astype(BF)


def inner_pack_kernel(info, first_ref, di_ref, keep_ref, send_ref):
    core = lax.rem(info[0], 2)
    for k, ref in ((0, keep_ref), (1, send_ref)):
        half = jnp.bitwise_xor(core, k)
        for x in range(2):
            for part in range(2):
                start = (2 * x + half) * 768 + 384 * part
                right = di_ref[:, pl.ds(aligned(start, 128), 384)]
                value = tn(first_ref[...], right).astype(BF)
                for f in range(8):
                    yr, z0, z1 = spots(info, f)
                    a, b = pair_index(info, k, x, yr)
                    ref[a, b, z0, z1, 96 * part : 96 * part + 96, :] = value[96 * f : 96 * f + 96]


def output_pack_kernel(info, context_ref, da_ref, keep_ref, send_ref):
    c = info[0]
    for k, ref in ((0, keep_ref), (1, send_ref)):
        half = jnp.bitwise_xor(lax.rem(c, 2), k)
        right = da_ref[:, pl.ds(aligned(half * 384, 128), 384)]
        for r in range(4):
            value = tn(context_ref[:, 256 * r : 256 * r + 256], right).astype(BF)
            for t in range(2):
                yr, z0, z1 = spots(info, 2 * jnp.bitwise_xor(c, r) + t)
                for x in range(2):
                    a, b = pair_index(info, k, x, yr)
                    start = 96 * t + 48 * x
                    ref[a, b, z0, z1] = value[start : start + 48]


def fast_device(
    tokens,
    dealt,
    segments,
    query_weight,
    key_weight,
    value_weight,
    query_bias,
    value_bias,
    output_weight,
    output_bias,
    first_gain,
    first_shift,
    inner_weight,
    inner_bias,
    outer_weight,
    outer_bias,
    second_gain,
    second_shift,
    project_weight,
    cotangent,
):
    c = lax.axis_index("ctx")
    f = lax.axis_index("fsdp")
    core = lax.rem(c, 2)
    total = segments.shape[1]
    x = tokens[0]

    place = jnp.stack([c, f, c * 0, c * 0]).astype(jnp.int32)
    (info,) = run(
        places_kernel, "places", place, [segments], [((16,), jnp.int32)], small=True
    )

    vectors = (
        query_bias,
        value_bias,
        output_bias,
        first_gain,
        first_shift,
        outer_bias,
        second_gain,
        second_shift,
    )
    (heads_pack,) = run(
        prepare_heads_kernel,
        "prepare_heads",
        place,
        [query_weight, key_weight, value_weight]
        + [vector.reshape(1, 96) for vector in vectors]
        + [inner_bias.reshape(4, 96)],
        [((96, 640), BF)],
        [pltpu.VMEM(query_weight.shape, BF)] * 3
        + [pltpu.VMEM((1, 96), BF)] * 8
        + [pltpu.SemaphoreType.DMA((11,))],
        limit=60,
        loose=range(11),
    )
    outer_pack, inner_pack = run(
        prepare_forward_kernel,
        "prepare_forward",
        after(place, heads_pack),
        [inner_weight, output_weight, outer_weight, project_weight],
        [((96, 1664), BF), ((96, 1920), BF)],
        [pltpu.SemaphoreType.DMA((5,))],
        limit=60,
        loose=range(4),
    )
    x_core = to_core(x)
    x_next = to_x(x)
    moved = [along_z(heads_pack, k) for k in range(1, 4)]
    moved_y = [to_fsdp(heads_pack, 1)]
    x_core, x_next, heads_pack, inner_pack, outer_pack, info, moved_y[0], *moved = together(
        x_core, x_next, heads_pack, inner_pack, outer_pack, info, moved_y[0], *moved
    )
    x_cross = to_core(x_next)
    inner_pack, moved, x_cross = together(inner_pack, moved, x_cross)
    moved_y += [to_fsdp(piece, 1) for piece in moved]
    inner_1, inner_3 = along_z(inner_pack, 1), along_z(inner_pack, 3)
    x_cross, inner_pack, outer_pack, *moved_y = together(
        x_cross, inner_pack, outer_pack, *moved_y
    )
    pieces = []
    for one, two in zip((heads_pack, *moved), moved_y):
        pieces += [one, two]
    inner_2 = along_z(inner_pack, 2)
    inner_0y, outer_0y = to_fsdp(inner_pack, 1), to_fsdp(outer_pack, 1)

    heads = (LOCAL, total, 128)
    q, k, v, kt, vt, heads_weight, vec = run(
        project_kernel,
        "project",
        info,
        [x, x_core, x_next, after(x_cross, inner_pack), *pieces, segments],
        [
            (heads, BF),
            (heads, BF),
            (heads, BF),
            ((LOCAL, 64, total), BF),
            ((LOCAL, 80, total), BF),
            ((WIDTH, 640), BF),
            ((16, WIDTH), F32),
        ],
        [pltpu.SemaphoreType.DMA((8,))],
        loose=range(4, 12),
    )
    q, inner_1, inner_3, inner_0y, outer_0y, outer_pack = together(
        q, inner_1, inner_3, inner_0y, outer_0y, outer_pack
    )
    inner_1y = to_fsdp(inner_1, 1)
    o_2, ql_2, pack_2, o_3, ql_3, pack_3 = attend_rows(
        info, after(q, inner_1), k, vt, cotangent[0], 1
    )
    pack_2, pack_3, inner_2, inner_1y, outer_pack, q = together(
        pack_2, pack_3, inner_2, inner_1y, outer_pack, q
    )
    inner_2y, inner_3y = to_fsdp(inner_2, 1), to_fsdp(after(inner_3, inner_2), 1)
    outer_1, outer_3, outer_2 = [along_z(outer_pack, k) for k in (1, 3, 2)]
    o_0, ql_0, pack_0, o_1, ql_1, pack_1 = attend_rows(info, q, k, vt, cotangent[0], 0)
    pack_0, pack_1, pack_2, pack_3, inner_2y, inner_3y, outer_1, outer_3 = together(
        pack_0, pack_1, pack_2, pack_3, inner_2y, inner_3y, outer_1, outer_3
    )
    from_x, from_cross = to_x(pack_2), to_cross(pack_3)
    outer_1y = to_fsdp(outer_1, 1)
    inner_half, output_own = lay(
        info,
        [inner_pack, inner_0y, inner_1, inner_1y, inner_2, inner_2y, inner_3, inner_3y],
        (1536, 384),
    )
    from_x, from_cross, inner_half, output_own, pack_1, outer_1y, outer_2, outer_3 = together(
        from_x, from_cross, inner_half, output_own, pack_1, outer_1y, outer_2, outer_3
    )
    from_core = to_core(pack_1)
    output_other = to_core(output_own)
    outer_2y, outer_3y = to_fsdp(outer_2, 1), to_fsdp(outer_3, 1)
    from_core, output_other = together(from_core, output_other)
    inner_other = to_core(after(inner_half, from_core))
    (
        normal,
        inverse,
        first_low,
        active,
        slope,
        context,
        output_full,
        inner_full,
        arrived,
    ) = run(
        inner_own_kernel,
        "inner_own",
        info,
        [
            x,
            pack_0,
            from_core,
            from_x,
            from_cross,
            vec,
            output_own,
            output_other,
            inner_half,
        ],
        [
            ((ROWS, WIDTH), F32),
            ((ROWS, 1), F32),
            ((ROWS, WIDTH), BF),
            ((ROWS, HIDDEN), BF),
            ((ROWS, HIDDEN), BF),
            ((ROWS, 1024), BF),
            ((1024, WIDTH), BF),
            ((WIDTH, HIDDEN), BF),
            ((ROWS, 128), BF),
        ],
        [pltpu.SemaphoreType.DMA((1,))],
        loose=(8,),
    )
    first_low, inner_other, outer_2y, outer_3y = together(
        first_low, inner_other, outer_2y, outer_3y
    )
    (outer_own,) = lay(
        info,
        [outer_pack, outer_0y, outer_1, outer_1y, outer_2, outer_2y, outer_3, outer_3y],
        (1664,),
    )
    outer_other = to_core(outer_own)
    active, slope, inner_full = run(
        inner_other_kernel,
        "inner_other",
        info,
        [after(first_low, outer_own), vec, inner_other, active, slope, inner_full],
        [((ROWS, HIDDEN), BF), ((ROWS, HIDDEN), BF), ((WIDTH, HIDDEN), BF)],
        [pltpu.SemaphoreType.DMA((1,))],
        loose=(2,),
        alias=((3, 0), (4, 1), (5, 2)),
    )
    residual_two, delta_outer, second_low, delta_projected, given, outer_sums, outer_full = run(
        outer_kernel,
        "outer",
        info,
        [active, outer_own, outer_other, normal, vec, dealt, arrived],
        [
            ((ROWS, WIDTH), F32),
            ((ROWS, WIDTH), BF),
            ((ROWS, WIDTH), BF),
            ((ROWS, 128), BF),
            ((ROWS, 128), BF),
            ((8, WIDTH), F32),
            ((HIDDEN, WIDTH), BF),
        ],
        [pltpu.VMEM((WIDTH, 128), BF), pltpu.SemaphoreType.DMA((33,))],
        loose=(1, 2),
    )
    keep_o, send_o = run(
        outer_pack_kernel,
        "outer_pack",
        info,
        [active, delta_outer, second_low, delta_projected],
        [((2, 2, 2, 2, 208, 384), BF)] * 2,
        [pltpu.VMEM((WIDTH, 128), F32)],
    )
    core_o = to_core(send_o)
    delta_inner, inner_side = run(
        hidden_back_kernel,
        "hidden_back",
        info,
        [after(delta_outer, send_o), outer_full, slope],
        [((ROWS, HIDDEN), BF), ((1, HIDDEN), F32)],
    )
    keep_i, send_i = run(
        inner_pack_kernel,
        "inner_pack",
        info,
        [first_low, delta_inner],
        [((2, 2, 2, 2, 192, 384), BF)] * 2,
    )
    core_o, delta_inner, inner_side, keep_i, send_i = together(
        core_o, delta_inner, inner_side, keep_i, send_i
    )

    core_i = to_core(send_i)
    give_o = added([keep_o[1], core_o[1]])
    one_o = to_mixed(give_o, True)
    residual_one, delta_attended, first_sums, *ups = run(
        first_kernel,
        "first",
        info,
        [
            after(delta_inner, give_o),
            inner_full,
            residual_two,
            normal,
            inverse,
            vec,
            output_full,
            given,
        ],
        [((ROWS, WIDTH), F32), ((ROWS, WIDTH), BF), ((8, WIDTH), F32)] + [((896, 128), BF)] * 4,
    )
    core_i, delta_attended, up_0, *ups = together(core_i, delta_attended, *ups)
    ups = [to_core(ups[0]), to_x(ups[1]), to_cross(ups[2])]
    keep_w, send_w = run(
        output_pack_kernel,
        "output_pack",
        info,
        [context, delta_attended],
        [((2, 2, 2, 2, 48, 384), BF)] * 2,
    )
    core_w = to_core(send_w)
    keys = (k, kt, v)
    dq_0, dk, dv = attend_back(info, 0, after(ql_0, send_w), up_0, o_0, *keys)
    one_o, core_w, dq_0, dk, dv, *ups = together(one_o, core_w, dq_0, dk, dv, *ups)

    give_i = jnp.concatenate([added([keep_i[1], core_i[1]]), added([keep_w[1], core_w[1]])], axis=3)
    one_i = to_mixed(give_i, True)
    give_o = added([keep_o[0, 1], core_o[0, 1], one_o[1]])
    two_o = to_mixed(give_o, False)
    dq_1, dk, dv = attend_back(info, 1, after(ql_1, give_i, give_o), ups[0], o_1, *keys, (dk, dv))
    dq_2, dk, dv = attend_back(info, 2, ql_2, ups[1], o_2, *keys, (dk, dv))
    delta_heads, embedded, own, for_core, for_next, _, _ = attend_back(
        info,
        3,
        ql_3,
        ups[2],
        o_3,
        *keys,
        (dk, dv),
        (dq_0, dq_1, dq_2, up_0, *ups[:2], heads_weight, residual_one),
    )
    one_i, two_o, delta_heads, embedded, own, for_core, for_next = together(
        one_i, two_o, delta_heads, embedded, own, for_core, for_next
    )

    came = to_core(for_core)
    sum_i = [keep_i[0, 1], core_i[0, 1]], [keep_w[0, 1], core_w[0, 1]]
    give_i = added([jnp.concatenate(parts, axis=2) for parts in zip(*sum_i)] + [one_i[1]])
    two_i = to_mixed(give_i, False)
    sum_o = [keep_o[0, 0], core_o[0, 0], one_o[0], two_o]
    give_o = added([part[1] for part in sum_o])
    three_o = to_fsdp(give_o, 2)
    (pack,) = run(
        heads_grad_kernel,
        "heads_grad",
        info,
        [
            x,
            x_core,
            x_next,
            x_cross,
            after(delta_heads, give_i, give_o),
            first_sums,
            outer_sums,
            inner_side,
        ],
        [((2, 2, 2, 96, 640), BF)],
    )
    two_i, three_o, pack, came = together(two_i, three_o, pack, came)

    one_h = to_fsdp(pack[1], 1)
    sum_i = [keep_i[0, 0], core_i[0, 0]], [keep_w[0, 0], core_w[0, 0]]
    sum_i = [jnp.concatenate(parts, axis=2) for parts in zip(*sum_i)] + [one_i[0], two_i]
    give_i = added([part[1] for part in sum_i])
    three_i = to_fsdp(give_i, 2)
    sum_o = [*(part[0] for part in sum_o), three_o]
    give_o = added([part[1] for part in sum_o])
    four_o = to_fsdp(give_o, 4)
    give_x = (for_next + wide(came[1])).astype(BF)
    passed = to_x(give_x)
    one_h, three_i, four_o = together(one_h, three_i, four_o)

    sum_i = [*(part[0] for part in sum_i), three_i]
    give_i = added([part[1] for part in sum_i])
    four_i = to_fsdp(give_i, 4)
    give_h = added([pack[0, 1], one_h[1]])
    two_h = to_fsdp(give_h, 2)
    four_i, two_h = together(four_i, two_h)

    give_h = added([pack[0, 0, 1], one_h[0, 1], two_h[1]])
    three_h = to_fsdp(give_h, 4)
    forward_sum = jnp.concatenate(
        [
            added([*(part[0] for part in sum_o), four_o]),
            added([*(part[0] for part in sum_i), four_i]),
        ],
        axis=0,
    )
    forward_next = to_x(forward_sum)
    three_h, passed, forward_next = together(three_h, passed, forward_next)
    mine = added([pack[0, 0, 0], one_h[0, 0], two_h[0], three_h])
    near = jnp.stack([forward_sum, forward_next])
    far = to_core(near)
    heads_all = lax.all_gather(after(mine, near), "ctx")
    square = (96, WIDTH)
    shapes = [
        ((96, HIDDEN), F32),
        ((384, WIDTH), F32),
        (square, F32),
        ((96, 128), F32),
        (square, F32),
        (square, F32),
        (square, F32),
        ((ROWS, WIDTH), BF),
    ]
    (
        inner_grad,
        outer_grad,
        output_grad,
        project_grad,
        query_grad,
        key_grad,
        value_grad,
        delta_home,
        *vec_all,
    ) = run(
        finish_kernel,
        "finish",
        info,
        [near, far, heads_all, own, came, passed],
        shapes + [((1, 96), F32)] * 8 + [((384,), F32)],
        [pltpu.VMEM(*shape) for shape in shapes] + [pltpu.SemaphoreType.DMA((8,))],
        limit=20,
        loose_outs=range(8),
    )
    return (
        embedded[None],
        delta_home[None],
        query_grad,
        key_grad,
        value_grad,
        vec_all[0].reshape(96),
        vec_all[1].reshape(96),
        output_grad,
        vec_all[2].reshape(96),
        vec_all[3].reshape(96),
        vec_all[4].reshape(96),
        inner_grad,
        vec_all[8],
        outer_grad,
        vec_all[5].reshape(96),
        vec_all[6].reshape(96),
        vec_all[7].reshape(96),
        project_grad,
    )


def suits(mesh):
    return mesh.shape["ctx"] == 4 and mesh.shape["fsdp"] == 8


def solution(mesh):
    on_device = fast_device if suits(mesh) else generic_device

    return jax.shard_map(
        on_device,
        mesh=mesh,
        in_specs=(
            P("fsdp", "ctx", None),
            P("fsdp", None),
            P("fsdp", None),
            P("fsdp", None),
            P("fsdp", None),
            P("fsdp", None),
            P("fsdp"),
            P("fsdp"),
            P("fsdp", None),
            P("fsdp"),
            P("fsdp"),
            P("fsdp"),
            P("fsdp", None),
            P("fsdp"),
            P("fsdp", None),
            P("fsdp"),
            P("fsdp"),
            P("fsdp"),
            P("fsdp", None),
            P("fsdp", "ctx", None),
        ),
        out_specs=(
            P("fsdp", "ctx", None),
            P("fsdp", "ctx", None),
            P("fsdp", None),
            P("fsdp", None),
            P("fsdp", None),
            P("fsdp"),
            P("fsdp"),
            P("fsdp", None),
            P("fsdp"),
            P("fsdp"),
            P("fsdp"),
            P("fsdp", None),
            P("fsdp"),
            P("fsdp", None),
            P("fsdp"),
            P("fsdp"),
            P("fsdp"),
            P("fsdp", None),
        ),
        check_vma=False,
    )
```

```python
import functools

import jax
import jax.numpy as jnp
from jax import lax
from jax.experimental import pallas as pl
from jax.experimental.pallas import tpu as pltpu
from jax.sharding import PartitionSpec as P

HEADS = 12
HEAD_DIM = 64


def matmul(left, right):
    return jnp.dot(left, right, preferred_element_type=jnp.float32)


def norm_forward(value, gain, shift):
    centred = value - jnp.mean(value, axis=-1, keepdims=True)
    inverse = lax.rsqrt(jnp.mean(centred * centred, axis=-1, keepdims=True) + 1e-12)
    normal = centred * inverse
    return (normal * gain + shift, normal, inverse)


def norm_backward(upstream, normal, inverse, gain):
    scaled = upstream * gain
    first_mean = jnp.mean(scaled, axis=-1, keepdims=True)
    second_mean = jnp.mean(scaled * normal, axis=-1, keepdims=True)
    inward = inverse * (scaled - first_mean - normal * second_mean)
    return (inward, jnp.sum(upstream * normal, axis=0), jnp.sum(upstream, axis=0))


def gelu_slope(value):
    cumulative = 0.5 * (1.0 + jax.scipy.special.erf(value * 0.7071067811865476))
    return cumulative + value * jnp.exp(-0.5 * value * value) * 0.3989422804014327


def scored(query_heads, key_block, query_segments, segment_block, scale):
    scores = (
        jnp.einsum("qhd,khd->hqk", query_heads, key_block, preferred_element_type=jnp.float32)
        * scale
    )
    allowed = (query_segments[:, None] == segment_block[None, :])[None]
    return (scores, allowed)


def probabilities(scores, allowed, log_total):
    return jnp.where(allowed, jnp.exp(scores - log_total[..., None]), 0.0)


def log_totals(query_heads, key_blocks, query_segments, segment_blocks, scale):

    def log_advance(carry, pieces):
        running_max, running_sum = carry
        scores, allowed = scored(query_heads, pieces[0], query_segments, pieces[1], scale)
        masked = jnp.where(allowed, scores, -1e30)
        new_max = jnp.maximum(running_max, jnp.max(masked, axis=-1))
        fresh = jnp.sum(jnp.where(allowed, jnp.exp(masked - new_max[..., None]), 0.0), axis=-1)
        return ((new_max, running_sum * jnp.exp(running_max - new_max) + fresh), None)

    shape = (query_heads.shape[1], query_heads.shape[0])
    start = (jnp.full(shape, -1e30, jnp.float32), jnp.zeros(shape, jnp.float32))
    final = lax.scan(log_advance, start, (key_blocks, segment_blocks))[0]
    return final[0] + jnp.log(final[1])


def attend(query_heads, key_blocks, value_blocks, query_segments, segment_blocks, scale):
    log_total = log_totals(query_heads, key_blocks, query_segments, segment_blocks, scale)

    def attend_advance(carry, pieces):
        scores, allowed = scored(query_heads, pieces[0], query_segments, pieces[2], scale)
        probs = probabilities(scores, allowed, log_total).astype(jnp.bfloat16)
        return (
            carry
            + jnp.einsum("hqk,khd->qhd", probs, pieces[1], preferred_element_type=jnp.float32),
            None,
        )

    start = jnp.zeros(query_heads.shape, jnp.float32)
    mixed = lax.scan(attend_advance, start, (key_blocks, value_blocks, segment_blocks))[0]
    return (mixed, log_total)


def attend_backward(
    query_heads,
    key_blocks,
    value_blocks,
    query_segments,
    segment_blocks,
    scale,
    log_total,
    upstream,
):

    def first_pass(carry, pieces):
        scores, allowed = scored(query_heads, pieces[0], query_segments, pieces[2], scale)
        probs = probabilities(scores, allowed, log_total)
        delta_probs = jnp.einsum(
            "qhd,khd->hqk", upstream, pieces[1], preferred_element_type=jnp.float32
        )
        value_terms = jnp.einsum(
            "hqk,qhd->khd", probs.astype(jnp.bfloat16), upstream, preferred_element_type=jnp.float32
        )
        return (carry + jnp.sum(probs * delta_probs, axis=-1), value_terms)

    shape = (query_heads.shape[1], query_heads.shape[0])
    weighted, value_terms = lax.scan(
        first_pass, jnp.zeros(shape, jnp.float32), (key_blocks, value_blocks, segment_blocks)
    )

    def second_pass(carry, pieces):
        scores, allowed = scored(query_heads, pieces[0], query_segments, pieces[2], scale)
        probs = probabilities(scores, allowed, log_total)
        delta_probs = jnp.einsum(
            "qhd,khd->hqk", upstream, pieces[1], preferred_element_type=jnp.float32
        )
        delta_scores = (probs * (delta_probs - weighted[..., None])).astype(jnp.bfloat16)
        key_terms = jnp.einsum(
            "hqk,qhd->khd", delta_scores, query_heads, preferred_element_type=jnp.float32
        )
        return (
            carry
            + jnp.einsum(
                "hqk,khd->qhd", delta_scores, pieces[0], preferred_element_type=jnp.float32
            ),
            key_terms,
        )

    query_terms, key_terms = lax.scan(
        second_pass,
        jnp.zeros(query_heads.shape, jnp.float32),
        (key_blocks, value_blocks, segment_blocks),
    )
    return (query_terms * scale, key_terms * scale, value_terms)


def generic_device(
    tokens,
    dealt,
    segments,
    query_weight,
    key_weight,
    value_weight,
    query_bias,
    value_bias,
    output_weight,
    output_bias,
    first_gain,
    first_shift,
    inner_weight,
    inner_bias,
    outer_weight,
    outer_bias,
    second_gain,
    second_shift,
    project_weight,
    cotangent,
):
    peers = lax.axis_size("ctx")
    place = lax.axis_index("ctx")
    local_rows = tokens.shape[1]
    share = local_rows // peers
    order = dealt[0]
    table = (
        lax.dynamic_index_in_dim(order.reshape(peers, peers, share), place, 1, keepdims=False)
        - place * local_rows
    )
    flat_table = table.reshape(-1)
    home_tokens = tokens[0]
    width = home_tokens.shape[1]
    (
        query_full,
        key_full,
        value_full,
        output_full,
        query_shift,
        value_shift,
        output_shift,
        gain_one,
        shift_one,
    ) = (
        lax.all_gather(query_weight, "fsdp", axis=0, tiled=True),
        lax.all_gather(key_weight, "fsdp", axis=0, tiled=True),
        lax.all_gather(value_weight, "fsdp", axis=0, tiled=True),
        lax.all_gather(output_weight, "fsdp", axis=0, tiled=True),
        lax.all_gather(query_bias, "fsdp", axis=0, tiled=True),
        lax.all_gather(value_bias, "fsdp", axis=0, tiled=True),
        lax.all_gather(output_bias, "fsdp", axis=0, tiled=True),
        lax.all_gather(first_gain, "fsdp", axis=0, tiled=True),
        lax.all_gather(first_shift, "fsdp", axis=0, tiled=True),
    )
    outgoing = jnp.take(home_tokens, table, axis=0)
    here_tokens = lax.all_to_all(outgoing, "ctx", split_axis=0, concat_axis=0, tiled=True).reshape(
        local_rows, width
    )
    key_segments = jnp.take(segments[0], order, axis=0)
    query_segments = lax.dynamic_slice_in_dim(key_segments, place * local_rows, local_rows)
    queries = (matmul(here_tokens, query_full) + query_shift.astype(jnp.float32)).astype(
        jnp.bfloat16
    )
    own_keys = matmul(here_tokens, key_full).astype(jnp.bfloat16)
    own_values = (matmul(here_tokens, value_full) + value_shift.astype(jnp.float32)).astype(
        jnp.bfloat16
    )
    all_keys, all_values = (
        lax.all_gather(own_keys, "ctx", axis=0, tiled=True),
        lax.all_gather(own_values, "ctx", axis=0, tiled=True),
    )
    total = all_keys.shape[0]
    block = min(1024, total)
    count = total // block
    scale = HEAD_DIM ** (-0.5)
    query_heads = queries.reshape(local_rows, HEADS, HEAD_DIM)
    key_blocks = all_keys.reshape(count, block, HEADS, HEAD_DIM)
    value_blocks = all_values.reshape(count, block, HEADS, HEAD_DIM)
    segment_blocks = key_segments.reshape(count, block)
    mixed, log_total = attend(
        query_heads, key_blocks, value_blocks, query_segments, segment_blocks, scale
    )
    context = mixed.reshape(local_rows, width).astype(jnp.bfloat16)
    inner_full, inner_shift, outer_full, outer_shift, gain_two, shift_two, project_full = (
        lax.all_gather(inner_weight, "fsdp", axis=0, tiled=True),
        lax.all_gather(inner_bias, "fsdp", axis=0, tiled=True),
        lax.all_gather(outer_weight, "fsdp", axis=0, tiled=True),
        lax.all_gather(outer_bias, "fsdp", axis=0, tiled=True),
        lax.all_gather(second_gain, "fsdp", axis=0, tiled=True),
        lax.all_gather(second_shift, "fsdp", axis=0, tiled=True),
        lax.all_gather(project_weight, "fsdp", axis=0, tiled=True),
    )
    attended = matmul(context, output_full) + output_shift.astype(jnp.float32)
    first, first_normal, first_inverse = norm_forward(
        here_tokens.astype(jnp.float32) + attended,
        gain_one.astype(jnp.float32),
        shift_one.astype(jnp.float32),
    )
    first_low = first.astype(jnp.bfloat16)
    inner = matmul(first_low, inner_full) + inner_shift.astype(jnp.float32)
    active = jax.nn.gelu(inner, approximate=False).astype(jnp.bfloat16)
    outer = matmul(active, outer_full) + outer_shift.astype(jnp.float32)
    second, second_normal, second_inverse = norm_forward(
        first + outer, gain_two.astype(jnp.float32), shift_two.astype(jnp.float32)
    )
    second_low = second.astype(jnp.bfloat16)
    projected = matmul(second_low, project_full)
    inverse_length = lax.rsqrt(jnp.sum(projected * projected, axis=-1, keepdims=True) + 1e-06)
    normed = projected * inverse_length
    embedded = normed.astype(jnp.bfloat16)
    incoming = cotangent[0].astype(jnp.float32)
    along = jnp.sum(normed * incoming, axis=-1, keepdims=True)
    delta_projected = (inverse_length * (incoming - normed * along)).astype(jnp.bfloat16)
    project_delta = matmul(second_low.T, delta_projected)
    delta_second = matmul(delta_projected, project_full.T)
    residual_two, second_gain_delta, second_shift_delta = norm_backward(
        delta_second, second_normal, second_inverse, gain_two.astype(jnp.float32)
    )
    delta_outer = residual_two.astype(jnp.bfloat16)
    outer_bias_delta = jnp.sum(delta_outer, axis=0, dtype=jnp.float32)
    outer_delta = matmul(active.T, delta_outer)
    delta_active = matmul(delta_outer, outer_full.T)
    delta_inner = (delta_active * gelu_slope(inner)).astype(jnp.bfloat16)
    inner_bias_delta = jnp.sum(delta_inner, axis=0, dtype=jnp.float32)
    inner_delta = matmul(first_low.T, delta_inner)
    delta_first = residual_two + matmul(delta_inner, inner_full.T)
    residual_one, first_gain_delta, first_shift_delta = norm_backward(
        delta_first, first_normal, first_inverse, gain_one.astype(jnp.float32)
    )
    delta_attended = residual_one.astype(jnp.bfloat16)
    output_bias_delta = jnp.sum(delta_attended, axis=0, dtype=jnp.float32)
    output_delta = matmul(context.T, delta_attended)
    delta_context = matmul(delta_attended, output_full.T).astype(jnp.bfloat16)
    upstream = delta_context.reshape(local_rows, HEADS, HEAD_DIM)
    query_terms, key_terms, value_terms = attend_backward(
        query_heads,
        key_blocks,
        value_blocks,
        query_segments,
        segment_blocks,
        scale,
        log_total,
        upstream,
    )
    key_sums, value_sums = (
        lax.psum_scatter(
            key_terms.reshape(total, width).astype(jnp.bfloat16),
            "ctx",
            scatter_dimension=0,
            tiled=True,
        ).astype(jnp.float32),
        lax.psum_scatter(
            value_terms.reshape(total, width).astype(jnp.bfloat16),
            "ctx",
            scatter_dimension=0,
            tiled=True,
        ).astype(jnp.float32),
    )
    delta_keys = key_sums.astype(jnp.bfloat16)
    delta_values = value_sums.astype(jnp.bfloat16)
    delta_queries = query_terms.reshape(local_rows, width).astype(jnp.bfloat16)
    query_bias_delta = jnp.sum(delta_queries, axis=0, dtype=jnp.float32)
    value_bias_delta = jnp.sum(delta_values, axis=0, dtype=jnp.float32)
    query_delta = matmul(here_tokens.T, delta_queries)
    key_delta = matmul(here_tokens.T, delta_keys)
    value_delta = matmul(here_tokens.T, delta_values)
    delta_here = (
        residual_one
        + matmul(delta_queries, query_full.T)
        + matmul(delta_keys, key_full.T)
        + matmul(delta_values, value_full.T)
    ).astype(jnp.bfloat16)
    coming_home = lax.all_to_all(
        delta_here.reshape(peers, share, width), "ctx", split_axis=0, concat_axis=0, tiled=True
    )
    delta_home = (
        jnp.zeros((local_rows, width), jnp.bfloat16)
        .at[flat_table]
        .set(coming_home.reshape(local_rows, width))
    )
    (
        inner_part,
        inner_bias_part,
        outer_part,
        outer_bias_part,
        second_gain_part,
        second_shift_part,
        project_part,
    ) = (
        lax.psum_scatter(
            inner_delta.astype(jnp.bfloat16), "fsdp", scatter_dimension=0, tiled=True
        ).astype(jnp.float32),
        lax.psum_scatter(
            inner_bias_delta.astype(jnp.bfloat16), "fsdp", scatter_dimension=0, tiled=True
        ).astype(jnp.float32),
        lax.psum_scatter(
            outer_delta.astype(jnp.bfloat16), "fsdp", scatter_dimension=0, tiled=True
        ).astype(jnp.float32),
        lax.psum_scatter(
            outer_bias_delta.astype(jnp.bfloat16), "fsdp", scatter_dimension=0, tiled=True
        ).astype(jnp.float32),
        lax.psum_scatter(
            second_gain_delta.astype(jnp.bfloat16), "fsdp", scatter_dimension=0, tiled=True
        ).astype(jnp.float32),
        lax.psum_scatter(
            second_shift_delta.astype(jnp.bfloat16), "fsdp", scatter_dimension=0, tiled=True
        ).astype(jnp.float32),
        lax.psum_scatter(
            project_delta.astype(jnp.bfloat16), "fsdp", scatter_dimension=0, tiled=True
        ).astype(jnp.float32),
    )
    (
        query_part,
        key_part,
        value_part,
        query_bias_part,
        value_bias_part,
        output_part,
        output_bias_part,
        first_gain_part,
        first_shift_part,
    ) = (
        lax.psum_scatter(
            query_delta.astype(jnp.bfloat16), "fsdp", scatter_dimension=0, tiled=True
        ).astype(jnp.float32),
        lax.psum_scatter(
            key_delta.astype(jnp.bfloat16), "fsdp", scatter_dimension=0, tiled=True
        ).astype(jnp.float32),
        lax.psum_scatter(
            value_delta.astype(jnp.bfloat16), "fsdp", scatter_dimension=0, tiled=True
        ).astype(jnp.float32),
        lax.psum_scatter(
            query_bias_delta.astype(jnp.bfloat16), "fsdp", scatter_dimension=0, tiled=True
        ).astype(jnp.float32),
        lax.psum_scatter(
            value_bias_delta.astype(jnp.bfloat16), "fsdp", scatter_dimension=0, tiled=True
        ).astype(jnp.float32),
        lax.psum_scatter(
            output_delta.astype(jnp.bfloat16), "fsdp", scatter_dimension=0, tiled=True
        ).astype(jnp.float32),
        lax.psum_scatter(
            output_bias_delta.astype(jnp.bfloat16), "fsdp", scatter_dimension=0, tiled=True
        ).astype(jnp.float32),
        lax.psum_scatter(
            first_gain_delta.astype(jnp.bfloat16), "fsdp", scatter_dimension=0, tiled=True
        ).astype(jnp.float32),
        lax.psum_scatter(
            first_shift_delta.astype(jnp.bfloat16), "fsdp", scatter_dimension=0, tiled=True
        ).astype(jnp.float32),
    )
    results = (
        lax.psum(query_part.astype(jnp.bfloat16), "ctx").astype(jnp.float32),
        lax.psum(key_part.astype(jnp.bfloat16), "ctx").astype(jnp.float32),
        lax.psum(value_part.astype(jnp.bfloat16), "ctx").astype(jnp.float32),
        lax.psum(query_bias_part.astype(jnp.bfloat16), "ctx").astype(jnp.float32),
        lax.psum(value_bias_part.astype(jnp.bfloat16), "ctx").astype(jnp.float32),
        lax.psum(output_part.astype(jnp.bfloat16), "ctx").astype(jnp.float32),
        lax.psum(output_bias_part.astype(jnp.bfloat16), "ctx").astype(jnp.float32),
        lax.psum(first_gain_part.astype(jnp.bfloat16), "ctx").astype(jnp.float32),
        lax.psum(first_shift_part.astype(jnp.bfloat16), "ctx").astype(jnp.float32),
        lax.psum(inner_part.astype(jnp.bfloat16), "ctx").astype(jnp.float32),
        lax.psum(inner_bias_part.astype(jnp.bfloat16), "ctx").astype(jnp.float32),
        lax.psum(outer_part.astype(jnp.bfloat16), "ctx").astype(jnp.float32),
        lax.psum(outer_bias_part.astype(jnp.bfloat16), "ctx").astype(jnp.float32),
        lax.psum(second_gain_part.astype(jnp.bfloat16), "ctx").astype(jnp.float32),
        lax.psum(second_shift_part.astype(jnp.bfloat16), "ctx").astype(jnp.float32),
        lax.psum(project_part.astype(jnp.bfloat16), "ctx").astype(jnp.float32),
    )
    return (
        embedded[None],
        delta_home[None],
        results[0],
        results[1],
        results[2],
        results[3],
        results[4],
        results[5],
        results[6],
        results[7],
        results[8],
        results[9],
        results[10],
        results[11],
        results[12],
        results[13],
        results[14],
        results[15],
    )


BF = jnp.bfloat16
F32 = jnp.float32
ROWS = 512
HALF = 256
WIDTH = 768
HIDDEN = 3072
LOCAL = 3
FAR = 2.0**100
KROWS = 256
SCALE = HEAD_DIM ** (-0.5)


def nt(left, right):
    return lax.dot_general(left, right, (((1,), (1,)), ((), ())), preferred_element_type=F32)


def nn(left, right):
    return lax.dot_general(left, right, (((1,), (0,)), ((), ())), preferred_element_type=F32)


def tn(left, right):
    return lax.dot_general(left, right, (((0,), (0,)), ((), ())), preferred_element_type=F32)


def wide(value):
    return value.astype(F32)


def to_core(value):
    return lax.ppermute(value, "ctx", [(i, i ^ 1) for i in range(4)])


def to_x(value):
    return lax.ppermute(value, "ctx", [(i, i ^ 2) for i in range(4)])


def to_cross(value):
    return lax.ppermute(value, "ctx", [(i, i ^ 3) for i in range(4)])


def to_fsdp(value, bit):
    return lax.ppermute(value, "fsdp", [(i, i ^ bit) for i in range(8)])


def along_z(value, step):
    return lax.ppermute(value, "fsdp", [(i, (i + 2 * step) % 8) for i in range(8)])


def to_mixed(value, first):
    pairs = []
    for c in range(4):
        for f in range(8):
            target = (c ^ 2) * 8 + f if (c % 2 == 0) == first else c * 8 + (f ^ 1)
            pairs.append((c * 8 + f, target))
    return lax.ppermute(value, ("ctx", "fsdp"), pairs)


def after(value, *others):
    return lax.optimization_barrier((value, *others))[0]


def added(parts):
    total = wide(parts[0])
    for part in parts[1:]:
        total = total + wide(part)
    return total.astype(BF)


def together(*values):
    return lax.optimization_barrier(values)


def three_parts(value):
    high = wide(value.astype(BF))
    rest = value - high
    middle = wide(rest.astype(BF))
    return high, middle, rest - middle


def lanes_of(rows, n=128):
    return lax.broadcasted_iota(jnp.int32, (rows, n), 1)


def run(
    kernel, name, info, inputs, outs, scratch=(), limit=6, loose=(), loose_outs=(), alias=(), small=False
):
    memory = pl.BlockSpec(memory_space=pltpu.VMEM)
    outside = pl.BlockSpec(memory_space=pltpu.HBM)
    return pl.pallas_call(
        kernel,
        in_specs=[pl.BlockSpec(memory_space=pltpu.SMEM)]
        + [outside if i in loose else memory for i in range(len(inputs))],
        out_specs=[pl.BlockSpec(memory_space=pltpu.SMEM)]
        if small
        else [outside if i in loose_outs else memory for i in range(len(outs))],
        out_shape=[jax.ShapeDtypeStruct(s, t) for s, t in outs],
        scratch_shapes=list(scratch),
        input_output_aliases={i + 1: o for i, o in alias},
        compiler_params=pltpu.CompilerParams(vmem_limit_bytes=limit << 20),
        cost_estimate=pl.CostEstimate(flops=1000, bytes_accessed=1000, transcendentals=0),
        name=name,
    )(info, *inputs)


def start_copies(pairs, sems):
    copies = [pltpu.make_async_copy(a, b, sems.at[i]) for i, (a, b) in enumerate(pairs)]
    for copy in copies:
        copy.start()
    return copies


def aligned(value, n):
    return pl.multiple_of(value, n)


def piece_rows(info, n):
    z, y = info[1] // 2, lax.rem(info[1], 2)
    rows = []
    for k in range(4):
        source = lax.rem(z + 4 - k, 4)
        rows += [aligned((source * 2 + t) * n, 32) for t in (y, 1 - y)]
    return rows


def prepare_forward_kernel(info, wi_in, wo_in, w2_in, p_in, outer_out, inner_out, sems):
    core = lax.rem(info[0], 2)
    copies = start_copies(
        [
            (w2_in.at[pl.ds(aligned(core * 192, 64), 96)], outer_out.at[:, 0:768]),
            (w2_in.at[pl.ds(aligned(core * 192 + 96, 32), 96)], outer_out.at[:, 768:1536]),
            (p_in, outer_out.at[:, 1536:1664]),
            (wi_in.at[:, pl.ds(aligned(core * 1536, 512), 1536)], inner_out.at[:, 0:1536]),
            (wo_in.at[:, pl.ds(aligned(core * 384, 128), 384)], inner_out.at[:, 1536:1920]),
        ],
        sems,
    )
    for copy in copies:
        copy.wait()


def prepare_heads_kernel(info, *refs):
    ins, last_ref, heads_out, held, sems = refs[:11], refs[11], refs[12], refs[13:24], refs[24]
    c = info[0]
    copies = start_copies(zip(ins, held), sems)
    q_ref, k_ref, v_ref, *rows = held
    for copy in copies:
        copy.wait()
    rows = [wide(ref[...]) for ref in (*rows, last_ref)]
    rows = jnp.concatenate([*rows, jnp.zeros((116, 96), F32)], axis=0)
    rows = jnp.concatenate([rows, jnp.zeros((128, 32), F32)], axis=1)
    side = rows.T[:96, :64]
    for value in range(4):

        @pl.when(c == value)
        def _():
            at = slice(192 * value, 192 * value + 192)
            parts = [wide(ref[:, at]) for ref in (q_ref, k_ref, v_ref)]
            heads_out[...] = jnp.concatenate([*parts, side], axis=1).astype(BF)


def lay_kernel(info, *refs):
    pieces, outs, sems = refs[:8], refs[8:-1], refs[-1]
    pairs, start = [], 0
    for out in outs:
        stop = start + out.shape[1]
        for ref, row in zip(pieces, piece_rows(info, 96)):
            pairs.append((ref.at[:, start:stop], out.at[pl.ds(row, 96)]))
        start = stop
    copies = start_copies(pairs, sems)
    for copy in copies:
        copy.wait()


def lay(info, pieces, widths):
    return run(
        lay_kernel,
        "lay",
        info,
        pieces,
        [((WIDTH, n), BF) for n in widths],
        [pltpu.SemaphoreType.DMA((8 * len(widths),))],
        loose=range(8),
    )


def places_kernel(place, seg_ref, info_out):
    seg = wide(seg_ref[...])
    at = lanes_of(1, seg.shape[1])
    for i in range(4):
        info_out[i] = place[i]
        info_out[20 + i] = 0
    for i in range(8):
        start = jnp.sum(jnp.where(at == HALF * i, seg, 0.0))
        end = jnp.sum(jnp.where(at == HALF * i + HALF - 1, seg, 0.0))
        low = jnp.sum(jnp.where(seg < start, 1.0, 0.0)).astype(jnp.int32)
        high = jnp.sum(jnp.where(seg <= end, 1.0, 0.0)).astype(jnp.int32)
        info_out[4 + i] = low // KROWS
        info_out[12 + i] = (high + KROWS - 1) // KROWS


def project_kernel(info, *refs):
    x_refs, w_refs = refs[0:4], refs[4:12]
    seg_ref = refs[12]
    q_out, k_out, v_out, kt_out, vt_out, w_out, vec_out, sems = refs[13:]
    c = info[0]
    copies = start_copies(
        [(ref, w_out.at[pl.ds(row, 96)]) for ref, row in zip(w_refs, piece_rows(info, 96))], sems
    )
    for copy in copies:
        copy.wait()
    weights = w_out[...]
    turned = wide(weights[:, 512:640]).T
    vec_out[...] = turned[64:80]
    lane = lanes_of(WIDTH, 640)
    row = lax.broadcasted_iota(jnp.int32, (WIDTH, 640), 0)
    wanted = jnp.where(lane < 384, lane, lane - 384) + 192 * c
    chosen = nn(turned[64:80].astype(BF), wide(row == wanted).astype(BF))
    lane1 = lanes_of(1, 640)
    bias = jnp.where(
        lane1 < 192,
        chosen[0:1],
        jnp.where((lane1 >= 384) & (lane1 < 576), chosen[1:2], 0.0),
    )
    lanes = lanes_of(ROWS)
    for r in range(4):
        rows = pl.ds(aligned(jnp.bitwise_xor(c, r) * ROWS, ROWS), ROWS)
        result = nn(x_refs[r][...], weights) + bias
        seg = seg_ref[:, pl.ds(aligned(jnp.bitwise_xor(c, r) * ROWS, ROWS), ROWS)]
        same = jnp.broadcast_to(wide(seg), (128, ROWS)).T == wide(lanes - 64)
        qa = jnp.where(same & (lanes < 67), 1.0, 0.0)
        ka = jnp.where(lanes < 67, jnp.where(same, 0.0, -FAR), jnp.where(lanes < 70, 1.0, 0.0))
        for slot in range(9):
            pair = result[:, 128 * (slot // 2) : 128 * (slot // 2) + 128]
            if slot % 2:
                pair = pltpu.roll(pair, 64, 1)
            kind, h = slot // 3, slot % 3
            if kind == 0:
                low = wide(pair.astype(BF)) * SCALE
                q_out[h, rows, :] = jnp.where(lanes < 64, low, qa).astype(BF)
            elif kind == 1:
                value = jnp.where(lanes < 64, pair, ka)
                k_out[h, rows, :] = value.astype(BF)
                kt_out[h, :, rows] = value.T[:64].astype(BF)
            else:
                value = jnp.where(lanes < 64, pair, jnp.where(lanes < 67, 1.0, 0.0))
                v_out[h, rows, :] = value.astype(BF)
                vt_out[h, :, rows] = value.T[:80].astype(BF)


def over_keys(info, place, step):
    low_0, low_1 = info[4 + 2 * place], info[5 + 2 * place]
    high_0, high_1 = info[12 + 2 * place], info[13 + 2 * place]
    stop = jnp.maximum(high_0, low_1)
    pairs = (stop - low_1) // 2

    def loop(start, count, width, rows):
        def body(i, carry):
            at = aligned((start + i * (width // KROWS)) * KROWS, KROWS)
            step(pl.ds(at, width), rows)
            return carry

        lax.fori_loop(0, count, body, 0)

    loop(low_0, jnp.minimum(low_1, high_0) - low_0, KROWS, slice(0, HALF))
    loop(low_1, pairs, 2 * KROWS, slice(0, ROWS))
    loop(low_1 + 2 * pairs, stop - low_1 - 2 * pairs, KROWS, slice(0, ROWS))
    loop(stop, high_1 - stop, KROWS, slice(HALF, ROWS))


def attend_kernel(info, q_ref, k_ref, vt_ref, cot_ref, *refs, chip):
    each = range(LOCAL)
    top_s, sum_s, q_s = refs[6:]
    for step in range(2):
        o_ref, ql_ref, pack_ref = refs[3 * step : 3 * step + 3]
        place = jnp.bitwise_xor(info[0], step + 2 * chip)
        mine = pl.ds(aligned(place * ROWS, ROWS), ROWS)
        q_s[...] = q_ref[:, mine]
        top_s[...] = jnp.full_like(top_s, -3e38)
        sum_s[...] = jnp.zeros_like(sum_s)

        def advance(rows, part):
            scores = [nt(k_ref[h, rows], q_s[h, part]) for h in each]
            before = [top_s[h, :1, part] for h in each]
            peaks = [
                jnp.maximum(before[h], jnp.max(scores[h], axis=0, keepdims=True)) for h in each
            ]
            probs = [jnp.exp(scores[h] - peaks[h]).astype(BF) for h in each]
            shrink = [jnp.exp(before[h] - peaks[h]) for h in each]
            fresh = [nn(vt_ref[h, :, rows], probs[h]) for h in each]
            for h in each:
                sum_s[h, :, part] = sum_s[h, :, part] * shrink[h] + fresh[h]
                top_s[h, :, part] = jnp.broadcast_to(peaks[h], (8, peaks[h].shape[1]))

        over_keys(info, place, advance)
        lanes = lanes_of(ROWS)
        subs = lax.broadcasted_iota(jnp.int32, (128, ROWS), 0)
        outs = []
        for h in each:
            sums = sum_s[h]
            total = sums[64:65]
            parts = three_parts(top_s[h, :1] + jnp.log(total))
            tall = jnp.concatenate([sums[:64] / total, jnp.zeros((64, ROWS), F32)], axis=0)
            for i in range(3):
                tall = jnp.where(subs == 67 + i, -parts[i], tall)
            turned = tall.T
            out = jnp.where(lanes < 64, turned, 0.0)
            outs.append(out)
            o_ref[h] = out.astype(BF)
            ql_ref[h] = jnp.where(lanes < 67, wide(q_s[h]), turned).astype(BF)
        pack_ref[0:512] = (outs[0] + pltpu.roll(outs[1], 64, 1)).astype(BF)
        pack_ref[512:768] = (outs[2][:256] + pltpu.roll(outs[2][256:], 64, 1)).astype(BF)
        pack_ref[768:896] = cot_ref[pl.ds(aligned(place * 128, 128), 128), :]


def attend_rows(info, q, k, vt, cotangent, chip):
    return run(
        functools.partial(attend_kernel, chip=chip),
        "attend_rows",
        info,
        [q, k, vt, cotangent],
        ([((LOCAL, ROWS, 128), BF)] * 2 + [((896, 128), BF)]) * 2,
        [
            pltpu.VMEM((LOCAL, 8, ROWS), F32),
            pltpu.VMEM((LOCAL, 80, ROWS), F32),
            pltpu.VMEM((LOCAL, ROWS, 128), BF),
        ],
    )


def attend_back_kernel(info, *refs, r):
    each = range(LOCAL)
    ql_ref, up_ref, o_ref, k_ref, kt_ref, v_ref = refs[:6]
    *outs, dk_s, dv_s, dq_s, do_s = refs[6:]
    lanes = lanes_of(ROWS)
    if r == 0:
        (dq_ref,) = outs
        dk_s[...] = jnp.zeros_like(dk_s)
        dv_s[...] = jnp.zeros_like(dv_s)
    elif r < 3:
        _, _, dq_ref = outs
    else:
        w_ref, residual_ref, all_ref, emb_ref, *grads = outs[8:]
        for i, ref in enumerate((*outs[5:8], up_ref)):
            at = pl.ds(aligned(jnp.bitwise_xor(info[0], i) * 128, 128), 128)
            emb_ref[at, :] = ref[768:896]
    place = jnp.bitwise_xor(info[0], r)
    dq_s[...] = jnp.zeros_like(dq_s)
    pair = wide(up_ref[0:512])
    last = wide(up_ref[512:768])
    ups = [
        pair,
        pltpu.roll(pair, 64, 1),
        jnp.concatenate([last, pltpu.roll(last, 64, 1)], axis=0),
    ]
    for h in each:
        up = jnp.where(lanes < 64, ups[h], 0.0)
        parts = three_parts(jnp.sum(up * wide(o_ref[h]), axis=1, keepdims=True))
        for i in range(3):
            up = jnp.where(lanes == 64 + i, -parts[i], up)
        do_s[h] = up.astype(BF)

    def advance(rows, part):
        scores = [nt(k_ref[h, rows], ql_ref[h, part]) for h in each]
        rises = [nt(v_ref[h, rows], do_s[h, part]) for h in each]
        probs = [jnp.exp(scores[h]) for h in each]
        deltas = [(probs[h] * rises[h]).astype(BF) for h in each]
        lows = [probs[h].astype(BF) for h in each]
        for_values = [nn(lows[h], do_s[h, part]) for h in each]
        for_keys = [nn(deltas[h], ql_ref[h, part]) for h in each]
        for_queries = [nn(kt_ref[h, :, rows], deltas[h]) for h in each]
        for h in each:
            dv_s[h, rows] += for_values[h]
            dk_s[h, rows] += for_keys[h]
            dq_s[h, :, part] += for_queries[h]

    over_keys(info, place, advance)
    turned = []
    for h in each:
        tall = jnp.concatenate([dq_s[h], jnp.zeros((64, ROWS), F32)], axis=0)
        turned.append(tall.T * SCALE)
    both = (turned[0] + pltpu.roll(turned[1], 64, 1)).astype(BF)
    if r < 3:
        dq_ref[:, 0:128] = both
        dq_ref[:, 128:256] = turned[2].astype(BF)
        return
    mine = pl.ds(aligned(place * ROWS, ROWS), ROWS)
    all_ref[mine, 0:128] = both
    all_ref[mine, 128:256] = turned[2].astype(BF)
    for i, ref in enumerate(outs[2:5]):
        at = pl.ds(aligned(jnp.bitwise_xor(info[0], i) * ROWS, ROWS), ROWS)
        all_ref[at, 0:256] = ref[...]
    for b in range(4):
        rows = pl.ds(b * ROWS, ROWS)
        low = [jnp.where(lanes < 64, ref[h, rows], 0.0) for ref in (dk_s, dv_s) for h in each]
        high = [pltpu.roll(value, 64, 1) for value in low]
        all_ref[rows, 128:256] = (wide(all_ref[rows, 128:256]) + high[0]).astype(BF)
        all_ref[rows, 256:384] = (low[1] + high[2]).astype(BF)
        all_ref[rows, 384:512] = (low[3] + high[4]).astype(BF)
        all_ref[rows, 512:640] = low[5].astype(BF)
    input_grad(info, all_ref, w_ref, residual_ref, *grads)


def attend_back(info, r, ql, up, o, k, kt, v, carried=(), earlier=()):
    sums = [(k.shape, F32)] * 2
    part = [((ROWS, 256), BF)]
    whole = [
        ((k.shape[1], 640), BF),
        ((ROWS, 128), BF),
        ((ROWS, WIDTH), F32),
        ((2, ROWS, WIDTH), BF),
        ((ROWS, WIDTH), F32),
    ]
    first = len(part if r < 3 else whole)
    return run(
        functools.partial(attend_back_kernel, r=r),
        "attend_back",
        info,
        [ql, up, o, k, kt, v, *carried, *earlier],
        (part if r < 3 else whole) + sums,
        [pltpu.VMEM((LOCAL, 64, ROWS), F32), pltpu.VMEM((LOCAL, ROWS, 128), BF)],
        limit=9,
        alias=((6, first), (7, first + 1)) if r else (),
    )


def gaussian(value):
    below = 0.5 * (1.0 + lax.erf(value * 0.7071067811865476))
    return below, jnp.exp(-0.5 * value * value) * 0.3989422804014327


def norm_rows(value):
    centred = value - jnp.mean(value, axis=-1, keepdims=True)
    inverse = lax.rsqrt(jnp.mean(centred * centred, axis=-1, keepdims=True) + 1e-12)
    return centred * inverse, inverse


def norm_rows_back(upstream, normal, inverse, gain):
    scaled = upstream * gain
    first_mean = jnp.mean(scaled, axis=-1, keepdims=True)
    second_mean = jnp.mean(scaled * normal, axis=-1, keepdims=True)
    return inverse * (scaled - first_mean - normal * second_mean)


def column_sums(value):
    return jnp.sum(value, axis=0, keepdims=True)


def hidden_half(half, first, wi_ref, vec_ref, active_out, slope_out):
    shift = jnp.concatenate(
        [vec_ref[8 + k : 9 + k, 96 * f : 96 * f + 96] for f in range(8) for k in range(4)], axis=1
    )
    shift = jnp.where(half == 0, shift[:, :1536], shift[:, 1536:])
    for block in range(3):
        at = pl.ds(aligned(half * 1536 + block * 512, 512), 512)
        value = nn(first, wi_ref[:, at]) + shift[:, block * 512 : block * 512 + 512]
        below, bell = gaussian(value)
        active_out[:, at] = (value * below).astype(BF)
        slope_out[:, at] = (below + value * bell).astype(BF)


def inner_own_kernel(info, *refs):
    x_ref, *packs = refs[:5]
    vec_ref, wo_own, wo_other, g_ref = refs[5:9]
    (
        normal_out,
        inverse_out,
        first_out,
        active_out,
        slope_out,
        context_out,
        wo_out,
        wi_out,
        arrived_out,
        sems,
    ) = refs[9:]
    c = info[0]
    core = lax.rem(c, 2)
    own = pl.ds(aligned(core * 1536, 512), 1536)
    (copy,) = start_copies([(g_ref, wi_out.at[:, own])], sems)
    for r in range(4):
        group = jnp.bitwise_xor(c, r)
        arrived_out[pl.ds(aligned(group * 128, 128), 128), :] = packs[r][768:896]
        rows = pl.ds(aligned(group * 192, 64), 192)
        for half, ref in ((core, wo_own), (1 - core, wo_other)):
            at = pl.ds(aligned(half * 384, 128), 384)
            wo_out[256 * r : 256 * r + 192, at] = ref[rows, :]
        wo_out[256 * r + 192 : 256 * r + 256, :] = jnp.zeros((64, WIDTH), BF)
        context_out[:, 256 * r : 256 * r + 128] = packs[r][0:512]
        last = wide(packs[r][512:768])
        last = jnp.concatenate([last, pltpu.roll(last, 64, 1)], axis=0)
        context_out[:, 256 * r + 128 : 256 * r + 256] = jnp.where(
            lanes_of(ROWS) < 64, last, 0.0
        ).astype(BF)
    attended = nn(context_out[...], wo_out[...]) + vec_ref[2:3]
    normal, inverse = norm_rows(wide(x_ref[...]) + attended)
    normal_out[...] = normal
    inverse_out[...] = inverse
    first = (normal * vec_ref[3:4] + vec_ref[4:5]).astype(BF)
    first_out[...] = first
    copy.wait()
    hidden_half(core, first, wi_out, vec_ref, active_out, slope_out)


def inner_other_kernel(info, first_ref, vec_ref, g_ref, a_ref, s_ref, w_ref, *refs):
    active_out, slope_out, wi_out, sems = refs
    core = 1 - lax.rem(info[0], 2)
    other = pl.ds(aligned(core * 1536, 512), 1536)
    (copy,) = start_copies([(g_ref, wi_out.at[:, other])], sems)
    copy.wait()
    hidden_half(core, first_ref[...], wi_out, vec_ref, active_out, slope_out)


def outer_kernel(
    info,
    active_ref,
    own_ref,
    other_ref,
    normal_ref,
    vec_ref,
    table_ref,
    arrived_ref,
    residual_out,
    do_out,
    second_out,
    dp_out,
    given_out,
    sums_out,
    w2_out,
    wp_ref,
    sems,
):
    core = lax.rem(info[0], 2)
    copies = start_copies(
        [
            (
                ref.at[pl.ds(96 * f, 96), 768 * t : 768 * t + 768],
                w2_out.at[pl.ds(aligned(384 * f + 192 * half + 96 * t, 32), 96)],
            )
            for f in range(8)
            for half, ref in ((core, own_ref), (1 - core, other_ref))
            for t in range(2)
        ]
        + [(own_ref.at[:, 1536:1664], wp_ref)],
        sems,
    )
    outer = vec_ref[5:6]
    for part in range(2):
        for copy in copies[16 * part : 16 * part + 16]:
            copy.wait()
        at = slice(1536 * part, 1536 * part + 1536)
        outer = outer + nn(active_ref[:, at], w2_out[at, :])
    copies[32].wait()
    first = normal_ref[...] * vec_ref[3:4] + vec_ref[4:5]
    normal, inverse = norm_rows(first + outer)
    second = (normal * vec_ref[6:7] + vec_ref[7:8]).astype(BF)
    second_out[...] = second
    projected = nn(second, wp_ref[...])
    scale = lax.rsqrt(jnp.sum(projected * projected, axis=-1, keepdims=True) + 1e-06)
    normed = projected * scale
    where = lax.broadcasted_iota(jnp.int32, (ROWS, ROWS), 0) + info[0] * ROWS
    table = jnp.concatenate(
        [table_ref[:, pl.ds(aligned(ROWS * d + info[0] * 128, 128), 128)] for d in range(4)],
        axis=1,
    )
    onehot = wide(table == where).astype(BF)
    given_out[...] = tn(onehot, normed.astype(BF)).astype(BF)
    incoming = nn(onehot, arrived_ref[...])
    along = jnp.sum(normed * incoming, axis=-1, keepdims=True)
    delta = (scale * (incoming - normed * along)).astype(BF)
    dp_out[...] = delta
    upstream = nt(delta, wp_ref[...])
    residual = norm_rows_back(upstream, normal, inverse, vec_ref[6:7])
    residual_out[...] = residual
    low = residual.astype(BF)
    do_out[...] = low
    sums_out[...] = jnp.concatenate(
        [
            column_sums(wide(low)),
            column_sums(upstream * normal),
            column_sums(upstream),
            jnp.zeros((5, WIDTH), F32),
        ],
        axis=0,
    )


def hidden_back_kernel(info, do_ref, w2_ref, slope_ref, di_out, side_out):
    for block in range(HIDDEN // 512):
        at = slice(block * 512, block * 512 + 512)
        value = nt(do_ref[...], w2_ref[at, :]) * wide(slope_ref[:, at])
        low = value.astype(BF)
        di_out[:, at] = low
        side_out[:, at] = column_sums(wide(low))


def first_kernel(
    info,
    di_ref,
    wi_ref,
    residual_ref,
    normal_ref,
    inverse_ref,
    vec_ref,
    wo_ref,
    given_ref,
    residual_out,
    da_out,
    sums_out,
    *up_outs,
):
    upstream = residual_ref[...] + nt(di_ref[...], wi_ref[...])
    normal = normal_ref[...]
    residual = norm_rows_back(upstream, normal, inverse_ref[...], vec_ref[3:4])
    residual_out[...] = residual
    low = residual.astype(BF)
    da_out[...] = low
    sums_out[...] = jnp.concatenate(
        [
            column_sums(wide(low)),
            column_sums(upstream * normal),
            column_sums(upstream),
            jnp.zeros((5, WIDTH), F32),
        ],
        axis=0,
    )
    for r in (2, 3, 1, 0):
        out = up_outs[r]
        up = nt(low, wo_ref[256 * r : 256 * r + 256, :])
        out[0:512] = up[:, 0:128].astype(BF)
        last = up[:, 128:256]
        out[512:768] = (last[:256] + pltpu.roll(last[256:], 64, 1)).astype(BF)
        place = jnp.bitwise_xor(info[0], r)
        out[768:896] = given_ref[pl.ds(aligned(place * 128, 128), 128), :]


def spots(info, f):
    mine = info[1]
    my_z, my_y = mine // 2, lax.rem(mine, 2)
    z, y = (f // 2, f % 2) if isinstance(f, int) else (f // 2, lax.rem(f, 2))
    apart = jnp.bitwise_xor(my_z, z)
    return jnp.bitwise_xor(my_y, y), lax.rem(apart, 2), apart // 2


def heads_grad_kernel(info, *refs):
    x_refs, (all_ref, first_ref, outer_ref, side_ref, pack_ref) = refs[:4], refs[4:]
    c = info[0]
    sums = column_sums(wide(all_ref[...]))
    row = lax.broadcasted_iota(jnp.int32, (640, WIDTH), 0)
    lane = lanes_of(640, WIDTH)
    at = lax.broadcasted_iota(jnp.int32, (16, WIDTH), 0)
    rows = [jnp.zeros((2, WIDTH), F32), first_ref[0:3], outer_ref[0:3]]
    for k in range(4):
        starts = [384 * f + 96 * k for f in range(8)]
        rows.append(jnp.concatenate([side_ref[:, i : i + 96] for i in starts], axis=1))
    vectors = jnp.concatenate([*rows, jnp.zeros((4, WIDTH), F32)], axis=0)
    parts = three_parts(sums)
    for kind, first in ((0, 0), (1, 384)):
        chosen = (row - first + 192 * c == lane) & (row >= first) & (row < first + 192)
        chosen = wide(chosen).astype(BF)
        value = sum(nn(jnp.broadcast_to(part, (16, 640)).astype(BF), chosen) for part in parts)
        vectors = jnp.where(at == kind, value, vectors)
    tall = jnp.concatenate(
        [jnp.zeros((64, WIDTH), F32), vectors, jnp.zeros((48, WIDTH), F32)], axis=0
    )
    side = tall.T
    delta = jnp.zeros((WIDTH, 640), F32)
    for r, ref in enumerate(x_refs):
        at = pl.ds(aligned(jnp.bitwise_xor(c, r) * ROWS, ROWS), ROWS)
        delta = delta + tn(ref[...], all_ref[at, :])
    for f in range(8):
        i, j, k = spots(info, f)
        piece = delta[96 * f : 96 * f + 96]
        pack_ref[i, j, k, :, 0:512] = piece[:, :512].astype(BF)
        pack_ref[i, j, k, :, 512:640] = (piece[:, 512:] + side[96 * f : 96 * f + 96]).astype(BF)


def input_grad(info, all_ref, w_ref, residual_ref, own_ref, core_ref, next_ref):
    for r in (1, 3, 2, 0):
        rows = pl.ds(aligned(jnp.bitwise_xor(info[0], r) * ROWS, ROWS), ROWS)
        value = nt(all_ref[rows, :], w_ref[...])
        if r == 0:
            own_ref[...] = residual_ref[...] + value
        elif r == 2:
            next_ref[...] = value
        else:
            core_ref[r // 2] = value.astype(BF)


def finish_kernel(info, near_ref, far_ref, heads_ref, own_ref, came_ref, passed_ref, *refs):
    wi_out, w2_out, wo_out, wp_out, q_out, k_out, v_out, home_out = refs[:8]
    vec_outs = refs[8:17]
    wi_s, w2_s, wo_s, wp_s, q_s, k_s, v_s, home_s, sems = refs[17:]
    for r in range(4):
        ref = far_ref if r % 2 else near_ref
        g = jnp.bitwise_xor(info[0], r)
        a, b = g // 2, lax.rem(g, 2)
        block = wide(ref[r // 2])
        across = pl.ds(aligned(b * 384, 128), 384)
        w2_s[pl.ds(aligned(a * 192, 64), 192), across] = block[0:192]
        for h in range(2):
            at = pl.ds(aligned(g * 768 + 384 * h, 128), 384)
            wi_s[:, at] = block[208 + 96 * h : 304 + 96 * h]
        wo_s[pl.ds(aligned(a * 48, 16), 48), across] = block[400:448]
        for t in range(3):
            at = pl.ds(aligned(24 * g + 8 * t, 8), 8)
            wp_s[at, :] = block[192:200, 128 * t : 128 * t + 128]
    copies = start_copies(
        [(wi_s, wi_out), (w2_s, w2_out), (wo_s, wo_out), (wp_s, wp_out)], sems
    )
    home_s[...] = (own_ref[...] + wide(came_ref[0]) + wide(passed_ref[...])).astype(BF)
    for kind, ref in enumerate((q_s, k_s, v_s)):
        parts = [wide(heads_ref[g, :, 192 * kind : 192 * kind + 192]) for g in range(4)]
        ref[...] = jnp.concatenate(parts, axis=1)
    for i, pair in enumerate(((q_s, q_out), (k_s, k_out), (v_s, v_out), (home_s, home_out))):
        copy = pltpu.make_async_copy(*pair, sems.at[4 + i])
        copy.start()
        copies.append(copy)
    side = sum(wide(heads_ref[g, :, 512:640]) for g in range(4))
    tall = jnp.concatenate([side, jnp.zeros((32, 128), F32)], axis=0).T
    for i in range(8):
        vec_outs[i][...] = tall[64 + i : 65 + i, :96]
    last = jnp.concatenate([tall[72 + i : 73 + i, :96] for i in range(4)], axis=1)
    vec_outs[8][...] = last.reshape(384)
    for copy in copies:
        copy.wait()


def pair_index(info, keep, x, yr):
    xr = jnp.bitwise_xor(info[0] // 2, x)
    order = jnp.bitwise_xor(lax.rem(info[0], 2), keep)
    first = jnp.where(order == 0, xr, yr)
    second = jnp.where(order == 0, yr, xr)
    return first, second


def outer_pack_kernel(info, active_ref, do_ref, second_ref, dp_ref, keep_ref, send_ref, proj_s):
    core = lax.rem(info[0], 2)
    proj_s[...] = tn(second_ref[...], dp_ref[...])
    for f in range(8):
        yr, z0, z1 = spots(info, f)
        left = active_ref[:, 384 * f : 384 * f + 384]
        for k, ref in ((0, keep_ref), (1, send_ref)):
            half = jnp.bitwise_xor(core, k)
            right = do_ref[:, pl.ds(aligned(half * 384, 128), 384)]
            value = tn(left, right).astype(BF)
            for x in range(2):
                a, b = pair_index(info, k, x, yr)
                ref[a, b, z0, z1, 0:192, :] = value[192 * x : 192 * x + 192]
                start = 96 * f + 24 * (2 * x + half)
                across = jnp.concatenate(
                    [proj_s[pl.ds(aligned(start + 8 * g, 8), 8), :] for g in range(3)], axis=1
                )
                ref[a, b, z0, z1, 192:208, :] = jnp.concatenate(
                    [across, jnp.zeros((8, 384), F32)], axis=0
                ).astype(BF)


def inner_pack_kernel(info, first_ref, di_ref, keep_ref, send_ref):
    core = lax.rem(info[0], 2)
    for k, ref in ((0, keep_ref), (1, send_ref)):
        half = jnp.bitwise_xor(core, k)
        for x in range(2):
            for part in range(2):
                start = (2 * x + half) * 768 + 384 * part
                right = di_ref[:, pl.ds(aligned(start, 128), 384)]
                value = tn(first_ref[...], right).astype(BF)
                for f in range(8):
                    yr, z0, z1 = spots(info, f)
                    a, b = pair_index(info, k, x, yr)
                    ref[a, b, z0, z1, 96 * part : 96 * part + 96, :] = value[96 * f : 96 * f + 96]


def output_pack_kernel(info, context_ref, da_ref, keep_ref, send_ref):
    c = info[0]
    for k, ref in ((0, keep_ref), (1, send_ref)):
        half = jnp.bitwise_xor(lax.rem(c, 2), k)
        right = da_ref[:, pl.ds(aligned(half * 384, 128), 384)]
        for r in range(4):
            value = tn(context_ref[:, 256 * r : 256 * r + 256], right).astype(BF)
            for t in range(2):
                yr, z0, z1 = spots(info, 2 * jnp.bitwise_xor(c, r) + t)
                for x in range(2):
                    a, b = pair_index(info, k, x, yr)
                    start = 96 * t + 48 * x
                    ref[a, b, z0, z1] = value[start : start + 48]


def fast_device(
    tokens,
    dealt,
    segments,
    query_weight,
    key_weight,
    value_weight,
    query_bias,
    value_bias,
    output_weight,
    output_bias,
    first_gain,
    first_shift,
    inner_weight,
    inner_bias,
    outer_weight,
    outer_bias,
    second_gain,
    second_shift,
    project_weight,
    cotangent,
):
    c = lax.axis_index("ctx")
    f = lax.axis_index("fsdp")
    core = lax.rem(c, 2)
    total = segments.shape[1]
    x = tokens[0]

    place = jnp.stack([c, f, c * 0, c * 0]).astype(jnp.int32)
    (info,) = run(
        places_kernel, "places", place, [segments], [((24,), jnp.int32)], small=True
    )

    vectors = (
        query_bias,
        value_bias,
        output_bias,
        first_gain,
        first_shift,
        outer_bias,
        second_gain,
        second_shift,
    )
    (heads_pack,) = run(
        prepare_heads_kernel,
        "prepare_heads",
        place,
        [query_weight, key_weight, value_weight]
        + [vector.reshape(1, 96) for vector in vectors]
        + [inner_bias.reshape(4, 96)],
        [((96, 640), BF)],
        [pltpu.VMEM(query_weight.shape, BF)] * 3
        + [pltpu.VMEM((1, 96), BF)] * 8
        + [pltpu.SemaphoreType.DMA((11,))],
        limit=60,
        loose=range(11),
    )
    outer_pack, inner_pack = run(
        prepare_forward_kernel,
        "prepare_forward",
        after(place, heads_pack),
        [inner_weight, output_weight, outer_weight, project_weight],
        [((96, 1664), BF), ((96, 1920), BF)],
        [pltpu.SemaphoreType.DMA((5,))],
        limit=60,
        loose=range(4),
    )
    x_core = to_core(x)
    x_next = to_x(x)
    moved = [along_z(heads_pack, k) for k in range(1, 4)]
    moved_y = [to_fsdp(heads_pack, 1)]
    x_core, x_next, heads_pack, inner_pack, outer_pack, info, moved_y[0], *moved = together(
        x_core, x_next, heads_pack, inner_pack, outer_pack, info, moved_y[0], *moved
    )
    x_cross = to_core(x_next)
    inner_pack, moved, x_cross = together(inner_pack, moved, x_cross)
    moved_y += [to_fsdp(piece, 1) for piece in moved]
    inner_1, inner_3 = along_z(inner_pack, 1), along_z(inner_pack, 3)
    x_cross, inner_pack, outer_pack, *moved_y = together(
        x_cross, inner_pack, outer_pack, *moved_y
    )
    pieces = []
    for one, two in zip((heads_pack, *moved), moved_y):
        pieces += [one, two]
    inner_2 = along_z(inner_pack, 2)
    inner_0y, outer_0y = to_fsdp(inner_pack, 1), to_fsdp(outer_pack, 1)

    heads = (LOCAL, total, 128)
    q, k, v, kt, vt, heads_weight, vec = run(
        project_kernel,
        "project",
        info,
        [x, x_core, x_next, after(x_cross, inner_pack), *pieces, segments],
        [
            (heads, BF),
            (heads, BF),
            (heads, BF),
            ((LOCAL, 64, total), BF),
            ((LOCAL, 80, total), BF),
            ((WIDTH, 640), BF),
            ((16, WIDTH), F32),
        ],
        [pltpu.SemaphoreType.DMA((8,))],
        limit=8,
        loose=range(4, 12),
    )
    q, inner_1, inner_3, inner_0y, outer_0y, outer_pack = together(
        q, inner_1, inner_3, inner_0y, outer_0y, outer_pack
    )
    inner_1y = to_fsdp(inner_1, 1)
    o_2, ql_2, pack_2, o_3, ql_3, pack_3 = attend_rows(
        info, after(q, inner_1), k, vt, cotangent[0], 1
    )
    pack_2, pack_3, inner_2, inner_1y, outer_pack, q = together(
        pack_2, pack_3, inner_2, inner_1y, outer_pack, q
    )
    inner_2y, inner_3y = to_fsdp(inner_2, 1), to_fsdp(after(inner_3, inner_2), 1)
    outer_1, outer_3, outer_2 = [along_z(outer_pack, k) for k in (1, 3, 2)]
    o_0, ql_0, pack_0, o_1, ql_1, pack_1 = attend_rows(info, q, k, vt, cotangent[0], 0)
    pack_0, pack_1, pack_2, pack_3, inner_2y, inner_3y, outer_1, outer_3 = together(
        pack_0, pack_1, pack_2, pack_3, inner_2y, inner_3y, outer_1, outer_3
    )
    from_x, from_cross = to_x(pack_2), to_cross(pack_3)
    outer_1y = to_fsdp(outer_1, 1)
    inner_half, output_own = lay(
        info,
        [inner_pack, inner_0y, inner_1, inner_1y, inner_2, inner_2y, inner_3, inner_3y],
        (1536, 384),
    )
    from_x, from_cross, inner_half, output_own, pack_1, outer_1y, outer_2, outer_3 = together(
        from_x, from_cross, inner_half, output_own, pack_1, outer_1y, outer_2, outer_3
    )
    from_core = to_core(pack_1)
    output_other = to_core(output_own)
    outer_2y, outer_3y = to_fsdp(outer_2, 1), to_fsdp(outer_3, 1)
    from_core, output_other = together(from_core, output_other)
    inner_other = to_core(after(inner_half, from_core))
    (
        normal,
        inverse,
        first_low,
        active,
        slope,
        context,
        output_full,
        inner_full,
        arrived,
    ) = run(
        inner_own_kernel,
        "inner_own",
        info,
        [
            x,
            pack_0,
            from_core,
            from_x,
            from_cross,
            vec,
            output_own,
            output_other,
            inner_half,
        ],
        [
            ((ROWS, WIDTH), F32),
            ((ROWS, 1), F32),
            ((ROWS, WIDTH), BF),
            ((ROWS, HIDDEN), BF),
            ((ROWS, HIDDEN), BF),
            ((ROWS, 1024), BF),
            ((1024, WIDTH), BF),
            ((WIDTH, HIDDEN), BF),
            ((ROWS, 128), BF),
        ],
        [pltpu.SemaphoreType.DMA((1,))],
        loose=(8,),
    )
    first_low, inner_other, outer_2y, outer_3y = together(
        first_low, inner_other, outer_2y, outer_3y
    )
    (outer_own,) = lay(
        info,
        [outer_pack, outer_0y, outer_1, outer_1y, outer_2, outer_2y, outer_3, outer_3y],
        (1664,),
    )
    outer_other = to_core(outer_own)
    active, slope, inner_full = run(
        inner_other_kernel,
        "inner_other",
        info,
        [after(first_low, outer_own), vec, inner_other, active, slope, inner_full],
        [((ROWS, HIDDEN), BF), ((ROWS, HIDDEN), BF), ((WIDTH, HIDDEN), BF)],
        [pltpu.SemaphoreType.DMA((1,))],
        loose=(2,),
        alias=((3, 0), (4, 1), (5, 2)),
    )
    residual_two, delta_outer, second_low, delta_projected, given, outer_sums, outer_full = run(
        outer_kernel,
        "outer",
        info,
        [active, outer_own, outer_other, normal, vec, dealt, arrived],
        [
            ((ROWS, WIDTH), F32),
            ((ROWS, WIDTH), BF),
            ((ROWS, WIDTH), BF),
            ((ROWS, 128), BF),
            ((ROWS, 128), BF),
            ((8, WIDTH), F32),
            ((HIDDEN, WIDTH), BF),
        ],
        [pltpu.VMEM((WIDTH, 128), BF), pltpu.SemaphoreType.DMA((33,))],
        loose=(1, 2),
    )
    keep_o, send_o = run(
        outer_pack_kernel,
        "outer_pack",
        info,
        [active, delta_outer, second_low, delta_projected],
        [((2, 2, 2, 2, 208, 384), BF)] * 2,
        [pltpu.VMEM((WIDTH, 128), F32)],
    )
    core_o = to_core(send_o)
    delta_inner, inner_side = run(
        hidden_back_kernel,
        "hidden_back",
        info,
        [after(delta_outer, send_o), outer_full, slope],
        [((ROWS, HIDDEN), BF), ((1, HIDDEN), F32)],
    )
    keep_i, send_i = run(
        inner_pack_kernel,
        "inner_pack",
        info,
        [first_low, delta_inner],
        [((2, 2, 2, 2, 192, 384), BF)] * 2,
    )
    core_o, delta_inner, inner_side, keep_i, send_i = together(
        core_o, delta_inner, inner_side, keep_i, send_i
    )

    core_i = to_core(send_i)
    give_o = added([keep_o[1], core_o[1]])
    one_o = to_mixed(give_o, True)
    residual_one, delta_attended, first_sums, *ups = run(
        first_kernel,
        "first",
        info,
        [
            after(delta_inner, give_o),
            inner_full,
            residual_two,
            normal,
            inverse,
            vec,
            output_full,
            given,
        ],
        [((ROWS, WIDTH), F32), ((ROWS, WIDTH), BF), ((8, WIDTH), F32)] + [((896, 128), BF)] * 4,
    )
    core_i, delta_attended, up_0, *ups = together(core_i, delta_attended, *ups)
    ups = [to_core(ups[0]), to_x(ups[1]), to_cross(ups[2])]
    keep_w, send_w = run(
        output_pack_kernel,
        "output_pack",
        info,
        [context, delta_attended],
        [((2, 2, 2, 2, 48, 384), BF)] * 2,
    )
    core_w = to_core(send_w)
    keys = (k, kt, v)
    dq_0, dk, dv = attend_back(info, 0, after(ql_0, send_w), up_0, o_0, *keys)
    dq_1, dk, dv = attend_back(info, 1, ql_1, ups[0], o_1, *keys, (dk, dv))
    one_o, core_w, dq_0, dq_1, dk, dv, *ups = together(one_o, core_w, dq_0, dq_1, dk, dv, *ups)

    give_i = jnp.concatenate([added([keep_i[1], core_i[1]]), added([keep_w[1], core_w[1]])], axis=3)
    one_i = to_mixed(give_i, True)
    give_o = added([keep_o[0, 1], core_o[0, 1], one_o[1]])
    two_o = to_mixed(give_o, False)
    dq_2, dk, dv = attend_back(
        info, 2, after(ql_2, give_i, give_o), ups[1], o_2, *keys, (dk, dv)
    )
    delta_heads, embedded, own, for_core, for_next, _, _ = attend_back(
        info,
        3,
        ql_3,
        ups[2],
        o_3,
        *keys,
        (dk, dv),
        (dq_0, dq_1, dq_2, up_0, *ups[:2], heads_weight, residual_one),
    )
    one_i, two_o, delta_heads, embedded, own, for_core, for_next = together(
        one_i, two_o, delta_heads, embedded, own, for_core, for_next
    )

    came = to_core(for_core)
    sum_i = [keep_i[0, 1], core_i[0, 1]], [keep_w[0, 1], core_w[0, 1]]
    give_i = added([jnp.concatenate(parts, axis=2) for parts in zip(*sum_i)] + [one_i[1]])
    two_i = to_mixed(give_i, False)
    sum_o = [keep_o[0, 0], core_o[0, 0], one_o[0], two_o]
    give_o = added([part[1] for part in sum_o])
    three_o = to_fsdp(give_o, 2)
    (pack,) = run(
        heads_grad_kernel,
        "heads_grad",
        info,
        [
            x,
            x_core,
            x_next,
            x_cross,
            after(delta_heads, give_i, give_o),
            first_sums,
            outer_sums,
            inner_side,
        ],
        [((2, 2, 2, 96, 640), BF)],
        limit=8,
    )
    two_i, three_o, pack, came = together(two_i, three_o, pack, came)

    one_h = to_fsdp(pack[1], 1)
    sum_i = [keep_i[0, 0], core_i[0, 0]], [keep_w[0, 0], core_w[0, 0]]
    sum_i = [jnp.concatenate(parts, axis=2) for parts in zip(*sum_i)] + [one_i[0], two_i]
    give_i = added([part[1] for part in sum_i])
    three_i = to_fsdp(give_i, 2)
    sum_o = [*(part[0] for part in sum_o), three_o]
    give_o = added([part[1] for part in sum_o])
    four_o = to_fsdp(give_o, 4)
    give_x = (for_next + wide(came[1])).astype(BF)
    passed = to_x(give_x)
    one_h, three_i, four_o = together(one_h, three_i, four_o)

    sum_i = [*(part[0] for part in sum_i), three_i]
    give_i = added([part[1] for part in sum_i])
    four_i = to_fsdp(give_i, 4)
    give_h = added([pack[0, 1], one_h[1]])
    two_h = to_fsdp(give_h, 2)
    four_i, two_h = together(four_i, two_h)

    give_h = added([pack[0, 0, 1], one_h[0, 1], two_h[1]])
    three_h = to_fsdp(give_h, 4)
    forward_sum = jnp.concatenate(
        [
            added([*(part[0] for part in sum_o), four_o]),
            added([*(part[0] for part in sum_i), four_i]),
        ],
        axis=0,
    )
    forward_next = to_x(forward_sum)
    three_h, passed, forward_next = together(three_h, passed, forward_next)
    mine = added([pack[0, 0, 0], one_h[0, 0], two_h[0], three_h])
    near = jnp.stack([forward_sum, forward_next])
    far = to_core(near)
    heads_all = lax.all_gather(after(mine, near), "ctx")
    square = (96, WIDTH)
    shapes = [
        ((96, HIDDEN), F32),
        ((384, WIDTH), F32),
        (square, F32),
        ((96, 128), F32),
        (square, F32),
        (square, F32),
        (square, F32),
        ((ROWS, WIDTH), BF),
    ]
    (
        inner_grad,
        outer_grad,
        output_grad,
        project_grad,
        query_grad,
        key_grad,
        value_grad,
        delta_home,
        *vec_all,
    ) = run(
        finish_kernel,
        "finish",
        info,
        [near, far, heads_all, own, came, passed],
        shapes + [((1, 96), F32)] * 8 + [((384,), F32)],
        [pltpu.VMEM(*shape) for shape in shapes] + [pltpu.SemaphoreType.DMA((8,))],
        limit=20,
        loose_outs=range(8),
    )
    return (
        embedded[None],
        delta_home[None],
        query_grad,
        key_grad,
        value_grad,
        vec_all[0].reshape(96),
        vec_all[1].reshape(96),
        output_grad,
        vec_all[2].reshape(96),
        vec_all[3].reshape(96),
        vec_all[4].reshape(96),
        inner_grad,
        vec_all[8],
        outer_grad,
        vec_all[5].reshape(96),
        vec_all[6].reshape(96),
        vec_all[7].reshape(96),
        project_grad,
    )


def suits(mesh):
    return mesh.shape["ctx"] == 4 and mesh.shape["fsdp"] == 8


def solution(mesh):
    on_device = fast_device if suits(mesh) else generic_device

    return jax.shard_map(
        on_device,
        mesh=mesh,
        in_specs=(
            P("fsdp", "ctx", None),
            P("fsdp", None),
            P("fsdp", None),
            P("fsdp", None),
            P("fsdp", None),
            P("fsdp", None),
            P("fsdp"),
            P("fsdp"),
            P("fsdp", None),
            P("fsdp"),
            P("fsdp"),
            P("fsdp"),
            P("fsdp", None),
            P("fsdp"),
            P("fsdp", None),
            P("fsdp"),
            P("fsdp"),
            P("fsdp"),
            P("fsdp", None),
            P("fsdp", "ctx", None),
        ),
        out_specs=(
            P("fsdp", "ctx", None),
            P("fsdp", "ctx", None),
            P("fsdp", None),
            P("fsdp", None),
            P("fsdp", None),
            P("fsdp"),
            P("fsdp"),
            P("fsdp", None),
            P("fsdp"),
            P("fsdp"),
            P("fsdp"),
            P("fsdp", None),
            P("fsdp"),
            P("fsdp", None),
            P("fsdp"),
            P("fsdp"),
            P("fsdp"),
            P("fsdp", None),
        ),
        check_vma=False,
    )
```

```python
import functools

import jax
import jax.numpy as jnp
from jax import lax
from jax.experimental import pallas as pl
from jax.experimental.pallas import tpu as pltpu
from jax.sharding import PartitionSpec as P

HEADS = 12
HEAD_DIM = 64


def matmul(left, right):
    return jnp.dot(left, right, preferred_element_type=jnp.float32)


def norm_forward(value, gain, shift):
    centred = value - jnp.mean(value, axis=-1, keepdims=True)
    inverse = lax.rsqrt(jnp.mean(centred * centred, axis=-1, keepdims=True) + 1e-12)
    normal = centred * inverse
    return (normal * gain + shift, normal, inverse)


def norm_backward(upstream, normal, inverse, gain):
    scaled = upstream * gain
    first_mean = jnp.mean(scaled, axis=-1, keepdims=True)
    second_mean = jnp.mean(scaled * normal, axis=-1, keepdims=True)
    inward = inverse * (scaled - first_mean - normal * second_mean)
    return (inward, jnp.sum(upstream * normal, axis=0), jnp.sum(upstream, axis=0))


def gelu_slope(value):
    cumulative = 0.5 * (1.0 + jax.scipy.special.erf(value * 0.7071067811865476))
    return cumulative + value * jnp.exp(-0.5 * value * value) * 0.3989422804014327


def scored(query_heads, key_block, query_segments, segment_block, scale):
    scores = (
        jnp.einsum("qhd,khd->hqk", query_heads, key_block, preferred_element_type=jnp.float32)
        * scale
    )
    allowed = (query_segments[:, None] == segment_block[None, :])[None]
    return (scores, allowed)


def probabilities(scores, allowed, log_total):
    return jnp.where(allowed, jnp.exp(scores - log_total[..., None]), 0.0)


def log_totals(query_heads, key_blocks, query_segments, segment_blocks, scale):

    def log_advance(carry, pieces):
        running_max, running_sum = carry
        scores, allowed = scored(query_heads, pieces[0], query_segments, pieces[1], scale)
        masked = jnp.where(allowed, scores, -1e30)
        new_max = jnp.maximum(running_max, jnp.max(masked, axis=-1))
        fresh = jnp.sum(jnp.where(allowed, jnp.exp(masked - new_max[..., None]), 0.0), axis=-1)
        return ((new_max, running_sum * jnp.exp(running_max - new_max) + fresh), None)

    shape = (query_heads.shape[1], query_heads.shape[0])
    start = (jnp.full(shape, -1e30, jnp.float32), jnp.zeros(shape, jnp.float32))
    final = lax.scan(log_advance, start, (key_blocks, segment_blocks))[0]
    return final[0] + jnp.log(final[1])


def attend(query_heads, key_blocks, value_blocks, query_segments, segment_blocks, scale):
    log_total = log_totals(query_heads, key_blocks, query_segments, segment_blocks, scale)

    def attend_advance(carry, pieces):
        scores, allowed = scored(query_heads, pieces[0], query_segments, pieces[2], scale)
        probs = probabilities(scores, allowed, log_total).astype(jnp.bfloat16)
        return (
            carry
            + jnp.einsum("hqk,khd->qhd", probs, pieces[1], preferred_element_type=jnp.float32),
            None,
        )

    start = jnp.zeros(query_heads.shape, jnp.float32)
    mixed = lax.scan(attend_advance, start, (key_blocks, value_blocks, segment_blocks))[0]
    return (mixed, log_total)


def attend_backward(
    query_heads,
    key_blocks,
    value_blocks,
    query_segments,
    segment_blocks,
    scale,
    log_total,
    upstream,
):

    def first_pass(carry, pieces):
        scores, allowed = scored(query_heads, pieces[0], query_segments, pieces[2], scale)
        probs = probabilities(scores, allowed, log_total)
        delta_probs = jnp.einsum(
            "qhd,khd->hqk", upstream, pieces[1], preferred_element_type=jnp.float32
        )
        value_terms = jnp.einsum(
            "hqk,qhd->khd", probs.astype(jnp.bfloat16), upstream, preferred_element_type=jnp.float32
        )
        return (carry + jnp.sum(probs * delta_probs, axis=-1), value_terms)

    shape = (query_heads.shape[1], query_heads.shape[0])
    weighted, value_terms = lax.scan(
        first_pass, jnp.zeros(shape, jnp.float32), (key_blocks, value_blocks, segment_blocks)
    )

    def second_pass(carry, pieces):
        scores, allowed = scored(query_heads, pieces[0], query_segments, pieces[2], scale)
        probs = probabilities(scores, allowed, log_total)
        delta_probs = jnp.einsum(
            "qhd,khd->hqk", upstream, pieces[1], preferred_element_type=jnp.float32
        )
        delta_scores = (probs * (delta_probs - weighted[..., None])).astype(jnp.bfloat16)
        key_terms = jnp.einsum(
            "hqk,qhd->khd", delta_scores, query_heads, preferred_element_type=jnp.float32
        )
        return (
            carry
            + jnp.einsum(
                "hqk,khd->qhd", delta_scores, pieces[0], preferred_element_type=jnp.float32
            ),
            key_terms,
        )

    query_terms, key_terms = lax.scan(
        second_pass,
        jnp.zeros(query_heads.shape, jnp.float32),
        (key_blocks, value_blocks, segment_blocks),
    )
    return (query_terms * scale, key_terms * scale, value_terms)


def generic_device(
    tokens,
    dealt,
    segments,
    query_weight,
    key_weight,
    value_weight,
    query_bias,
    value_bias,
    output_weight,
    output_bias,
    first_gain,
    first_shift,
    inner_weight,
    inner_bias,
    outer_weight,
    outer_bias,
    second_gain,
    second_shift,
    project_weight,
    cotangent,
):
    peers = lax.axis_size("ctx")
    place = lax.axis_index("ctx")
    local_rows = tokens.shape[1]
    share = local_rows // peers
    order = dealt[0]
    table = (
        lax.dynamic_index_in_dim(order.reshape(peers, peers, share), place, 1, keepdims=False)
        - place * local_rows
    )
    flat_table = table.reshape(-1)
    home_tokens = tokens[0]
    width = home_tokens.shape[1]
    (
        query_full,
        key_full,
        value_full,
        output_full,
        query_shift,
        value_shift,
        output_shift,
        gain_one,
        shift_one,
    ) = (
        lax.all_gather(query_weight, "fsdp", axis=0, tiled=True),
        lax.all_gather(key_weight, "fsdp", axis=0, tiled=True),
        lax.all_gather(value_weight, "fsdp", axis=0, tiled=True),
        lax.all_gather(output_weight, "fsdp", axis=0, tiled=True),
        lax.all_gather(query_bias, "fsdp", axis=0, tiled=True),
        lax.all_gather(value_bias, "fsdp", axis=0, tiled=True),
        lax.all_gather(output_bias, "fsdp", axis=0, tiled=True),
        lax.all_gather(first_gain, "fsdp", axis=0, tiled=True),
        lax.all_gather(first_shift, "fsdp", axis=0, tiled=True),
    )
    outgoing = jnp.take(home_tokens, table, axis=0)
    here_tokens = lax.all_to_all(outgoing, "ctx", split_axis=0, concat_axis=0, tiled=True).reshape(
        local_rows, width
    )
    key_segments = jnp.take(segments[0], order, axis=0)
    query_segments = lax.dynamic_slice_in_dim(key_segments, place * local_rows, local_rows)
    queries = (matmul(here_tokens, query_full) + query_shift.astype(jnp.float32)).astype(
        jnp.bfloat16
    )
    own_keys = matmul(here_tokens, key_full).astype(jnp.bfloat16)
    own_values = (matmul(here_tokens, value_full) + value_shift.astype(jnp.float32)).astype(
        jnp.bfloat16
    )
    all_keys, all_values = (
        lax.all_gather(own_keys, "ctx", axis=0, tiled=True),
        lax.all_gather(own_values, "ctx", axis=0, tiled=True),
    )
    total = all_keys.shape[0]
    block = min(1024, total)
    count = total // block
    scale = HEAD_DIM ** (-0.5)
    query_heads = queries.reshape(local_rows, HEADS, HEAD_DIM)
    key_blocks = all_keys.reshape(count, block, HEADS, HEAD_DIM)
    value_blocks = all_values.reshape(count, block, HEADS, HEAD_DIM)
    segment_blocks = key_segments.reshape(count, block)
    mixed, log_total = attend(
        query_heads, key_blocks, value_blocks, query_segments, segment_blocks, scale
    )
    context = mixed.reshape(local_rows, width).astype(jnp.bfloat16)
    inner_full, inner_shift, outer_full, outer_shift, gain_two, shift_two, project_full = (
        lax.all_gather(inner_weight, "fsdp", axis=0, tiled=True),
        lax.all_gather(inner_bias, "fsdp", axis=0, tiled=True),
        lax.all_gather(outer_weight, "fsdp", axis=0, tiled=True),
        lax.all_gather(outer_bias, "fsdp", axis=0, tiled=True),
        lax.all_gather(second_gain, "fsdp", axis=0, tiled=True),
        lax.all_gather(second_shift, "fsdp", axis=0, tiled=True),
        lax.all_gather(project_weight, "fsdp", axis=0, tiled=True),
    )
    attended = matmul(context, output_full) + output_shift.astype(jnp.float32)
    first, first_normal, first_inverse = norm_forward(
        here_tokens.astype(jnp.float32) + attended,
        gain_one.astype(jnp.float32),
        shift_one.astype(jnp.float32),
    )
    first_low = first.astype(jnp.bfloat16)
    inner = matmul(first_low, inner_full) + inner_shift.astype(jnp.float32)
    active = jax.nn.gelu(inner, approximate=False).astype(jnp.bfloat16)
    outer = matmul(active, outer_full) + outer_shift.astype(jnp.float32)
    second, second_normal, second_inverse = norm_forward(
        first + outer, gain_two.astype(jnp.float32), shift_two.astype(jnp.float32)
    )
    second_low = second.astype(jnp.bfloat16)
    projected = matmul(second_low, project_full)
    inverse_length = lax.rsqrt(jnp.sum(projected * projected, axis=-1, keepdims=True) + 1e-06)
    normed = projected * inverse_length
    embedded = normed.astype(jnp.bfloat16)
    incoming = cotangent[0].astype(jnp.float32)
    along = jnp.sum(normed * incoming, axis=-1, keepdims=True)
    delta_projected = (inverse_length * (incoming - normed * along)).astype(jnp.bfloat16)
    project_delta = matmul(second_low.T, delta_projected)
    delta_second = matmul(delta_projected, project_full.T)
    residual_two, second_gain_delta, second_shift_delta = norm_backward(
        delta_second, second_normal, second_inverse, gain_two.astype(jnp.float32)
    )
    delta_outer = residual_two.astype(jnp.bfloat16)
    outer_bias_delta = jnp.sum(delta_outer, axis=0, dtype=jnp.float32)
    outer_delta = matmul(active.T, delta_outer)
    delta_active = matmul(delta_outer, outer_full.T)
    delta_inner = (delta_active * gelu_slope(inner)).astype(jnp.bfloat16)
    inner_bias_delta = jnp.sum(delta_inner, axis=0, dtype=jnp.float32)
    inner_delta = matmul(first_low.T, delta_inner)
    delta_first = residual_two + matmul(delta_inner, inner_full.T)
    residual_one, first_gain_delta, first_shift_delta = norm_backward(
        delta_first, first_normal, first_inverse, gain_one.astype(jnp.float32)
    )
    delta_attended = residual_one.astype(jnp.bfloat16)
    output_bias_delta = jnp.sum(delta_attended, axis=0, dtype=jnp.float32)
    output_delta = matmul(context.T, delta_attended)
    delta_context = matmul(delta_attended, output_full.T).astype(jnp.bfloat16)
    upstream = delta_context.reshape(local_rows, HEADS, HEAD_DIM)
    query_terms, key_terms, value_terms = attend_backward(
        query_heads,
        key_blocks,
        value_blocks,
        query_segments,
        segment_blocks,
        scale,
        log_total,
        upstream,
    )
    key_sums, value_sums = (
        lax.psum_scatter(
            key_terms.reshape(total, width).astype(jnp.bfloat16),
            "ctx",
            scatter_dimension=0,
            tiled=True,
        ).astype(jnp.float32),
        lax.psum_scatter(
            value_terms.reshape(total, width).astype(jnp.bfloat16),
            "ctx",
            scatter_dimension=0,
            tiled=True,
        ).astype(jnp.float32),
    )
    delta_keys = key_sums.astype(jnp.bfloat16)
    delta_values = value_sums.astype(jnp.bfloat16)
    delta_queries = query_terms.reshape(local_rows, width).astype(jnp.bfloat16)
    query_bias_delta = jnp.sum(delta_queries, axis=0, dtype=jnp.float32)
    value_bias_delta = jnp.sum(delta_values, axis=0, dtype=jnp.float32)
    query_delta = matmul(here_tokens.T, delta_queries)
    key_delta = matmul(here_tokens.T, delta_keys)
    value_delta = matmul(here_tokens.T, delta_values)
    delta_here = (
        residual_one
        + matmul(delta_queries, query_full.T)
        + matmul(delta_keys, key_full.T)
        + matmul(delta_values, value_full.T)
    ).astype(jnp.bfloat16)
    coming_home = lax.all_to_all(
        delta_here.reshape(peers, share, width), "ctx", split_axis=0, concat_axis=0, tiled=True
    )
    delta_home = (
        jnp.zeros((local_rows, width), jnp.bfloat16)
        .at[flat_table]
        .set(coming_home.reshape(local_rows, width))
    )
    (
        inner_part,
        inner_bias_part,
        outer_part,
        outer_bias_part,
        second_gain_part,
        second_shift_part,
        project_part,
    ) = (
        lax.psum_scatter(
            inner_delta.astype(jnp.bfloat16), "fsdp", scatter_dimension=0, tiled=True
        ).astype(jnp.float32),
        lax.psum_scatter(
            inner_bias_delta.astype(jnp.bfloat16), "fsdp", scatter_dimension=0, tiled=True
        ).astype(jnp.float32),
        lax.psum_scatter(
            outer_delta.astype(jnp.bfloat16), "fsdp", scatter_dimension=0, tiled=True
        ).astype(jnp.float32),
        lax.psum_scatter(
            outer_bias_delta.astype(jnp.bfloat16), "fsdp", scatter_dimension=0, tiled=True
        ).astype(jnp.float32),
        lax.psum_scatter(
            second_gain_delta.astype(jnp.bfloat16), "fsdp", scatter_dimension=0, tiled=True
        ).astype(jnp.float32),
        lax.psum_scatter(
            second_shift_delta.astype(jnp.bfloat16), "fsdp", scatter_dimension=0, tiled=True
        ).astype(jnp.float32),
        lax.psum_scatter(
            project_delta.astype(jnp.bfloat16), "fsdp", scatter_dimension=0, tiled=True
        ).astype(jnp.float32),
    )
    (
        query_part,
        key_part,
        value_part,
        query_bias_part,
        value_bias_part,
        output_part,
        output_bias_part,
        first_gain_part,
        first_shift_part,
    ) = (
        lax.psum_scatter(
            query_delta.astype(jnp.bfloat16), "fsdp", scatter_dimension=0, tiled=True
        ).astype(jnp.float32),
        lax.psum_scatter(
            key_delta.astype(jnp.bfloat16), "fsdp", scatter_dimension=0, tiled=True
        ).astype(jnp.float32),
        lax.psum_scatter(
            value_delta.astype(jnp.bfloat16), "fsdp", scatter_dimension=0, tiled=True
        ).astype(jnp.float32),
        lax.psum_scatter(
            query_bias_delta.astype(jnp.bfloat16), "fsdp", scatter_dimension=0, tiled=True
        ).astype(jnp.float32),
        lax.psum_scatter(
            value_bias_delta.astype(jnp.bfloat16), "fsdp", scatter_dimension=0, tiled=True
        ).astype(jnp.float32),
        lax.psum_scatter(
            output_delta.astype(jnp.bfloat16), "fsdp", scatter_dimension=0, tiled=True
        ).astype(jnp.float32),
        lax.psum_scatter(
            output_bias_delta.astype(jnp.bfloat16), "fsdp", scatter_dimension=0, tiled=True
        ).astype(jnp.float32),
        lax.psum_scatter(
            first_gain_delta.astype(jnp.bfloat16), "fsdp", scatter_dimension=0, tiled=True
        ).astype(jnp.float32),
        lax.psum_scatter(
            first_shift_delta.astype(jnp.bfloat16), "fsdp", scatter_dimension=0, tiled=True
        ).astype(jnp.float32),
    )
    results = (
        lax.psum(query_part.astype(jnp.bfloat16), "ctx").astype(jnp.float32),
        lax.psum(key_part.astype(jnp.bfloat16), "ctx").astype(jnp.float32),
        lax.psum(value_part.astype(jnp.bfloat16), "ctx").astype(jnp.float32),
        lax.psum(query_bias_part.astype(jnp.bfloat16), "ctx").astype(jnp.float32),
        lax.psum(value_bias_part.astype(jnp.bfloat16), "ctx").astype(jnp.float32),
        lax.psum(output_part.astype(jnp.bfloat16), "ctx").astype(jnp.float32),
        lax.psum(output_bias_part.astype(jnp.bfloat16), "ctx").astype(jnp.float32),
        lax.psum(first_gain_part.astype(jnp.bfloat16), "ctx").astype(jnp.float32),
        lax.psum(first_shift_part.astype(jnp.bfloat16), "ctx").astype(jnp.float32),
        lax.psum(inner_part.astype(jnp.bfloat16), "ctx").astype(jnp.float32),
        lax.psum(inner_bias_part.astype(jnp.bfloat16), "ctx").astype(jnp.float32),
        lax.psum(outer_part.astype(jnp.bfloat16), "ctx").astype(jnp.float32),
        lax.psum(outer_bias_part.astype(jnp.bfloat16), "ctx").astype(jnp.float32),
        lax.psum(second_gain_part.astype(jnp.bfloat16), "ctx").astype(jnp.float32),
        lax.psum(second_shift_part.astype(jnp.bfloat16), "ctx").astype(jnp.float32),
        lax.psum(project_part.astype(jnp.bfloat16), "ctx").astype(jnp.float32),
    )
    return (
        embedded[None],
        delta_home[None],
        results[0],
        results[1],
        results[2],
        results[3],
        results[4],
        results[5],
        results[6],
        results[7],
        results[8],
        results[9],
        results[10],
        results[11],
        results[12],
        results[13],
        results[14],
        results[15],
    )


BF = jnp.bfloat16
F32 = jnp.float32
ROWS = 512
HALF = 256
WIDTH = 768
HIDDEN = 3072
LOCAL = 3
FAR = 2.0**100
KROWS = 256
SCALE = HEAD_DIM ** (-0.5)


def nt(left, right):
    return lax.dot_general(left, right, (((1,), (1,)), ((), ())), preferred_element_type=F32)


def nn(left, right):
    return lax.dot_general(left, right, (((1,), (0,)), ((), ())), preferred_element_type=F32)


def tn(left, right):
    return lax.dot_general(left, right, (((0,), (0,)), ((), ())), preferred_element_type=F32)


def wide(value):
    return value.astype(F32)


def to_core(value):
    return lax.ppermute(value, "ctx", [(i, i ^ 1) for i in range(4)])


def to_x(value):
    return lax.ppermute(value, "ctx", [(i, i ^ 2) for i in range(4)])


def to_cross(value):
    return lax.ppermute(value, "ctx", [(i, i ^ 3) for i in range(4)])


def to_fsdp(value, bit):
    return lax.ppermute(value, "fsdp", [(i, i ^ bit) for i in range(8)])


def along_z(value, step):
    return lax.ppermute(value, "fsdp", [(i, (i + 2 * step) % 8) for i in range(8)])


def to_mixed(value, first):
    pairs = []
    for c in range(4):
        for f in range(8):
            target = (c ^ 2) * 8 + f if (c % 2 == 0) == first else c * 8 + (f ^ 1)
            pairs.append((c * 8 + f, target))
    return lax.ppermute(value, ("ctx", "fsdp"), pairs)


def after(value, *others):
    return lax.optimization_barrier((value, *others))[0]


def added(parts):
    total = wide(parts[0])
    for part in parts[1:]:
        total = total + wide(part)
    return total.astype(BF)


def together(*values):
    return lax.optimization_barrier(values)


def three_parts(value):
    high = wide(value.astype(BF))
    rest = value - high
    middle = wide(rest.astype(BF))
    return high, middle, rest - middle


def lanes_of(rows, n=128):
    return lax.broadcasted_iota(jnp.int32, (rows, n), 1)


def run(
    kernel, name, info, inputs, outs, scratch=(), limit=6, loose=(), loose_outs=(), alias=(), small=False
):
    memory = pl.BlockSpec(memory_space=pltpu.VMEM)
    outside = pl.BlockSpec(memory_space=pltpu.HBM)
    return pl.pallas_call(
        kernel,
        in_specs=[pl.BlockSpec(memory_space=pltpu.SMEM)]
        + [outside if i in loose else memory for i in range(len(inputs))],
        out_specs=[pl.BlockSpec(memory_space=pltpu.SMEM)]
        if small
        else [outside if i in loose_outs else memory for i in range(len(outs))],
        out_shape=[jax.ShapeDtypeStruct(s, t) for s, t in outs],
        scratch_shapes=list(scratch),
        input_output_aliases={i + 1: o for i, o in alias},
        compiler_params=pltpu.CompilerParams(vmem_limit_bytes=limit << 20),
        cost_estimate=pl.CostEstimate(flops=1000, bytes_accessed=1000, transcendentals=0),
        name=name,
    )(info, *inputs)


def start_copies(pairs, sems):
    copies = [pltpu.make_async_copy(a, b, sems.at[i]) for i, (a, b) in enumerate(pairs)]
    for copy in copies:
        copy.start()
    return copies


def aligned(value, n):
    return pl.multiple_of(value, n)


def piece_rows(info, n):
    z, y = info[1] // 2, lax.rem(info[1], 2)
    rows = []
    for k in range(4):
        source = lax.rem(z + 4 - k, 4)
        rows += [aligned((source * 2 + t) * n, 32) for t in (y, 1 - y)]
    return rows


def prepare_forward_kernel(info, wi_in, wo_in, w2_in, p_in, outer_out, inner_out, sems):
    core = lax.rem(info[0], 2)
    copies = start_copies(
        [
            (w2_in.at[pl.ds(aligned(core * 192, 64), 96)], outer_out.at[:, 0:768]),
            (w2_in.at[pl.ds(aligned(core * 192 + 96, 32), 96)], outer_out.at[:, 768:1536]),
            (p_in, outer_out.at[:, 1536:1664]),
            (wi_in.at[:, pl.ds(aligned(core * 1536, 512), 1536)], inner_out.at[:, 0:1536]),
            (wo_in.at[:, pl.ds(aligned(core * 384, 128), 384)], inner_out.at[:, 1536:1920]),
        ],
        sems,
    )
    for copy in copies:
        copy.wait()


def prepare_heads_kernel(info, *refs):
    ins, last_ref, heads_out, held, sems = refs[:11], refs[11], refs[12], refs[13:24], refs[24]
    c = info[0]
    copies = start_copies(zip(ins, held), sems)
    q_ref, k_ref, v_ref, *rows = held
    for copy in copies:
        copy.wait()
    rows = [wide(ref[...]) for ref in (*rows, last_ref)]
    rows = jnp.concatenate([*rows, jnp.zeros((116, 96), F32)], axis=0)
    rows = jnp.concatenate([rows, jnp.zeros((128, 32), F32)], axis=1)
    side = rows.T[:96, :64]
    for value in range(4):

        @pl.when(c == value)
        def _():
            at = slice(192 * value, 192 * value + 192)
            parts = [wide(ref[:, at]) for ref in (q_ref, k_ref, v_ref)]
            heads_out[...] = jnp.concatenate([*parts, side], axis=1).astype(BF)


def lay_kernel(info, *refs):
    pieces, outs, sems = refs[:8], refs[8:-1], refs[-1]
    pairs, start = [], 0
    for out in outs:
        stop = start + out.shape[1]
        for ref, row in zip(pieces, piece_rows(info, 96)):
            pairs.append((ref.at[:, start:stop], out.at[pl.ds(row, 96)]))
        start = stop
    copies = start_copies(pairs, sems)
    for copy in copies:
        copy.wait()


def lay(info, pieces, widths):
    return run(
        lay_kernel,
        "lay",
        info,
        pieces,
        [((WIDTH, n), BF) for n in widths],
        [pltpu.SemaphoreType.DMA((8 * len(widths),))],
        loose=range(8),
    )


def stack_kernel(info, *refs):
    pieces, out, sems = refs[:-2], refs[-2], refs[-1]
    copies = start_copies([(ref, out.at[i]) for i, ref in enumerate(pieces)], sems)
    for copy in copies:
        copy.wait()


def places_kernel(place, seg_ref, info_out):
    seg = wide(seg_ref[...])
    at = lanes_of(1, seg.shape[1])
    for i in range(4):
        info_out[i] = place[i]
        info_out[20 + i] = 0
    for i in range(8):
        start = jnp.sum(jnp.where(at == HALF * i, seg, 0.0))
        end = jnp.sum(jnp.where(at == HALF * i + HALF - 1, seg, 0.0))
        low = jnp.sum(jnp.where(seg < start, 1.0, 0.0)).astype(jnp.int32)
        high = jnp.sum(jnp.where(seg <= end, 1.0, 0.0)).astype(jnp.int32)
        info_out[4 + i] = low // KROWS
        info_out[12 + i] = (high + KROWS - 1) // KROWS


def project_kernel(info, *refs):
    x_refs, w_refs = refs[0:4], refs[4:12]
    seg_ref = refs[12]
    q_out, k_out, v_out, kt_out, vt_out, w_out, vec_out, sems = refs[13:]
    c = info[0]
    copies = start_copies(
        [(ref, w_out.at[pl.ds(row, 96)]) for ref, row in zip(w_refs, piece_rows(info, 96))], sems
    )
    for copy in copies:
        copy.wait()
    weights = w_out[...]
    turned = wide(weights[:, 512:640]).T
    vec_out[...] = turned[64:80]
    lane = lanes_of(WIDTH, 640)
    row = lax.broadcasted_iota(jnp.int32, (WIDTH, 640), 0)
    wanted = jnp.where(lane < 384, lane, lane - 384) + 192 * c
    chosen = nn(turned[64:80].astype(BF), wide(row == wanted).astype(BF))
    lane1 = lanes_of(1, 640)
    bias = jnp.where(
        lane1 < 192,
        chosen[0:1],
        jnp.where((lane1 >= 384) & (lane1 < 576), chosen[1:2], 0.0),
    )
    lanes = lanes_of(ROWS)
    for r in range(4):
        rows = pl.ds(aligned(jnp.bitwise_xor(c, r) * ROWS, ROWS), ROWS)
        result = nn(x_refs[r][...], weights) + bias
        seg = seg_ref[:, pl.ds(aligned(jnp.bitwise_xor(c, r) * ROWS, ROWS), ROWS)]
        same = jnp.broadcast_to(wide(seg), (128, ROWS)).T == wide(lanes - 64)
        qa = jnp.where(same & (lanes < 67), 1.0, 0.0)
        ka = jnp.where(lanes < 67, jnp.where(same, 0.0, -FAR), jnp.where(lanes < 70, 1.0, 0.0))
        for slot in range(9):
            pair = result[:, 128 * (slot // 2) : 128 * (slot // 2) + 128]
            if slot % 2:
                pair = pltpu.roll(pair, 64, 1)
            kind, h = slot // 3, slot % 3
            if kind == 0:
                low = wide(pair.astype(BF)) * SCALE
                q_out[h, rows, :] = jnp.where(lanes < 64, low, qa).astype(BF)
            elif kind == 1:
                value = jnp.where(lanes < 64, pair, ka)
                k_out[h, rows, :] = value.astype(BF)
                kt_out[h, :, rows] = value.T[:64].astype(BF)
            else:
                value = jnp.where(lanes < 64, pair, jnp.where(lanes < 67, 1.0, 0.0))
                v_out[h, rows, :] = value.astype(BF)
                vt_out[h, :, rows] = value.T[:80].astype(BF)


def over_keys(info, place, step):
    low_0, low_1 = info[4 + 2 * place], info[5 + 2 * place]
    high_0, high_1 = info[12 + 2 * place], info[13 + 2 * place]
    stop = jnp.maximum(high_0, low_1)
    pairs = (stop - low_1) // 2

    def loop(start, count, width, rows):
        def body(i, carry):
            at = aligned((start + i * (width // KROWS)) * KROWS, KROWS)
            step(pl.ds(at, width), rows)
            return carry

        lax.fori_loop(0, count, body, 0)

    loop(low_0, jnp.minimum(low_1, high_0) - low_0, KROWS, slice(0, HALF))
    loop(low_1, pairs, 2 * KROWS, slice(0, ROWS))
    loop(low_1 + 2 * pairs, stop - low_1 - 2 * pairs, KROWS, slice(0, ROWS))
    loop(stop, high_1 - stop, KROWS, slice(HALF, ROWS))


def attend_kernel(info, q_ref, k_ref, vt_ref, cot_ref, *refs, chip):
    each = range(LOCAL)
    top_s, sum_s, q_s = refs[6:]
    for step in range(2):
        o_ref, ql_ref, pack_ref = refs[3 * step : 3 * step + 3]
        place = jnp.bitwise_xor(info[0], step + 2 * chip)
        mine = pl.ds(aligned(place * ROWS, ROWS), ROWS)
        q_s[...] = q_ref[:, mine]
        top_s[...] = jnp.full_like(top_s, -3e38)
        sum_s[...] = jnp.zeros_like(sum_s)

        def advance(rows, part):
            scores = [nt(k_ref[h, rows], q_s[h, part]) for h in each]
            before = [top_s[h, :1, part] for h in each]
            peaks = [
                jnp.maximum(before[h], jnp.max(scores[h], axis=0, keepdims=True)) for h in each
            ]
            probs = [jnp.exp(scores[h] - peaks[h]).astype(BF) for h in each]
            shrink = [jnp.exp(before[h] - peaks[h]) for h in each]
            fresh = [nn(vt_ref[h, :, rows], probs[h]) for h in each]
            for h in each:
                sum_s[h, :, part] = sum_s[h, :, part] * shrink[h] + fresh[h]
                top_s[h, :, part] = jnp.broadcast_to(peaks[h], (8, peaks[h].shape[1]))

        over_keys(info, place, advance)
        lanes = lanes_of(ROWS)
        subs = lax.broadcasted_iota(jnp.int32, (128, ROWS), 0)
        outs = []
        for h in each:
            sums = sum_s[h]
            total = sums[64:65]
            parts = three_parts(top_s[h, :1] + jnp.log(total))
            tall = jnp.concatenate([sums[:64] / total, jnp.zeros((64, ROWS), F32)], axis=0)
            for i in range(3):
                tall = jnp.where(subs == 67 + i, -parts[i], tall)
            turned = tall.T
            out = jnp.where(lanes < 64, turned, 0.0)
            outs.append(out)
            o_ref[h] = out.astype(BF)
            ql_ref[h] = jnp.where(lanes < 67, wide(q_s[h]), turned).astype(BF)
        pack_ref[0:512] = (outs[0] + pltpu.roll(outs[1], 64, 1)).astype(BF)
        pack_ref[512:768] = (outs[2][:256] + pltpu.roll(outs[2][256:], 64, 1)).astype(BF)
        pack_ref[768:896] = cot_ref[pl.ds(aligned(place * 128, 128), 128), :]


def attend_rows(info, q, k, vt, cotangent, chip):
    return run(
        functools.partial(attend_kernel, chip=chip),
        "attend_rows",
        info,
        [q, k, vt, cotangent],
        ([((LOCAL, ROWS, 128), BF)] * 2 + [((896, 128), BF)]) * 2,
        [
            pltpu.VMEM((LOCAL, 8, ROWS), F32),
            pltpu.VMEM((LOCAL, 80, ROWS), F32),
            pltpu.VMEM((LOCAL, ROWS, 128), BF),
        ],
    )


def attend_back_kernel(info, *refs, r):
    each = range(LOCAL)
    ql_ref, up_ref, o_ref, k_ref, kt_ref, v_ref = refs[:6]
    *outs, dk_s, dv_s, dq_s, do_s = refs[6:]
    lanes = lanes_of(ROWS)
    if r == 0:
        (dq_ref,) = outs
        dk_s[...] = jnp.zeros_like(dk_s)
        dv_s[...] = jnp.zeros_like(dv_s)
    elif r < 3:
        _, _, dq_ref = outs
    else:
        w_ref, residual_ref, all_ref, emb_ref, *grads = outs[8:]
        for i, ref in enumerate((*outs[5:8], up_ref)):
            at = pl.ds(aligned(jnp.bitwise_xor(info[0], i) * 128, 128), 128)
            emb_ref[at, :] = ref[768:896]
    place = jnp.bitwise_xor(info[0], r)
    dq_s[...] = jnp.zeros_like(dq_s)
    pair = wide(up_ref[0:512])
    last = wide(up_ref[512:768])
    ups = [
        pair,
        pltpu.roll(pair, 64, 1),
        jnp.concatenate([last, pltpu.roll(last, 64, 1)], axis=0),
    ]
    for h in each:
        up = jnp.where(lanes < 64, ups[h], 0.0)
        parts = three_parts(jnp.sum(up * wide(o_ref[h]), axis=1, keepdims=True))
        for i in range(3):
            up = jnp.where(lanes == 64 + i, -parts[i], up)
        do_s[h] = up.astype(BF)

    def advance(rows, part):
        scores = [nt(k_ref[h, rows], ql_ref[h, part]) for h in each]
        rises = [nt(v_ref[h, rows], do_s[h, part]) for h in each]
        probs = [jnp.exp(scores[h]) for h in each]
        deltas = [(probs[h] * rises[h]).astype(BF) for h in each]
        lows = [probs[h].astype(BF) for h in each]
        for_values = [nn(lows[h], do_s[h, part]) for h in each]
        for_keys = [nn(deltas[h], ql_ref[h, part]) for h in each]
        for_queries = [nn(kt_ref[h, :, rows], deltas[h]) for h in each]
        for h in each:
            dv_s[h, rows] += for_values[h]
            dk_s[h, rows] += for_keys[h]
            dq_s[h, :, part] += for_queries[h]

    over_keys(info, place, advance)
    turned = []
    for h in each:
        tall = jnp.concatenate([dq_s[h], jnp.zeros((64, ROWS), F32)], axis=0)
        turned.append(tall.T * SCALE)
    both = (turned[0] + pltpu.roll(turned[1], 64, 1)).astype(BF)
    if r < 3:
        dq_ref[:, 0:128] = both
        dq_ref[:, 128:256] = turned[2].astype(BF)
        return
    mine = pl.ds(aligned(place * ROWS, ROWS), ROWS)
    all_ref[mine, 0:128] = both
    all_ref[mine, 128:256] = turned[2].astype(BF)
    for i, ref in enumerate(outs[2:5]):
        at = pl.ds(aligned(jnp.bitwise_xor(info[0], i) * ROWS, ROWS), ROWS)
        all_ref[at, 0:256] = ref[...]
    for b in range(4):
        rows = pl.ds(b * ROWS, ROWS)
        low = [jnp.where(lanes < 64, ref[h, rows], 0.0) for ref in (dk_s, dv_s) for h in each]
        high = [pltpu.roll(value, 64, 1) for value in low]
        all_ref[rows, 128:256] = (wide(all_ref[rows, 128:256]) + high[0]).astype(BF)
        all_ref[rows, 256:384] = (low[1] + high[2]).astype(BF)
        all_ref[rows, 384:512] = (low[3] + high[4]).astype(BF)
        all_ref[rows, 512:640] = low[5].astype(BF)
    input_grad(info, all_ref, w_ref, residual_ref, *grads)


def attend_back(info, r, ql, up, o, k, kt, v, carried=(), earlier=()):
    sums = [(k.shape, F32)] * 2
    part = [((ROWS, 256), BF)]
    whole = [
        ((k.shape[1], 640), BF),
        ((ROWS, 128), BF),
        ((ROWS, WIDTH), F32),
        ((2, ROWS, WIDTH), BF),
        ((ROWS, WIDTH), F32),
    ]
    first = len(part if r < 3 else whole)
    return run(
        functools.partial(attend_back_kernel, r=r),
        "attend_back",
        info,
        [ql, up, o, k, kt, v, *carried, *earlier],
        (part if r < 3 else whole) + sums,
        [pltpu.VMEM((LOCAL, 64, ROWS), F32), pltpu.VMEM((LOCAL, ROWS, 128), BF)],
        limit=9,
        alias=((6, first), (7, first + 1)) if r else (),
    )


def gaussian(value):
    below = 0.5 * (1.0 + lax.erf(value * 0.7071067811865476))
    return below, jnp.exp(-0.5 * value * value) * 0.3989422804014327


def norm_rows(value):
    centred = value - jnp.mean(value, axis=-1, keepdims=True)
    inverse = lax.rsqrt(jnp.mean(centred * centred, axis=-1, keepdims=True) + 1e-12)
    return centred * inverse, inverse


def norm_rows_back(upstream, normal, inverse, gain):
    scaled = upstream * gain
    first_mean = jnp.mean(scaled, axis=-1, keepdims=True)
    second_mean = jnp.mean(scaled * normal, axis=-1, keepdims=True)
    return inverse * (scaled - first_mean - normal * second_mean)


def column_sums(value):
    return jnp.sum(value, axis=0, keepdims=True)


def hidden_half(half, first, wi_ref, vec_ref, active_out, slope_out):
    shift = jnp.concatenate(
        [vec_ref[8 + k : 9 + k, 96 * f : 96 * f + 96] for f in range(8) for k in range(4)], axis=1
    )
    shift = jnp.where(half == 0, shift[:, :1536], shift[:, 1536:])
    for block in range(3):
        at = pl.ds(aligned(half * 1536 + block * 512, 512), 512)
        value = nn(first, wi_ref[:, at]) + shift[:, block * 512 : block * 512 + 512]
        below, bell = gaussian(value)
        active_out[:, at] = (value * below).astype(BF)
        slope_out[:, at] = (below + value * bell).astype(BF)


def inner_own_kernel(info, *refs):
    x_ref, *packs = refs[:5]
    vec_ref, wo_own, wo_other, g_ref = refs[5:9]
    (
        normal_out,
        inverse_out,
        first_out,
        active_out,
        slope_out,
        context_out,
        wo_out,
        wi_out,
        arrived_out,
        sems,
    ) = refs[9:]
    c = info[0]
    core = lax.rem(c, 2)
    own = pl.ds(aligned(core * 1536, 512), 1536)
    (copy,) = start_copies([(g_ref, wi_out.at[:, own])], sems)
    for r in range(4):
        group = jnp.bitwise_xor(c, r)
        arrived_out[pl.ds(aligned(group * 128, 128), 128), :] = packs[r][768:896]
        rows = pl.ds(aligned(group * 192, 64), 192)
        for half, ref in ((core, wo_own), (1 - core, wo_other)):
            at = pl.ds(aligned(half * 384, 128), 384)
            wo_out[256 * r : 256 * r + 192, at] = ref[rows, :]
        wo_out[256 * r + 192 : 256 * r + 256, :] = jnp.zeros((64, WIDTH), BF)
        context_out[:, 256 * r : 256 * r + 128] = packs[r][0:512]
        last = wide(packs[r][512:768])
        last = jnp.concatenate([last, pltpu.roll(last, 64, 1)], axis=0)
        context_out[:, 256 * r + 128 : 256 * r + 256] = jnp.where(
            lanes_of(ROWS) < 64, last, 0.0
        ).astype(BF)
    attended = nn(context_out[...], wo_out[...]) + vec_ref[2:3]
    normal, inverse = norm_rows(wide(x_ref[...]) + attended)
    normal_out[...] = normal
    inverse_out[...] = inverse
    first = (normal * vec_ref[3:4] + vec_ref[4:5]).astype(BF)
    first_out[...] = first
    copy.wait()
    hidden_half(core, first, wi_out, vec_ref, active_out, slope_out)


def inner_other_kernel(info, first_ref, vec_ref, g_ref, a_ref, s_ref, w_ref, *refs):
    active_out, slope_out, wi_out, sems = refs
    core = 1 - lax.rem(info[0], 2)
    other = pl.ds(aligned(core * 1536, 512), 1536)
    (copy,) = start_copies([(g_ref, wi_out.at[:, other])], sems)
    copy.wait()
    hidden_half(core, first_ref[...], wi_out, vec_ref, active_out, slope_out)


def outer_kernel(
    info,
    active_ref,
    own_ref,
    own_last_ref,
    other_ref,
    other_last_ref,
    normal_ref,
    vec_ref,
    table_ref,
    arrived_ref,
    residual_out,
    do_out,
    second_out,
    dp_out,
    given_out,
    sums_out,
    w2_out,
    wp_ref,
    sems,
):
    core = lax.rem(info[0], 2)
    pairs = []
    for i, row in enumerate(piece_rows(info, 96)):
        for half, ref, last_ref in (
            (core, own_ref, own_last_ref),
            (1 - core, other_ref, other_last_ref),
        ):
            piece = last_ref if i == 5 else ref.at[i - (i > 5)]
            for t in range(2):
                at = pl.ds(aligned(4 * row + 192 * half + 96 * t, 32), 96)
                pairs.append((piece.at[:, 768 * t : 768 * t + 768], w2_out.at[at]))
        piece = own_last_ref if i == 5 else own_ref.at[i - (i > 5)]
        pairs.append((piece.at[:, 1536:1664], wp_ref.at[pl.ds(row, 96)]))
    copies = start_copies(pairs, sems)
    for copy in copies:
        copy.wait()
    outer = nn(active_ref[...], w2_out[...]) + vec_ref[5:6]
    first = normal_ref[...] * vec_ref[3:4] + vec_ref[4:5]
    normal, inverse = norm_rows(first + outer)
    second = (normal * vec_ref[6:7] + vec_ref[7:8]).astype(BF)
    second_out[...] = second
    projected = nn(second, wp_ref[...])
    scale = lax.rsqrt(jnp.sum(projected * projected, axis=-1, keepdims=True) + 1e-06)
    normed = projected * scale
    where = lax.broadcasted_iota(jnp.int32, (ROWS, ROWS), 0) + info[0] * ROWS
    table = jnp.concatenate(
        [table_ref[:, pl.ds(aligned(ROWS * d + info[0] * 128, 128), 128)] for d in range(4)],
        axis=1,
    )
    onehot = wide(table == where).astype(BF)
    given_out[...] = tn(onehot, normed.astype(BF)).astype(BF)
    incoming = nn(onehot, arrived_ref[...])
    along = jnp.sum(normed * incoming, axis=-1, keepdims=True)
    delta = (scale * (incoming - normed * along)).astype(BF)
    dp_out[...] = delta
    upstream = nt(delta, wp_ref[...])
    residual = norm_rows_back(upstream, normal, inverse, vec_ref[6:7])
    residual_out[...] = residual
    low = residual.astype(BF)
    do_out[...] = low
    sums_out[...] = jnp.concatenate(
        [
            column_sums(wide(low)),
            column_sums(upstream * normal),
            column_sums(upstream),
            jnp.zeros((5, WIDTH), F32),
        ],
        axis=0,
    )


def hidden_back_kernel(info, do_ref, w2_ref, slope_ref, di_out, side_out):
    for block in range(HIDDEN // 512):
        at = slice(block * 512, block * 512 + 512)
        value = nt(do_ref[...], w2_ref[at, :]) * wide(slope_ref[:, at])
        low = value.astype(BF)
        di_out[:, at] = low
        side_out[:, at] = column_sums(wide(low))


def first_kernel(
    info,
    di_ref,
    wi_ref,
    residual_ref,
    normal_ref,
    inverse_ref,
    vec_ref,
    wo_ref,
    given_ref,
    residual_out,
    da_out,
    sums_out,
    *up_outs,
):
    upstream = residual_ref[...] + nt(di_ref[...], wi_ref[...])
    normal = normal_ref[...]
    residual = norm_rows_back(upstream, normal, inverse_ref[...], vec_ref[3:4])
    residual_out[...] = residual
    low = residual.astype(BF)
    da_out[...] = low
    sums_out[...] = jnp.concatenate(
        [
            column_sums(wide(low)),
            column_sums(upstream * normal),
            column_sums(upstream),
            jnp.zeros((5, WIDTH), F32),
        ],
        axis=0,
    )
    for r in (2, 3, 1, 0):
        out = up_outs[r]
        up = nt(low, wo_ref[256 * r : 256 * r + 256, :])
        out[0:512] = up[:, 0:128].astype(BF)
        last = up[:, 128:256]
        out[512:768] = (last[:256] + pltpu.roll(last[256:], 64, 1)).astype(BF)
        place = jnp.bitwise_xor(info[0], r)
        out[768:896] = given_ref[pl.ds(aligned(place * 128, 128), 128), :]


def spots(info, f):
    mine = info[1]
    my_z, my_y = mine // 2, lax.rem(mine, 2)
    z, y = (f // 2, f % 2) if isinstance(f, int) else (f // 2, lax.rem(f, 2))
    apart = jnp.bitwise_xor(my_z, z)
    return jnp.bitwise_xor(my_y, y), lax.rem(apart, 2), apart // 2


def heads_grad_kernel(info, *refs):
    x_refs, (all_ref, first_ref, outer_ref, side_ref, pack_ref) = refs[:4], refs[4:]
    c = info[0]
    sums = column_sums(wide(all_ref[...]))
    row = lax.broadcasted_iota(jnp.int32, (640, WIDTH), 0)
    lane = lanes_of(640, WIDTH)
    at = lax.broadcasted_iota(jnp.int32, (16, WIDTH), 0)
    rows = [jnp.zeros((2, WIDTH), F32), first_ref[0:3], outer_ref[0:3]]
    for k in range(4):
        starts = [384 * f + 96 * k for f in range(8)]
        rows.append(jnp.concatenate([side_ref[:, i : i + 96] for i in starts], axis=1))
    vectors = jnp.concatenate([*rows, jnp.zeros((4, WIDTH), F32)], axis=0)
    parts = three_parts(sums)
    for kind, first in ((0, 0), (1, 384)):
        chosen = (row - first + 192 * c == lane) & (row >= first) & (row < first + 192)
        chosen = wide(chosen).astype(BF)
        value = sum(nn(jnp.broadcast_to(part, (16, 640)).astype(BF), chosen) for part in parts)
        vectors = jnp.where(at == kind, value, vectors)
    tall = jnp.concatenate(
        [jnp.zeros((64, WIDTH), F32), vectors, jnp.zeros((48, WIDTH), F32)], axis=0
    )
    side = tall.T
    delta = jnp.zeros((WIDTH, 640), F32)
    for r, ref in enumerate(x_refs):
        at = pl.ds(aligned(jnp.bitwise_xor(c, r) * ROWS, ROWS), ROWS)
        delta = delta + tn(ref[...], all_ref[at, :])
    for f in range(8):
        i, j, k = spots(info, f)
        piece = delta[96 * f : 96 * f + 96]
        pack_ref[i, j, k, :, 0:512] = piece[:, :512].astype(BF)
        pack_ref[i, j, k, :, 512:640] = (piece[:, 512:] + side[96 * f : 96 * f + 96]).astype(BF)


def input_grad(info, all_ref, w_ref, residual_ref, own_ref, core_ref, next_ref):
    for r in (1, 3, 2, 0):
        rows = pl.ds(aligned(jnp.bitwise_xor(info[0], r) * ROWS, ROWS), ROWS)
        value = nt(all_ref[rows, :], w_ref[...])
        if r == 0:
            own_ref[...] = residual_ref[...] + value
        elif r == 2:
            next_ref[...] = value
        else:
            core_ref[r // 2] = value.astype(BF)


def finish_kernel(info, near_ref, far_ref, heads_ref, own_ref, came_ref, passed_ref, *refs):
    wi_out, w2_out, wo_out, wp_out, q_out, k_out, v_out, home_out = refs[:8]
    vec_outs = refs[8:17]
    wi_s, w2_s, wo_s, wp_s, q_s, k_s, v_s, home_s, sems = refs[17:]
    for r in range(4):
        ref = far_ref if r % 2 else near_ref
        g = jnp.bitwise_xor(info[0], r)
        a, b = g // 2, lax.rem(g, 2)
        block = wide(ref[r // 2])
        across = pl.ds(aligned(b * 384, 128), 384)
        w2_s[pl.ds(aligned(a * 192, 64), 192), across] = block[0:192]
        for h in range(2):
            at = pl.ds(aligned(g * 768 + 384 * h, 128), 384)
            wi_s[:, at] = block[208 + 96 * h : 304 + 96 * h]
        wo_s[pl.ds(aligned(a * 48, 16), 48), across] = block[400:448]
        for t in range(3):
            at = pl.ds(aligned(24 * g + 8 * t, 8), 8)
            wp_s[at, :] = block[192:200, 128 * t : 128 * t + 128]
    copies = start_copies(
        [(wi_s, wi_out), (w2_s, w2_out), (wo_s, wo_out), (wp_s, wp_out)], sems
    )
    home_s[...] = (own_ref[...] + wide(came_ref[0]) + wide(passed_ref[...])).astype(BF)
    for kind, ref in enumerate((q_s, k_s, v_s)):
        parts = [wide(heads_ref[g, :, 192 * kind : 192 * kind + 192]) for g in range(4)]
        ref[...] = jnp.concatenate(parts, axis=1)
    for i, pair in enumerate(((q_s, q_out), (k_s, k_out), (v_s, v_out), (home_s, home_out))):
        copy = pltpu.make_async_copy(*pair, sems.at[4 + i])
        copy.start()
        copies.append(copy)
    side = sum(wide(heads_ref[g, :, 512:640]) for g in range(4))
    tall = jnp.concatenate([side, jnp.zeros((32, 128), F32)], axis=0).T
    for i in range(8):
        vec_outs[i][...] = tall[64 + i : 65 + i, :96]
    last = jnp.concatenate([tall[72 + i : 73 + i, :96] for i in range(4)], axis=1)
    vec_outs[8][...] = last.reshape(384)
    for copy in copies:
        copy.wait()


def pair_index(info, keep, x, yr):
    xr = jnp.bitwise_xor(info[0] // 2, x)
    order = jnp.bitwise_xor(lax.rem(info[0], 2), keep)
    first = jnp.where(order == 0, xr, yr)
    second = jnp.where(order == 0, yr, xr)
    return first, second


def outer_pack_kernel(info, active_ref, do_ref, second_ref, dp_ref, keep_ref, send_ref, proj_s):
    core = lax.rem(info[0], 2)
    proj_s[...] = tn(second_ref[...], dp_ref[...])
    for f in range(8):
        yr, z0, z1 = spots(info, f)
        left = active_ref[:, 384 * f : 384 * f + 384]
        for k, ref in ((0, keep_ref), (1, send_ref)):
            half = jnp.bitwise_xor(core, k)
            right = do_ref[:, pl.ds(aligned(half * 384, 128), 384)]
            value = tn(left, right).astype(BF)
            for x in range(2):
                a, b = pair_index(info, k, x, yr)
                ref[a, b, z0, z1, 0:192, :] = value[192 * x : 192 * x + 192]
                start = 96 * f + 24 * (2 * x + half)
                across = jnp.concatenate(
                    [proj_s[pl.ds(aligned(start + 8 * g, 8), 8), :] for g in range(3)], axis=1
                )
                ref[a, b, z0, z1, 192:208, :] = jnp.concatenate(
                    [across, jnp.zeros((8, 384), F32)], axis=0
                ).astype(BF)


def inner_pack_kernel(info, first_ref, di_ref, keep_ref, send_ref):
    core = lax.rem(info[0], 2)
    for k, ref in ((0, keep_ref), (1, send_ref)):
        half = jnp.bitwise_xor(core, k)
        for x in range(2):
            for part in range(2):
                start = (2 * x + half) * 768 + 384 * part
                right = di_ref[:, pl.ds(aligned(start, 128), 384)]
                value = tn(first_ref[...], right).astype(BF)
                for f in range(8):
                    yr, z0, z1 = spots(info, f)
                    a, b = pair_index(info, k, x, yr)
                    ref[a, b, z0, z1, 96 * part : 96 * part + 96, :] = value[96 * f : 96 * f + 96]


def output_pack_kernel(info, context_ref, da_ref, keep_ref, send_ref):
    c = info[0]
    for k, ref in ((0, keep_ref), (1, send_ref)):
        half = jnp.bitwise_xor(lax.rem(c, 2), k)
        right = da_ref[:, pl.ds(aligned(half * 384, 128), 384)]
        for r in range(4):
            value = tn(context_ref[:, 256 * r : 256 * r + 256], right).astype(BF)
            for t in range(2):
                yr, z0, z1 = spots(info, 2 * jnp.bitwise_xor(c, r) + t)
                for x in range(2):
                    a, b = pair_index(info, k, x, yr)
                    start = 96 * t + 48 * x
                    ref[a, b, z0, z1] = value[start : start + 48]


def fast_device(
    tokens,
    dealt,
    segments,
    query_weight,
    key_weight,
    value_weight,
    query_bias,
    value_bias,
    output_weight,
    output_bias,
    first_gain,
    first_shift,
    inner_weight,
    inner_bias,
    outer_weight,
    outer_bias,
    second_gain,
    second_shift,
    project_weight,
    cotangent,
):
    c = lax.axis_index("ctx")
    f = lax.axis_index("fsdp")
    core = lax.rem(c, 2)
    total = segments.shape[1]
    x = tokens[0]

    place = jnp.stack([c, f, c * 0, c * 0]).astype(jnp.int32)
    (info,) = run(
        places_kernel, "places", place, [segments], [((24,), jnp.int32)], small=True
    )

    vectors = (
        query_bias,
        value_bias,
        output_bias,
        first_gain,
        first_shift,
        outer_bias,
        second_gain,
        second_shift,
    )
    (heads_pack,) = run(
        prepare_heads_kernel,
        "prepare_heads",
        place,
        [query_weight, key_weight, value_weight]
        + [vector.reshape(1, 96) for vector in vectors]
        + [inner_bias.reshape(4, 96)],
        [((96, 640), BF)],
        [pltpu.VMEM(query_weight.shape, BF)] * 3
        + [pltpu.VMEM((1, 96), BF)] * 8
        + [pltpu.SemaphoreType.DMA((11,))],
        limit=60,
        loose=range(11),
    )
    outer_pack, inner_pack = run(
        prepare_forward_kernel,
        "prepare_forward",
        after(place, heads_pack),
        [inner_weight, output_weight, outer_weight, project_weight],
        [((96, 1664), BF), ((96, 1920), BF)],
        [pltpu.SemaphoreType.DMA((5,))],
        limit=60,
        loose=range(4),
    )
    x_core = to_core(x)
    x_next = to_x(x)
    moved = [along_z(heads_pack, k) for k in range(1, 4)]
    moved_y = [to_fsdp(heads_pack, 1)]
    x_core, x_next, heads_pack, inner_pack, outer_pack, info, moved_y[0], *moved = together(
        x_core, x_next, heads_pack, inner_pack, outer_pack, info, moved_y[0], *moved
    )
    x_cross = to_core(x_next)
    inner_pack, moved, x_cross = together(inner_pack, moved, x_cross)
    moved_y += [to_fsdp(piece, 1) for piece in moved]
    inner_1, inner_3 = along_z(inner_pack, 1), along_z(inner_pack, 3)
    x_cross, inner_pack, outer_pack, *moved_y = together(
        x_cross, inner_pack, outer_pack, *moved_y
    )
    pieces = []
    for one, two in zip((heads_pack, *moved), moved_y):
        pieces += [one, two]
    inner_2 = along_z(inner_pack, 2)
    inner_0y, outer_0y = to_fsdp(inner_pack, 1), to_fsdp(outer_pack, 1)

    heads = (LOCAL, total, 128)
    q, k, v, kt, vt, heads_weight, vec = run(
        project_kernel,
        "project",
        info,
        [x, x_core, x_next, after(x_cross, inner_pack), *pieces, segments],
        [
            (heads, BF),
            (heads, BF),
            (heads, BF),
            ((LOCAL, 64, total), BF),
            ((LOCAL, 80, total), BF),
            ((WIDTH, 640), BF),
            ((16, WIDTH), F32),
        ],
        [pltpu.SemaphoreType.DMA((8,))],
        limit=8,
        loose=range(4, 12),
    )
    q, inner_1, inner_3, inner_0y, outer_0y, outer_pack = together(
        q, inner_1, inner_3, inner_0y, outer_0y, outer_pack
    )
    inner_1y = to_fsdp(inner_1, 1)
    o_2, ql_2, pack_2, o_3, ql_3, pack_3 = attend_rows(
        info, after(q, inner_1), k, vt, cotangent[0], 1
    )
    pack_2, pack_3, inner_2, inner_1y, outer_pack, q = together(
        pack_2, pack_3, inner_2, inner_1y, outer_pack, q
    )
    inner_2y, inner_3y = to_fsdp(inner_2, 1), to_fsdp(after(inner_3, inner_2), 1)
    outer_1, outer_3, outer_2 = [along_z(outer_pack, k) for k in (1, 3, 2)]
    o_0, ql_0, pack_0, o_1, ql_1, pack_1 = attend_rows(info, q, k, vt, cotangent[0], 0)
    pack_0, pack_1, pack_2, pack_3, inner_2y, inner_3y, outer_1, outer_3 = together(
        pack_0, pack_1, pack_2, pack_3, inner_2y, inner_3y, outer_1, outer_3
    )
    from_x, from_cross = to_x(pack_2), to_cross(pack_3)
    outer_1y, outer_3y = to_fsdp(outer_1, 1), to_fsdp(outer_3, 1)
    inner_half, output_own = lay(
        info,
        [inner_pack, inner_0y, inner_1, inner_1y, inner_2, inner_2y, inner_3, inner_3y],
        (1536, 384),
    )
    from_x, from_cross, inner_half, output_own, pack_1, outer_1y, outer_2, outer_3y = together(
        from_x, from_cross, inner_half, output_own, pack_1, outer_1y, outer_2, outer_3y
    )
    outer_2y = to_fsdp(outer_2, 1)
    from_core = to_core(pack_1)
    output_other = to_core(output_own)
    (outer_own,) = run(
        stack_kernel,
        "stack",
        info,
        [outer_pack, outer_0y, outer_1, outer_1y, outer_2, outer_3, outer_3y],
        [((7, 96, 1664), BF)],
        [pltpu.SemaphoreType.DMA((7,))],
        loose=range(7),
    )
    from_core, output_other, outer_own = together(from_core, output_other, outer_own)
    inner_other = to_core(after(inner_half, from_core))
    outer_other = to_core(outer_own)
    (
        normal,
        inverse,
        first_low,
        active,
        slope,
        context,
        output_full,
        inner_full,
        arrived,
    ) = run(
        inner_own_kernel,
        "inner_own",
        info,
        [
            x,
            pack_0,
            from_core,
            from_x,
            from_cross,
            vec,
            output_own,
            output_other,
            inner_half,
        ],
        [
            ((ROWS, WIDTH), F32),
            ((ROWS, 1), F32),
            ((ROWS, WIDTH), BF),
            ((ROWS, HIDDEN), BF),
            ((ROWS, HIDDEN), BF),
            ((ROWS, 1024), BF),
            ((1024, WIDTH), BF),
            ((WIDTH, HIDDEN), BF),
            ((ROWS, 128), BF),
        ],
        [pltpu.SemaphoreType.DMA((1,))],
        loose=(8,),
    )
    first_low, inner_other, outer_2y, outer_other = together(
        first_low, inner_other, outer_2y, outer_other
    )
    outer_last = to_core(outer_2y)
    active, slope, inner_full = run(
        inner_other_kernel,
        "inner_other",
        info,
        [first_low, vec, inner_other, active, slope, inner_full],
        [((ROWS, HIDDEN), BF), ((ROWS, HIDDEN), BF), ((WIDTH, HIDDEN), BF)],
        [pltpu.SemaphoreType.DMA((1,))],
        loose=(2,),
        alias=((3, 0), (4, 1), (5, 2)),
    )
    residual_two, delta_outer, second_low, delta_projected, given, outer_sums, outer_full = run(
        outer_kernel,
        "outer",
        info,
        [
            active,
            outer_own,
            outer_2y,
            outer_other,
            outer_last,
            normal,
            vec,
            dealt,
            arrived,
        ],
        [
            ((ROWS, WIDTH), F32),
            ((ROWS, WIDTH), BF),
            ((ROWS, WIDTH), BF),
            ((ROWS, 128), BF),
            ((ROWS, 128), BF),
            ((8, WIDTH), F32),
            ((HIDDEN, WIDTH), BF),
        ],
        [pltpu.VMEM((WIDTH, 128), BF), pltpu.SemaphoreType.DMA((40,))],
        loose=(1, 2, 3, 4),
    )
    keep_o, send_o = run(
        outer_pack_kernel,
        "outer_pack",
        info,
        [active, delta_outer, second_low, delta_projected],
        [((2, 2, 2, 2, 208, 384), BF)] * 2,
        [pltpu.VMEM((WIDTH, 128), F32)],
    )
    core_o = to_core(send_o)
    delta_inner, inner_side = run(
        hidden_back_kernel,
        "hidden_back",
        info,
        [after(delta_outer, send_o), outer_full, slope],
        [((ROWS, HIDDEN), BF), ((1, HIDDEN), F32)],
    )
    keep_i, send_i = run(
        inner_pack_kernel,
        "inner_pack",
        info,
        [first_low, delta_inner],
        [((2, 2, 2, 2, 192, 384), BF)] * 2,
    )
    core_o, delta_inner, inner_side, keep_i, send_i = together(
        core_o, delta_inner, inner_side, keep_i, send_i
    )

    core_i = to_core(send_i)
    give_o = added([keep_o[1], core_o[1]])
    one_o = to_mixed(give_o, True)
    residual_one, delta_attended, first_sums, *ups = run(
        first_kernel,
        "first",
        info,
        [
            after(delta_inner, give_o),
            inner_full,
            residual_two,
            normal,
            inverse,
            vec,
            output_full,
            given,
        ],
        [((ROWS, WIDTH), F32), ((ROWS, WIDTH), BF), ((8, WIDTH), F32)] + [((896, 128), BF)] * 4,
    )
    core_i, delta_attended, up_0, *ups = together(core_i, delta_attended, *ups)
    ups = [to_core(ups[0]), to_x(ups[1]), to_cross(ups[2])]
    keep_w, send_w = run(
        output_pack_kernel,
        "output_pack",
        info,
        [context, delta_attended],
        [((2, 2, 2, 2, 48, 384), BF)] * 2,
    )
    core_w = to_core(send_w)
    keys = (k, kt, v)
    dq_0, dk, dv = attend_back(info, 0, after(ql_0, send_w), up_0, o_0, *keys)
    dq_1, dk, dv = attend_back(info, 1, ql_1, ups[0], o_1, *keys, (dk, dv))
    one_o, core_w, dq_0, dq_1, dk, dv, *ups = together(one_o, core_w, dq_0, dq_1, dk, dv, *ups)

    give_i = jnp.concatenate([added([keep_i[1], core_i[1]]), added([keep_w[1], core_w[1]])], axis=3)
    one_i = to_mixed(give_i, True)
    give_o = added([keep_o[0, 1], core_o[0, 1], one_o[1]])
    two_o = to_mixed(give_o, False)
    dq_2, dk, dv = attend_back(
        info, 2, after(ql_2, give_i, give_o), ups[1], o_2, *keys, (dk, dv)
    )
    delta_heads, embedded, own, for_core, for_next, _, _ = attend_back(
        info,
        3,
        ql_3,
        ups[2],
        o_3,
        *keys,
        (dk, dv),
        (dq_0, dq_1, dq_2, up_0, *ups[:2], heads_weight, residual_one),
    )
    one_i, two_o, delta_heads, embedded, own, for_core, for_next = together(
        one_i, two_o, delta_heads, embedded, own, for_core, for_next
    )

    came = to_core(for_core)
    sum_i = [keep_i[0, 1], core_i[0, 1]], [keep_w[0, 1], core_w[0, 1]]
    give_i = added([jnp.concatenate(parts, axis=2) for parts in zip(*sum_i)] + [one_i[1]])
    two_i = to_mixed(give_i, False)
    sum_o = [keep_o[0, 0], core_o[0, 0], one_o[0], two_o]
    give_o = added([part[1] for part in sum_o])
    three_o = to_fsdp(give_o, 2)
    (pack,) = run(
        heads_grad_kernel,
        "heads_grad",
        info,
        [
            x,
            x_core,
            x_next,
            x_cross,
            after(delta_heads, give_i, give_o),
            first_sums,
            outer_sums,
            inner_side,
        ],
        [((2, 2, 2, 96, 640), BF)],
        limit=8,
    )
    two_i, three_o, pack, came = together(two_i, three_o, pack, came)

    one_h = to_fsdp(pack[1], 1)
    sum_i = [keep_i[0, 0], core_i[0, 0]], [keep_w[0, 0], core_w[0, 0]]
    sum_i = [jnp.concatenate(parts, axis=2) for parts in zip(*sum_i)] + [one_i[0], two_i]
    give_i = added([part[1] for part in sum_i])
    three_i = to_fsdp(give_i, 2)
    sum_o = [*(part[0] for part in sum_o), three_o]
    give_o = added([part[1] for part in sum_o])
    four_o = to_fsdp(give_o, 4)
    give_x = (for_next + wide(came[1])).astype(BF)
    passed = to_x(give_x)
    one_h, three_i, four_o = together(one_h, three_i, four_o)

    sum_i = [*(part[0] for part in sum_i), three_i]
    give_i = added([part[1] for part in sum_i])
    four_i = to_fsdp(give_i, 4)
    give_h = added([pack[0, 1], one_h[1]])
    two_h = to_fsdp(give_h, 2)
    four_i, two_h = together(four_i, two_h)

    give_h = added([pack[0, 0, 1], one_h[0, 1], two_h[1]])
    three_h = to_fsdp(give_h, 4)
    forward_sum = jnp.concatenate(
        [
            added([*(part[0] for part in sum_o), four_o]),
            added([*(part[0] for part in sum_i), four_i]),
        ],
        axis=0,
    )
    forward_next = to_x(forward_sum)
    three_h, passed, forward_next = together(three_h, passed, forward_next)
    mine = added([pack[0, 0, 0], one_h[0, 0], two_h[0], three_h])
    near = jnp.stack([forward_sum, forward_next])
    far = to_core(near)
    heads_all = lax.all_gather(after(mine, near), "ctx")
    square = (96, WIDTH)
    shapes = [
        ((96, HIDDEN), F32),
        ((384, WIDTH), F32),
        (square, F32),
        ((96, 128), F32),
        (square, F32),
        (square, F32),
        (square, F32),
        ((ROWS, WIDTH), BF),
    ]
    (
        inner_grad,
        outer_grad,
        output_grad,
        project_grad,
        query_grad,
        key_grad,
        value_grad,
        delta_home,
        *vec_all,
    ) = run(
        finish_kernel,
        "finish",
        info,
        [near, far, heads_all, own, came, passed],
        shapes + [((1, 96), F32)] * 8 + [((384,), F32)],
        [pltpu.VMEM(*shape) for shape in shapes] + [pltpu.SemaphoreType.DMA((8,))],
        limit=20,
        loose_outs=range(8),
    )
    return (
        embedded[None],
        delta_home[None],
        query_grad,
        key_grad,
        value_grad,
        vec_all[0].reshape(96),
        vec_all[1].reshape(96),
        output_grad,
        vec_all[2].reshape(96),
        vec_all[3].reshape(96),
        vec_all[4].reshape(96),
        inner_grad,
        vec_all[8],
        outer_grad,
        vec_all[5].reshape(96),
        vec_all[6].reshape(96),
        vec_all[7].reshape(96),
        project_grad,
    )


def suits(mesh):
    return mesh.shape["ctx"] == 4 and mesh.shape["fsdp"] == 8


def solution(mesh):
    on_device = fast_device if suits(mesh) else generic_device

    return jax.shard_map(
        on_device,
        mesh=mesh,
        in_specs=(
            P("fsdp", "ctx", None),
            P("fsdp", None),
            P("fsdp", None),
            P("fsdp", None),
            P("fsdp", None),
            P("fsdp", None),
            P("fsdp"),
            P("fsdp"),
            P("fsdp", None),
            P("fsdp"),
            P("fsdp"),
            P("fsdp"),
            P("fsdp", None),
            P("fsdp"),
            P("fsdp", None),
            P("fsdp"),
            P("fsdp"),
            P("fsdp"),
            P("fsdp", None),
            P("fsdp", "ctx", None),
        ),
        out_specs=(
            P("fsdp", "ctx", None),
            P("fsdp", "ctx", None),
            P("fsdp", None),
            P("fsdp", None),
            P("fsdp", None),
            P("fsdp"),
            P("fsdp"),
            P("fsdp", None),
            P("fsdp"),
            P("fsdp"),
            P("fsdp"),
            P("fsdp", None),
            P("fsdp"),
            P("fsdp", None),
            P("fsdp"),
            P("fsdp"),
            P("fsdp"),
            P("fsdp", None),
        ),
        check_vma=False,
    )
```

```python
import functools

import jax
import jax.numpy as jnp
from jax import lax
from jax.experimental import pallas as pl
from jax.experimental.pallas import tpu as pltpu
from jax.sharding import PartitionSpec as P

HEADS = 12
HEAD_DIM = 64


def matmul(left, right):
    return jnp.dot(left, right, preferred_element_type=jnp.float32)


def norm_forward(value, gain, shift):
    centred = value - jnp.mean(value, axis=-1, keepdims=True)
    inverse = lax.rsqrt(jnp.mean(centred * centred, axis=-1, keepdims=True) + 1e-12)
    normal = centred * inverse
    return (normal * gain + shift, normal, inverse)


def norm_backward(upstream, normal, inverse, gain):
    scaled = upstream * gain
    first_mean = jnp.mean(scaled, axis=-1, keepdims=True)
    second_mean = jnp.mean(scaled * normal, axis=-1, keepdims=True)
    inward = inverse * (scaled - first_mean - normal * second_mean)
    return (inward, jnp.sum(upstream * normal, axis=0), jnp.sum(upstream, axis=0))


def gelu_slope(value):
    cumulative = 0.5 * (1.0 + jax.scipy.special.erf(value * 0.7071067811865476))
    return cumulative + value * jnp.exp(-0.5 * value * value) * 0.3989422804014327


def scored(query_heads, key_block, query_segments, segment_block, scale):
    scores = (
        jnp.einsum("qhd,khd->hqk", query_heads, key_block, preferred_element_type=jnp.float32)
        * scale
    )
    allowed = (query_segments[:, None] == segment_block[None, :])[None]
    return (scores, allowed)


def probabilities(scores, allowed, log_total):
    return jnp.where(allowed, jnp.exp(scores - log_total[..., None]), 0.0)


def log_totals(query_heads, key_blocks, query_segments, segment_blocks, scale):

    def log_advance(carry, pieces):
        running_max, running_sum = carry
        scores, allowed = scored(query_heads, pieces[0], query_segments, pieces[1], scale)
        masked = jnp.where(allowed, scores, -1e30)
        new_max = jnp.maximum(running_max, jnp.max(masked, axis=-1))
        fresh = jnp.sum(jnp.where(allowed, jnp.exp(masked - new_max[..., None]), 0.0), axis=-1)
        return ((new_max, running_sum * jnp.exp(running_max - new_max) + fresh), None)

    shape = (query_heads.shape[1], query_heads.shape[0])
    start = (jnp.full(shape, -1e30, jnp.float32), jnp.zeros(shape, jnp.float32))
    final = lax.scan(log_advance, start, (key_blocks, segment_blocks))[0]
    return final[0] + jnp.log(final[1])


def attend(query_heads, key_blocks, value_blocks, query_segments, segment_blocks, scale):
    log_total = log_totals(query_heads, key_blocks, query_segments, segment_blocks, scale)

    def attend_advance(carry, pieces):
        scores, allowed = scored(query_heads, pieces[0], query_segments, pieces[2], scale)
        probs = probabilities(scores, allowed, log_total).astype(jnp.bfloat16)
        return (
            carry
            + jnp.einsum("hqk,khd->qhd", probs, pieces[1], preferred_element_type=jnp.float32),
            None,
        )

    start = jnp.zeros(query_heads.shape, jnp.float32)
    mixed = lax.scan(attend_advance, start, (key_blocks, value_blocks, segment_blocks))[0]
    return (mixed, log_total)


def attend_backward(
    query_heads,
    key_blocks,
    value_blocks,
    query_segments,
    segment_blocks,
    scale,
    log_total,
    upstream,
):

    def first_pass(carry, pieces):
        scores, allowed = scored(query_heads, pieces[0], query_segments, pieces[2], scale)
        probs = probabilities(scores, allowed, log_total)
        delta_probs = jnp.einsum(
            "qhd,khd->hqk", upstream, pieces[1], preferred_element_type=jnp.float32
        )
        value_terms = jnp.einsum(
            "hqk,qhd->khd", probs.astype(jnp.bfloat16), upstream, preferred_element_type=jnp.float32
        )
        return (carry + jnp.sum(probs * delta_probs, axis=-1), value_terms)

    shape = (query_heads.shape[1], query_heads.shape[0])
    weighted, value_terms = lax.scan(
        first_pass, jnp.zeros(shape, jnp.float32), (key_blocks, value_blocks, segment_blocks)
    )

    def second_pass(carry, pieces):
        scores, allowed = scored(query_heads, pieces[0], query_segments, pieces[2], scale)
        probs = probabilities(scores, allowed, log_total)
        delta_probs = jnp.einsum(
            "qhd,khd->hqk", upstream, pieces[1], preferred_element_type=jnp.float32
        )
        delta_scores = (probs * (delta_probs - weighted[..., None])).astype(jnp.bfloat16)
        key_terms = jnp.einsum(
            "hqk,qhd->khd", delta_scores, query_heads, preferred_element_type=jnp.float32
        )
        return (
            carry
            + jnp.einsum(
                "hqk,khd->qhd", delta_scores, pieces[0], preferred_element_type=jnp.float32
            ),
            key_terms,
        )

    query_terms, key_terms = lax.scan(
        second_pass,
        jnp.zeros(query_heads.shape, jnp.float32),
        (key_blocks, value_blocks, segment_blocks),
    )
    return (query_terms * scale, key_terms * scale, value_terms)


def generic_device(
    tokens,
    dealt,
    segments,
    query_weight,
    key_weight,
    value_weight,
    query_bias,
    value_bias,
    output_weight,
    output_bias,
    first_gain,
    first_shift,
    inner_weight,
    inner_bias,
    outer_weight,
    outer_bias,
    second_gain,
    second_shift,
    project_weight,
    cotangent,
):
    peers = lax.axis_size("ctx")
    place = lax.axis_index("ctx")
    local_rows = tokens.shape[1]
    share = local_rows // peers
    order = dealt[0]
    table = (
        lax.dynamic_index_in_dim(order.reshape(peers, peers, share), place, 1, keepdims=False)
        - place * local_rows
    )
    flat_table = table.reshape(-1)
    home_tokens = tokens[0]
    width = home_tokens.shape[1]
    (
        query_full,
        key_full,
        value_full,
        output_full,
        query_shift,
        value_shift,
        output_shift,
        gain_one,
        shift_one,
    ) = (
        lax.all_gather(query_weight, "fsdp", axis=0, tiled=True),
        lax.all_gather(key_weight, "fsdp", axis=0, tiled=True),
        lax.all_gather(value_weight, "fsdp", axis=0, tiled=True),
        lax.all_gather(output_weight, "fsdp", axis=0, tiled=True),
        lax.all_gather(query_bias, "fsdp", axis=0, tiled=True),
        lax.all_gather(value_bias, "fsdp", axis=0, tiled=True),
        lax.all_gather(output_bias, "fsdp", axis=0, tiled=True),
        lax.all_gather(first_gain, "fsdp", axis=0, tiled=True),
        lax.all_gather(first_shift, "fsdp", axis=0, tiled=True),
    )
    outgoing = jnp.take(home_tokens, table, axis=0)
    here_tokens = lax.all_to_all(outgoing, "ctx", split_axis=0, concat_axis=0, tiled=True).reshape(
        local_rows, width
    )
    key_segments = jnp.take(segments[0], order, axis=0)
    query_segments = lax.dynamic_slice_in_dim(key_segments, place * local_rows, local_rows)
    queries = (matmul(here_tokens, query_full) + query_shift.astype(jnp.float32)).astype(
        jnp.bfloat16
    )
    own_keys = matmul(here_tokens, key_full).astype(jnp.bfloat16)
    own_values = (matmul(here_tokens, value_full) + value_shift.astype(jnp.float32)).astype(
        jnp.bfloat16
    )
    all_keys, all_values = (
        lax.all_gather(own_keys, "ctx", axis=0, tiled=True),
        lax.all_gather(own_values, "ctx", axis=0, tiled=True),
    )
    total = all_keys.shape[0]
    block = min(1024, total)
    count = total // block
    scale = HEAD_DIM ** (-0.5)
    query_heads = queries.reshape(local_rows, HEADS, HEAD_DIM)
    key_blocks = all_keys.reshape(count, block, HEADS, HEAD_DIM)
    value_blocks = all_values.reshape(count, block, HEADS, HEAD_DIM)
    segment_blocks = key_segments.reshape(count, block)
    mixed, log_total = attend(
        query_heads, key_blocks, value_blocks, query_segments, segment_blocks, scale
    )
    context = mixed.reshape(local_rows, width).astype(jnp.bfloat16)
    inner_full, inner_shift, outer_full, outer_shift, gain_two, shift_two, project_full = (
        lax.all_gather(inner_weight, "fsdp", axis=0, tiled=True),
        lax.all_gather(inner_bias, "fsdp", axis=0, tiled=True),
        lax.all_gather(outer_weight, "fsdp", axis=0, tiled=True),
        lax.all_gather(outer_bias, "fsdp", axis=0, tiled=True),
        lax.all_gather(second_gain, "fsdp", axis=0, tiled=True),
        lax.all_gather(second_shift, "fsdp", axis=0, tiled=True),
        lax.all_gather(project_weight, "fsdp", axis=0, tiled=True),
    )
    attended = matmul(context, output_full) + output_shift.astype(jnp.float32)
    first, first_normal, first_inverse = norm_forward(
        here_tokens.astype(jnp.float32) + attended,
        gain_one.astype(jnp.float32),
        shift_one.astype(jnp.float32),
    )
    first_low = first.astype(jnp.bfloat16)
    inner = matmul(first_low, inner_full) + inner_shift.astype(jnp.float32)
    active = jax.nn.gelu(inner, approximate=False).astype(jnp.bfloat16)
    outer = matmul(active, outer_full) + outer_shift.astype(jnp.float32)
    second, second_normal, second_inverse = norm_forward(
        first + outer, gain_two.astype(jnp.float32), shift_two.astype(jnp.float32)
    )
    second_low = second.astype(jnp.bfloat16)
    projected = matmul(second_low, project_full)
    inverse_length = lax.rsqrt(jnp.sum(projected * projected, axis=-1, keepdims=True) + 1e-06)
    normed = projected * inverse_length
    embedded = normed.astype(jnp.bfloat16)
    incoming = cotangent[0].astype(jnp.float32)
    along = jnp.sum(normed * incoming, axis=-1, keepdims=True)
    delta_projected = (inverse_length * (incoming - normed * along)).astype(jnp.bfloat16)
    project_delta = matmul(second_low.T, delta_projected)
    delta_second = matmul(delta_projected, project_full.T)
    residual_two, second_gain_delta, second_shift_delta = norm_backward(
        delta_second, second_normal, second_inverse, gain_two.astype(jnp.float32)
    )
    delta_outer = residual_two.astype(jnp.bfloat16)
    outer_bias_delta = jnp.sum(delta_outer, axis=0, dtype=jnp.float32)
    outer_delta = matmul(active.T, delta_outer)
    delta_active = matmul(delta_outer, outer_full.T)
    delta_inner = (delta_active * gelu_slope(inner)).astype(jnp.bfloat16)
    inner_bias_delta = jnp.sum(delta_inner, axis=0, dtype=jnp.float32)
    inner_delta = matmul(first_low.T, delta_inner)
    delta_first = residual_two + matmul(delta_inner, inner_full.T)
    residual_one, first_gain_delta, first_shift_delta = norm_backward(
        delta_first, first_normal, first_inverse, gain_one.astype(jnp.float32)
    )
    delta_attended = residual_one.astype(jnp.bfloat16)
    output_bias_delta = jnp.sum(delta_attended, axis=0, dtype=jnp.float32)
    output_delta = matmul(context.T, delta_attended)
    delta_context = matmul(delta_attended, output_full.T).astype(jnp.bfloat16)
    upstream = delta_context.reshape(local_rows, HEADS, HEAD_DIM)
    query_terms, key_terms, value_terms = attend_backward(
        query_heads,
        key_blocks,
        value_blocks,
        query_segments,
        segment_blocks,
        scale,
        log_total,
        upstream,
    )
    key_sums, value_sums = (
        lax.psum_scatter(
            key_terms.reshape(total, width).astype(jnp.bfloat16),
            "ctx",
            scatter_dimension=0,
            tiled=True,
        ).astype(jnp.float32),
        lax.psum_scatter(
            value_terms.reshape(total, width).astype(jnp.bfloat16),
            "ctx",
            scatter_dimension=0,
            tiled=True,
        ).astype(jnp.float32),
    )
    delta_keys = key_sums.astype(jnp.bfloat16)
    delta_values = value_sums.astype(jnp.bfloat16)
    delta_queries = query_terms.reshape(local_rows, width).astype(jnp.bfloat16)
    query_bias_delta = jnp.sum(delta_queries, axis=0, dtype=jnp.float32)
    value_bias_delta = jnp.sum(delta_values, axis=0, dtype=jnp.float32)
    query_delta = matmul(here_tokens.T, delta_queries)
    key_delta = matmul(here_tokens.T, delta_keys)
    value_delta = matmul(here_tokens.T, delta_values)
    delta_here = (
        residual_one
        + matmul(delta_queries, query_full.T)
        + matmul(delta_keys, key_full.T)
        + matmul(delta_values, value_full.T)
    ).astype(jnp.bfloat16)
    coming_home = lax.all_to_all(
        delta_here.reshape(peers, share, width), "ctx", split_axis=0, concat_axis=0, tiled=True
    )
    delta_home = (
        jnp.zeros((local_rows, width), jnp.bfloat16)
        .at[flat_table]
        .set(coming_home.reshape(local_rows, width))
    )
    (
        inner_part,
        inner_bias_part,
        outer_part,
        outer_bias_part,
        second_gain_part,
        second_shift_part,
        project_part,
    ) = (
        lax.psum_scatter(
            inner_delta.astype(jnp.bfloat16), "fsdp", scatter_dimension=0, tiled=True
        ).astype(jnp.float32),
        lax.psum_scatter(
            inner_bias_delta.astype(jnp.bfloat16), "fsdp", scatter_dimension=0, tiled=True
        ).astype(jnp.float32),
        lax.psum_scatter(
            outer_delta.astype(jnp.bfloat16), "fsdp", scatter_dimension=0, tiled=True
        ).astype(jnp.float32),
        lax.psum_scatter(
            outer_bias_delta.astype(jnp.bfloat16), "fsdp", scatter_dimension=0, tiled=True
        ).astype(jnp.float32),
        lax.psum_scatter(
            second_gain_delta.astype(jnp.bfloat16), "fsdp", scatter_dimension=0, tiled=True
        ).astype(jnp.float32),
        lax.psum_scatter(
            second_shift_delta.astype(jnp.bfloat16), "fsdp", scatter_dimension=0, tiled=True
        ).astype(jnp.float32),
        lax.psum_scatter(
            project_delta.astype(jnp.bfloat16), "fsdp", scatter_dimension=0, tiled=True
        ).astype(jnp.float32),
    )
    (
        query_part,
        key_part,
        value_part,
        query_bias_part,
        value_bias_part,
        output_part,
        output_bias_part,
        first_gain_part,
        first_shift_part,
    ) = (
        lax.psum_scatter(
            query_delta.astype(jnp.bfloat16), "fsdp", scatter_dimension=0, tiled=True
        ).astype(jnp.float32),
        lax.psum_scatter(
            key_delta.astype(jnp.bfloat16), "fsdp", scatter_dimension=0, tiled=True
        ).astype(jnp.float32),
        lax.psum_scatter(
            value_delta.astype(jnp.bfloat16), "fsdp", scatter_dimension=0, tiled=True
        ).astype(jnp.float32),
        lax.psum_scatter(
            query_bias_delta.astype(jnp.bfloat16), "fsdp", scatter_dimension=0, tiled=True
        ).astype(jnp.float32),
        lax.psum_scatter(
            value_bias_delta.astype(jnp.bfloat16), "fsdp", scatter_dimension=0, tiled=True
        ).astype(jnp.float32),
        lax.psum_scatter(
            output_delta.astype(jnp.bfloat16), "fsdp", scatter_dimension=0, tiled=True
        ).astype(jnp.float32),
        lax.psum_scatter(
            output_bias_delta.astype(jnp.bfloat16), "fsdp", scatter_dimension=0, tiled=True
        ).astype(jnp.float32),
        lax.psum_scatter(
            first_gain_delta.astype(jnp.bfloat16), "fsdp", scatter_dimension=0, tiled=True
        ).astype(jnp.float32),
        lax.psum_scatter(
            first_shift_delta.astype(jnp.bfloat16), "fsdp", scatter_dimension=0, tiled=True
        ).astype(jnp.float32),
    )
    results = (
        lax.psum(query_part.astype(jnp.bfloat16), "ctx").astype(jnp.float32),
        lax.psum(key_part.astype(jnp.bfloat16), "ctx").astype(jnp.float32),
        lax.psum(value_part.astype(jnp.bfloat16), "ctx").astype(jnp.float32),
        lax.psum(query_bias_part.astype(jnp.bfloat16), "ctx").astype(jnp.float32),
        lax.psum(value_bias_part.astype(jnp.bfloat16), "ctx").astype(jnp.float32),
        lax.psum(output_part.astype(jnp.bfloat16), "ctx").astype(jnp.float32),
        lax.psum(output_bias_part.astype(jnp.bfloat16), "ctx").astype(jnp.float32),
        lax.psum(first_gain_part.astype(jnp.bfloat16), "ctx").astype(jnp.float32),
        lax.psum(first_shift_part.astype(jnp.bfloat16), "ctx").astype(jnp.float32),
        lax.psum(inner_part.astype(jnp.bfloat16), "ctx").astype(jnp.float32),
        lax.psum(inner_bias_part.astype(jnp.bfloat16), "ctx").astype(jnp.float32),
        lax.psum(outer_part.astype(jnp.bfloat16), "ctx").astype(jnp.float32),
        lax.psum(outer_bias_part.astype(jnp.bfloat16), "ctx").astype(jnp.float32),
        lax.psum(second_gain_part.astype(jnp.bfloat16), "ctx").astype(jnp.float32),
        lax.psum(second_shift_part.astype(jnp.bfloat16), "ctx").astype(jnp.float32),
        lax.psum(project_part.astype(jnp.bfloat16), "ctx").astype(jnp.float32),
    )
    return (
        embedded[None],
        delta_home[None],
        results[0],
        results[1],
        results[2],
        results[3],
        results[4],
        results[5],
        results[6],
        results[7],
        results[8],
        results[9],
        results[10],
        results[11],
        results[12],
        results[13],
        results[14],
        results[15],
    )


BF = jnp.bfloat16
F32 = jnp.float32
ROWS = 512
HALF = 256
WIDTH = 768
HIDDEN = 3072
LOCAL = 3
FAR = 2.0**100
KROWS = 256
SCALE = HEAD_DIM ** (-0.5)


def nt(left, right):
    return lax.dot_general(left, right, (((1,), (1,)), ((), ())), preferred_element_type=F32)


def nn(left, right):
    return lax.dot_general(left, right, (((1,), (0,)), ((), ())), preferred_element_type=F32)


def tn(left, right):
    return lax.dot_general(left, right, (((0,), (0,)), ((), ())), preferred_element_type=F32)


def wide(value):
    return value.astype(F32)


def to_core(value):
    return lax.ppermute(value, "ctx", [(i, i ^ 1) for i in range(4)])


def to_x(value):
    return lax.ppermute(value, "ctx", [(i, i ^ 2) for i in range(4)])


def to_cross(value):
    return lax.ppermute(value, "ctx", [(i, i ^ 3) for i in range(4)])


def to_fsdp(value, bit):
    return lax.ppermute(value, "fsdp", [(i, i ^ bit) for i in range(8)])


def along_z(value, step):
    return lax.ppermute(value, "fsdp", [(i, (i + 2 * step) % 8) for i in range(8)])


def to_mixed(value, first):
    pairs = []
    for c in range(4):
        for f in range(8):
            target = (c ^ 2) * 8 + f if (c % 2 == 0) == first else c * 8 + (f ^ 1)
            pairs.append((c * 8 + f, target))
    return lax.ppermute(value, ("ctx", "fsdp"), pairs)


def after(value, *others):
    return lax.optimization_barrier((value, *others))[0]


def added(parts):
    total = wide(parts[0])
    for part in parts[1:]:
        total = total + wide(part)
    return total.astype(BF)


def together(*values):
    return lax.optimization_barrier(values)


def three_parts(value):
    high = wide(value.astype(BF))
    rest = value - high
    middle = wide(rest.astype(BF))
    return high, middle, rest - middle


def lanes_of(rows, n=128):
    return lax.broadcasted_iota(jnp.int32, (rows, n), 1)


def run(
    kernel, name, info, inputs, outs, scratch=(), limit=6, loose=(), loose_outs=(), alias=(), small=False
):
    memory = pl.BlockSpec(memory_space=pltpu.VMEM)
    outside = pl.BlockSpec(memory_space=pltpu.HBM)
    return pl.pallas_call(
        kernel,
        in_specs=[pl.BlockSpec(memory_space=pltpu.SMEM)]
        + [outside if i in loose else memory for i in range(len(inputs))],
        out_specs=[pl.BlockSpec(memory_space=pltpu.SMEM)]
        if small
        else [outside if i in loose_outs else memory for i in range(len(outs))],
        out_shape=[jax.ShapeDtypeStruct(s, t) for s, t in outs],
        scratch_shapes=list(scratch),
        input_output_aliases={i + 1: o for i, o in alias},
        compiler_params=pltpu.CompilerParams(vmem_limit_bytes=limit << 20),
        cost_estimate=pl.CostEstimate(flops=1000, bytes_accessed=1000, transcendentals=0),
        name=name,
    )(info, *inputs)


def start_copies(pairs, sems):
    copies = [pltpu.make_async_copy(a, b, sems.at[i]) for i, (a, b) in enumerate(pairs)]
    for copy in copies:
        copy.start()
    return copies


def aligned(value, n):
    return pl.multiple_of(value, n)


def piece_rows(info, n):
    z, y = info[1] // 2, lax.rem(info[1], 2)
    rows = []
    for k in range(4):
        source = lax.rem(z + 4 - k, 4)
        rows += [aligned((source * 2 + t) * n, 32) for t in (y, 1 - y)]
    return rows


def prepare_forward_kernel(info, wi_in, wo_in, w2_in, p_in, outer_out, inner_out, sems):
    core = lax.rem(info[0], 2)
    copies = start_copies(
        [
            (w2_in.at[pl.ds(aligned(core * 192, 64), 96)], outer_out.at[:, 0:768]),
            (w2_in.at[pl.ds(aligned(core * 192 + 96, 32), 96)], outer_out.at[:, 768:1536]),
            (p_in, outer_out.at[:, 1536:1664]),
            (wi_in.at[:, pl.ds(aligned(core * 1536, 512), 1536)], inner_out.at[:, 0:1536]),
            (wo_in.at[:, pl.ds(aligned(core * 384, 128), 384)], inner_out.at[:, 1536:1920]),
        ],
        sems,
    )
    for copy in copies:
        copy.wait()


def prepare_heads_kernel(info, *refs):
    ins, heads_out, held, sems = refs[:12], refs[12], refs[13:25], refs[25]
    c = info[0]
    copies = start_copies(zip(ins, held), sems)
    q_ref, k_ref, v_ref, *rows, last_ref = held
    for copy in copies:
        copy.wait()
    rows = [wide(ref[...]) for ref in rows]
    last = wide(last_ref[...]).reshape(1, 384)
    rows += [last[:, 96 * i : 96 * i + 96] for i in range(4)]
    rows = jnp.concatenate([*rows, jnp.zeros((116, 96), F32)], axis=0)
    rows = jnp.concatenate([rows, jnp.zeros((128, 32), F32)], axis=1)
    side = rows.T[:96, :64]
    for value in range(4):

        @pl.when(c == value)
        def _():
            at = slice(192 * value, 192 * value + 192)
            parts = [wide(ref[:, at]) for ref in (q_ref, k_ref, v_ref)]
            heads_out[...] = jnp.concatenate([*parts, side], axis=1).astype(BF)


def lay_kernel(info, *refs):
    pieces, outs, sems = refs[:8], refs[8:-1], refs[-1]
    pairs, start = [], 0
    for out in outs:
        stop = start + out.shape[1]
        for ref, row in zip(pieces, piece_rows(info, 96)):
            pairs.append((ref.at[:, start:stop], out.at[pl.ds(row, 96)]))
        start = stop
    copies = start_copies(pairs, sems)
    for copy in copies:
        copy.wait()


def lay(info, pieces, widths):
    return run(
        lay_kernel,
        "lay",
        info,
        pieces,
        [((WIDTH, n), BF) for n in widths],
        [pltpu.SemaphoreType.DMA((8 * len(widths),))],
        loose=range(8),
    )


def stack_kernel(info, *refs):
    pieces, out, sems = refs[:-2], refs[-2], refs[-1]
    copies = start_copies([(ref, out.at[i]) for i, ref in enumerate(pieces)], sems)
    for copy in copies:
        copy.wait()


def places_kernel(place, seg_ref, info_out):
    seg = wide(seg_ref[...])
    at = lanes_of(1, seg.shape[1])
    for i in range(4):
        info_out[i] = place[i]
        info_out[20 + i] = 0
    for i in range(8):
        start = jnp.sum(jnp.where(at == HALF * i, seg, 0.0))
        end = jnp.sum(jnp.where(at == HALF * i + HALF - 1, seg, 0.0))
        low = jnp.sum(jnp.where(seg < start, 1.0, 0.0)).astype(jnp.int32)
        high = jnp.sum(jnp.where(seg <= end, 1.0, 0.0)).astype(jnp.int32)
        info_out[4 + i] = low // KROWS
        info_out[12 + i] = (high + KROWS - 1) // KROWS


def project_kernel(info, *refs):
    x_refs, w_refs = refs[0:4], refs[4:12]
    seg_ref = refs[12]
    q_out, k_out, v_out, kt_out, vt_out, w_out, vec_out, sems = refs[13:]
    c = info[0]
    copies = start_copies(
        [(ref, w_out.at[pl.ds(row, 96)]) for ref, row in zip(w_refs, piece_rows(info, 96))], sems
    )
    for copy in copies:
        copy.wait()
    weights = w_out[...]
    turned = wide(weights[:, 512:640]).T
    vec_out[...] = turned[64:80]
    mine = pltpu.roll(turned[64:72], lax.rem(WIDTH - 192 * c, WIDTH), 1)
    gap = jnp.zeros((1, 192), F32)
    bias = jnp.concatenate([mine[0:1, :192], gap, mine[1:2, :192], gap[:, :64]], axis=1)
    lanes = lanes_of(ROWS)
    for r in range(4):
        rows = pl.ds(aligned(jnp.bitwise_xor(c, r) * ROWS, ROWS), ROWS)
        result = nn(x_refs[r][...], weights) + bias
        seg = seg_ref[:, pl.ds(aligned(jnp.bitwise_xor(c, r) * ROWS, ROWS), ROWS)]
        same = jnp.broadcast_to(wide(seg), (128, ROWS)).T == wide(lanes - 64)
        qa = jnp.where(same & (lanes < 67), 1.0, 0.0)
        ka = jnp.where(lanes < 67, jnp.where(same, 0.0, -FAR), jnp.where(lanes < 70, 1.0, 0.0))
        for slot in range(9):
            pair = result[:, 128 * (slot // 2) : 128 * (slot // 2) + 128]
            if slot % 2:
                pair = pltpu.roll(pair, 64, 1)
            kind, h = slot // 3, slot % 3
            if kind == 0:
                low = wide(pair.astype(BF)) * SCALE
                q_out[h, rows, :] = jnp.where(lanes < 64, low, qa).astype(BF)
            elif kind == 1:
                value = jnp.where(lanes < 64, pair, ka)
                k_out[h, rows, :] = value.astype(BF)
                kt_out[h, :, rows] = value.T[:64].astype(BF)
            else:
                value = jnp.where(lanes < 64, pair, jnp.where(lanes < 67, 1.0, 0.0))
                v_out[h, rows, :] = value.astype(BF)
                vt_out[h, :, rows] = value.T[:80].astype(BF)


def over_keys(info, place, step):
    low_0, low_1 = info[4 + 2 * place], info[5 + 2 * place]
    high_0, high_1 = info[12 + 2 * place], info[13 + 2 * place]
    stop = jnp.maximum(high_0, low_1)
    pairs = (stop - low_1) // 2

    def loop(start, count, width, rows):
        def body(i, carry):
            at = aligned((start + i * (width // KROWS)) * KROWS, KROWS)
            step(pl.ds(at, width), rows)
            return carry

        lax.fori_loop(0, count, body, 0)

    loop(low_0, jnp.minimum(low_1, high_0) - low_0, KROWS, slice(0, HALF))
    loop(low_1, pairs, 2 * KROWS, slice(0, ROWS))
    loop(low_1 + 2 * pairs, stop - low_1 - 2 * pairs, KROWS, slice(0, ROWS))
    loop(stop, high_1 - stop, KROWS, slice(HALF, ROWS))


def attend_kernel(info, q_ref, k_ref, vt_ref, cot_ref, *refs, chip):
    each = range(LOCAL)
    top_s, sum_s, q_s = refs[6:]
    for step in range(2):
        o_ref, ql_ref, pack_ref = refs[3 * step : 3 * step + 3]
        place = jnp.bitwise_xor(info[0], step + 2 * chip)
        mine = pl.ds(aligned(place * ROWS, ROWS), ROWS)
        q_s[...] = q_ref[:, mine]
        top_s[...] = jnp.full_like(top_s, -3e38)
        sum_s[...] = jnp.zeros_like(sum_s)

        def advance(rows, part):
            scores = [nt(k_ref[h, rows], q_s[h, part]) for h in each]
            before = [top_s[h, :1, part] for h in each]
            peaks = [
                jnp.maximum(before[h], jnp.max(scores[h], axis=0, keepdims=True)) for h in each
            ]
            probs = [jnp.exp(scores[h] - peaks[h]).astype(BF) for h in each]
            shrink = [jnp.exp(before[h] - peaks[h]) for h in each]
            fresh = [nn(vt_ref[h, :, rows], probs[h]) for h in each]
            for h in each:
                sum_s[h, :, part] = sum_s[h, :, part] * shrink[h] + fresh[h]
                top_s[h, :, part] = jnp.broadcast_to(peaks[h], (8, peaks[h].shape[1]))

        over_keys(info, place, advance)
        lanes = lanes_of(ROWS)
        subs = lax.broadcasted_iota(jnp.int32, (128, ROWS), 0)
        outs = []
        for h in each:
            sums = sum_s[h]
            total = sums[64:65]
            parts = three_parts(top_s[h, :1] + jnp.log(total))
            tall = jnp.concatenate([sums[:64] / total, jnp.zeros((64, ROWS), F32)], axis=0)
            for i in range(3):
                tall = jnp.where(subs == 67 + i, -parts[i], tall)
            turned = tall.T
            out = jnp.where(lanes < 64, turned, 0.0)
            outs.append(out)
            o_ref[h] = out.astype(BF)
            ql_ref[h] = jnp.where(lanes < 67, wide(q_s[h]), turned).astype(BF)
        pack_ref[0:512] = (outs[0] + pltpu.roll(outs[1], 64, 1)).astype(BF)
        pack_ref[512:768] = (outs[2][:256] + pltpu.roll(outs[2][256:], 64, 1)).astype(BF)
        pack_ref[768:896] = cot_ref[pl.ds(aligned(place * 128, 128), 128), :]


def attend_rows(info, q, k, vt, cotangent, chip):
    return run(
        functools.partial(attend_kernel, chip=chip),
        "attend_rows",
        info,
        [q, k, vt, cotangent],
        ([((LOCAL, ROWS, 128), BF)] * 2 + [((896, 128), BF)]) * 2,
        [
            pltpu.VMEM((LOCAL, 8, ROWS), F32),
            pltpu.VMEM((LOCAL, 80, ROWS), F32),
            pltpu.VMEM((LOCAL, ROWS, 128), BF),
        ],
    )


def attend_back_kernel(info, *refs, r):
    each = range(LOCAL)
    ql_ref, up_ref, o_ref, k_ref, kt_ref, v_ref = refs[:6]
    *outs, dk_s, dv_s, dq_s, do_s = refs[6:]
    lanes = lanes_of(ROWS)
    if r == 0:
        (dq_ref,) = outs
        dk_s[...] = jnp.zeros_like(dk_s)
        dv_s[...] = jnp.zeros_like(dv_s)
    elif r < 3:
        _, _, dq_ref = outs
    else:
        w_ref, residual_ref, all_ref, emb_ref, *grads = outs[8:]
        for i, ref in enumerate((*outs[5:8], up_ref)):
            at = pl.ds(aligned(jnp.bitwise_xor(info[0], i) * 128, 128), 128)
            emb_ref[at, :] = ref[768:896]
    place = jnp.bitwise_xor(info[0], r)
    dq_s[...] = jnp.zeros_like(dq_s)
    pair = wide(up_ref[0:512])
    last = wide(up_ref[512:768])
    ups = [
        pair,
        pltpu.roll(pair, 64, 1),
        jnp.concatenate([last, pltpu.roll(last, 64, 1)], axis=0),
    ]
    for h in each:
        up = jnp.where(lanes < 64, ups[h], 0.0)
        parts = three_parts(jnp.sum(up * wide(o_ref[h]), axis=1, keepdims=True))
        for i in range(3):
            up = jnp.where(lanes == 64 + i, -parts[i], up)
        do_s[h] = up.astype(BF)

    def advance(rows, part):
        scores = [nt(k_ref[h, rows], ql_ref[h, part]) for h in each]
        rises = [nt(v_ref[h, rows], do_s[h, part]) for h in each]
        probs = [jnp.exp(scores[h]) for h in each]
        deltas = [(probs[h] * rises[h]).astype(BF) for h in each]
        lows = [probs[h].astype(BF) for h in each]
        for_values = [nn(lows[h], do_s[h, part]) for h in each]
        for_keys = [nn(deltas[h], ql_ref[h, part]) for h in each]
        for_queries = [nn(kt_ref[h, :, rows], deltas[h]) for h in each]
        for h in each:
            dv_s[h, rows] += for_values[h]
            dk_s[h, rows] += for_keys[h]
            dq_s[h, :, part] += for_queries[h]

    over_keys(info, place, advance)
    turned = []
    for h in each:
        tall = jnp.concatenate([dq_s[h], jnp.zeros((64, ROWS), F32)], axis=0)
        turned.append(tall.T * SCALE)
    both = (turned[0] + pltpu.roll(turned[1], 64, 1)).astype(BF)
    if r < 3:
        dq_ref[:, 0:128] = both
        dq_ref[:, 128:256] = turned[2].astype(BF)
        return
    mine = pl.ds(aligned(place * ROWS, ROWS), ROWS)
    all_ref[mine, 0:128] = both
    all_ref[mine, 128:256] = turned[2].astype(BF)
    for i, ref in enumerate(outs[2:5]):
        at = pl.ds(aligned(jnp.bitwise_xor(info[0], i) * ROWS, ROWS), ROWS)
        all_ref[at, 0:256] = ref[...]
    for b in range(4):
        rows = pl.ds(b * ROWS, ROWS)
        low = [jnp.where(lanes < 64, ref[h, rows], 0.0) for ref in (dk_s, dv_s) for h in each]
        high = [pltpu.roll(value, 64, 1) for value in low]
        all_ref[rows, 128:256] = (wide(all_ref[rows, 128:256]) + high[0]).astype(BF)
        all_ref[rows, 256:384] = (low[1] + high[2]).astype(BF)
        all_ref[rows, 384:512] = (low[3] + high[4]).astype(BF)
        all_ref[rows, 512:640] = low[5].astype(BF)
    input_grad(info, all_ref, w_ref, residual_ref, *grads)


def attend_back(info, r, ql, up, o, k, kt, v, carried=(), earlier=()):
    sums = [(k.shape, F32)] * 2
    part = [((ROWS, 256), BF)]
    whole = [
        ((k.shape[1], 640), BF),
        ((ROWS, 128), BF),
        ((ROWS, WIDTH), F32),
        ((2, ROWS, WIDTH), BF),
        ((ROWS, WIDTH), F32),
    ]
    first = len(part if r < 3 else whole)
    return run(
        functools.partial(attend_back_kernel, r=r),
        "attend_back",
        info,
        [ql, up, o, k, kt, v, *carried, *earlier],
        (part if r < 3 else whole) + sums,
        [pltpu.VMEM((LOCAL, 64, ROWS), F32), pltpu.VMEM((LOCAL, ROWS, 128), BF)],
        limit=9,
        alias=((6, first), (7, first + 1)) if r else (),
    )


def gaussian(value):
    below = 0.5 * (1.0 + lax.erf(value * 0.7071067811865476))
    return below, jnp.exp(-0.5 * value * value) * 0.3989422804014327


def norm_rows(value):
    centred = value - jnp.mean(value, axis=-1, keepdims=True)
    inverse = lax.rsqrt(jnp.mean(centred * centred, axis=-1, keepdims=True) + 1e-12)
    return centred * inverse, inverse


def norm_rows_back(upstream, normal, inverse, gain):
    scaled = upstream * gain
    first_mean = jnp.mean(scaled, axis=-1, keepdims=True)
    second_mean = jnp.mean(scaled * normal, axis=-1, keepdims=True)
    return inverse * (scaled - first_mean - normal * second_mean)


def column_sums(value):
    return jnp.sum(value, axis=0, keepdims=True)


def hidden_half(half, first, wi_ref, vec_ref, active_out, slope_out):
    shift = jnp.concatenate(
        [vec_ref[8 + k : 9 + k, 96 * f : 96 * f + 96] for f in range(8) for k in range(4)], axis=1
    )
    shift = jnp.where(half == 0, shift[:, :1536], shift[:, 1536:])
    for block in range(3):
        at = pl.ds(aligned(half * 1536 + block * 512, 512), 512)
        value = nn(first, wi_ref[:, at]) + shift[:, block * 512 : block * 512 + 512]
        below, bell = gaussian(value)
        active_out[:, at] = (value * below).astype(BF)
        slope_out[:, at] = (below + value * bell).astype(BF)


def inner_own_kernel(info, *refs):
    x_ref, *packs = refs[:5]
    vec_ref, wo_own, wo_other, g_ref = refs[5:9]
    (
        normal_out,
        inverse_out,
        first_out,
        active_out,
        slope_out,
        context_out,
        wo_out,
        wi_out,
        arrived_out,
        sems,
    ) = refs[9:]
    c = info[0]
    core = lax.rem(c, 2)
    own = pl.ds(aligned(core * 1536, 512), 1536)
    (copy,) = start_copies([(g_ref, wi_out.at[:, own])], sems)
    for r in range(4):
        group = jnp.bitwise_xor(c, r)
        arrived_out[pl.ds(aligned(group * 128, 128), 128), :] = packs[r][768:896]
        rows = pl.ds(aligned(group * 192, 64), 192)
        for half, ref in ((core, wo_own), (1 - core, wo_other)):
            at = pl.ds(aligned(half * 384, 128), 384)
            wo_out[256 * r : 256 * r + 192, at] = ref[rows, :]
        wo_out[256 * r + 192 : 256 * r + 256, :] = jnp.zeros((64, WIDTH), BF)
        context_out[:, 256 * r : 256 * r + 128] = packs[r][0:512]
        last = wide(packs[r][512:768])
        last = jnp.concatenate([last, pltpu.roll(last, 64, 1)], axis=0)
        context_out[:, 256 * r + 128 : 256 * r + 256] = jnp.where(
            lanes_of(ROWS) < 64, last, 0.0
        ).astype(BF)
    attended = nn(context_out[...], wo_out[...]) + vec_ref[2:3]
    normal, inverse = norm_rows(wide(x_ref[...]) + attended)
    normal_out[...] = normal
    inverse_out[...] = inverse
    first = (normal * vec_ref[3:4] + vec_ref[4:5]).astype(BF)
    first_out[...] = first
    copy.wait()
    hidden_half(core, first, wi_out, vec_ref, active_out, slope_out)


def outer_pairs(info, pieces, w2_out):
    core = lax.rem(info[0], 2)
    rows = piece_rows(info, 96)
    pairs = []
    for i, own, other in pieces:
        for half, piece in ((core, own), (1 - core, other)):
            for t in range(2):
                at = pl.ds(aligned(4 * rows[i] + 192 * half + 96 * t, 32), 96)
                pairs.append((piece.at[:, 768 * t : 768 * t + 768], w2_out.at[at]))
    return pairs


def inner_other_kernel(info, first_ref, vec_ref, g_ref, own_ref, other_ref, *refs):
    active_out, slope_out, wi_out, w2_out, sems = refs[3:]
    core = 1 - lax.rem(info[0], 2)
    other = pl.ds(aligned(core * 1536, 512), 1536)
    early = [(i, own_ref.at[i - (i > 5)], other_ref.at[i - (i > 5)]) for i in range(8) if i != 5]
    copies = start_copies(
        [(g_ref, wi_out.at[:, other])] + outer_pairs(info, early, w2_out), sems
    )
    copies[0].wait()
    hidden_half(core, first_ref[...], wi_out, vec_ref, active_out, slope_out)
    for copy in copies[1:]:
        copy.wait()


def outer_kernel(
    info,
    active_ref,
    own_ref,
    own_last_ref,
    other_last_ref,
    normal_ref,
    vec_ref,
    table_ref,
    arrived_ref,
    _,
    residual_out,
    do_out,
    second_out,
    dp_out,
    given_out,
    sums_out,
    w2_out,
    wp_ref,
    sems,
):
    pairs = outer_pairs(info, [(5, own_last_ref, other_last_ref)], w2_out)
    for i, row in enumerate(piece_rows(info, 96)):
        piece = own_last_ref if i == 5 else own_ref.at[i - (i > 5)]
        pairs.append((piece.at[:, 1536:1664], wp_ref.at[pl.ds(row, 96)]))
    copies = start_copies(pairs, sems)
    for copy in copies:
        copy.wait()
    outer = nn(active_ref[...], w2_out[...]) + vec_ref[5:6]
    first = normal_ref[...] * vec_ref[3:4] + vec_ref[4:5]
    normal, inverse = norm_rows(first + outer)
    second = (normal * vec_ref[6:7] + vec_ref[7:8]).astype(BF)
    second_out[...] = second
    projected = nn(second, wp_ref[...])
    scale = lax.rsqrt(jnp.sum(projected * projected, axis=-1, keepdims=True) + 1e-06)
    normed = projected * scale
    where = lax.broadcasted_iota(jnp.int32, (ROWS, ROWS), 0) + info[0] * ROWS
    table = jnp.concatenate(
        [table_ref[:, pl.ds(aligned(ROWS * d + info[0] * 128, 128), 128)] for d in range(4)],
        axis=1,
    )
    onehot = wide(table == where).astype(BF)
    given_out[...] = tn(onehot, normed.astype(BF)).astype(BF)
    incoming = nn(onehot, arrived_ref[...])
    along = jnp.sum(normed * incoming, axis=-1, keepdims=True)
    delta = (scale * (incoming - normed * along)).astype(BF)
    dp_out[...] = delta
    upstream = nt(delta, wp_ref[...])
    residual = norm_rows_back(upstream, normal, inverse, vec_ref[6:7])
    residual_out[...] = residual
    low = residual.astype(BF)
    do_out[...] = low
    sums_out[...] = jnp.concatenate(
        [
            column_sums(wide(low)),
            column_sums(upstream * normal),
            column_sums(upstream),
            jnp.zeros((5, WIDTH), F32),
        ],
        axis=0,
    )


def hidden_back_kernel(info, do_ref, w2_ref, slope_ref, di_out, side_out):
    for block in range(HIDDEN // 512):
        at = slice(block * 512, block * 512 + 512)
        value = nt(do_ref[...], w2_ref[at, :]) * wide(slope_ref[:, at])
        low = value.astype(BF)
        di_out[:, at] = low
        side_out[:, at] = column_sums(wide(low))


def first_kernel(
    info,
    di_ref,
    wi_ref,
    residual_ref,
    normal_ref,
    inverse_ref,
    vec_ref,
    wo_ref,
    given_ref,
    residual_out,
    da_out,
    sums_out,
    *up_outs,
):
    upstream = residual_ref[...] + nt(di_ref[...], wi_ref[...])
    normal = normal_ref[...]
    residual = norm_rows_back(upstream, normal, inverse_ref[...], vec_ref[3:4])
    residual_out[...] = residual
    low = residual.astype(BF)
    da_out[...] = low
    sums_out[...] = jnp.concatenate(
        [
            column_sums(wide(low)),
            column_sums(upstream * normal),
            column_sums(upstream),
            jnp.zeros((5, WIDTH), F32),
        ],
        axis=0,
    )
    for r in (2, 3, 1, 0):
        out = up_outs[r]
        up = nt(low, wo_ref[256 * r : 256 * r + 256, :])
        out[0:512] = up[:, 0:128].astype(BF)
        last = up[:, 128:256]
        out[512:768] = (last[:256] + pltpu.roll(last[256:], 64, 1)).astype(BF)
        place = jnp.bitwise_xor(info[0], r)
        out[768:896] = given_ref[pl.ds(aligned(place * 128, 128), 128), :]


def spots(info, f):
    mine = info[1]
    my_z, my_y = mine // 2, lax.rem(mine, 2)
    z, y = (f // 2, f % 2) if isinstance(f, int) else (f // 2, lax.rem(f, 2))
    apart = jnp.bitwise_xor(my_z, z)
    return jnp.bitwise_xor(my_y, y), lax.rem(apart, 2), apart // 2


def heads_grad_kernel(info, *refs):
    x_refs, (all_ref, first_ref, outer_ref, side_ref, pack_ref) = refs[:4], refs[4:]
    c = info[0]
    sums = column_sums(wide(all_ref[...]))
    pair = jnp.concatenate([sums[:, 0:192], sums[:, 384:576], jnp.zeros((6, 192), F32)], axis=0)
    pair = jnp.concatenate([pair, jnp.zeros((8, 576), F32)], axis=1)
    rows = [pltpu.roll(pair, 192 * c, 1)[0:2], first_ref[0:3], outer_ref[0:3]]
    for k in range(4):
        starts = [384 * f + 96 * k for f in range(8)]
        rows.append(jnp.concatenate([side_ref[:, i : i + 96] for i in starts], axis=1))
    vectors = jnp.concatenate([*rows, jnp.zeros((4, WIDTH), F32)], axis=0)
    tall = jnp.concatenate(
        [jnp.zeros((64, WIDTH), F32), vectors, jnp.zeros((48, WIDTH), F32)], axis=0
    )
    side = tall.T
    delta = jnp.zeros((WIDTH, 640), F32)
    for r, ref in enumerate(x_refs):
        at = pl.ds(aligned(jnp.bitwise_xor(c, r) * ROWS, ROWS), ROWS)
        delta = delta + tn(ref[...], all_ref[at, :])
    for f in range(8):
        i, j, k = spots(info, f)
        piece = delta[96 * f : 96 * f + 96]
        pack_ref[i, j, k, :, 0:512] = piece[:, :512].astype(BF)
        pack_ref[i, j, k, :, 512:640] = (piece[:, 512:] + side[96 * f : 96 * f + 96]).astype(BF)


def input_grad(info, all_ref, w_ref, residual_ref, own_ref, core_ref, next_ref):
    for r in (1, 3, 2, 0):
        rows = pl.ds(aligned(jnp.bitwise_xor(info[0], r) * ROWS, ROWS), ROWS)
        value = nt(all_ref[rows, :], w_ref[...])
        if r == 0:
            own_ref[...] = residual_ref[...] + value
        elif r == 2:
            next_ref[...] = value
        else:
            core_ref[r // 2] = value.astype(BF)


def finish_kernel(info, near_ref, far_ref, heads_ref, own_ref, came_ref, passed_ref, *refs):
    wi_out, w2_out, wo_out, wp_out, q_out, k_out, v_out, home_out = refs[:8]
    vec_outs = refs[8:17]
    wi_s, w2_s, wo_s, wp_s, q_s, k_s, v_s, home_s, sems = refs[17:]
    for r in range(4):
        ref = far_ref if r % 2 else near_ref
        g = jnp.bitwise_xor(info[0], r)
        a, b = g // 2, lax.rem(g, 2)
        block = wide(ref[r // 2])
        across = pl.ds(aligned(b * 384, 128), 384)
        w2_s[pl.ds(aligned(a * 192, 64), 192), across] = block[0:192]
        for h in range(2):
            at = pl.ds(aligned(g * 768 + 384 * h, 128), 384)
            wi_s[:, at] = block[208 + 96 * h : 304 + 96 * h]
        wo_s[pl.ds(aligned(a * 48, 16), 48), across] = block[400:448]
        for t in range(3):
            at = pl.ds(aligned(24 * g + 8 * t, 8), 8)
            wp_s[at, :] = block[192:200, 128 * t : 128 * t + 128]
    copies = start_copies(
        [(wi_s, wi_out), (w2_s, w2_out), (wo_s, wo_out), (wp_s, wp_out)], sems
    )
    home_s[...] = (own_ref[...] + wide(came_ref[0]) + wide(passed_ref[...])).astype(BF)
    for kind, ref in enumerate((q_s, k_s, v_s)):
        parts = [wide(heads_ref[g, :, 192 * kind : 192 * kind + 192]) for g in range(4)]
        ref[...] = jnp.concatenate(parts, axis=1)
    for i, pair in enumerate(((q_s, q_out), (k_s, k_out), (v_s, v_out), (home_s, home_out))):
        copy = pltpu.make_async_copy(*pair, sems.at[4 + i])
        copy.start()
        copies.append(copy)
    side = sum(wide(heads_ref[g, :, 512:640]) for g in range(4))
    tall = jnp.concatenate([side, jnp.zeros((32, 128), F32)], axis=0).T
    for i in range(8):
        vec_outs[i][...] = tall[64 + i : 65 + i, :96]
    last = jnp.concatenate([tall[72 + i : 73 + i, :96] for i in range(4)], axis=1)
    vec_outs[8][...] = last.reshape(384)
    for copy in copies:
        copy.wait()


def pair_index(info, keep, x, yr):
    xr = jnp.bitwise_xor(info[0] // 2, x)
    order = jnp.bitwise_xor(lax.rem(info[0], 2), keep)
    first = jnp.where(order == 0, xr, yr)
    second = jnp.where(order == 0, yr, xr)
    return first, second


def outer_pack_kernel(info, active_ref, do_ref, second_ref, dp_ref, keep_ref, send_ref, proj_s):
    core = lax.rem(info[0], 2)
    proj_s[...] = tn(second_ref[...], dp_ref[...])
    for f in range(8):
        yr, z0, z1 = spots(info, f)
        left = active_ref[:, 384 * f : 384 * f + 384]
        for k, ref in ((0, keep_ref), (1, send_ref)):
            half = jnp.bitwise_xor(core, k)
            right = do_ref[:, pl.ds(aligned(half * 384, 128), 384)]
            value = tn(left, right).astype(BF)
            for x in range(2):
                a, b = pair_index(info, k, x, yr)
                ref[a, b, z0, z1, 0:192, :] = value[192 * x : 192 * x + 192]
                start = 96 * f + 24 * (2 * x + half)
                across = jnp.concatenate(
                    [proj_s[pl.ds(aligned(start + 8 * g, 8), 8), :] for g in range(3)], axis=1
                )
                ref[a, b, z0, z1, 192:208, :] = jnp.concatenate(
                    [across, jnp.zeros((8, 384), F32)], axis=0
                ).astype(BF)


def inner_pack_kernel(info, first_ref, di_ref, keep_ref, send_ref):
    core = lax.rem(info[0], 2)
    for k, ref in ((0, keep_ref), (1, send_ref)):
        half = jnp.bitwise_xor(core, k)
        for x in range(2):
            for part in range(2):
                start = (2 * x + half) * 768 + 384 * part
                right = di_ref[:, pl.ds(aligned(start, 128), 384)]
                value = tn(first_ref[...], right).astype(BF)
                for f in range(8):
                    yr, z0, z1 = spots(info, f)
                    a, b = pair_index(info, k, x, yr)
                    ref[a, b, z0, z1, 96 * part : 96 * part + 96, :] = value[96 * f : 96 * f + 96]


def output_pack_kernel(info, context_ref, da_ref, keep_ref, send_ref):
    c = info[0]
    for k, ref in ((0, keep_ref), (1, send_ref)):
        half = jnp.bitwise_xor(lax.rem(c, 2), k)
        right = da_ref[:, pl.ds(aligned(half * 384, 128), 384)]
        for r in range(4):
            value = tn(context_ref[:, 256 * r : 256 * r + 256], right).astype(BF)
            for t in range(2):
                yr, z0, z1 = spots(info, 2 * jnp.bitwise_xor(c, r) + t)
                for x in range(2):
                    a, b = pair_index(info, k, x, yr)
                    start = 96 * t + 48 * x
                    ref[a, b, z0, z1] = value[start : start + 48]


def fast_device(
    tokens,
    dealt,
    segments,
    query_weight,
    key_weight,
    value_weight,
    query_bias,
    value_bias,
    output_weight,
    output_bias,
    first_gain,
    first_shift,
    inner_weight,
    inner_bias,
    outer_weight,
    outer_bias,
    second_gain,
    second_shift,
    project_weight,
    cotangent,
):
    c = lax.axis_index("ctx")
    f = lax.axis_index("fsdp")
    core = lax.rem(c, 2)
    total = segments.shape[1]
    x = tokens[0]

    place = jnp.stack([c, f, c * 0, c * 0]).astype(jnp.int32)
    (info,) = run(
        places_kernel, "places", place, [segments], [((24,), jnp.int32)], small=True
    )

    vectors = (
        query_bias,
        value_bias,
        output_bias,
        first_gain,
        first_shift,
        outer_bias,
        second_gain,
        second_shift,
    )
    (heads_pack,) = run(
        prepare_heads_kernel,
        "prepare_heads",
        place,
        [query_weight, key_weight, value_weight]
        + [vector.reshape(1, 96) for vector in vectors]
        + [inner_bias],
        [((96, 640), BF)],
        [pltpu.VMEM(query_weight.shape, BF)] * 3
        + [pltpu.VMEM((1, 96), BF)] * 8
        + [pltpu.VMEM((384,), BF), pltpu.SemaphoreType.DMA((12,))],
        limit=60,
        loose=range(12),
    )
    outer_pack, inner_pack = run(
        prepare_forward_kernel,
        "prepare_forward",
        after(place, heads_pack),
        [inner_weight, output_weight, outer_weight, project_weight],
        [((96, 1664), BF), ((96, 1920), BF)],
        [pltpu.SemaphoreType.DMA((5,))],
        limit=60,
        loose=range(4),
    )
    x_core = to_core(x)
    x_next = to_x(x)
    moved = [along_z(heads_pack, k) for k in range(1, 4)]
    moved_y = [to_fsdp(heads_pack, 1)]
    x_core, x_next, heads_pack, inner_pack, outer_pack, info, moved_y[0], *moved = together(
        x_core, x_next, heads_pack, inner_pack, outer_pack, info, moved_y[0], *moved
    )
    x_cross = to_core(x_next)
    inner_pack, moved, x_cross = together(inner_pack, moved, x_cross)
    moved_y += [to_fsdp(piece, 1) for piece in moved]
    inner_1, inner_3 = along_z(inner_pack, 1), along_z(inner_pack, 3)
    x_cross, inner_pack, outer_pack, *moved_y = together(
        x_cross, inner_pack, outer_pack, *moved_y
    )
    pieces = []
    for one, two in zip((heads_pack, *moved), moved_y):
        pieces += [one, two]
    inner_2 = along_z(inner_pack, 2)
    inner_0y, outer_0y = to_fsdp(inner_pack, 1), to_fsdp(outer_pack, 1)

    heads = (LOCAL, total, 128)
    q, k, v, kt, vt, heads_weight, vec = run(
        project_kernel,
        "project",
        info,
        [x, x_core, x_next, after(x_cross, inner_pack), *pieces, segments],
        [
            (heads, BF),
            (heads, BF),
            (heads, BF),
            ((LOCAL, 64, total), BF),
            ((LOCAL, 80, total), BF),
            ((WIDTH, 640), BF),
            ((16, WIDTH), F32),
        ],
        [pltpu.SemaphoreType.DMA((8,))],
        limit=8,
        loose=range(4, 12),
    )
    q, inner_1, inner_3, inner_0y, outer_0y, outer_pack = together(
        q, inner_1, inner_3, inner_0y, outer_0y, outer_pack
    )
    inner_1y = to_fsdp(inner_1, 1)
    o_2, ql_2, pack_2, o_3, ql_3, pack_3 = attend_rows(
        info, after(q, inner_1), k, vt, cotangent[0], 1
    )
    pack_2, pack_3, inner_2, inner_1y, outer_pack, q = together(
        pack_2, pack_3, inner_2, inner_1y, outer_pack, q
    )
    inner_2y, inner_3y = to_fsdp(inner_2, 1), to_fsdp(after(inner_3, inner_2), 1)
    outer_1, outer_3, outer_2 = [along_z(outer_pack, k) for k in (1, 3, 2)]
    o_0, ql_0, pack_0, o_1, ql_1, pack_1 = attend_rows(info, q, k, vt, cotangent[0], 0)
    pack_0, pack_1, pack_2, pack_3, inner_2y, inner_3y, outer_1, outer_3 = together(
        pack_0, pack_1, pack_2, pack_3, inner_2y, inner_3y, outer_1, outer_3
    )
    from_x, from_cross = to_x(pack_2), to_cross(pack_3)
    outer_1y, outer_3y = to_fsdp(outer_1, 1), to_fsdp(outer_3, 1)
    inner_half, output_own = lay(
        info,
        [inner_pack, inner_0y, inner_1, inner_1y, inner_2, inner_2y, inner_3, inner_3y],
        (1536, 384),
    )
    from_x, from_cross, inner_half, output_own, pack_1, outer_1y, outer_2, outer_3y = together(
        from_x, from_cross, inner_half, output_own, pack_1, outer_1y, outer_2, outer_3y
    )
    outer_2y = to_fsdp(outer_2, 1)
    from_core = to_core(pack_1)
    output_other = to_core(output_own)
    (outer_own,) = run(
        stack_kernel,
        "stack",
        info,
        [outer_pack, outer_0y, outer_1, outer_1y, outer_2, outer_3, outer_3y],
        [((7, 96, 1664), BF)],
        [pltpu.SemaphoreType.DMA((7,))],
        loose=range(7),
    )
    from_core, output_other, outer_own = together(from_core, output_other, outer_own)
    inner_other = to_core(after(inner_half, from_core))
    outer_other = to_core(outer_own)
    (
        normal,
        inverse,
        first_low,
        active,
        slope,
        context,
        output_full,
        inner_full,
        arrived,
    ) = run(
        inner_own_kernel,
        "inner_own",
        info,
        [
            x,
            pack_0,
            from_core,
            from_x,
            from_cross,
            vec,
            output_own,
            output_other,
            inner_half,
        ],
        [
            ((ROWS, WIDTH), F32),
            ((ROWS, 1), F32),
            ((ROWS, WIDTH), BF),
            ((ROWS, HIDDEN), BF),
            ((ROWS, HIDDEN), BF),
            ((ROWS, 1024), BF),
            ((1024, WIDTH), BF),
            ((WIDTH, HIDDEN), BF),
            ((ROWS, 128), BF),
        ],
        [pltpu.SemaphoreType.DMA((1,))],
        loose=(8,),
    )
    first_low, inner_other, outer_2y, outer_other = together(
        first_low, inner_other, outer_2y, outer_other
    )
    outer_last = to_core(outer_2y)
    active, slope, inner_full, outer_full = run(
        inner_other_kernel,
        "inner_other",
        info,
        [first_low, vec, inner_other, outer_own, outer_other, active, slope, inner_full],
        [
            ((ROWS, HIDDEN), BF),
            ((ROWS, HIDDEN), BF),
            ((WIDTH, HIDDEN), BF),
            ((HIDDEN, WIDTH), BF),
        ],
        [pltpu.SemaphoreType.DMA((29,))],
        loose=(2, 3, 4),
        alias=((5, 0), (6, 1), (7, 2)),
    )
    residual_two, delta_outer, second_low, delta_projected, given, outer_sums, outer_full = run(
        outer_kernel,
        "outer",
        info,
        [
            active,
            outer_own,
            outer_2y,
            outer_last,
            normal,
            vec,
            dealt,
            arrived,
            outer_full,
        ],
        [
            ((ROWS, WIDTH), F32),
            ((ROWS, WIDTH), BF),
            ((ROWS, WIDTH), BF),
            ((ROWS, 128), BF),
            ((ROWS, 128), BF),
            ((8, WIDTH), F32),
            ((HIDDEN, WIDTH), BF),
        ],
        [pltpu.VMEM((WIDTH, 128), BF), pltpu.SemaphoreType.DMA((12,))],
        loose=(1, 2, 3),
        alias=((8, 6),),
    )
    keep_o, send_o = run(
        outer_pack_kernel,
        "outer_pack",
        info,
        [active, delta_outer, second_low, delta_projected],
        [((2, 2, 2, 2, 208, 384), BF)] * 2,
        [pltpu.VMEM((WIDTH, 128), F32)],
    )
    core_o = to_core(send_o)
    delta_inner, inner_side = run(
        hidden_back_kernel,
        "hidden_back",
        info,
        [after(delta_outer, send_o), outer_full, slope],
        [((ROWS, HIDDEN), BF), ((1, HIDDEN), F32)],
    )
    keep_i, send_i = run(
        inner_pack_kernel,
        "inner_pack",
        info,
        [first_low, delta_inner],
        [((2, 2, 2, 2, 192, 384), BF)] * 2,
    )
    core_o, delta_inner, inner_side, keep_i, send_i = together(
        core_o, delta_inner, inner_side, keep_i, send_i
    )

    core_i = to_core(send_i)
    give_o = added([keep_o[1], core_o[1]])
    one_o = to_mixed(give_o, True)
    residual_one, delta_attended, first_sums, *ups = run(
        first_kernel,
        "first",
        info,
        [
            after(delta_inner, give_o),
            inner_full,
            residual_two,
            normal,
            inverse,
            vec,
            output_full,
            given,
        ],
        [((ROWS, WIDTH), F32), ((ROWS, WIDTH), BF), ((8, WIDTH), F32)] + [((896, 128), BF)] * 4,
    )
    core_i, delta_attended, up_0, *ups = together(core_i, delta_attended, *ups)
    ups = [to_core(ups[0]), to_x(ups[1]), to_cross(ups[2])]
    keep_w, send_w = run(
        output_pack_kernel,
        "output_pack",
        info,
        [context, delta_attended],
        [((2, 2, 2, 2, 48, 384), BF)] * 2,
    )
    core_w = to_core(send_w)
    keys = (k, kt, v)
    dq_0, dk, dv = attend_back(info, 0, after(ql_0, send_w), up_0, o_0, *keys)
    dq_1, dk, dv = attend_back(info, 1, ql_1, ups[0], o_1, *keys, (dk, dv))
    one_o, core_w, dq_0, dq_1, dk, dv, *ups = together(one_o, core_w, dq_0, dq_1, dk, dv, *ups)

    give_i = jnp.concatenate([added([keep_i[1], core_i[1]]), added([keep_w[1], core_w[1]])], axis=3)
    one_i = to_mixed(give_i, True)
    give_o = added([keep_o[0, 1], core_o[0, 1], one_o[1]])
    two_o = to_mixed(give_o, False)
    dq_2, dk, dv = attend_back(
        info, 2, after(ql_2, give_i, give_o), ups[1], o_2, *keys, (dk, dv)
    )
    delta_heads, embedded, own, for_core, for_next, _, _ = attend_back(
        info,
        3,
        ql_3,
        ups[2],
        o_3,
        *keys,
        (dk, dv),
        (dq_0, dq_1, dq_2, up_0, *ups[:2], heads_weight, residual_one),
    )
    one_i, two_o, delta_heads, embedded, own, for_core, for_next = together(
        one_i, two_o, delta_heads, embedded, own, for_core, for_next
    )

    came = to_core(for_core)
    sum_i = [keep_i[0, 1], core_i[0, 1]], [keep_w[0, 1], core_w[0, 1]]
    give_i = added([jnp.concatenate(parts, axis=2) for parts in zip(*sum_i)] + [one_i[1]])
    two_i = to_mixed(give_i, False)
    sum_o = [keep_o[0, 0], core_o[0, 0], one_o[0], two_o]
    give_o = added([part[1] for part in sum_o])
    three_o = to_fsdp(give_o, 2)
    (pack,) = run(
        heads_grad_kernel,
        "heads_grad",
        info,
        [
            x,
            x_core,
            x_next,
            x_cross,
            after(delta_heads, give_i, give_o),
            first_sums,
            outer_sums,
            inner_side,
        ],
        [((2, 2, 2, 96, 640), BF)],
        limit=8,
    )
    two_i, three_o, pack, came = together(two_i, three_o, pack, came)

    one_h = to_fsdp(pack[1], 1)
    sum_i = [keep_i[0, 0], core_i[0, 0]], [keep_w[0, 0], core_w[0, 0]]
    sum_i = [jnp.concatenate(parts, axis=2) for parts in zip(*sum_i)] + [one_i[0], two_i]
    give_i = added([part[1] for part in sum_i])
    three_i = to_fsdp(give_i, 2)
    sum_o = [*(part[0] for part in sum_o), three_o]
    give_o = added([part[1] for part in sum_o])
    four_o = to_fsdp(give_o, 4)
    give_x = (for_next + wide(came[1])).astype(BF)
    passed = to_x(give_x)
    one_h, three_i, four_o = together(one_h, three_i, four_o)

    sum_i = [*(part[0] for part in sum_i), three_i]
    give_i = added([part[1] for part in sum_i])
    four_i = to_fsdp(give_i, 4)
    give_h = added([pack[0, 1], one_h[1]])
    two_h = to_fsdp(give_h, 2)
    four_i, two_h = together(four_i, two_h)

    give_h = added([pack[0, 0, 1], one_h[0, 1], two_h[1]])
    three_h = to_fsdp(give_h, 4)
    forward_sum = jnp.concatenate(
        [
            added([*(part[0] for part in sum_o), four_o]),
            added([*(part[0] for part in sum_i), four_i]),
        ],
        axis=0,
    )
    forward_next = to_x(forward_sum)
    three_h, passed, forward_next = together(three_h, passed, forward_next)
    mine = added([pack[0, 0, 0], one_h[0, 0], two_h[0], three_h])
    near = jnp.stack([forward_sum, forward_next])
    far = to_core(near)
    heads_all = lax.all_gather(after(mine, near), "ctx")
    square = (96, WIDTH)
    shapes = [
        ((96, HIDDEN), F32),
        ((384, WIDTH), F32),
        (square, F32),
        ((96, 128), F32),
        (square, F32),
        (square, F32),
        (square, F32),
        ((ROWS, WIDTH), BF),
    ]
    (
        inner_grad,
        outer_grad,
        output_grad,
        project_grad,
        query_grad,
        key_grad,
        value_grad,
        delta_home,
        *vec_all,
    ) = run(
        finish_kernel,
        "finish",
        info,
        [near, far, heads_all, own, came, passed],
        shapes + [((1, 96), F32)] * 8 + [((384,), F32)],
        [pltpu.VMEM(*shape) for shape in shapes] + [pltpu.SemaphoreType.DMA((8,))],
        limit=20,
        loose_outs=range(8),
    )
    return (
        embedded[None],
        delta_home[None],
        query_grad,
        key_grad,
        value_grad,
        vec_all[0].reshape(96),
        vec_all[1].reshape(96),
        output_grad,
        vec_all[2].reshape(96),
        vec_all[3].reshape(96),
        vec_all[4].reshape(96),
        inner_grad,
        vec_all[8],
        outer_grad,
        vec_all[5].reshape(96),
        vec_all[6].reshape(96),
        vec_all[7].reshape(96),
        project_grad,
    )


def suits(mesh):
    return mesh.shape["ctx"] == 4 and mesh.shape["fsdp"] == 8


def solution(mesh):
    on_device = fast_device if suits(mesh) else generic_device

    return jax.shard_map(
        on_device,
        mesh=mesh,
        in_specs=(
            P("fsdp", "ctx", None),
            P("fsdp", None),
            P("fsdp", None),
            P("fsdp", None),
            P("fsdp", None),
            P("fsdp", None),
            P("fsdp"),
            P("fsdp"),
            P("fsdp", None),
            P("fsdp"),
            P("fsdp"),
            P("fsdp"),
            P("fsdp", None),
            P("fsdp"),
            P("fsdp", None),
            P("fsdp"),
            P("fsdp"),
            P("fsdp"),
            P("fsdp", None),
            P("fsdp", "ctx", None),
        ),
        out_specs=(
            P("fsdp", "ctx", None),
            P("fsdp", "ctx", None),
            P("fsdp", None),
            P("fsdp", None),
            P("fsdp", None),
            P("fsdp"),
            P("fsdp"),
            P("fsdp", None),
            P("fsdp"),
            P("fsdp"),
            P("fsdp"),
            P("fsdp", None),
            P("fsdp"),
            P("fsdp", None),
            P("fsdp"),
            P("fsdp"),
            P("fsdp"),
            P("fsdp", None),
        ),
        check_vma=False,
    )
```

```python
import functools

import jax
import jax.numpy as jnp
from jax import lax
from jax.experimental import pallas as pl
from jax.experimental.pallas import tpu as pltpu
from jax.sharding import PartitionSpec as P

HEADS = 12
HEAD_DIM = 64


def matmul(left, right):
    return jnp.dot(left, right, preferred_element_type=jnp.float32)


def norm_forward(value, gain, shift):
    centred = value - jnp.mean(value, axis=-1, keepdims=True)
    inverse = lax.rsqrt(jnp.mean(centred * centred, axis=-1, keepdims=True) + 1e-12)
    normal = centred * inverse
    return (normal * gain + shift, normal, inverse)


def norm_backward(upstream, normal, inverse, gain):
    scaled = upstream * gain
    first_mean = jnp.mean(scaled, axis=-1, keepdims=True)
    second_mean = jnp.mean(scaled * normal, axis=-1, keepdims=True)
    inward = inverse * (scaled - first_mean - normal * second_mean)
    return (inward, jnp.sum(upstream * normal, axis=0), jnp.sum(upstream, axis=0))


def gelu_slope(value):
    cumulative = 0.5 * (1.0 + jax.scipy.special.erf(value * 0.7071067811865476))
    return cumulative + value * jnp.exp(-0.5 * value * value) * 0.3989422804014327


def scored(query_heads, key_block, query_segments, segment_block, scale):
    scores = (
        jnp.einsum("qhd,khd->hqk", query_heads, key_block, preferred_element_type=jnp.float32)
        * scale
    )
    allowed = (query_segments[:, None] == segment_block[None, :])[None]
    return (scores, allowed)


def probabilities(scores, allowed, log_total):
    return jnp.where(allowed, jnp.exp(scores - log_total[..., None]), 0.0)


def log_totals(query_heads, key_blocks, query_segments, segment_blocks, scale):

    def log_advance(carry, pieces):
        running_max, running_sum = carry
        scores, allowed = scored(query_heads, pieces[0], query_segments, pieces[1], scale)
        masked = jnp.where(allowed, scores, -1e30)
        new_max = jnp.maximum(running_max, jnp.max(masked, axis=-1))
        fresh = jnp.sum(jnp.where(allowed, jnp.exp(masked - new_max[..., None]), 0.0), axis=-1)
        return ((new_max, running_sum * jnp.exp(running_max - new_max) + fresh), None)

    shape = (query_heads.shape[1], query_heads.shape[0])
    start = (jnp.full(shape, -1e30, jnp.float32), jnp.zeros(shape, jnp.float32))
    final = lax.scan(log_advance, start, (key_blocks, segment_blocks))[0]
    return final[0] + jnp.log(final[1])


def attend(query_heads, key_blocks, value_blocks, query_segments, segment_blocks, scale):
    log_total = log_totals(query_heads, key_blocks, query_segments, segment_blocks, scale)

    def attend_advance(carry, pieces):
        scores, allowed = scored(query_heads, pieces[0], query_segments, pieces[2], scale)
        probs = probabilities(scores, allowed, log_total).astype(jnp.bfloat16)
        return (
            carry
            + jnp.einsum("hqk,khd->qhd", probs, pieces[1], preferred_element_type=jnp.float32),
            None,
        )

    start = jnp.zeros(query_heads.shape, jnp.float32)
    mixed = lax.scan(attend_advance, start, (key_blocks, value_blocks, segment_blocks))[0]
    return (mixed, log_total)


def attend_backward(
    query_heads,
    key_blocks,
    value_blocks,
    query_segments,
    segment_blocks,
    scale,
    log_total,
    upstream,
):

    def first_pass(carry, pieces):
        scores, allowed = scored(query_heads, pieces[0], query_segments, pieces[2], scale)
        probs = probabilities(scores, allowed, log_total)
        delta_probs = jnp.einsum(
            "qhd,khd->hqk", upstream, pieces[1], preferred_element_type=jnp.float32
        )
        value_terms = jnp.einsum(
            "hqk,qhd->khd", probs.astype(jnp.bfloat16), upstream, preferred_element_type=jnp.float32
        )
        return (carry + jnp.sum(probs * delta_probs, axis=-1), value_terms)

    shape = (query_heads.shape[1], query_heads.shape[0])
    weighted, value_terms = lax.scan(
        first_pass, jnp.zeros(shape, jnp.float32), (key_blocks, value_blocks, segment_blocks)
    )

    def second_pass(carry, pieces):
        scores, allowed = scored(query_heads, pieces[0], query_segments, pieces[2], scale)
        probs = probabilities(scores, allowed, log_total)
        delta_probs = jnp.einsum(
            "qhd,khd->hqk", upstream, pieces[1], preferred_element_type=jnp.float32
        )
        delta_scores = (probs * (delta_probs - weighted[..., None])).astype(jnp.bfloat16)
        key_terms = jnp.einsum(
            "hqk,qhd->khd", delta_scores, query_heads, preferred_element_type=jnp.float32
        )
        return (
            carry
            + jnp.einsum(
                "hqk,khd->qhd", delta_scores, pieces[0], preferred_element_type=jnp.float32
            ),
            key_terms,
        )

    query_terms, key_terms = lax.scan(
        second_pass,
        jnp.zeros(query_heads.shape, jnp.float32),
        (key_blocks, value_blocks, segment_blocks),
    )
    return (query_terms * scale, key_terms * scale, value_terms)


def generic_device(
    tokens,
    dealt,
    segments,
    query_weight,
    key_weight,
    value_weight,
    query_bias,
    value_bias,
    output_weight,
    output_bias,
    first_gain,
    first_shift,
    inner_weight,
    inner_bias,
    outer_weight,
    outer_bias,
    second_gain,
    second_shift,
    project_weight,
    cotangent,
):
    peers = lax.axis_size("ctx")
    place = lax.axis_index("ctx")
    local_rows = tokens.shape[1]
    share = local_rows // peers
    order = dealt[0]
    table = (
        lax.dynamic_index_in_dim(order.reshape(peers, peers, share), place, 1, keepdims=False)
        - place * local_rows
    )
    flat_table = table.reshape(-1)
    home_tokens = tokens[0]
    width = home_tokens.shape[1]
    (
        query_full,
        key_full,
        value_full,
        output_full,
        query_shift,
        value_shift,
        output_shift,
        gain_one,
        shift_one,
    ) = (
        lax.all_gather(query_weight, "fsdp", axis=0, tiled=True),
        lax.all_gather(key_weight, "fsdp", axis=0, tiled=True),
        lax.all_gather(value_weight, "fsdp", axis=0, tiled=True),
        lax.all_gather(output_weight, "fsdp", axis=0, tiled=True),
        lax.all_gather(query_bias, "fsdp", axis=0, tiled=True),
        lax.all_gather(value_bias, "fsdp", axis=0, tiled=True),
        lax.all_gather(output_bias, "fsdp", axis=0, tiled=True),
        lax.all_gather(first_gain, "fsdp", axis=0, tiled=True),
        lax.all_gather(first_shift, "fsdp", axis=0, tiled=True),
    )
    outgoing = jnp.take(home_tokens, table, axis=0)
    here_tokens = lax.all_to_all(outgoing, "ctx", split_axis=0, concat_axis=0, tiled=True).reshape(
        local_rows, width
    )
    key_segments = jnp.take(segments[0], order, axis=0)
    query_segments = lax.dynamic_slice_in_dim(key_segments, place * local_rows, local_rows)
    queries = (matmul(here_tokens, query_full) + query_shift.astype(jnp.float32)).astype(
        jnp.bfloat16
    )
    own_keys = matmul(here_tokens, key_full).astype(jnp.bfloat16)
    own_values = (matmul(here_tokens, value_full) + value_shift.astype(jnp.float32)).astype(
        jnp.bfloat16
    )
    all_keys, all_values = (
        lax.all_gather(own_keys, "ctx", axis=0, tiled=True),
        lax.all_gather(own_values, "ctx", axis=0, tiled=True),
    )
    total = all_keys.shape[0]
    block = min(1024, total)
    count = total // block
    scale = HEAD_DIM ** (-0.5)
    query_heads = queries.reshape(local_rows, HEADS, HEAD_DIM)
    key_blocks = all_keys.reshape(count, block, HEADS, HEAD_DIM)
    value_blocks = all_values.reshape(count, block, HEADS, HEAD_DIM)
    segment_blocks = key_segments.reshape(count, block)
    mixed, log_total = attend(
        query_heads, key_blocks, value_blocks, query_segments, segment_blocks, scale
    )
    context = mixed.reshape(local_rows, width).astype(jnp.bfloat16)
    inner_full, inner_shift, outer_full, outer_shift, gain_two, shift_two, project_full = (
        lax.all_gather(inner_weight, "fsdp", axis=0, tiled=True),
        lax.all_gather(inner_bias, "fsdp", axis=0, tiled=True),
        lax.all_gather(outer_weight, "fsdp", axis=0, tiled=True),
        lax.all_gather(outer_bias, "fsdp", axis=0, tiled=True),
        lax.all_gather(second_gain, "fsdp", axis=0, tiled=True),
        lax.all_gather(second_shift, "fsdp", axis=0, tiled=True),
        lax.all_gather(project_weight, "fsdp", axis=0, tiled=True),
    )
    attended = matmul(context, output_full) + output_shift.astype(jnp.float32)
    first, first_normal, first_inverse = norm_forward(
        here_tokens.astype(jnp.float32) + attended,
        gain_one.astype(jnp.float32),
        shift_one.astype(jnp.float32),
    )
    first_low = first.astype(jnp.bfloat16)
    inner = matmul(first_low, inner_full) + inner_shift.astype(jnp.float32)
    active = jax.nn.gelu(inner, approximate=False).astype(jnp.bfloat16)
    outer = matmul(active, outer_full) + outer_shift.astype(jnp.float32)
    second, second_normal, second_inverse = norm_forward(
        first + outer, gain_two.astype(jnp.float32), shift_two.astype(jnp.float32)
    )
    second_low = second.astype(jnp.bfloat16)
    projected = matmul(second_low, project_full)
    inverse_length = lax.rsqrt(jnp.sum(projected * projected, axis=-1, keepdims=True) + 1e-06)
    normed = projected * inverse_length
    embedded = normed.astype(jnp.bfloat16)
    incoming = cotangent[0].astype(jnp.float32)
    along = jnp.sum(normed * incoming, axis=-1, keepdims=True)
    delta_projected = (inverse_length * (incoming - normed * along)).astype(jnp.bfloat16)
    project_delta = matmul(second_low.T, delta_projected)
    delta_second = matmul(delta_projected, project_full.T)
    residual_two, second_gain_delta, second_shift_delta = norm_backward(
        delta_second, second_normal, second_inverse, gain_two.astype(jnp.float32)
    )
    delta_outer = residual_two.astype(jnp.bfloat16)
    outer_bias_delta = jnp.sum(delta_outer, axis=0, dtype=jnp.float32)
    outer_delta = matmul(active.T, delta_outer)
    delta_active = matmul(delta_outer, outer_full.T)
    delta_inner = (delta_active * gelu_slope(inner)).astype(jnp.bfloat16)
    inner_bias_delta = jnp.sum(delta_inner, axis=0, dtype=jnp.float32)
    inner_delta = matmul(first_low.T, delta_inner)
    delta_first = residual_two + matmul(delta_inner, inner_full.T)
    residual_one, first_gain_delta, first_shift_delta = norm_backward(
        delta_first, first_normal, first_inverse, gain_one.astype(jnp.float32)
    )
    delta_attended = residual_one.astype(jnp.bfloat16)
    output_bias_delta = jnp.sum(delta_attended, axis=0, dtype=jnp.float32)
    output_delta = matmul(context.T, delta_attended)
    delta_context = matmul(delta_attended, output_full.T).astype(jnp.bfloat16)
    upstream = delta_context.reshape(local_rows, HEADS, HEAD_DIM)
    query_terms, key_terms, value_terms = attend_backward(
        query_heads,
        key_blocks,
        value_blocks,
        query_segments,
        segment_blocks,
        scale,
        log_total,
        upstream,
    )
    key_sums, value_sums = (
        lax.psum_scatter(
            key_terms.reshape(total, width).astype(jnp.bfloat16),
            "ctx",
            scatter_dimension=0,
            tiled=True,
        ).astype(jnp.float32),
        lax.psum_scatter(
            value_terms.reshape(total, width).astype(jnp.bfloat16),
            "ctx",
            scatter_dimension=0,
            tiled=True,
        ).astype(jnp.float32),
    )
    delta_keys = key_sums.astype(jnp.bfloat16)
    delta_values = value_sums.astype(jnp.bfloat16)
    delta_queries = query_terms.reshape(local_rows, width).astype(jnp.bfloat16)
    query_bias_delta = jnp.sum(delta_queries, axis=0, dtype=jnp.float32)
    value_bias_delta = jnp.sum(delta_values, axis=0, dtype=jnp.float32)
    query_delta = matmul(here_tokens.T, delta_queries)
    key_delta = matmul(here_tokens.T, delta_keys)
    value_delta = matmul(here_tokens.T, delta_values)
    delta_here = (
        residual_one
        + matmul(delta_queries, query_full.T)
        + matmul(delta_keys, key_full.T)
        + matmul(delta_values, value_full.T)
    ).astype(jnp.bfloat16)
    coming_home = lax.all_to_all(
        delta_here.reshape(peers, share, width), "ctx", split_axis=0, concat_axis=0, tiled=True
    )
    delta_home = (
        jnp.zeros((local_rows, width), jnp.bfloat16)
        .at[flat_table]
        .set(coming_home.reshape(local_rows, width))
    )
    (
        inner_part,
        inner_bias_part,
        outer_part,
        outer_bias_part,
        second_gain_part,
        second_shift_part,
        project_part,
    ) = (
        lax.psum_scatter(
            inner_delta.astype(jnp.bfloat16), "fsdp", scatter_dimension=0, tiled=True
        ).astype(jnp.float32),
        lax.psum_scatter(
            inner_bias_delta.astype(jnp.bfloat16), "fsdp", scatter_dimension=0, tiled=True
        ).astype(jnp.float32),
        lax.psum_scatter(
            outer_delta.astype(jnp.bfloat16), "fsdp", scatter_dimension=0, tiled=True
        ).astype(jnp.float32),
        lax.psum_scatter(
            outer_bias_delta.astype(jnp.bfloat16), "fsdp", scatter_dimension=0, tiled=True
        ).astype(jnp.float32),
        lax.psum_scatter(
            second_gain_delta.astype(jnp.bfloat16), "fsdp", scatter_dimension=0, tiled=True
        ).astype(jnp.float32),
        lax.psum_scatter(
            second_shift_delta.astype(jnp.bfloat16), "fsdp", scatter_dimension=0, tiled=True
        ).astype(jnp.float32),
        lax.psum_scatter(
            project_delta.astype(jnp.bfloat16), "fsdp", scatter_dimension=0, tiled=True
        ).astype(jnp.float32),
    )
    (
        query_part,
        key_part,
        value_part,
        query_bias_part,
        value_bias_part,
        output_part,
        output_bias_part,
        first_gain_part,
        first_shift_part,
    ) = (
        lax.psum_scatter(
            query_delta.astype(jnp.bfloat16), "fsdp", scatter_dimension=0, tiled=True
        ).astype(jnp.float32),
        lax.psum_scatter(
            key_delta.astype(jnp.bfloat16), "fsdp", scatter_dimension=0, tiled=True
        ).astype(jnp.float32),
        lax.psum_scatter(
            value_delta.astype(jnp.bfloat16), "fsdp", scatter_dimension=0, tiled=True
        ).astype(jnp.float32),
        lax.psum_scatter(
            query_bias_delta.astype(jnp.bfloat16), "fsdp", scatter_dimension=0, tiled=True
        ).astype(jnp.float32),
        lax.psum_scatter(
            value_bias_delta.astype(jnp.bfloat16), "fsdp", scatter_dimension=0, tiled=True
        ).astype(jnp.float32),
        lax.psum_scatter(
            output_delta.astype(jnp.bfloat16), "fsdp", scatter_dimension=0, tiled=True
        ).astype(jnp.float32),
        lax.psum_scatter(
            output_bias_delta.astype(jnp.bfloat16), "fsdp", scatter_dimension=0, tiled=True
        ).astype(jnp.float32),
        lax.psum_scatter(
            first_gain_delta.astype(jnp.bfloat16), "fsdp", scatter_dimension=0, tiled=True
        ).astype(jnp.float32),
        lax.psum_scatter(
            first_shift_delta.astype(jnp.bfloat16), "fsdp", scatter_dimension=0, tiled=True
        ).astype(jnp.float32),
    )
    results = (
        lax.psum(query_part.astype(jnp.bfloat16), "ctx").astype(jnp.float32),
        lax.psum(key_part.astype(jnp.bfloat16), "ctx").astype(jnp.float32),
        lax.psum(value_part.astype(jnp.bfloat16), "ctx").astype(jnp.float32),
        lax.psum(query_bias_part.astype(jnp.bfloat16), "ctx").astype(jnp.float32),
        lax.psum(value_bias_part.astype(jnp.bfloat16), "ctx").astype(jnp.float32),
        lax.psum(output_part.astype(jnp.bfloat16), "ctx").astype(jnp.float32),
        lax.psum(output_bias_part.astype(jnp.bfloat16), "ctx").astype(jnp.float32),
        lax.psum(first_gain_part.astype(jnp.bfloat16), "ctx").astype(jnp.float32),
        lax.psum(first_shift_part.astype(jnp.bfloat16), "ctx").astype(jnp.float32),
        lax.psum(inner_part.astype(jnp.bfloat16), "ctx").astype(jnp.float32),
        lax.psum(inner_bias_part.astype(jnp.bfloat16), "ctx").astype(jnp.float32),
        lax.psum(outer_part.astype(jnp.bfloat16), "ctx").astype(jnp.float32),
        lax.psum(outer_bias_part.astype(jnp.bfloat16), "ctx").astype(jnp.float32),
        lax.psum(second_gain_part.astype(jnp.bfloat16), "ctx").astype(jnp.float32),
        lax.psum(second_shift_part.astype(jnp.bfloat16), "ctx").astype(jnp.float32),
        lax.psum(project_part.astype(jnp.bfloat16), "ctx").astype(jnp.float32),
    )
    return (
        embedded[None],
        delta_home[None],
        results[0],
        results[1],
        results[2],
        results[3],
        results[4],
        results[5],
        results[6],
        results[7],
        results[8],
        results[9],
        results[10],
        results[11],
        results[12],
        results[13],
        results[14],
        results[15],
    )


BF = jnp.bfloat16
F32 = jnp.float32
ROWS = 512
HALF = 256
WIDTH = 768
HIDDEN = 3072
LOCAL = 3
FAR = 2.0**100
KROWS = 256
SCALE = HEAD_DIM ** (-0.5)


def nt(left, right):
    return lax.dot_general(left, right, (((1,), (1,)), ((), ())), preferred_element_type=F32)


def nn(left, right):
    return lax.dot_general(left, right, (((1,), (0,)), ((), ())), preferred_element_type=F32)


def tn(left, right):
    return lax.dot_general(left, right, (((0,), (0,)), ((), ())), preferred_element_type=F32)


def wide(value):
    return value.astype(F32)


def to_core(value):
    return lax.ppermute(value, "ctx", [(i, i ^ 1) for i in range(4)])


def to_x(value):
    return lax.ppermute(value, "ctx", [(i, i ^ 2) for i in range(4)])


def to_cross(value):
    return lax.ppermute(value, "ctx", [(i, i ^ 3) for i in range(4)])


def to_fsdp(value, bit):
    return lax.ppermute(value, "fsdp", [(i, i ^ bit) for i in range(8)])


def along_z(value, step):
    return lax.ppermute(value, "fsdp", [(i, (i + 2 * step) % 8) for i in range(8)])


def to_mixed(value, first):
    pairs = []
    for c in range(4):
        for f in range(8):
            target = (c ^ 2) * 8 + f if (c % 2 == 0) == first else c * 8 + (f ^ 1)
            pairs.append((c * 8 + f, target))
    return lax.ppermute(value, ("ctx", "fsdp"), pairs)


def after(value, *others):
    return lax.optimization_barrier((value, *others))[0]


def added(parts):
    total = wide(parts[0])
    for part in parts[1:]:
        total = total + wide(part)
    return total.astype(BF)


def together(*values):
    return lax.optimization_barrier(values)


def three_parts(value):
    high = wide(value.astype(BF))
    rest = value - high
    middle = wide(rest.astype(BF))
    return high, middle, rest - middle


def lanes_of(rows, n=128):
    return lax.broadcasted_iota(jnp.int32, (rows, n), 1)


def run(
    kernel, name, info, inputs, outs, scratch=(), limit=6, loose=(), loose_outs=(), alias=(), small=False
):
    memory = pl.BlockSpec(memory_space=pltpu.VMEM)
    outside = pl.BlockSpec(memory_space=pltpu.HBM)
    return pl.pallas_call(
        kernel,
        in_specs=[pl.BlockSpec(memory_space=pltpu.SMEM)]
        + [outside if i in loose else memory for i in range(len(inputs))],
        out_specs=[pl.BlockSpec(memory_space=pltpu.SMEM)]
        if small
        else [outside if i in loose_outs else memory for i in range(len(outs))],
        out_shape=[jax.ShapeDtypeStruct(s, t) for s, t in outs],
        scratch_shapes=list(scratch),
        input_output_aliases={i + 1: o for i, o in alias},
        compiler_params=pltpu.CompilerParams(vmem_limit_bytes=limit << 20),
        cost_estimate=pl.CostEstimate(flops=1000, bytes_accessed=1000, transcendentals=0),
        name=name,
    )(info, *inputs)


def start_copies(pairs, sems):
    copies = [pltpu.make_async_copy(a, b, sems.at[i]) for i, (a, b) in enumerate(pairs)]
    for copy in copies:
        copy.start()
    return copies


def aligned(value, n):
    return pl.multiple_of(value, n)


def piece_rows(info, n):
    z, y = info[1] // 2, lax.rem(info[1], 2)
    rows = []
    for k in range(4):
        source = lax.rem(z + 4 - k, 4)
        rows += [aligned((source * 2 + t) * n, 32) for t in (y, 1 - y)]
    return rows


def prepare_forward_kernel(info, wi_in, wo_in, w2_in, p_in, outer_out, inner_out, sems):
    core = lax.rem(info[0], 2)
    copies = start_copies(
        [
            (w2_in.at[pl.ds(aligned(core * 192, 64), 96)], outer_out.at[:, 0:768]),
            (w2_in.at[pl.ds(aligned(core * 192 + 96, 32), 96)], outer_out.at[:, 768:1536]),
            (p_in, outer_out.at[:, 1536:1664]),
            (wi_in.at[:, pl.ds(aligned(core * 1536, 512), 1536)], inner_out.at[:, 0:1536]),
            (wo_in.at[:, pl.ds(aligned(core * 384, 128), 384)], inner_out.at[:, 1536:1920]),
        ],
        sems,
    )
    for copy in copies:
        copy.wait()


def prepare_heads_kernel(info, *refs):
    ins, heads_out, held, sems = refs[:12], refs[12], refs[13:25], refs[25]
    c = info[0]
    copies = start_copies(zip(ins, held), sems)
    q_ref, k_ref, v_ref, *rows, last_ref = held
    for copy in copies:
        copy.wait()
    rows = [wide(ref[...]) for ref in rows]
    last = wide(last_ref[...]).reshape(1, 384)
    rows += [last[:, 96 * i : 96 * i + 96] for i in range(4)]
    rows = jnp.concatenate([*rows, jnp.zeros((116, 96), F32)], axis=0)
    rows = jnp.concatenate([rows, jnp.zeros((128, 32), F32)], axis=1)
    side = rows.T[:96, :64]
    for value in range(4):

        @pl.when(c == value)
        def _():
            at = slice(192 * value, 192 * value + 192)
            parts = [wide(ref[:, at]) for ref in (q_ref, k_ref, v_ref)]
            heads_out[...] = jnp.concatenate([*parts, side], axis=1).astype(BF)


def lay_kernel(info, *refs):
    pieces, outs, sems = refs[:8], refs[8:-1], refs[-1]
    pairs, start = [], 0
    for out in outs:
        stop = start + out.shape[1]
        for ref, row in zip(pieces, piece_rows(info, 96)):
            pairs.append((ref.at[:, start:stop], out.at[pl.ds(row, 96)]))
        start = stop
    copies = start_copies(pairs, sems)
    for copy in copies:
        copy.wait()


def lay(info, pieces, widths):
    return run(
        lay_kernel,
        "lay",
        info,
        pieces,
        [((WIDTH, n), BF) for n in widths],
        [pltpu.SemaphoreType.DMA((8 * len(widths),))],
        loose=range(8),
    )


def stack_kernel(info, *refs):
    pieces, out, sems = refs[:-2], refs[-2], refs[-1]
    copies = start_copies([(ref, out.at[i]) for i, ref in enumerate(pieces)], sems)
    for copy in copies:
        copy.wait()


def places_kernel(place, seg_ref, info_out):
    seg = wide(seg_ref[...])
    at = lanes_of(1, seg.shape[1])
    for i in range(4):
        info_out[i] = place[i]
        info_out[20 + i] = 0
    for i in range(8):
        start = jnp.sum(jnp.where(at == HALF * i, seg, 0.0))
        end = jnp.sum(jnp.where(at == HALF * i + HALF - 1, seg, 0.0))
        low = jnp.sum(jnp.where(seg < start, 1.0, 0.0)).astype(jnp.int32)
        high = jnp.sum(jnp.where(seg <= end, 1.0, 0.0)).astype(jnp.int32)
        info_out[4 + i] = low // KROWS
        info_out[12 + i] = (high + KROWS - 1) // KROWS


def project_kernel(info, *refs):
    x_refs, w_refs = refs[0:4], refs[4:12]
    seg_ref = refs[12]
    q_out, k_out, v_out, kt_out, vt_out, w_out, vec_out, sems = refs[13:]
    c = info[0]
    copies = start_copies(
        [(ref, w_out.at[pl.ds(row, 96)]) for ref, row in zip(w_refs, piece_rows(info, 96))], sems
    )
    for copy in copies:
        copy.wait()
    weights = w_out[...]
    turned = wide(weights[:, 512:640]).T
    vec_out[...] = turned[64:80]
    mine = pltpu.roll(turned[64:72], lax.rem(WIDTH - 192 * c, WIDTH), 1)
    gap = jnp.zeros((1, 192), F32)
    bias = jnp.concatenate([mine[0:1, :192], gap, mine[1:2, :192], gap[:, :64]], axis=1)
    lanes = lanes_of(ROWS)
    for r in range(4):
        rows = pl.ds(aligned(jnp.bitwise_xor(c, r) * ROWS, ROWS), ROWS)
        result = nn(x_refs[r][...], weights) + bias
        seg = seg_ref[:, pl.ds(aligned(jnp.bitwise_xor(c, r) * ROWS, ROWS), ROWS)]
        same = jnp.broadcast_to(wide(seg), (128, ROWS)).T == wide(lanes - 64)
        qa = jnp.where(same & (lanes < 67), 1.0, 0.0)
        ka = jnp.where(lanes < 67, jnp.where(same, 0.0, -FAR), jnp.where(lanes < 70, 1.0, 0.0))
        for slot in range(9):
            pair = result[:, 128 * (slot // 2) : 128 * (slot // 2) + 128]
            if slot % 2:
                pair = pltpu.roll(pair, 64, 1)
            kind, h = slot // 3, slot % 3
            if kind == 0:
                low = wide(pair.astype(BF)) * SCALE
                q_out[h, rows, :] = jnp.where(lanes < 64, low, qa).astype(BF)
            elif kind == 1:
                value = jnp.where(lanes < 64, pair, ka)
                k_out[h, rows, :] = value.astype(BF)
                kt_out[h, :, rows] = value.T[:64].astype(BF)
            else:
                value = jnp.where(lanes < 64, pair, jnp.where(lanes < 67, 1.0, 0.0))
                v_out[h, rows, :] = value.astype(BF)
                vt_out[h, :, rows] = value.T[:80].astype(BF)


def over_keys(info, place, step):
    low_0, low_1 = info[4 + 2 * place], info[5 + 2 * place]
    high_0, high_1 = info[12 + 2 * place], info[13 + 2 * place]
    stop = jnp.maximum(high_0, low_1)
    pairs = (stop - low_1) // 2

    def loop(start, count, width, rows):
        def body(i, carry):
            at = aligned((start + i * (width // KROWS)) * KROWS, KROWS)
            step(pl.ds(at, width), rows)
            return carry

        lax.fori_loop(0, count, body, 0)

    loop(low_0, jnp.minimum(low_1, high_0) - low_0, KROWS, slice(0, HALF))
    loop(low_1, pairs, 2 * KROWS, slice(0, ROWS))
    loop(low_1 + 2 * pairs, stop - low_1 - 2 * pairs, KROWS, slice(0, ROWS))
    loop(stop, high_1 - stop, KROWS, slice(HALF, ROWS))


def attend_kernel(info, q_ref, k_ref, vt_ref, cot_ref, *refs, chip):
    each = range(LOCAL)
    top_s, sum_s, q_s = refs[6:]
    for step in range(2):
        o_ref, ql_ref, pack_ref = refs[3 * step : 3 * step + 3]
        place = jnp.bitwise_xor(info[0], step + 2 * chip)
        mine = pl.ds(aligned(place * ROWS, ROWS), ROWS)
        q_s[...] = q_ref[:, mine]
        top_s[...] = jnp.full_like(top_s, -3e38)
        sum_s[...] = jnp.zeros_like(sum_s)

        def advance(rows, part):
            scores = [nt(k_ref[h, rows], q_s[h, part]) for h in each]
            before = [top_s[h, :1, part] for h in each]
            peaks = [
                jnp.maximum(before[h], jnp.max(scores[h], axis=0, keepdims=True)) for h in each
            ]
            probs = [jnp.exp(scores[h] - peaks[h]).astype(BF) for h in each]
            shrink = [jnp.exp(before[h] - peaks[h]) for h in each]
            fresh = [nn(vt_ref[h, :, rows], probs[h]) for h in each]
            for h in each:
                sum_s[h, :, part] = sum_s[h, :, part] * shrink[h] + fresh[h]
                top_s[h, :, part] = jnp.broadcast_to(peaks[h], (8, peaks[h].shape[1]))

        over_keys(info, place, advance)
        lanes = lanes_of(ROWS)
        subs = lax.broadcasted_iota(jnp.int32, (128, ROWS), 0)
        outs = []
        for h in each:
            sums = sum_s[h]
            total = sums[64:65]
            parts = three_parts(top_s[h, :1] + jnp.log(total))
            tall = jnp.concatenate([sums[:64] / total, jnp.zeros((64, ROWS), F32)], axis=0)
            for i in range(3):
                tall = jnp.where(subs == 67 + i, -parts[i], tall)
            turned = tall.T
            out = jnp.where(lanes < 64, turned, 0.0)
            outs.append(out)
            o_ref[h] = out.astype(BF)
            ql_ref[h] = jnp.where(lanes < 67, wide(q_s[h]), turned).astype(BF)
        pack_ref[0:512] = (outs[0] + pltpu.roll(outs[1], 64, 1)).astype(BF)
        pack_ref[512:768] = (outs[2][:256] + pltpu.roll(outs[2][256:], 64, 1)).astype(BF)
        pack_ref[768:896] = cot_ref[pl.ds(aligned(place * 128, 128), 128), :]


def attend_rows(info, q, k, vt, cotangent, chip):
    return run(
        functools.partial(attend_kernel, chip=chip),
        "attend_rows",
        info,
        [q, k, vt, cotangent],
        ([((LOCAL, ROWS, 128), BF)] * 2 + [((896, 128), BF)]) * 2,
        [
            pltpu.VMEM((LOCAL, 8, ROWS), F32),
            pltpu.VMEM((LOCAL, 80, ROWS), F32),
            pltpu.VMEM((LOCAL, ROWS, 128), BF),
        ],
    )


def attend_back_kernel(info, *refs, r):
    each = range(LOCAL)
    ql_ref, up_ref, o_ref, k_ref, kt_ref, v_ref = refs[:6]
    *outs, dk_s, dv_s, dq_s, do_s = refs[6:]
    lanes = lanes_of(ROWS)
    if r == 0:
        (dq_ref,) = outs
        dk_s[...] = jnp.zeros_like(dk_s)
        dv_s[...] = jnp.zeros_like(dv_s)
    elif r < 3:
        _, _, dq_ref = outs
    else:
        w_ref, residual_ref, all_ref, emb_ref, *grads = outs[8:]
        for i, ref in enumerate((*outs[5:8], up_ref)):
            at = pl.ds(aligned(jnp.bitwise_xor(info[0], i) * 128, 128), 128)
            emb_ref[at, :] = ref[768:896]
    place = jnp.bitwise_xor(info[0], r)
    dq_s[...] = jnp.zeros_like(dq_s)
    pair = wide(up_ref[0:512])
    last = wide(up_ref[512:768])
    ups = [
        pair,
        pltpu.roll(pair, 64, 1),
        jnp.concatenate([last, pltpu.roll(last, 64, 1)], axis=0),
    ]
    for h in each:
        up = jnp.where(lanes < 64, ups[h], 0.0)
        parts = three_parts(jnp.sum(up * wide(o_ref[h]), axis=1, keepdims=True))
        for i in range(3):
            up = jnp.where(lanes == 64 + i, -parts[i], up)
        do_s[h] = up.astype(BF)

    def advance(rows, part):
        scores = [nt(k_ref[h, rows], ql_ref[h, part]) for h in each]
        rises = [nt(v_ref[h, rows], do_s[h, part]) for h in each]
        probs = [jnp.exp(scores[h]) for h in each]
        deltas = [(probs[h] * rises[h]).astype(BF) for h in each]
        lows = [probs[h].astype(BF) for h in each]
        for_values = [nn(lows[h], do_s[h, part]) for h in each]
        for_keys = [nn(deltas[h], ql_ref[h, part]) for h in each]
        for_queries = [nn(kt_ref[h, :, rows], deltas[h]) for h in each]
        for h in each:
            dv_s[h, rows] += for_values[h]
            dk_s[h, rows] += for_keys[h]
            dq_s[h, :, part] += for_queries[h]

    over_keys(info, place, advance)
    turned = []
    for h in each:
        tall = jnp.concatenate([dq_s[h], jnp.zeros((64, ROWS), F32)], axis=0)
        turned.append(tall.T * SCALE)
    both = (turned[0] + pltpu.roll(turned[1], 64, 1)).astype(BF)
    if r < 3:
        dq_ref[:, 0:128] = both
        dq_ref[:, 128:256] = turned[2].astype(BF)
        return
    mine = pl.ds(aligned(place * ROWS, ROWS), ROWS)
    all_ref[mine, 0:128] = both
    all_ref[mine, 128:256] = turned[2].astype(BF)
    for i, ref in enumerate(outs[2:5]):
        at = pl.ds(aligned(jnp.bitwise_xor(info[0], i) * ROWS, ROWS), ROWS)
        all_ref[at, 0:256] = ref[...]
    for b in range(4):
        rows = pl.ds(b * ROWS, ROWS)
        low = [jnp.where(lanes < 64, ref[h, rows], 0.0) for ref in (dk_s, dv_s) for h in each]
        high = [pltpu.roll(value, 64, 1) for value in low]
        all_ref[rows, 128:256] = (wide(all_ref[rows, 128:256]) + high[0]).astype(BF)
        all_ref[rows, 256:384] = (low[1] + high[2]).astype(BF)
        all_ref[rows, 384:512] = (low[3] + high[4]).astype(BF)
        all_ref[rows, 512:640] = low[5].astype(BF)
    input_grad(info, all_ref, w_ref, residual_ref, *grads)


def attend_back(info, r, ql, up, o, k, kt, v, carried=(), earlier=()):
    sums = [(k.shape, F32)] * 2
    part = [((ROWS, 256), BF)]
    whole = [
        ((k.shape[1], 640), BF),
        ((ROWS, 128), BF),
        ((ROWS, WIDTH), F32),
        ((2, ROWS, WIDTH), BF),
        ((ROWS, WIDTH), F32),
    ]
    first = len(part if r < 3 else whole)
    return run(
        functools.partial(attend_back_kernel, r=r),
        "attend_back",
        info,
        [ql, up, o, k, kt, v, *carried, *earlier],
        (part if r < 3 else whole) + sums,
        [pltpu.VMEM((LOCAL, 64, ROWS), F32), pltpu.VMEM((LOCAL, ROWS, 128), BF)],
        limit=9,
        alias=((6, first), (7, first + 1)) if r else (),
    )


def gaussian(value):
    below = 0.5 * (1.0 + lax.erf(value * 0.7071067811865476))
    return below, jnp.exp(-0.5 * value * value) * 0.3989422804014327


def norm_rows(value):
    centred = value - jnp.mean(value, axis=-1, keepdims=True)
    inverse = lax.rsqrt(jnp.mean(centred * centred, axis=-1, keepdims=True) + 1e-12)
    return centred * inverse, inverse


def norm_rows_back(upstream, normal, inverse, gain):
    scaled = upstream * gain
    first_mean = jnp.mean(scaled, axis=-1, keepdims=True)
    second_mean = jnp.mean(scaled * normal, axis=-1, keepdims=True)
    return inverse * (scaled - first_mean - normal * second_mean)


def column_sums(value):
    return jnp.sum(value, axis=0, keepdims=True)


def hidden_half(half, first, wi_ref, vec_ref, active_out, slope_out):
    shift = jnp.concatenate(
        [vec_ref[8 + k : 9 + k, 96 * f : 96 * f + 96] for f in range(8) for k in range(4)], axis=1
    )
    shift = jnp.where(half == 0, shift[:, :1536], shift[:, 1536:])
    for block in range(3):
        at = pl.ds(aligned(half * 1536 + block * 512, 512), 512)
        value = nn(first, wi_ref[:, at]) + shift[:, block * 512 : block * 512 + 512]
        below, bell = gaussian(value)
        active_out[:, at] = (value * below).astype(BF)
        slope_out[:, at] = (below + value * bell).astype(BF)


def inner_own_kernel(info, *refs):
    x_ref, *packs = refs[:5]
    vec_ref, wo_own, wo_other, g_ref = refs[5:9]
    (
        normal_out,
        inverse_out,
        first_out,
        active_out,
        slope_out,
        context_out,
        wo_out,
        wi_out,
        arrived_out,
        sems,
    ) = refs[9:]
    c = info[0]
    core = lax.rem(c, 2)
    own = pl.ds(aligned(core * 1536, 512), 1536)
    (copy,) = start_copies([(g_ref, wi_out.at[:, own])], sems)
    for r in range(4):
        group = jnp.bitwise_xor(c, r)
        arrived_out[pl.ds(aligned(group * 128, 128), 128), :] = packs[r][768:896]
        rows = pl.ds(aligned(group * 192, 64), 192)
        for half, ref in ((core, wo_own), (1 - core, wo_other)):
            at = pl.ds(aligned(half * 384, 128), 384)
            wo_out[256 * r : 256 * r + 192, at] = ref[rows, :]
        wo_out[256 * r + 192 : 256 * r + 256, :] = jnp.zeros((64, WIDTH), BF)
        context_out[:, 256 * r : 256 * r + 128] = packs[r][0:512]
        last = wide(packs[r][512:768])
        last = jnp.concatenate([last, pltpu.roll(last, 64, 1)], axis=0)
        context_out[:, 256 * r + 128 : 256 * r + 256] = jnp.where(
            lanes_of(ROWS) < 64, last, 0.0
        ).astype(BF)
    attended = nn(context_out[...], wo_out[...]) + vec_ref[2:3]
    normal, inverse = norm_rows(wide(x_ref[...]) + attended)
    normal_out[...] = normal
    inverse_out[...] = inverse
    first = (normal * vec_ref[3:4] + vec_ref[4:5]).astype(BF)
    first_out[...] = first
    copy.wait()
    hidden_half(core, first, wi_out, vec_ref, active_out, slope_out)


def outer_pairs(info, pieces, w2_out):
    core = lax.rem(info[0], 2)
    rows = piece_rows(info, 96)
    pairs = []
    for i, own, other in pieces:
        for half, piece in ((core, own), (1 - core, other)):
            for t in range(2):
                at = pl.ds(aligned(4 * rows[i] + 192 * half + 96 * t, 32), 96)
                pairs.append((piece.at[:, 768 * t : 768 * t + 768], w2_out.at[at]))
    return pairs


def inner_other_kernel(info, first_ref, vec_ref, g_ref, own_ref, other_ref, *refs):
    active_out, slope_out, wi_out, w2_out, sems = refs[3:]
    core = 1 - lax.rem(info[0], 2)
    other = pl.ds(aligned(core * 1536, 512), 1536)
    early = [(i, own_ref.at[i - (i > 5)], other_ref.at[i - (i > 5)]) for i in range(8) if i != 5]
    copies = start_copies(
        [(g_ref, wi_out.at[:, other])] + outer_pairs(info, early, w2_out), sems
    )
    copies[0].wait()
    hidden_half(core, first_ref[...], wi_out, vec_ref, active_out, slope_out)
    for copy in copies[1:]:
        copy.wait()


def outer_kernel(
    info,
    active_ref,
    own_ref,
    own_last_ref,
    other_last_ref,
    normal_ref,
    vec_ref,
    table_ref,
    arrived_ref,
    _,
    residual_out,
    do_out,
    second_out,
    dp_out,
    given_out,
    sums_out,
    w2_out,
    wp_ref,
    sems,
):
    pairs = outer_pairs(info, [(5, own_last_ref, other_last_ref)], w2_out)
    for i, row in enumerate(piece_rows(info, 96)):
        piece = own_last_ref if i == 5 else own_ref.at[i - (i > 5)]
        pairs.append((piece.at[:, 1536:1664], wp_ref.at[pl.ds(row, 96)]))
    copies = start_copies(pairs, sems)
    for copy in copies:
        copy.wait()
    outer = nn(active_ref[...], w2_out[...]) + vec_ref[5:6]
    first = normal_ref[...] * vec_ref[3:4] + vec_ref[4:5]
    normal, inverse = norm_rows(first + outer)
    second = (normal * vec_ref[6:7] + vec_ref[7:8]).astype(BF)
    second_out[...] = second
    projected = nn(second, wp_ref[...])
    scale = lax.rsqrt(jnp.sum(projected * projected, axis=-1, keepdims=True) + 1e-06)
    normed = projected * scale
    where = lax.broadcasted_iota(jnp.int32, (ROWS, ROWS), 0) + info[0] * ROWS
    table = jnp.concatenate(
        [table_ref[:, pl.ds(aligned(ROWS * d + info[0] * 128, 128), 128)] for d in range(4)],
        axis=1,
    )
    onehot = wide(table == where).astype(BF)
    given_out[...] = tn(onehot, normed.astype(BF)).astype(BF)
    incoming = nn(onehot, arrived_ref[...])
    along = jnp.sum(normed * incoming, axis=-1, keepdims=True)
    delta = (scale * (incoming - normed * along)).astype(BF)
    dp_out[...] = delta
    upstream = nt(delta, wp_ref[...])
    residual = norm_rows_back(upstream, normal, inverse, vec_ref[6:7])
    residual_out[...] = residual
    low = residual.astype(BF)
    do_out[...] = low
    sums_out[...] = jnp.concatenate(
        [
            column_sums(wide(low)),
            column_sums(upstream * normal),
            column_sums(upstream),
            jnp.zeros((5, WIDTH), F32),
        ],
        axis=0,
    )


def hidden_back_kernel(info, do_ref, w2_ref, slope_ref, di_out, side_out):
    for block in range(HIDDEN // 512):
        at = slice(block * 512, block * 512 + 512)
        value = nt(do_ref[...], w2_ref[at, :]) * wide(slope_ref[:, at])
        low = value.astype(BF)
        di_out[:, at] = low
        side_out[:, at] = column_sums(wide(low))


def first_kernel(
    info,
    di_ref,
    wi_ref,
    residual_ref,
    normal_ref,
    inverse_ref,
    vec_ref,
    wo_ref,
    given_ref,
    residual_out,
    da_out,
    sums_out,
    *up_outs,
):
    upstream = residual_ref[...] + nt(di_ref[...], wi_ref[...])
    normal = normal_ref[...]
    residual = norm_rows_back(upstream, normal, inverse_ref[...], vec_ref[3:4])
    residual_out[...] = residual
    low = residual.astype(BF)
    da_out[...] = low
    sums_out[...] = jnp.concatenate(
        [
            column_sums(wide(low)),
            column_sums(upstream * normal),
            column_sums(upstream),
            jnp.zeros((5, WIDTH), F32),
        ],
        axis=0,
    )
    for r in (2, 3, 1, 0):
        out = up_outs[r]
        up = nt(low, wo_ref[256 * r : 256 * r + 256, :])
        out[0:512] = up[:, 0:128].astype(BF)
        last = up[:, 128:256]
        out[512:768] = (last[:256] + pltpu.roll(last[256:], 64, 1)).astype(BF)
        place = jnp.bitwise_xor(info[0], r)
        out[768:896] = given_ref[pl.ds(aligned(place * 128, 128), 128), :]


def spots(info, f):
    mine = info[1]
    my_z, my_y = mine // 2, lax.rem(mine, 2)
    z, y = (f // 2, f % 2) if isinstance(f, int) else (f // 2, lax.rem(f, 2))
    apart = jnp.bitwise_xor(my_z, z)
    return jnp.bitwise_xor(my_y, y), lax.rem(apart, 2), apart // 2


def heads_grad_kernel(info, *refs):
    x_refs, (all_ref, first_ref, outer_ref, side_ref, pack_ref) = refs[:4], refs[4:]
    c = info[0]
    sums = column_sums(wide(all_ref[...]))
    pair = jnp.concatenate([sums[:, 0:192], sums[:, 384:576], jnp.zeros((6, 192), F32)], axis=0)
    pair = jnp.concatenate([pair, jnp.zeros((8, 576), F32)], axis=1)
    rows = [pltpu.roll(pair, 192 * c, 1)[0:2], first_ref[0:3], outer_ref[0:3]]
    for k in range(4):
        starts = [384 * f + 96 * k for f in range(8)]
        rows.append(jnp.concatenate([side_ref[:, i : i + 96] for i in starts], axis=1))
    vectors = jnp.concatenate([*rows, jnp.zeros((4, WIDTH), F32)], axis=0)
    tall = jnp.concatenate(
        [jnp.zeros((64, WIDTH), F32), vectors, jnp.zeros((48, WIDTH), F32)], axis=0
    )
    side = tall.T
    delta = jnp.zeros((WIDTH, 640), F32)
    for r, ref in enumerate(x_refs):
        at = pl.ds(aligned(jnp.bitwise_xor(c, r) * ROWS, ROWS), ROWS)
        delta = delta + tn(ref[...], all_ref[at, :])
    for f in range(8):
        i, j, k = spots(info, f)
        piece = delta[96 * f : 96 * f + 96]
        pack_ref[i, j, k, :, 0:512] = piece[:, :512].astype(BF)
        pack_ref[i, j, k, :, 512:640] = (piece[:, 512:] + side[96 * f : 96 * f + 96]).astype(BF)


def input_grad(info, all_ref, w_ref, residual_ref, own_ref, core_ref, next_ref):
    for r in (1, 3, 2, 0):
        rows = pl.ds(aligned(jnp.bitwise_xor(info[0], r) * ROWS, ROWS), ROWS)
        value = nt(all_ref[rows, :], w_ref[...])
        if r == 0:
            own_ref[...] = residual_ref[...] + value
        elif r == 2:
            next_ref[...] = value
        else:
            core_ref[r // 2] = value.astype(BF)


def finish_kernel(info, near_ref, far_ref, heads_ref, own_ref, came_ref, passed_ref, *refs):
    wi_out, w2_out, wo_out, wp_out, q_out, k_out, v_out, home_out = refs[:8]
    vec_outs = refs[8:17]
    wi_s, w2_s, wo_s, wp_s, q_s, k_s, v_s, home_s, sems = refs[17:]
    for r in range(4):
        ref = far_ref if r % 2 else near_ref
        g = jnp.bitwise_xor(info[0], r)
        a, b = g // 2, lax.rem(g, 2)
        block = wide(ref[r // 2])
        across = pl.ds(aligned(b * 384, 128), 384)
        w2_s[pl.ds(aligned(a * 192, 64), 192), across] = block[0:192]
        for h in range(2):
            at = pl.ds(aligned(g * 768 + 384 * h, 128), 384)
            wi_s[:, at] = block[208 + 96 * h : 304 + 96 * h]
        wo_s[pl.ds(aligned(a * 48, 16), 48), across] = block[400:448]
        for t in range(3):
            at = pl.ds(aligned(24 * g + 8 * t, 8), 8)
            wp_s[at, :] = block[192:200, 128 * t : 128 * t + 128]
    copies = start_copies(
        [(wi_s, wi_out), (w2_s, w2_out), (wo_s, wo_out), (wp_s, wp_out)], sems
    )
    home_s[...] = (own_ref[...] + wide(came_ref[0]) + wide(passed_ref[...])).astype(BF)
    for kind, ref in enumerate((q_s, k_s, v_s)):
        parts = [wide(heads_ref[g, :, 192 * kind : 192 * kind + 192]) for g in range(4)]
        ref[...] = jnp.concatenate(parts, axis=1)
    for i, pair in enumerate(((q_s, q_out), (k_s, k_out), (v_s, v_out), (home_s, home_out))):
        copy = pltpu.make_async_copy(*pair, sems.at[4 + i])
        copy.start()
        copies.append(copy)
    side = sum(wide(heads_ref[g, :, 512:640]) for g in range(4))
    tall = jnp.concatenate([side, jnp.zeros((32, 128), F32)], axis=0).T
    for i in range(8):
        vec_outs[i][...] = tall[64 + i : 65 + i, :96]
    last = jnp.concatenate([tall[72 + i : 73 + i, :96] for i in range(4)], axis=1)
    vec_outs[8][...] = last.reshape(384)
    for copy in copies:
        copy.wait()


def pair_index(info, keep, x, yr):
    xr = jnp.bitwise_xor(info[0] // 2, x)
    order = jnp.bitwise_xor(lax.rem(info[0], 2), keep)
    first = jnp.where(order == 0, xr, yr)
    second = jnp.where(order == 0, yr, xr)
    return first, second


def outer_pack_kernel(info, active_ref, do_ref, second_ref, dp_ref, keep_ref, send_ref, proj_s):
    core = lax.rem(info[0], 2)
    proj_s[...] = tn(second_ref[...], dp_ref[...])
    for f in range(8):
        yr, z0, z1 = spots(info, f)
        left = active_ref[:, 384 * f : 384 * f + 384]
        for k, ref in ((0, keep_ref), (1, send_ref)):
            half = jnp.bitwise_xor(core, k)
            right = do_ref[:, pl.ds(aligned(half * 384, 128), 384)]
            value = tn(left, right).astype(BF)
            for x in range(2):
                a, b = pair_index(info, k, x, yr)
                ref[a, b, z0, z1, 0:192, :] = value[192 * x : 192 * x + 192]
                start = 96 * f + 24 * (2 * x + half)
                across = jnp.concatenate(
                    [proj_s[pl.ds(aligned(start + 8 * g, 8), 8), :] for g in range(3)], axis=1
                )
                ref[a, b, z0, z1, 192:208, :] = jnp.concatenate(
                    [across, jnp.zeros((8, 384), F32)], axis=0
                ).astype(BF)


def inner_pack_kernel(info, first_ref, di_ref, keep_ref, send_ref):
    core = lax.rem(info[0], 2)
    for k, ref in ((0, keep_ref), (1, send_ref)):
        half = jnp.bitwise_xor(core, k)
        for x in range(2):
            for part in range(2):
                start = (2 * x + half) * 768 + 384 * part
                right = di_ref[:, pl.ds(aligned(start, 128), 384)]
                value = tn(first_ref[...], right).astype(BF)
                for f in range(8):
                    yr, z0, z1 = spots(info, f)
                    a, b = pair_index(info, k, x, yr)
                    ref[a, b, z0, z1, 96 * part : 96 * part + 96, :] = value[96 * f : 96 * f + 96]


def output_pack_kernel(info, context_ref, da_ref, keep_ref, send_ref):
    c = info[0]
    for k, ref in ((0, keep_ref), (1, send_ref)):
        half = jnp.bitwise_xor(lax.rem(c, 2), k)
        right = da_ref[:, pl.ds(aligned(half * 384, 128), 384)]
        for r in range(4):
            value = tn(context_ref[:, 256 * r : 256 * r + 256], right).astype(BF)
            for t in range(2):
                yr, z0, z1 = spots(info, 2 * jnp.bitwise_xor(c, r) + t)
                for x in range(2):
                    a, b = pair_index(info, k, x, yr)
                    start = 96 * t + 48 * x
                    ref[a, b, z0, z1] = value[start : start + 48]


def fast_device(
    tokens,
    dealt,
    segments,
    query_weight,
    key_weight,
    value_weight,
    query_bias,
    value_bias,
    output_weight,
    output_bias,
    first_gain,
    first_shift,
    inner_weight,
    inner_bias,
    outer_weight,
    outer_bias,
    second_gain,
    second_shift,
    project_weight,
    cotangent,
):
    c = lax.axis_index("ctx")
    f = lax.axis_index("fsdp")
    core = lax.rem(c, 2)
    total = segments.shape[1]
    x = tokens[0]

    place = jnp.stack([c, f, c * 0, c * 0]).astype(jnp.int32)
    (info,) = run(
        places_kernel, "places", place, [segments], [((24,), jnp.int32)], small=True
    )

    vectors = (
        query_bias,
        value_bias,
        output_bias,
        first_gain,
        first_shift,
        outer_bias,
        second_gain,
        second_shift,
    )
    (heads_pack,) = run(
        prepare_heads_kernel,
        "prepare_heads",
        place,
        [query_weight, key_weight, value_weight]
        + [vector.reshape(1, 96) for vector in vectors]
        + [inner_bias],
        [((96, 640), BF)],
        [pltpu.VMEM(query_weight.shape, BF)] * 3
        + [pltpu.VMEM((1, 96), BF)] * 8
        + [pltpu.VMEM((384,), BF), pltpu.SemaphoreType.DMA((12,))],
        limit=60,
        loose=range(12),
    )
    outer_pack, inner_pack = run(
        prepare_forward_kernel,
        "prepare_forward",
        after(place, heads_pack),
        [inner_weight, output_weight, outer_weight, project_weight],
        [((96, 1664), BF), ((96, 1920), BF)],
        [pltpu.SemaphoreType.DMA((5,))],
        limit=60,
        loose=range(4),
    )
    x_core = to_core(x)
    x_next = to_x(x)
    moved = [along_z(heads_pack, k) for k in range(1, 4)]
    moved_y = [to_fsdp(heads_pack, 1)]
    x_core, x_next, heads_pack, inner_pack, outer_pack, info, moved_y[0], *moved = together(
        x_core, x_next, heads_pack, inner_pack, outer_pack, info, moved_y[0], *moved
    )
    x_cross = to_core(x_next)
    inner_pack, moved, x_cross = together(inner_pack, moved, x_cross)
    moved_y += [to_fsdp(piece, 1) for piece in moved]
    inner_1, inner_3 = along_z(inner_pack, 1), along_z(inner_pack, 3)
    x_cross, inner_pack, outer_pack, *moved_y = together(
        x_cross, inner_pack, outer_pack, *moved_y
    )
    pieces = []
    for one, two in zip((heads_pack, *moved), moved_y):
        pieces += [one, two]
    inner_2 = along_z(inner_pack, 2)
    inner_0y, outer_0y = to_fsdp(inner_pack, 1), to_fsdp(outer_pack, 1)

    heads = (LOCAL, total, 128)
    q, k, v, kt, vt, heads_weight, vec = run(
        project_kernel,
        "project",
        info,
        [x, x_core, x_next, after(x_cross, inner_pack), *pieces, segments],
        [
            (heads, BF),
            (heads, BF),
            (heads, BF),
            ((LOCAL, 64, total), BF),
            ((LOCAL, 80, total), BF),
            ((WIDTH, 640), BF),
            ((16, WIDTH), F32),
        ],
        [pltpu.SemaphoreType.DMA((8,))],
        limit=8,
        loose=range(4, 12),
    )
    q, inner_1, inner_3, inner_0y, outer_0y, outer_pack = together(
        q, inner_1, inner_3, inner_0y, outer_0y, outer_pack
    )
    inner_1y = to_fsdp(inner_1, 1)
    o_2, ql_2, pack_2, o_3, ql_3, pack_3 = attend_rows(
        info, after(q, inner_1), k, vt, cotangent[0], 1
    )
    pack_2, pack_3, inner_2, inner_1y, outer_pack, q = together(
        pack_2, pack_3, inner_2, inner_1y, outer_pack, q
    )
    inner_2y, inner_3y = to_fsdp(inner_2, 1), to_fsdp(after(inner_3, inner_2), 1)
    outer_1, outer_3, outer_2 = [along_z(outer_pack, k) for k in (1, 3, 2)]
    o_0, ql_0, pack_0, o_1, ql_1, pack_1 = attend_rows(info, q, k, vt, cotangent[0], 0)
    pack_0, pack_1, pack_2, pack_3, inner_2y, inner_3y, outer_1, outer_3 = together(
        pack_0, pack_1, pack_2, pack_3, inner_2y, inner_3y, outer_1, outer_3
    )
    from_x, from_cross = to_x(pack_2), to_cross(pack_3)
    outer_1y, outer_3y = to_fsdp(outer_1, 1), to_fsdp(outer_3, 1)
    inner_half, output_own = lay(
        info,
        [inner_pack, inner_0y, inner_1, inner_1y, inner_2, inner_2y, inner_3, inner_3y],
        (1536, 384),
    )
    from_x, from_cross, inner_half, output_own, pack_1, outer_1y, outer_2, outer_3y = together(
        from_x, from_cross, inner_half, output_own, pack_1, outer_1y, outer_2, outer_3y
    )
    outer_2y = to_fsdp(outer_2, 1)
    from_core = to_core(pack_1)
    output_other = to_core(output_own)
    (outer_own,) = run(
        stack_kernel,
        "stack",
        info,
        [outer_pack, outer_0y, outer_1, outer_1y, outer_2, outer_3, outer_3y],
        [((7, 96, 1664), BF)],
        [pltpu.SemaphoreType.DMA((7,))],
        loose=range(7),
    )
    from_core, output_other, outer_own = together(from_core, output_other, outer_own)
    inner_other = to_core(after(inner_half, from_core))
    outer_other = to_core(outer_own)
    (
        normal,
        inverse,
        first_low,
        active,
        slope,
        context,
        output_full,
        inner_full,
        arrived,
    ) = run(
        inner_own_kernel,
        "inner_own",
        info,
        [
            x,
            pack_0,
            from_core,
            from_x,
            from_cross,
            vec,
            output_own,
            output_other,
            inner_half,
        ],
        [
            ((ROWS, WIDTH), F32),
            ((ROWS, 1), F32),
            ((ROWS, WIDTH), BF),
            ((ROWS, HIDDEN), BF),
            ((ROWS, HIDDEN), BF),
            ((ROWS, 1024), BF),
            ((1024, WIDTH), BF),
            ((WIDTH, HIDDEN), BF),
            ((ROWS, 128), BF),
        ],
        [pltpu.SemaphoreType.DMA((1,))],
        loose=(8,),
    )
    first_low, inner_other, outer_2y, outer_other = together(
        first_low, inner_other, outer_2y, outer_other
    )
    outer_last = to_core(outer_2y)
    active, slope, inner_full, outer_full = run(
        inner_other_kernel,
        "inner_other",
        info,
        [first_low, vec, inner_other, outer_own, outer_other, active, slope, inner_full],
        [
            ((ROWS, HIDDEN), BF),
            ((ROWS, HIDDEN), BF),
            ((WIDTH, HIDDEN), BF),
            ((HIDDEN, WIDTH), BF),
        ],
        [pltpu.SemaphoreType.DMA((29,))],
        loose=(2, 3, 4),
        alias=((5, 0), (6, 1), (7, 2)),
    )
    residual_two, delta_outer, second_low, delta_projected, given, outer_sums, outer_full = run(
        outer_kernel,
        "outer",
        info,
        [
            active,
            outer_own,
            outer_2y,
            outer_last,
            normal,
            vec,
            dealt,
            arrived,
            outer_full,
        ],
        [
            ((ROWS, WIDTH), F32),
            ((ROWS, WIDTH), BF),
            ((ROWS, WIDTH), BF),
            ((ROWS, 128), BF),
            ((ROWS, 128), BF),
            ((8, WIDTH), F32),
            ((HIDDEN, WIDTH), BF),
        ],
        [pltpu.VMEM((WIDTH, 128), BF), pltpu.SemaphoreType.DMA((12,))],
        loose=(1, 2, 3),
        alias=((8, 6),),
    )
    keep_o, send_o = run(
        outer_pack_kernel,
        "outer_pack",
        info,
        [active, delta_outer, second_low, delta_projected],
        [((2, 2, 2, 2, 208, 384), BF)] * 2,
        [pltpu.VMEM((WIDTH, 128), F32)],
    )
    core_o = to_core(send_o)
    delta_inner, inner_side = run(
        hidden_back_kernel,
        "hidden_back",
        info,
        [after(delta_outer, send_o), outer_full, slope],
        [((ROWS, HIDDEN), BF), ((1, HIDDEN), F32)],
    )
    keep_i, send_i = run(
        inner_pack_kernel,
        "inner_pack",
        info,
        [first_low, delta_inner],
        [((2, 2, 2, 2, 192, 384), BF)] * 2,
    )
    core_o, delta_inner, inner_side, keep_i, send_i = together(
        core_o, delta_inner, inner_side, keep_i, send_i
    )

    core_i = to_core(send_i)
    give_o = added([keep_o[1], core_o[1]])
    one_o = to_mixed(give_o, True)
    residual_one, delta_attended, first_sums, *ups = run(
        first_kernel,
        "first",
        info,
        [
            after(delta_inner, give_o),
            inner_full,
            residual_two,
            normal,
            inverse,
            vec,
            output_full,
            given,
        ],
        [((ROWS, WIDTH), F32), ((ROWS, WIDTH), BF), ((8, WIDTH), F32)] + [((896, 128), BF)] * 4,
    )
    core_i, delta_attended, up_0, *ups = together(core_i, delta_attended, *ups)
    ups = [to_core(ups[0]), to_x(ups[1]), to_cross(ups[2])]
    keep_w, send_w = run(
        output_pack_kernel,
        "output_pack",
        info,
        [context, delta_attended],
        [((2, 2, 2, 2, 48, 384), BF)] * 2,
    )
    core_w = to_core(send_w)
    keys = (k, kt, v)
    dq_0, dk, dv = attend_back(info, 0, after(ql_0, send_w), up_0, o_0, *keys)
    dq_1, dk, dv = attend_back(info, 1, ql_1, ups[0], o_1, *keys, (dk, dv))
    one_o, core_w, dq_0, dq_1, dk, dv, *ups = together(one_o, core_w, dq_0, dq_1, dk, dv, *ups)

    give_i = jnp.concatenate([added([keep_i[1], core_i[1]]), added([keep_w[1], core_w[1]])], axis=3)
    one_i = to_mixed(give_i, True)
    give_o = added([keep_o[0, 1], core_o[0, 1], one_o[1]])
    two_o = to_mixed(give_o, False)
    dq_2, dk, dv = attend_back(
        info, 2, after(ql_2, give_i, give_o), ups[1], o_2, *keys, (dk, dv)
    )
    delta_heads, embedded, own, for_core, for_next, _, _ = attend_back(
        info,
        3,
        ql_3,
        ups[2],
        o_3,
        *keys,
        (dk, dv),
        (dq_0, dq_1, dq_2, up_0, *ups[:2], heads_weight, residual_one),
    )
    one_i, two_o, delta_heads, embedded, own, for_core, for_next = together(
        one_i, two_o, delta_heads, embedded, own, for_core, for_next
    )

    came = to_core(for_core)
    sum_i = [keep_i[0, 1], core_i[0, 1]], [keep_w[0, 1], core_w[0, 1]]
    give_i = added([jnp.concatenate(parts, axis=2) for parts in zip(*sum_i)] + [one_i[1]])
    two_i = to_mixed(give_i, False)
    sum_o = [keep_o[0, 0], core_o[0, 0], one_o[0], two_o]
    give_o = added([part[1] for part in sum_o])
    three_o = to_fsdp(give_o, 2)
    (pack,) = run(
        heads_grad_kernel,
        "heads_grad",
        info,
        [
            x,
            x_core,
            x_next,
            x_cross,
            after(delta_heads, give_i),
            first_sums,
            outer_sums,
            inner_side,
        ],
        [((2, 2, 2, 96, 640), BF)],
        limit=8,
    )
    two_i, three_o, pack, came = together(two_i, three_o, pack, came)

    one_h = to_fsdp(pack[1], 1)
    sum_i = [keep_i[0, 0], core_i[0, 0]], [keep_w[0, 0], core_w[0, 0]]
    sum_i = [jnp.concatenate(parts, axis=2) for parts in zip(*sum_i)] + [one_i[0], two_i]
    give_i = added([part[1] for part in sum_i])
    three_i = to_fsdp(give_i, 2)
    sum_o = [*(part[0] for part in sum_o), three_o]
    give_o = added([part[1] for part in sum_o])
    four_o = to_fsdp(give_o, 4)
    give_x = (for_next + wide(came[1])).astype(BF)
    passed = to_x(give_x)
    one_h, three_i, four_o = together(one_h, three_i, four_o)

    sum_i = [*(part[0] for part in sum_i), three_i]
    give_i = added([part[1] for part in sum_i])
    four_i = to_fsdp(give_i, 4)
    give_h = added([pack[0, 1], one_h[1]])
    two_h = to_fsdp(give_h, 2)
    four_i, two_h = together(four_i, two_h)

    give_h = added([pack[0, 0, 1], one_h[0, 1], two_h[1]])
    three_h = to_fsdp(give_h, 4)
    forward_sum = jnp.concatenate(
        [
            added([*(part[0] for part in sum_o), four_o]),
            added([*(part[0] for part in sum_i), four_i]),
        ],
        axis=0,
    )
    forward_next = to_x(forward_sum)
    three_h, passed, forward_next = together(three_h, passed, forward_next)
    mine = added([pack[0, 0, 0], one_h[0, 0], two_h[0], three_h])
    near = jnp.stack([forward_sum, forward_next])
    far = to_core(near)
    heads_all = lax.all_gather(after(mine, near), "ctx")
    square = (96, WIDTH)
    shapes = [
        ((96, HIDDEN), F32),
        ((384, WIDTH), F32),
        (square, F32),
        ((96, 128), F32),
        (square, F32),
        (square, F32),
        (square, F32),
        ((ROWS, WIDTH), BF),
    ]
    (
        inner_grad,
        outer_grad,
        output_grad,
        project_grad,
        query_grad,
        key_grad,
        value_grad,
        delta_home,
        *vec_all,
    ) = run(
        finish_kernel,
        "finish",
        info,
        [near, far, heads_all, own, came, passed],
        shapes + [((1, 96), F32)] * 8 + [((384,), F32)],
        [pltpu.VMEM(*shape) for shape in shapes] + [pltpu.SemaphoreType.DMA((8,))],
        limit=20,
        loose_outs=range(8),
    )
    return (
        embedded[None],
        delta_home[None],
        query_grad,
        key_grad,
        value_grad,
        vec_all[0].reshape(96),
        vec_all[1].reshape(96),
        output_grad,
        vec_all[2].reshape(96),
        vec_all[3].reshape(96),
        vec_all[4].reshape(96),
        inner_grad,
        vec_all[8],
        outer_grad,
        vec_all[5].reshape(96),
        vec_all[6].reshape(96),
        vec_all[7].reshape(96),
        project_grad,
    )


def suits(mesh):
    return mesh.shape["ctx"] == 4 and mesh.shape["fsdp"] == 8


def solution(mesh):
    on_device = fast_device if suits(mesh) else generic_device

    return jax.shard_map(
        on_device,
        mesh=mesh,
        in_specs=(
            P("fsdp", "ctx", None),
            P("fsdp", None),
            P("fsdp", None),
            P("fsdp", None),
            P("fsdp", None),
            P("fsdp", None),
            P("fsdp"),
            P("fsdp"),
            P("fsdp", None),
            P("fsdp"),
            P("fsdp"),
            P("fsdp"),
            P("fsdp", None),
            P("fsdp"),
            P("fsdp", None),
            P("fsdp"),
            P("fsdp"),
            P("fsdp"),
            P("fsdp", None),
            P("fsdp", "ctx", None),
        ),
        out_specs=(
            P("fsdp", "ctx", None),
            P("fsdp", "ctx", None),
            P("fsdp", None),
            P("fsdp", None),
            P("fsdp", None),
            P("fsdp"),
            P("fsdp"),
            P("fsdp", None),
            P("fsdp"),
            P("fsdp"),
            P("fsdp"),
            P("fsdp", None),
            P("fsdp"),
            P("fsdp", None),
            P("fsdp"),
            P("fsdp"),
            P("fsdp"),
            P("fsdp", None),
        ),
        check_vma=False,
    )
```
